256 devices in a mesh: wide: 32 (over y_lo, z, core), blk: 8 (over y_hi, x).
Axes of the slice: x: 4, y: 4 (y_hi: 2, y_lo: 2; y = y_hi * 2 + y_lo), z: 8, core: 2. Of those that a mesh axis runs over, the one named last changes fastest.
Arguments:
- records: bfloat16 [8, 2304, 4, 8192], P('blk', 'wide'), may hold values from -6 to 6
- lengths: int32 [8, 2304], P('blk', 'wide'), may hold values from 8192 to 32768
- owners: int32 [8, 2304], P('blk', 'wide'), may hold values from -1 to 767, as said below
- own_pick: int32 [8, 32, 8, 2, 4], P('blk', 'wide'), may hold values from 0 to 23
- visit_pick: int32 [8, 32, 8, 2, 4], P('blk', 'wide'), may hold values from 0 to 23
- pair_mask: int32 [8, 32, 8, 2, 4, 4], P('blk', 'wide'), may hold values 0 or 1
Outputs:
- correlations: float32 [8, 32, 8, 2, 4, 4, 1024], P('blk', 'wide')
The draws below stay inside these ranges and needn't reach their ends.
Inputs may be any that keep to these rules, and one draw needn't show every extreme that they name: `owners`: in each group every station number 0 to 767 is named by exactly one slot. A device's valid slots come first and its other slots hold -1. The busiest device of each group fills all 72 slots and two devices hold none. At most 3 slots of one device name stations of one owner (stations w * 24 to w * 24 + 23 belong to owner w), and this most is reached in every group.
All inputs are finite; a program needn't handle non-finite values. No bound on the sum of `pair_mask` on one device may be relied on, other than what follows from the above.
Results may differ from the reference program's by a relative error of at most 0.0049.
Values may be sent and summed in bfloat16 or wider, within the bound.
No kernel may reach another device: no remote copies, remote signals or barrier semaphores. Data moves between devices by JAX's collectives and lax.ppermute only.
A program may use at most 192 MiB of HBM per device.

```python
import math
import jax
import jax.numpy as jnp
from jax import lax

ST_DEV = 24
SEG = 4
P_SIZE = 64
NT = 8192
NF = 4096
LAGS = 1024
NB = 2
PB = 4
GROUP_ST = 768
IN_ALL = 2304
N_WIDE = 32
N_BLK = 8


def owner_group(key):
    korder, kpair, kshift = jax.random.split(key, 3)
    places = jnp.arange(N_WIDE, dtype=jnp.int32)
    base = jnp.where(places == 0, 3 * ST_DEV, jnp.where(places < 3, 0, ST_DEV))
    offset = jnp.maximum(places - 3, 0)
    paired = offset // 2
    spread = jax.random.randint(kpair, (N_WIDE,), 0, ST_DEV // 2 + 1)
    moved = spread[paired]
    signed = jnp.where(offset % 2 == 0, moved, -moved)
    partner = (places >= 3) & (3 + 2 * paired + 1 < N_WIDE)
    counts_place = (base + jnp.where(partner, signed, 0)).astype(jnp.int32)
    order = jax.random.permutation(korder, N_WIDE)
    counts = jnp.zeros((N_WIDE,), jnp.int32).at[order].set(counts_place)
    starts = jnp.cumsum(counts) - counts
    rotate = jax.random.randint(kshift, (), 0, N_WIDE)
    slots = jnp.arange(3 * ST_DEV, dtype=jnp.int32)
    units = starts[:, None] + slots[None, :]
    column = (units + rotate) % N_WIDE
    station = column * ST_DEV + units // N_WIDE
    return jnp.where(slots[None, :] < counts[:, None], station, -1).reshape(-1).astype(jnp.int32)


def draw_owners(key, part):
    key = jax.random.fold_in(key, 11)
    keys = jax.random.split(key, N_BLK)
    return jax.vmap(owner_group)(keys)


def plant(entries, key, smallest, largest):
    index_at = [jax.random.randint(jax.random.fold_in(key, axis), (), 0, length) for axis, length in enumerate(entries.shape)]
    main_axis = entries.shape.index(max(entries.shape))
    next_to = index_at[:main_axis] + [(index_at[main_axis] + 1) % entries.shape[main_axis]] + index_at[main_axis + 1:]
    return entries.at[tuple(index_at)].set(smallest).at[tuple(next_to)].set(largest)


def level_of(own_key, shape, cuts, low, high):
    gain, own = 1.0, jax.random.fold_in(own_key, 6)
    for axis_at, shards_of in cuts:
        steps = jnp.exp(jax.random.uniform(jax.random.fold_in(own, axis_at), (shards_of,), jnp.float32, low / len(cuts), high / len(cuts)))
        gain = gain * jnp.repeat(steps, shape[axis_at] // shards_of).reshape([-1 if axis == axis_at else 1 for axis in range(len(shape))])
    return gain


def normal_values(key, dims, scale, reach, cuts=(), held_as=jnp.bfloat16):
    values = scale * jax.random.normal(key, dims, jnp.float32)
    if cuts:
        values = values * level_of(key, dims, cuts, -0.22, 0.18)
    return jnp.clip(values, -reach, reach).astype(held_as)


def setup_inputs(seed: int = 0) -> dict:
    arg_keys = jax.random.split(jax.random.key(seed), 7)
    records = normal_values(arg_keys[0], (N_BLK, IN_ALL, SEG, NT), 1.0, 6.0, ((0, 8), (1, 32)))
    lengths = plant(jax.random.randint(arg_keys[1], (N_BLK, IN_ALL), SEG * NT // 4, SEG * NT + 1), jax.random.fold_in(arg_keys[1], 1), SEG * NT // 4, SEG * NT).astype(jnp.int32)
    owners = draw_owners(jax.random.fold_in(arg_keys[6], 71), 0)
    own_pick = plant(jax.random.randint(arg_keys[3], (N_BLK, N_WIDE, N_BLK, NB, PB), 0, ST_DEV), jax.random.fold_in(arg_keys[3], 1), 0, ST_DEV - 1).astype(jnp.int32)
    visit_pick = plant(jax.random.randint(arg_keys[4], (N_BLK, N_WIDE, N_BLK, NB, PB), 0, ST_DEV), jax.random.fold_in(arg_keys[4], 1), 0, ST_DEV - 1).astype(jnp.int32)
    pair_mask = plant((jax.random.randint(arg_keys[5], (N_BLK, N_WIDE, N_BLK, NB, PB, PB), 0, 4) < 3).astype(jnp.int32), jax.random.fold_in(arg_keys[5], 1), 0, 1)
    return dict(records=records, lengths=lengths, owners=owners, own_pick=own_pick, visit_pick=visit_pick, pair_mask=pair_mask)


def lag_table():
    bins = jnp.arange(NF, dtype=jnp.int32)
    delay = jnp.arange(LAGS, dtype=jnp.int32) - LAGS // 2
    phase = bins[:, None] * (delay % NT)[None, :] % NT
    angle = phase.astype(jnp.float32) * (2.0 * math.pi / NT)
    weight = jnp.where(bins == 0, 0.5, 1.0).astype(jnp.float32) / math.sqrt(NF * SEG)
    upper = weight[:, None] * jnp.cos(angle)
    lower = -weight[:, None] * jnp.sin(angle)
    return jnp.concatenate([upper, lower], 0).astype(jnp.bfloat16)

def reference(records, lengths, owners, own_pick, visit_pick, pair_mask):
    position = jnp.arange(SEG * NT, dtype=jnp.int32).reshape(SEG, NT)
    kept = jnp.where(position[None, None] < lengths[:, :, None, None], records, jnp.zeros((), records.dtype))
    target = jnp.where(owners >= 0, owners, GROUP_ST).astype(jnp.int32)
    groups = jnp.arange(N_BLK, dtype=jnp.int32)[:, None]
    owned = jnp.zeros((N_BLK, GROUP_ST + 1, SEG, NT), records.dtype).at[groups, target].set(kept)[:, :GROUP_ST]
    spectrum = jnp.fft.rfft(owned.astype(jnp.float32), axis=-1)[..., :NF]
    real_part = jnp.real(spectrum).reshape(N_BLK, GROUP_ST, SEG, NF // P_SIZE, P_SIZE)
    imag_part = jnp.imag(spectrum).reshape(N_BLK, GROUP_ST, SEG, NF // P_SIZE, P_SIZE)
    power = lax.optimization_barrier(jnp.mean(real_part * real_part + imag_part * imag_part, axis=-1, keepdims=True))
    norm_scale = jnp.sqrt(power + 1e-06)
    white = jnp.stack([real_part / norm_scale, imag_part / norm_scale], 3)
    white = white.reshape(N_BLK, GROUP_ST, SEG, 2, NF).astype(jnp.bfloat16)
    table = lag_table().astype(jnp.float32)

    def one_device(item):
        group = item // N_WIDE
        column = item % N_WIDE
        stops = jnp.arange(N_BLK, dtype=jnp.int32)
        visit_group = (group - stops) % N_BLK
        near = white[group][column * ST_DEV + own_pick[group, column]].astype(jnp.float32)
        far = white[visit_group[:, None, None], column * ST_DEV + visit_pick[group, column]].astype(jnp.float32)
        near_re = near[:, :, :, None, :, 0]
        near_im = near[:, :, :, None, :, 1]
        far_re = far[:, :, None, :, :, 0]
        far_im = far[:, :, None, :, :, 1]
        cross_re = lax.optimization_barrier(jnp.sum(near_re * far_re + near_im * far_im, axis=4))
        cross_im = lax.optimization_barrier(jnp.sum(near_im * far_re - near_re * far_im, axis=4))
        cross = jnp.stack([cross_re, cross_im], 4).astype(jnp.bfloat16)
        cross = lax.optimization_barrier(cross).astype(jnp.float32).reshape(N_BLK * NB * PB * PB, 2 * NF)
        lagged = jnp.dot(cross, table, precision=lax.Precision.HIGHEST).reshape(N_BLK, NB, PB, PB, LAGS)
        return lagged * pair_mask[group, column].astype(jnp.float32)[..., None]
    result = lax.map(one_device, jnp.arange(N_BLK * N_WIDE, dtype=jnp.int32))
    return result.reshape(N_BLK, N_WIDE, N_BLK, NB, PB, PB, LAGS)
```

```python
import functools
import math

import jax
import jax.numpy as jnp
import numpy as np
from jax import lax
from jax.experimental import pallas as pl
from jax.experimental.pallas import tpu as pltpu
from jax.sharding import PartitionSpec as P

ST_DEV = 24
SEG = 4
NT = 8192
NF = 4096
LAGS = 1024
ROWS = 64
LANES = 128
BASE = 4
EXTRA = 2
LEN_BITS = 16
SMEM = pl.BlockSpec(memory_space=pltpu.SMEM)
VMEM = pl.BlockSpec(memory_space=pltpu.VMEM)
ANY = pl.BlockSpec(memory_space=pl.ANY)


def split_bf16(values):
    high = values.astype(jnp.bfloat16)
    low = (values - high.astype(np.float64)).astype(jnp.bfloat16)
    return high, low


def transform_tables():
    first = np.arange(ROWS)
    second = np.arange(LANES)
    half = np.arange(LANES // 2)
    angle = 2.0 * math.pi / ROWS * (first[:, None] * first[None, :] % ROWS)
    wave = np.concatenate([np.cos(angle), -np.sin(angle)], 0)
    first_table = np.concatenate(split_bf16(wave), 1)
    twist = 2.0 * math.pi / NT * (first[:, None] * second[None, :] % NT)
    twist_table = np.stack([np.cos(twist), np.sin(twist)]).astype(np.float32)
    angle = 2.0 * math.pi / LANES * (second[:, None] * half[None, :] % LANES)
    cos, sin = np.cos(angle), np.sin(angle)
    wave = np.concatenate([np.concatenate([cos, -sin], 1), np.concatenate([sin, cos], 1)], 0)
    second_table = np.concatenate(split_bf16(wave), 1)
    return first_table, twist_table, second_table


def lag_table():
    bins = np.arange(NF, dtype=np.int64)
    delay = np.arange(LAGS, dtype=np.int64) - LAGS // 2
    phase = bins[:, None] * (delay % NT)[None, :] % NT
    angle = phase.astype(np.float32) * np.float32(2.0 * math.pi / NT)
    weight = np.where(bins == 0, 0.5, 1.0).astype(np.float32) / np.float32(math.sqrt(NF * SEG))
    upper = (weight[:, None] * np.cos(angle)).reshape(ROWS, ROWS, LAGS).transpose(1, 0, 2)
    lower = (-weight[:, None] * np.sin(angle)).reshape(ROWS, ROWS, LAGS).transpose(1, 0, 2)
    joined = np.concatenate([upper, lower], 1).astype(np.float32)
    return joined.reshape(ROWS * LANES, LAGS).astype(jnp.bfloat16)


def pack_kernel(part, low, count, packed, core_ref, own, mate, out, fill, sem):
    core = core_ref[0]
    slots = packed.shape[0] // 2

    @pl.loop(0, out.shape[0])
    def _(dev):
        fill[dev] = 0

    def place(at, started, half):
        value = packed[at + half * slots]
        valid = value >= 0
        dev = jnp.where(valid, value >> LEN_BITS, 0) // ST_DEV
        rank = fill[dev]
        fill[dev] = rank + valid.astype(jnp.int32)
        take = valid & (rank >= low) & (rank < low + count)

        @pl.when(take & (core == half))
        def _():
            pltpu.make_async_copy(own.at[at, 2 * core + part], out.at[dev, rank - low], sem).start()

        @pl.when(take & (core != half))
        def _():
            pltpu.make_async_copy(mate.at[at], out.at[dev, rank - low], sem).start()

        return started + take.astype(jnp.int32)

    started = lax.fori_loop(0, slots, functools.partial(place, half=0), 0)
    started = lax.fori_loop(0, slots, functools.partial(place, half=1), started)

    @pl.loop(0, started)
    def _(_):
        pltpu.make_async_copy(mate.at[0], out.at[0, 0], sem).wait()


def pack(part, low, count, wide_count, packed, core, own, mate):
    return pl.pallas_call(
        functools.partial(pack_kernel, part, low, count),
        out_shape=jax.ShapeDtypeStruct((wide_count, count, ROWS, LANES), jnp.bfloat16),
        in_specs=[SMEM, SMEM, ANY, ANY],
        out_specs=ANY,
        scratch_shapes=[pltpu.SMEM((wide_count,), jnp.int32), pltpu.SemaphoreType.DMA],
        cost_estimate=pl.CostEstimate(flops=0, bytes_accessed=wide_count * count * NT * 4, transcendentals=0),
        name="pack",
    )(packed, core, own, mate)


def whiten_kernel(
    part, source, length, picks, got, more, first, twist, second, white, payload, held, spectra, sem
):
    stations = held.shape[0]

    @pl.loop(0, stations)
    def _(station):
        code = source[station]
        over = code - 16 * BASE
        for core in range(2):

            @pl.when(over < 0)
            def _():
                pltpu.make_async_copy(
                    got.at[2 * (code // BASE) + core, code % BASE], held.at[station, core], sem
                ).start()

            @pl.when(over >= 0)
            def _():
                pltpu.make_async_copy(
                    more.at[2 * (over // EXTRA) + core, over % EXTRA], held.at[station, core], sem
                ).start()

    @pl.loop(0, 2 * stations)
    def _(_):
        pltpu.make_async_copy(got.at[0, 0], held.at[0, 0], sem).wait()

    row = lax.broadcasted_iota(jnp.int32, (ROWS, LANES), 0)
    place = row * LANES + lax.broadcasted_iota(jnp.int32, (ROWS, LANES), 1)

    def one_station(station):
        sides = []
        for core in range(2):
            bound = length[station] - (2 * core + part) * NT
            values = held[station, core].astype(jnp.float32)
            sides.append(jnp.where(place < bound, values, 0.0).astype(jnp.bfloat16))
        values = jnp.concatenate(sides, 1)
        values = jnp.concatenate([values, values], 0)
        mixed = jnp.dot(first[...], values, preferred_element_type=jnp.float32)
        parts = []
        for core in range(2):
            real = mixed[:ROWS, core * LANES : (core + 1) * LANES]
            imag = mixed[ROWS:, core * LANES : (core + 1) * LANES]
            turned_re = real * twist[0] + imag * twist[1]
            turned_im = imag * twist[0] - real * twist[1]
            parts.append(jnp.concatenate([turned_re, turned_im], 1))
        turned = jnp.concatenate(parts, 0)
        high = turned.astype(jnp.bfloat16)
        low = (turned - high.astype(jnp.float32)).astype(jnp.bfloat16)
        upper = jnp.dot(high, second[...], preferred_element_type=jnp.float32)
        lower = jnp.dot(low, second[:, :LANES], preferred_element_type=jnp.float32)
        spectrum = upper[:, :LANES] + (upper[:, LANES:] + lower)
        for core in range(2):
            side = spectrum[core * ROWS : (core + 1) * ROWS]
            power = jnp.sum(side * side, axis=0, keepdims=True)
            power = (power + pltpu.roll(power, LANES // 2, 1)) * (1.0 / ROWS)
            scale = 1.0 / jnp.sqrt(power + 1e-06)
            spectra[station, core] = (side * scale).astype(jnp.bfloat16)

    @pl.loop(0, stations // 2)
    def _(pair):
        one_station(2 * pair)
        one_station(2 * pair + 1)

    whole = pltpu.make_async_copy(spectra, white, sem)
    whole.start()
    stops, rows = picks.shape

    @pl.loop(0, stops)
    def _(stop):
        for at in range(rows):
            pltpu.make_async_copy(spectra.at[picks[stop, at]], payload.at[stop, at], sem).start()

    whole.wait()

    @pl.loop(0, stops * rows)
    def _(_):
        pltpu.make_async_copy(spectra.at[0], payload.at[0, 0], sem).wait()


def whiten(part, source, length, picks, got, more, tables):
    stops, rows = picks.shape
    return pl.pallas_call(
        functools.partial(whiten_kernel, part),
        out_shape=(
            jax.ShapeDtypeStruct((ST_DEV, 2, ROWS, LANES), jnp.bfloat16),
            jax.ShapeDtypeStruct((stops, rows, 2, ROWS, LANES), jnp.bfloat16),
        ),
        in_specs=[SMEM, SMEM, SMEM, ANY, ANY, VMEM, VMEM, VMEM],
        out_specs=(ANY, ANY),
        scratch_shapes=[
            pltpu.VMEM((ST_DEV, 2, ROWS, LANES), jnp.bfloat16),
            pltpu.VMEM((ST_DEV, 2, ROWS, LANES), jnp.bfloat16),
            pltpu.SemaphoreType.DMA,
        ],
        cost_estimate=pl.CostEstimate(
            flops=2 * ST_DEV * 2 * ROWS * 256 * 400, bytes_accessed=4 * 1024 * 1024, transcendentals=0
        ),
        name="whiten",
    )(source, length, picks, got, more, *tables)


def lag_kernel(stops, near_pick, far_at, *refs):
    white_a, white_b, home = refs[:3]
    far_a = refs[3 : 2 + stops]
    far_b, table, mask, out, near, far, cross, tables, sem, table_sem = refs[2 + stops :]
    rows = near_pick.shape[1]
    load_table = pltpu.make_async_copy(table, tables, table_sem)
    copies = [
        pltpu.make_async_copy(white_a, near.at[0], sem),
        pltpu.make_async_copy(white_b, near.at[1], sem),
        pltpu.make_async_copy(home.at[0], far.at[0, 0], sem),
    ]
    for stop in range(1, stops):
        copies.append(pltpu.make_async_copy(far_a[stop - 1], far.at[0, stop], sem))
    for stop in range(stops):
        copies.append(pltpu.make_async_copy(far_b.at[far_at[stop]], far.at[1, stop], sem))
    for copy in copies:
        copy.start()
    load_table.start()
    for copy in copies:
        copy.wait()
    step = 16
    side = rows // 2
    left = lax.broadcasted_iota(jnp.int32, (step, LANES), 1) < LANES // 2

    @pl.loop(0, stops * 2)
    def _(block):
        stop = block // 2
        first = (block % 2) * side
        own = [near_pick[stop, first + i] for i in range(side)]

        @pl.loop(0, ROWS // step)
        def _(chunk):
            band = pl.ds(pl.multiple_of(chunk * step, step), step)
            here = [
                [near[s % 2, own[i], s // 2, band, :].astype(jnp.float32) for s in range(SEG)]
                for i in range(side)
            ]
            for j in range(side):
                straight, crossed = [], []
                for s in range(SEG):
                    value = far[s % 2, stop, first + j, s // 2, band, :].astype(jnp.float32)
                    other = pltpu.roll(value, LANES // 2, 1)
                    straight.append(jnp.where(left, value, other))
                    crossed.append(jnp.where(left, -other, value))
                for i in range(side):
                    direct = here[i][0] * straight[0]
                    turned = here[i][0] * crossed[0]
                    for s in range(1, SEG):
                        direct += here[i][s] * straight[s]
                        turned += here[i][s] * crossed[s]
                    pair = (block * side + i) * side + j
                    cross[pl.ds(pl.multiple_of(pair * ROWS + chunk * step, step), step), :] = (
                        direct + pltpu.roll(turned, LANES // 2, 1)
                    )

    load_table.wait()
    pairs = stops * 2 * side * side
    group = 8
    out[...] = jnp.zeros_like(out)

    @pl.loop(0, ROWS // group)
    def _(at):
        slabs = [
            cross[pl.ds(at * group + k, pairs, stride=ROWS), :].astype(jnp.bfloat16) for k in range(group)
        ]
        depth = group * LANES
        out[...] += jnp.dot(
            jnp.concatenate(slabs, 1),
            tables[pl.ds(pl.multiple_of(at * depth, depth), depth), :],
            preferred_element_type=jnp.float32,
        )

    out[...] = out[...] * mask[...]


def lagged(near_pick, far_at, white_a, white_b, home, far_a, far_b, table, mask):
    stops, rows = near_pick.shape
    pairs = mask.shape[0]
    return pl.pallas_call(
        functools.partial(lag_kernel, stops),
        out_shape=jax.ShapeDtypeStruct((pairs, LAGS), jnp.float32),
        in_specs=[SMEM, SMEM] + [ANY] * (stops + 4) + [VMEM],
        out_specs=VMEM,
        scratch_shapes=[
            pltpu.VMEM((2, ST_DEV, 2, ROWS, LANES), jnp.bfloat16),
            pltpu.VMEM((2, stops, rows, 2, ROWS, LANES), jnp.bfloat16),
            pltpu.VMEM((pairs * ROWS, LANES), jnp.float32),
            pltpu.VMEM(table.shape, jnp.bfloat16),
            pltpu.SemaphoreType.DMA,
            pltpu.SemaphoreType.DMA,
        ],
        compiler_params=pltpu.CompilerParams(vmem_limit_bytes=48 * 1024 * 1024),
        cost_estimate=pl.CostEstimate(
            flops=2 * pairs * 2 * NF * LAGS, bytes_accessed=24 * 1024 * 1024, transcendentals=0
        ),
        name="lagged",
    )(near_pick, far_at, white_a, white_b, home, *far_a, far_b, table, mask)


def on_device(records, lengths, owners, own_pick, visit_pick, pair_mask):
    wide_count = lax.axis_size("wide")
    stops = lax.axis_size("blk")
    column = lax.axis_index("wide")
    group = lax.axis_index("blk")
    core = column % 2
    swap = [(i, i ^ 1) for i in range(wide_count)]
    slots = records.shape[1]

    packed = jnp.where(owners[0] >= 0, (owners[0] << LEN_BITS) + lengths[0], -1)
    mate_packed = lax.ppermute(packed, "wide", swap)
    all_packed = lax.all_gather(packed, "wide").reshape(wide_count // 2, 2 * slots)
    all_visits = lax.all_gather(visit_pick[0, 0].reshape(stops, -1), "blk")

    own = records[0].reshape(slots, SEG, ROWS, LANES)
    chip_packed = jnp.where(
        core == 0, jnp.concatenate([packed, mate_packed]), jnp.concatenate([mate_packed, packed])
    )
    core_at = core.reshape(1)
    mates = [
        lax.ppermute(lax.dynamic_index_in_dim(own, 2 * (1 - core) + part, 1, False), "wide", swap)
        for part in range(2)
    ]

    def deliver(low, count, part):
        payload = pack(part, low, count, wide_count, chip_packed, core_at, own, mates[part])
        return lax.all_to_all(payload, "wide", split_axis=0, concat_axis=0, tiled=True)

    got = [deliver(0, BASE, part) for part in range(2)]

    station = all_packed >> LEN_BITS
    owner_dev = station // ST_DEV
    everyone = jnp.arange(wide_count, dtype=jnp.int32)
    counts = jnp.sum((owner_dev[:, :, None] == everyone).astype(jnp.int32), axis=1)
    spilled = lax.pmax(jnp.max(counts), "blk") > BASE
    mine = owner_dev == column
    rank = jnp.cumsum(mine.astype(jnp.int32), axis=1) - 1
    chip = jnp.arange(wide_count // 2, dtype=jnp.int32)[:, None]
    code = jnp.where(rank < BASE, chip * BASE + rank, 16 * BASE + chip * EXTRA + rank - BASE)
    local = column * ST_DEV + jnp.arange(ST_DEV, dtype=jnp.int32)
    chosen = station[None] == local[:, None, None]
    source = jnp.sum(jnp.where(chosen, code[None], 0), axis=(1, 2))
    length = jnp.sum(jnp.where(chosen, (all_packed & ((1 << LEN_BITS) - 1))[None], 0), axis=(1, 2))

    more = lax.cond(
        spilled,
        lambda: tuple(deliver(BASE, EXTRA, part) for part in range(2)),
        lambda: tuple(jnp.zeros((wide_count, EXTRA, ROWS, LANES), jnp.bfloat16) for _ in range(2)),
    )

    steps = jnp.arange(stops, dtype=jnp.int32)
    by_stop = all_visits[(group + steps) % stops, steps]
    by_dest = all_visits[steps, (steps - group) % stops]
    tables = [jnp.asarray(table) for table in transform_tables()]

    white_a, payload_a = whiten(0, source, length, by_stop, got[0], more[0], tables)
    far_a = [
        lax.ppermute(payload_a[stop], "blk", [(i, (i + stop) % stops) for i in range(stops)])
        for stop in range(1, stops)
    ]
    white_b, payload_b = whiten(1, source, length, by_dest, got[1], more[1], tables)
    far_b = lax.all_to_all(payload_b, "blk", split_axis=0, concat_axis=0, tiled=True)

    near_pick = own_pick[0, 0].reshape(stops, -1)
    far_at = (group - steps) % stops
    mask = pair_mask[0, 0].astype(jnp.float32).reshape(-1, 1)
    result = lagged(near_pick, far_at, white_a, white_b, payload_a, far_a, far_b, jnp.asarray(lag_table()), mask)
    return result.reshape((1, 1) + pair_mask.shape[2:] + (LAGS,))


def solution(mesh):
    return jax.shard_map(
        on_device,
        mesh=mesh,
        in_specs=(
            P("blk", "wide", None, None),
            P("blk", "wide"),
            P("blk", "wide"),
            P("blk", "wide", None, None, None),
            P("blk", "wide", None, None, None),
            P("blk", "wide", None, None, None, None),
        ),
        out_specs=P("blk", "wide", None, None, None, None, None),
        check_vma=False,
    )
```

```python
import functools
import math

import jax
import jax.numpy as jnp
import numpy as np
from jax import lax
from jax.experimental import pallas as pl
from jax.experimental.pallas import tpu as pltpu
from jax.sharding import PartitionSpec as P

ST_DEV = 24
SEG = 4
NT = 8192
NF = 4096
LAGS = 1024
ROWS = 64
LANES = 128
BASE = 2
EXTRA = 1
LEN_BITS = 16
SMEM = pl.BlockSpec(memory_space=pltpu.SMEM)
VMEM = pl.BlockSpec(memory_space=pltpu.VMEM)
ANY = pl.BlockSpec(memory_space=pl.ANY)


def split_bf16(values):
    high = values.astype(jnp.bfloat16)
    low = (values - high.astype(np.float64)).astype(jnp.bfloat16)
    return high, low


def transform_tables():
    first = np.arange(ROWS)
    second = np.arange(LANES)
    half = np.arange(LANES // 2)
    angle = 2.0 * math.pi / ROWS * (first[:, None] * first[None, :] % ROWS)
    wave = np.concatenate([np.cos(angle), -np.sin(angle)], 0)
    wave = np.einsum("ab,kn->aknb", np.eye(2), wave).reshape(4 * ROWS, 2 * ROWS)
    first_table = np.concatenate(split_bf16(wave), 1)
    twist = 2.0 * math.pi / NT * (first[:, None] * second[None, :] % NT)
    twist_table = np.stack([np.cos(twist), np.sin(twist)]).astype(np.float32)
    angle = 2.0 * math.pi / LANES * (second[:, None] * half[None, :] % LANES)
    cos, sin = np.cos(angle), np.sin(angle)
    wave = np.concatenate([np.concatenate([cos, -sin], 1), np.concatenate([sin, cos], 1)], 0)
    second_table = np.concatenate(split_bf16(wave), 1)
    return first_table, twist_table, second_table


def lag_table():
    bins = np.arange(NF, dtype=np.int64)
    delay = np.arange(LAGS, dtype=np.int64) - LAGS // 2
    phase = bins[:, None] * (delay % NT)[None, :] % NT
    angle = phase.astype(np.float32) * np.float32(2.0 * math.pi / NT)
    weight = np.where(bins == 0, 0.5, 1.0).astype(np.float32) / np.float32(math.sqrt(NF * SEG))
    upper = (weight[:, None] * np.cos(angle)).reshape(ROWS, ROWS, LAGS).transpose(1, 0, 2)
    lower = (-weight[:, None] * np.sin(angle)).reshape(ROWS, ROWS, LAGS).transpose(1, 0, 2)
    joined = np.concatenate([upper, lower], 1).astype(np.float32)
    return joined.reshape(ROWS * LANES, LAGS).astype(jnp.bfloat16)


def pack_kernel(low, count, packed, core_ref, own, mate, out, fill, started, sem):
    core = core_ref[0]
    slots = packed.shape[1]
    started[0] = 0

    @pl.loop(0, out.shape[0])
    def _(dev):
        fill[dev] = 0

    def place(half, source):
        @pl.loop(0, slots)
        def _(at):
            value = packed[half, at]

            @pl.when(value >= 0)
            def _():
                dev = ((value >> LEN_BITS) * 2731) >> 16
                rank = fill[dev]
                fill[dev] = rank + 1
                slot = (rank >> 1) - low

                @pl.when(((rank & 1) == core) & (slot >= 0) & (slot < count))
                def _():
                    started[0] += 1
                    pltpu.make_async_copy(source.at[at], out.at[dev, slot], sem).start()

    for half in range(2):

        @pl.when(core == half)
        def _():
            place(half, own)

        @pl.when(core != half)
        def _():
            place(half, mate)

    @pl.loop(0, started[0])
    def _(_):
        pltpu.make_async_copy(own.at[0], out.at[0, 0], sem).wait()


def pack(low, count, wide_count, packed, core, own, mate):
    return pl.pallas_call(
        functools.partial(pack_kernel, low, count),
        out_shape=jax.ShapeDtypeStruct((wide_count, count, 2 * ROWS, LANES), jnp.bfloat16),
        in_specs=[SMEM, SMEM, ANY, ANY],
        out_specs=ANY,
        scratch_shapes=[
            pltpu.SMEM((wide_count,), jnp.int32),
            pltpu.SMEM((1,), jnp.int32),
            pltpu.SemaphoreType.DMA,
        ],
        cost_estimate=pl.CostEstimate(flops=0, bytes_accessed=wide_count * count * NT * 8, transcendentals=0),
        name="pack",
    )(packed, core, own, mate)


def whiten_kernel(
    part, source, length, picks, got, more, first, twist, second, white, payload, held, spectra, sem
):
    stations = held.shape[0]
    first_more = got.shape[0] * BASE

    @pl.loop(0, stations)
    def _(station):
        code = source[station]
        over = code - first_more

        @pl.when(over < 0)
        def _():
            pltpu.make_async_copy(got.at[code >> 1, code & 1], held.at[station], sem).start()

        @pl.when(over >= 0)
        def _():
            pltpu.make_async_copy(more.at[over, 0], held.at[station], sem).start()

    @pl.loop(0, stations)
    def _(_):
        pltpu.make_async_copy(got.at[0, 0], held.at[0], sem).wait()

    row = lax.broadcasted_iota(jnp.int32, (2 * ROWS, LANES), 0)
    lane = lax.broadcasted_iota(jnp.int32, (2 * ROWS, LANES), 1)
    place = (2 * part + (row & 1)) * NT + (row >> 1) * LANES + lane

    def two_stations(station):
        sides = []
        for at in range(2):
            values = held[station + at].astype(jnp.float32)
            sides.append(jnp.where(place < length[station + at], values, 0.0).astype(jnp.bfloat16))
        values = jnp.concatenate(sides, 1)
        values = jnp.concatenate([values, values], 0)
        mixed = jnp.dot(first[...], values, preferred_element_type=jnp.float32)
        parts = []
        for at in range(2):
            for seg in range(2):
                real = mixed[2 * seg * ROWS : (2 * seg + 1) * ROWS, at * LANES : (at + 1) * LANES]
                imag = mixed[(2 * seg + 1) * ROWS : (2 * seg + 2) * ROWS, at * LANES : (at + 1) * LANES]
                turned_re = real * twist[0] + imag * twist[1]
                turned_im = imag * twist[0] - real * twist[1]
                parts.append(jnp.concatenate([turned_re, turned_im], 1))
        turned = jnp.concatenate(parts, 0)
        high = turned.astype(jnp.bfloat16)
        low = (turned - high.astype(jnp.float32)).astype(jnp.bfloat16)
        upper = jnp.dot(high, second[...], preferred_element_type=jnp.float32)
        lower = jnp.dot(low, second[:, :LANES], preferred_element_type=jnp.float32)
        spectrum = upper[:, :LANES] + (upper[:, LANES:] + lower)
        for at in range(2):
            for seg in range(2):
                begin = (2 * at + seg) * ROWS
                side = spectrum[begin : begin + ROWS]
                power = jnp.sum(side * side, axis=0, keepdims=True)
                power = (power + pltpu.roll(power, LANES // 2, 1)) * (1.0 / ROWS)
                scale = 1.0 / jnp.sqrt(power + 1e-06)
                spectra[station + at, seg] = (side * scale).astype(jnp.bfloat16)

    @pl.loop(0, stations // 4)
    def _(four):
        two_stations(4 * four)
        two_stations(4 * four + 2)

    whole = pltpu.make_async_copy(spectra, white, sem)
    whole.start()
    stops, rows = picks.shape

    @pl.loop(0, stops)
    def _(stop):
        for at in range(rows):
            pltpu.make_async_copy(spectra.at[picks[stop, at]], payload.at[stop, at], sem).start()

    whole.wait()
    pltpu.make_async_copy(payload, payload, sem).wait()


def whiten(part, source, length, picks, got, more, tables):
    stops, rows = picks.shape
    return pl.pallas_call(
        functools.partial(whiten_kernel, part),
        out_shape=(
            jax.ShapeDtypeStruct((ST_DEV, 2, ROWS, LANES), jnp.bfloat16),
            jax.ShapeDtypeStruct((stops, rows, 2, ROWS, LANES), jnp.bfloat16),
        ),
        in_specs=[SMEM, SMEM, SMEM, ANY, ANY, VMEM, VMEM, VMEM],
        out_specs=(ANY, ANY),
        scratch_shapes=[
            pltpu.VMEM((ST_DEV, 2 * ROWS, LANES), jnp.bfloat16),
            pltpu.VMEM((ST_DEV, 2, ROWS, LANES), jnp.bfloat16),
            pltpu.SemaphoreType.DMA,
        ],
        cost_estimate=pl.CostEstimate(
            flops=2 * ST_DEV * 2 * ROWS * 256 * 400, bytes_accessed=4 * 1024 * 1024, transcendentals=0
        ),
        name="whiten",
    )(source, length, picks, got, more, *tables)


def lag_kernel(stops, near_pick, far_at, *refs):
    white_a, white_b, home = refs[:3]
    far_a = refs[3 : 2 + stops]
    far_b, table, mask, out, near, far, cross, tables, sem, table_sem = refs[2 + stops :]
    rows = near_pick.shape[1]
    load_table = pltpu.make_async_copy(table, tables, table_sem)
    copies = [
        pltpu.make_async_copy(white_a, near.at[0], sem),
        pltpu.make_async_copy(white_b, near.at[1], sem),
        pltpu.make_async_copy(home.at[0], far.at[0, 0], sem),
    ]
    for stop in range(1, stops):
        copies.append(pltpu.make_async_copy(far_a[stop - 1], far.at[0, stop], sem))
    for stop in range(stops):
        copies.append(pltpu.make_async_copy(far_b.at[far_at[stop]], far.at[1, stop], sem))
    for copy in copies:
        copy.start()
    load_table.start()
    for copy in copies:
        copy.wait()
    step = 16
    side = rows // 2
    left = lax.broadcasted_iota(jnp.int32, (step, LANES), 1) < LANES // 2

    @pl.loop(0, stops * 2)
    def _(block):
        stop = block // 2
        first = (block % 2) * side
        own = [near_pick[stop, first + i] for i in range(side)]

        @pl.loop(0, ROWS // step)
        def _(chunk):
            band = pl.ds(pl.multiple_of(chunk * step, step), step)
            here = [
                [near[s // 2, own[i], s % 2, band, :].astype(jnp.float32) for s in range(SEG)]
                for i in range(side)
            ]
            for j in range(side):
                straight, crossed = [], []
                for s in range(SEG):
                    value = far[s // 2, stop, first + j, s % 2, band, :].astype(jnp.float32)
                    other = pltpu.roll(value, LANES // 2, 1)
                    straight.append(jnp.where(left, value, other))
                    crossed.append(jnp.where(left, -other, value))
                for i in range(side):
                    direct = here[i][0] * straight[0]
                    turned = here[i][0] * crossed[0]
                    for s in range(1, SEG):
                        direct += here[i][s] * straight[s]
                        turned += here[i][s] * crossed[s]
                    pair = (block * side + i) * side + j
                    cross[pl.ds(pl.multiple_of(pair * ROWS + chunk * step, step), step), :] = (
                        direct + pltpu.roll(turned, LANES // 2, 1)
                    )

    load_table.wait()
    pairs = stops * 2 * side * side
    group = 8
    out[...] = jnp.zeros_like(out)

    @pl.loop(0, ROWS // group)
    def _(at):
        slabs = [
            cross[pl.ds(at * group + k, pairs, stride=ROWS), :].astype(jnp.bfloat16) for k in range(group)
        ]
        depth = group * LANES
        out[...] += jnp.dot(
            jnp.concatenate(slabs, 1),
            tables[pl.ds(pl.multiple_of(at * depth, depth), depth), :],
            preferred_element_type=jnp.float32,
        )

    out[...] = out[...] * mask[...]


def lagged(near_pick, far_at, white_a, white_b, home, far_a, far_b, table, mask):
    stops, rows = near_pick.shape
    pairs = mask.shape[0]
    return pl.pallas_call(
        functools.partial(lag_kernel, stops),
        out_shape=jax.ShapeDtypeStruct((pairs, LAGS), jnp.float32),
        in_specs=[SMEM, SMEM] + [ANY] * (stops + 4) + [VMEM],
        out_specs=VMEM,
        scratch_shapes=[
            pltpu.VMEM((2, ST_DEV, 2, ROWS, LANES), jnp.bfloat16),
            pltpu.VMEM((2, stops, rows, 2, ROWS, LANES), jnp.bfloat16),
            pltpu.VMEM((pairs * ROWS, LANES), jnp.float32),
            pltpu.VMEM(table.shape, jnp.bfloat16),
            pltpu.SemaphoreType.DMA,
            pltpu.SemaphoreType.DMA,
        ],
        compiler_params=pltpu.CompilerParams(vmem_limit_bytes=48 * 1024 * 1024),
        cost_estimate=pl.CostEstimate(
            flops=2 * pairs * 2 * NF * LAGS, bytes_accessed=24 * 1024 * 1024, transcendentals=0
        ),
        name="lagged",
    )(near_pick, far_at, white_a, white_b, home, *far_a, far_b, table, mask)


def empty(shape):
    return pl.pallas_call(
        lambda out: None,
        out_shape=jax.ShapeDtypeStruct(shape, jnp.bfloat16),
        out_specs=ANY,
        name="empty",
    )()


def on_device(records, lengths, owners, own_pick, visit_pick, pair_mask):
    wide_count = lax.axis_size("wide")
    stops = lax.axis_size("blk")
    column = lax.axis_index("wide")
    group = lax.axis_index("blk")
    core = column % 2
    swap = [(i, i ^ 1) for i in range(wide_count)]
    slots = records.shape[1]
    steps = jnp.arange(stops, dtype=jnp.int32)

    packed = jnp.where(owners[0] >= 0, (owners[0] << LEN_BITS) + lengths[0], -1)
    spread = jnp.broadcast_to(packed[None], (wide_count, slots))
    table = lax.all_to_all(spread, "wide", split_axis=0, concat_axis=0, tiled=True)
    table = table.reshape(wide_count // 2, 2, slots)
    visits = visit_pick[0, 0].reshape(stops, -1)
    asked = [visits[0]] + [
        lax.ppermute(visits[stop], "blk", [(i, (i - stop) % stops) for i in range(stops)])
        for stop in range(1, stops)
    ]
    by_stop = jnp.stack(asked)
    by_dest = by_stop[(steps - group) % stops]

    tiles = records[0].reshape(slots, SEG, ROWS, LANES)
    own = [
        tiles[:, 2 * part : 2 * part + 2].transpose(0, 2, 1, 3).reshape(slots, 2 * ROWS, LANES)
        for part in range(2)
    ]
    mates = [lax.ppermute(half, "wide", swap) for half in own]
    chip_packed = lax.dynamic_index_in_dim(table, column // 2, 0, False)
    core_at = core.reshape(1)

    def load(low, count, part):
        return pack(low, count, wide_count, chip_packed, core_at, own[part], mates[part])

    def send(payload):
        return lax.all_to_all(payload, "wide", split_axis=0, concat_axis=0, tiled=True)

    station = table.reshape(wide_count // 2, 2 * slots) >> LEN_BITS
    owner_dev = station // ST_DEV
    everyone = jnp.arange(wide_count, dtype=jnp.int32)
    counts = jnp.sum((owner_dev[:, :, None] == everyone).astype(jnp.int32), axis=1)
    spilled = lax.pmax(jnp.max(counts), "blk") > 2 * BASE
    mine = owner_dev == column
    rank = jnp.cumsum(mine.astype(jnp.int32), axis=1) - 1
    chip = jnp.arange(wide_count // 2, dtype=jnp.int32)[:, None]
    sender = 2 * chip + rank % 2
    code = jnp.where(rank < 2 * BASE, sender * BASE + rank // 2, wide_count * BASE + sender)
    local = column * ST_DEV + jnp.arange(ST_DEV, dtype=jnp.int32)
    chosen = station[None] == local[:, None, None]
    source = jnp.sum(jnp.where(chosen, code[None], 0), axis=(1, 2))
    length = table.reshape(wide_count // 2, 2 * slots) & ((1 << LEN_BITS) - 1)
    length = jnp.sum(jnp.where(chosen, length[None], 0), axis=(1, 2))

    load_a = load(0, BASE, 0)
    got_a = send(load_a)
    load_b = load(0, BASE, 1)
    spilled, load_b = lax.optimization_barrier((spilled, load_b))
    more = lax.cond(
        spilled,
        lambda: tuple(send(load(BASE, EXTRA, part)) for part in range(2)),
        lambda: tuple(empty((wide_count, EXTRA, 2 * ROWS, LANES)) for _ in range(2)),
    )
    got_a, load_b = lax.optimization_barrier((got_a, load_b))
    got_b = send(load_b)

    tables = [jnp.asarray(table) for table in transform_tables()]
    white_a, payload_a = whiten(0, source, length, by_stop, got_a, more[0], tables)
    far_a = [
        lax.ppermute(payload_a[stop], "blk", [(i, (i + stop) % stops) for i in range(stops)])
        for stop in range(1, stops)
    ]
    white_b, payload_b = whiten(1, source, length, by_dest, got_b, more[1], tables)
    far_b = lax.all_to_all(payload_b, "blk", split_axis=0, concat_axis=0, tiled=True)

    near_pick = own_pick[0, 0].reshape(stops, -1)
    far_at = (group - steps) % stops
    mask = pair_mask[0, 0].astype(jnp.float32).reshape(-1, 1)
    result = lagged(near_pick, far_at, white_a, white_b, payload_a, far_a, far_b, jnp.asarray(lag_table()), mask)
    return result.reshape((1, 1) + pair_mask.shape[2:] + (LAGS,))


def solution(mesh):
    return jax.shard_map(
        on_device,
        mesh=mesh,
        in_specs=(
            P("blk", "wide", None, None),
            P("blk", "wide"),
            P("blk", "wide"),
            P("blk", "wide", None, None, None),
            P("blk", "wide", None, None, None),
            P("blk", "wide", None, None, None, None),
        ),
        out_specs=P("blk", "wide", None, None, None, None, None),
        check_vma=False,
    )
```

```python
import functools
import math

import jax
import jax.numpy as jnp
import numpy as np
from jax import lax
from jax.experimental import pallas as pl
from jax.experimental.pallas import tpu as pltpu
from jax.sharding import PartitionSpec as P

ST_DEV = 24
SEG = 4
NT = 8192
NF = 4096
LAGS = 1024
ROWS = 64
LANES = 128
BASE = 2
EXTRA = 1
LEN_BITS = 16
SMEM = pl.BlockSpec(memory_space=pltpu.SMEM)
VMEM = pl.BlockSpec(memory_space=pltpu.VMEM)
ANY = pl.BlockSpec(memory_space=pl.ANY)


def split_bf16(values):
    high = values.astype(jnp.bfloat16)
    low = (values - high.astype(np.float64)).astype(jnp.bfloat16)
    return high, low


def transform_tables():
    first = np.arange(ROWS)
    second = np.arange(LANES)
    half = np.arange(LANES // 2)
    angle = 2.0 * math.pi / ROWS * (first[:, None] * first[None, :] % ROWS)
    wave = np.concatenate([np.cos(angle), -np.sin(angle)], 0)
    wave = np.einsum("ab,kn->aknb", np.eye(2), wave).reshape(4 * ROWS, 2 * ROWS)
    first_table = np.concatenate(split_bf16(wave), 1)
    twist = 2.0 * math.pi / NT * (first[:, None] * second[None, :] % NT)
    twist_table = np.stack([np.cos(twist), np.sin(twist)]).astype(np.float32)
    angle = 2.0 * math.pi / LANES * (second[:, None] * half[None, :] % LANES)
    cos, sin = np.cos(angle), np.sin(angle)
    wave = np.concatenate([np.concatenate([cos, -sin], 1), np.concatenate([sin, cos], 1)], 0)
    second_table = np.concatenate(split_bf16(wave), 1)
    return first_table, twist_table, second_table


def lag_table():
    bins = np.arange(NF, dtype=np.int64)
    delay = np.arange(LAGS, dtype=np.int64) - LAGS // 2
    phase = bins[:, None] * (delay % NT)[None, :] % NT
    angle = phase.astype(np.float32) * np.float32(2.0 * math.pi / NT)
    weight = np.where(bins == 0, 0.5, 1.0).astype(np.float32) / np.float32(math.sqrt(NF * SEG))
    upper = (weight[:, None] * np.cos(angle)).reshape(ROWS, ROWS, LAGS).transpose(1, 0, 2)
    lower = (-weight[:, None] * np.sin(angle)).reshape(ROWS, ROWS, LAGS).transpose(1, 0, 2)
    joined = np.concatenate([upper, lower], 1).astype(np.float32)
    return joined.reshape(ROWS * LANES, LAGS).astype(jnp.bfloat16)


def pack_kernel(low, count, packed, core_ref, own, mate, after, out, flag, fill, started, sem):
    core = core_ref[0]
    slots = packed.shape[1]
    started[0] = 0
    flag[0] = 0

    @pl.loop(0, out.shape[0])
    def _(dev):
        fill[dev] = 0

    def place(half, source):
        @pl.loop(0, slots)
        def _(at):
            value = packed[half, at]

            @pl.when(value >= 0)
            def _():
                dev = ((value >> LEN_BITS) * 2731) >> 16
                rank = fill[dev]
                fill[dev] = rank + 1
                slot = (rank >> 1) - low

                @pl.when(((rank & 1) == core) & (slot >= 0) & (slot < count))
                def _():
                    started[0] += 1
                    pltpu.make_async_copy(source.at[at], out.at[dev, slot], sem).start()

                @pl.when(slot >= count)
                def _():
                    flag[0] = 1

    for half in range(2):

        @pl.when(core == half)
        def _():
            place(half, own)

        @pl.when(core != half)
        def _():
            place(half, mate)

    @pl.loop(0, started[0])
    def _(_):
        pltpu.make_async_copy(own.at[0], out.at[0, 0], sem).wait()


def pack(low, count, wide_count, packed, core, own, mate, after):
    return pl.pallas_call(
        functools.partial(pack_kernel, low, count),
        out_shape=(
            jax.ShapeDtypeStruct((wide_count, count, 2 * ROWS, LANES), jnp.bfloat16),
            jax.ShapeDtypeStruct((1,), jnp.int32),
        ),
        in_specs=[SMEM, SMEM, ANY, ANY, ANY],
        out_specs=(VMEM, SMEM),
        scratch_shapes=[
            pltpu.SMEM((wide_count,), jnp.int32),
            pltpu.SMEM((1,), jnp.int32),
            pltpu.SemaphoreType.DMA,
        ],
        cost_estimate=pl.CostEstimate(flops=0, bytes_accessed=wide_count * count * NT * 8, transcendentals=0),
        name="pack",
    )(packed, core, own, mate, after)


def whiten_kernel(
    part, source, length, picks, got, more, first, twist, second, *refs
):
    white, payload, held, spectra, sem = refs[-5:]
    stations = held.shape[0]
    first_more = got.shape[0] * BASE

    @pl.loop(0, stations)
    def _(station):
        code = source[station]
        over = code - first_more

        @pl.when(over < 0)
        def _():
            pltpu.make_async_copy(got.at[code >> 1, code & 1], held.at[station], sem).start()

        @pl.when(over >= 0)
        def _():
            pltpu.make_async_copy(more.at[over, 0], held.at[station], sem).start()

    @pl.loop(0, stations)
    def _(_):
        pltpu.make_async_copy(got.at[0, 0], held.at[0], sem).wait()

    row = lax.broadcasted_iota(jnp.int32, (2 * ROWS, LANES), 0)
    lane = lax.broadcasted_iota(jnp.int32, (2 * ROWS, LANES), 1)
    place = (2 * part + (row & 1)) * NT + (row >> 1) * LANES + lane

    def two_stations(station):
        sides = []
        for at in range(2):
            values = held[station + at].astype(jnp.float32)
            sides.append(jnp.where(place < length[station + at], values, 0.0).astype(jnp.bfloat16))
        values = jnp.concatenate(sides, 1)
        values = jnp.concatenate([values, values], 0)
        mixed = jnp.dot(first[...], values, preferred_element_type=jnp.float32)
        parts = []
        for at in range(2):
            for seg in range(2):
                real = mixed[2 * seg * ROWS : (2 * seg + 1) * ROWS, at * LANES : (at + 1) * LANES]
                imag = mixed[(2 * seg + 1) * ROWS : (2 * seg + 2) * ROWS, at * LANES : (at + 1) * LANES]
                turned_re = real * twist[0] + imag * twist[1]
                turned_im = imag * twist[0] - real * twist[1]
                parts.append(jnp.concatenate([turned_re, turned_im], 1))
        turned = jnp.concatenate(parts, 0)
        high = turned.astype(jnp.bfloat16)
        low = (turned - high.astype(jnp.float32)).astype(jnp.bfloat16)
        upper = jnp.dot(high, second[...], preferred_element_type=jnp.float32)
        lower = jnp.dot(low, second[:, :LANES], preferred_element_type=jnp.float32)
        spectrum = upper[:, :LANES] + (upper[:, LANES:] + lower)
        for at in range(2):
            for seg in range(2):
                begin = (2 * at + seg) * ROWS
                side = spectrum[begin : begin + ROWS]
                power = jnp.sum(side * side, axis=0, keepdims=True)
                power = (power + pltpu.roll(power, LANES // 2, 1)) * (1.0 / ROWS)
                scale = 1.0 / jnp.sqrt(power + 1e-06)
                spectra[station + at, seg] = (side * scale).astype(jnp.bfloat16)

    @pl.loop(0, stations // 4)
    def _(four):
        two_stations(4 * four)
        two_stations(4 * four + 2)

    whole = pltpu.make_async_copy(spectra, white, sem)
    whole.start()
    stops, rows = picks.shape

    @pl.loop(0, stops)
    def _(stop):
        for at in range(rows):
            pltpu.make_async_copy(spectra.at[picks[stop, at]], payload.at[stop, at], sem).start()

    whole.wait()
    pltpu.make_async_copy(payload, payload, sem).wait()


def whiten(part, source, length, picks, got, more, tables, after):
    stops, rows = picks.shape
    return pl.pallas_call(
        functools.partial(whiten_kernel, part),
        out_shape=(
            jax.ShapeDtypeStruct((ST_DEV, 2, ROWS, LANES), jnp.bfloat16),
            jax.ShapeDtypeStruct((stops, rows, 2, ROWS, LANES), jnp.bfloat16),
        ),
        in_specs=[SMEM, SMEM, SMEM, ANY, ANY, VMEM, VMEM, VMEM] + [ANY] * len(after),
        out_specs=(ANY, ANY),
        scratch_shapes=[
            pltpu.VMEM((ST_DEV, 2 * ROWS, LANES), jnp.bfloat16),
            pltpu.VMEM((ST_DEV, 2, ROWS, LANES), jnp.bfloat16),
            pltpu.SemaphoreType.DMA,
        ],
        cost_estimate=pl.CostEstimate(
            flops=2 * ST_DEV * 2 * ROWS * 256 * 400, bytes_accessed=4 * 1024 * 1024, transcendentals=0
        ),
        name="whiten",
    )(source, length, picks, got, more, *tables, *after)


def cross_rows(near_pick, near, far, cross, fresh):
    stops, rows = near_pick.shape
    side = rows // 2
    step = 16
    left = lax.broadcasted_iota(jnp.int32, (step, LANES), 1) < LANES // 2

    @pl.loop(0, stops * 2)
    def _(block):
        stop = block // 2
        first = (block % 2) * side
        own = [near_pick[stop, first + i] for i in range(side)]

        @pl.loop(0, ROWS // step)
        def _(chunk):
            band = pl.ds(pl.multiple_of(chunk * step, step), step)
            here = [[near[own[i], s, band, :].astype(jnp.float32) for s in range(2)] for i in range(side)]
            for j in range(side):
                straight, crossed = [], []
                for s in range(2):
                    value = far[stop, first + j, s, band, :].astype(jnp.float32)
                    other = pltpu.roll(value, LANES // 2, 1)
                    straight.append(jnp.where(left, value, other))
                    crossed.append(jnp.where(left, -other, value))
                for i in range(side):
                    direct = here[i][0] * straight[0] + here[i][1] * straight[1]
                    turned = here[i][0] * crossed[0] + here[i][1] * crossed[1]
                    total = direct + pltpu.roll(turned, LANES // 2, 1)
                    pair = (block * side + i) * side + j
                    at = pl.ds(pl.multiple_of(pair * ROWS + chunk * step, step), step)
                    if fresh:
                        cross[at, :] = total
                    else:
                        cross[at, :] += total


def cross_kernel(stops, near_pick, white, home, *refs):
    far_in = refs[: stops - 1]
    out, near, far, cross, sem, out_sem = refs[stops - 1 :]
    copies = [pltpu.make_async_copy(white, near, sem), pltpu.make_async_copy(home.at[0], far.at[0], sem)]
    for stop in range(1, stops):
        copies.append(pltpu.make_async_copy(far_in[stop - 1], far.at[stop], sem))
    for copy in copies:
        copy.start()
    for copy in copies:
        copy.wait()
    cross_rows(near_pick, near, far, cross, True)
    copy = pltpu.make_async_copy(cross, out, out_sem)
    copy.start()
    copy.wait()


def cross_first(near_pick, white, home, far):
    stops, rows = near_pick.shape
    pairs = stops * rows * rows // 2
    return pl.pallas_call(
        functools.partial(cross_kernel, stops),
        out_shape=jax.ShapeDtypeStruct((pairs * ROWS, LANES), jnp.float32),
        in_specs=[SMEM] + [ANY] * (stops + 1),
        out_specs=ANY,
        scratch_shapes=[
            pltpu.VMEM(white.shape, jnp.bfloat16),
            pltpu.VMEM(home.shape, jnp.bfloat16),
            pltpu.VMEM((pairs * ROWS, LANES), jnp.float32),
            pltpu.SemaphoreType.DMA,
            pltpu.SemaphoreType.DMA,
        ],
        compiler_params=pltpu.CompilerParams(vmem_limit_bytes=20 * 1024 * 1024),
        cost_estimate=pl.CostEstimate(
            flops=pairs * ROWS * LANES * 16, bytes_accessed=24 * 1024 * 1024, transcendentals=0
        ),
        name="cross_first",
    )(near_pick, white, home, *far)


def lag_kernel(near_pick, far_at, begun, white, far_in, table, mask, out, near, far, cross, tables, sem, table_sem):
    stops = near_pick.shape[0]
    load_table = pltpu.make_async_copy(table, tables, table_sem)
    copies = [pltpu.make_async_copy(white, near, sem), pltpu.make_async_copy(begun, cross, sem)]
    for stop in range(stops):
        copies.append(pltpu.make_async_copy(far_in.at[far_at[stop]], far.at[stop], sem))
    for copy in copies:
        copy.start()
    load_table.start()
    for copy in copies:
        copy.wait()
    cross_rows(near_pick, near, far, cross, False)
    load_table.wait()
    pairs = out.shape[0]
    group = 8
    out[...] = jnp.zeros_like(out)

    @pl.loop(0, ROWS // group)
    def _(at):
        slabs = [
            cross[pl.ds(at * group + k, pairs, stride=ROWS), :].astype(jnp.bfloat16) for k in range(group)
        ]
        depth = group * LANES
        out[...] += jnp.dot(
            jnp.concatenate(slabs, 1),
            tables[pl.ds(pl.multiple_of(at * depth, depth), depth), :],
            preferred_element_type=jnp.float32,
        )

    out[...] = out[...] * mask[...]


def lagged(near_pick, far_at, begun, white, far, table, mask):
    pairs = mask.shape[0]
    return pl.pallas_call(
        lag_kernel,
        out_shape=jax.ShapeDtypeStruct((pairs, LAGS), jnp.float32),
        in_specs=[SMEM, SMEM] + [ANY] * 4 + [VMEM],
        out_specs=VMEM,
        scratch_shapes=[
            pltpu.VMEM(white.shape, jnp.bfloat16),
            pltpu.VMEM(far.shape, jnp.bfloat16),
            pltpu.VMEM((pairs * ROWS, LANES), jnp.float32),
            pltpu.VMEM(table.shape, jnp.bfloat16),
            pltpu.SemaphoreType.DMA,
            pltpu.SemaphoreType.DMA,
        ],
        compiler_params=pltpu.CompilerParams(vmem_limit_bytes=48 * 1024 * 1024),
        cost_estimate=pl.CostEstimate(
            flops=2 * pairs * 2 * NF * LAGS, bytes_accessed=24 * 1024 * 1024, transcendentals=0
        ),
        name="lagged",
    )(near_pick, far_at, begun, white, far, table, mask)


def empty(shape):
    return pl.pallas_call(
        lambda out: None,
        out_shape=jax.ShapeDtypeStruct(shape, jnp.bfloat16),
        out_specs=ANY,
        name="empty",
    )()


def on_device(records, lengths, owners, own_pick, visit_pick, pair_mask):
    wide_count = lax.axis_size("wide")
    stops = lax.axis_size("blk")
    column = lax.axis_index("wide")
    group = lax.axis_index("blk")
    core = column % 2
    swap = [(i, i ^ 1) for i in range(wide_count)]
    slots = records.shape[1]
    steps = jnp.arange(stops, dtype=jnp.int32)

    packed = jnp.where(owners[0] >= 0, (owners[0] << LEN_BITS) + lengths[0], -1)
    spread = jnp.broadcast_to(packed[None], (wide_count, slots))
    table = lax.all_to_all(spread, "wide", split_axis=0, concat_axis=0, tiled=True)
    table = table.reshape(wide_count // 2, 2, slots)
    chip_packed = lax.dynamic_index_in_dim(table, column // 2, 0, False)
    core_at = core.reshape(1)

    tiles = records[0].reshape(slots, SEG, ROWS, LANES)

    def halves(part):
        return tiles[:, 2 * part : 2 * part + 2].transpose(0, 2, 1, 3).reshape(slots, 2 * ROWS, LANES)

    def send(payload):
        return lax.all_to_all(payload, "wide", split_axis=0, concat_axis=0, tiled=True)

    own_a = halves(0)
    mate_a = lax.ppermute(own_a, "wide", swap)
    load_a, flag_a = pack(0, BASE, wide_count, chip_packed, core_at, own_a, mate_a, core_at)
    got_a = send(load_a)
    own_b = jnp.where(flag_a[0] >= 0, halves(1), 0.0)
    mate_b = lax.ppermute(own_b, "wide", swap)
    load_b, flag_b = pack(0, BASE, wide_count, chip_packed, core_at, own_b, mate_b, load_a)
    got_b = send(load_b)

    def late():
        rows = [
            pack(BASE, EXTRA, wide_count, chip_packed, core_at, own, mate, core_at)[0]
            for own, mate in ((own_a, mate_a), (own_b, mate_b))
        ]
        return tuple(send(row) for row in rows)

    more = lax.cond(
        lax.pmax(flag_b[0], ("blk", "wide")) > 0,
        late,
        lambda: tuple(empty((wide_count, EXTRA, 2 * ROWS, LANES)) for _ in range(2)),
    )

    visits = visit_pick[0, 0].reshape(stops, -1)[(group - steps) % stops]
    visits = jnp.where(flag_b[0] >= 0, visits, 0)
    by_dest = lax.all_to_all(visits, "blk", split_axis=0, concat_axis=0, tiled=True)
    by_stop = by_dest[(group + steps) % stops]

    flat = table.reshape(wide_count // 2, 2 * slots)
    flat = jnp.where(flag_a[0] >= 0, flat, 0)
    station = flat >> LEN_BITS
    mine = (station // ST_DEV) == column
    rank = jnp.cumsum(mine.astype(jnp.int32), axis=1) - 1
    chip = jnp.arange(wide_count // 2, dtype=jnp.int32)[:, None]
    sender = 2 * chip + rank % 2
    code = jnp.where(rank < 2 * BASE, sender * BASE + rank // 2, wide_count * BASE + sender)
    local = column * ST_DEV + jnp.arange(ST_DEV, dtype=jnp.int32)
    chosen = station[None] == local[:, None, None]
    source = jnp.sum(jnp.where(chosen, code[None], 0), axis=(1, 2))
    length = flat & ((1 << LEN_BITS) - 1)
    length = jnp.sum(jnp.where(chosen, length[None], 0), axis=(1, 2))

    tables = [jnp.asarray(table) for table in transform_tables()]
    near_pick = own_pick[0, 0].reshape(stops, -1)
    white_a, payload_a = whiten(0, source, length, by_stop, got_a, more[0], tables, [])
    far_a = [
        lax.ppermute(payload_a[stop], "blk", [(i, (i + stop) % stops) for i in range(stops)])
        for stop in range(1, stops)
    ]
    white_b, payload_b = whiten(1, source, length, by_dest, got_b, more[1], tables, far_a)
    far_b = lax.all_to_all(payload_b, "blk", split_axis=0, concat_axis=0, tiled=True)

    begun = cross_first(near_pick, white_a, payload_a, far_a)
    far_at = (group - steps) % stops
    mask = pair_mask[0, 0].astype(jnp.float32).reshape(-1, 1)
    result = lagged(near_pick, far_at, begun, white_b, far_b, jnp.asarray(lag_table()), mask)
    return result.reshape((1, 1) + pair_mask.shape[2:] + (LAGS,))


def solution(mesh):
    return jax.shard_map(
        on_device,
        mesh=mesh,
        in_specs=(
            P("blk", "wide", None, None),
            P("blk", "wide"),
            P("blk", "wide"),
            P("blk", "wide", None, None, None),
            P("blk", "wide", None, None, None),
            P("blk", "wide", None, None, None, None),
        ),
        out_specs=P("blk", "wide", None, None, None, None, None),
        check_vma=False,
    )
```

```python
import functools
import math

import jax
import jax.numpy as jnp
import numpy as np
from jax import lax
from jax.experimental import pallas as pl
from jax.experimental.pallas import tpu as pltpu
from jax.sharding import PartitionSpec as P

ST_DEV = 24
SEG = 4
NT = 8192
NF = 4096
LAGS = 1024
ROWS = 64
LANES = 128
BASE = 2
EXTRA = 1
LEN_BITS = 16
NOTES = 16
SMEM = pl.BlockSpec(memory_space=pltpu.SMEM)
VMEM = pl.BlockSpec(memory_space=pltpu.VMEM)
ANY = pl.BlockSpec(memory_space=pl.ANY)


def split_bf16(values):
    high = values.astype(jnp.bfloat16)
    low = (values - high.astype(np.float64)).astype(jnp.bfloat16)
    return high, low


def transform_tables():
    first = np.arange(ROWS)
    second = np.arange(LANES)
    half = np.arange(LANES // 2)
    angle = 2.0 * math.pi / ROWS * (first[:, None] * first[None, :] % ROWS)
    wave = np.concatenate([np.cos(angle), -np.sin(angle)], 0)
    wave = np.einsum("ab,kn->aknb", np.eye(2), wave).reshape(4 * ROWS, 2 * ROWS)
    first_table = np.concatenate(split_bf16(wave), 1)
    twist = 2.0 * math.pi / NT * (first[:, None] * second[None, :] % NT)
    twist_table = np.stack([np.cos(twist), np.sin(twist)]).astype(np.float32)
    angle = 2.0 * math.pi / LANES * (second[:, None] * half[None, :] % LANES)
    cos, sin = np.cos(angle), np.sin(angle)
    wave = np.concatenate([np.concatenate([cos, -sin], 1), np.concatenate([sin, cos], 1)], 0)
    second_table = np.concatenate(split_bf16(wave), 1)
    return first_table, twist_table, second_table


def lag_tables():
    row = np.arange(ROWS // 2, dtype=np.int64)
    lane = np.arange(LANES, dtype=np.int64)
    bins = (row[:, None] + ROWS // 2 * (lane // ROWS)) + ROWS * (lane % ROWS)
    bins = bins.reshape(-1)
    weight = np.where(bins == 0, 0.5, 1.0).astype(np.float32) / np.float32(math.sqrt(NF * SEG))

    def at(delay):
        phase = bins[:, None] * delay[None, :] % NT
        return phase.astype(np.float32) * np.float32(2.0 * math.pi / NT)

    ahead = at(np.arange(LAGS // 2, dtype=np.int64))
    edge = at(np.array([NT - LAGS // 2], dtype=np.int64))
    cos = weight[:, None] * np.cos(ahead)
    sin = -weight[:, None] * np.sin(ahead)
    sin[:, :1] = -weight[:, None] * np.sin(edge)
    last = (weight[:, None] * np.cos(edge)).reshape(ROWS // 2, 1, LANES)
    return (
        np.concatenate([cos, sin], 0).astype(jnp.bfloat16),
        last.astype(jnp.bfloat16).astype(np.float32),
    )


def pack_kernel(low, count, noted, packed, core_ref, own, mate, after, out, flag, fill, notes, started, sem):
    core = core_ref[0]
    slots = packed.shape[1]
    devices = out.shape[0]
    started[0] = 0
    flag[0] = 0

    @pl.loop(0, devices)
    def _(dev):
        fill[dev] = 0
        for slot in range(count):
            notes[dev, slot] = -1

    def place(half, source):
        @pl.loop(0, slots)
        def _(at):
            value = packed[half, at]

            @pl.when(value >= 0)
            def _():
                dev = ((value >> LEN_BITS) * 2731) >> 16
                rank = fill[dev]
                fill[dev] = rank + 1
                slot = (rank >> 1) - low

                @pl.when(((rank & 1) == core) & (slot >= 0) & (slot < count))
                def _():
                    started[0] += 1
                    notes[dev, slot] = value - ((dev * ST_DEV) << LEN_BITS)
                    place_at = pl.ds(pl.multiple_of(slot * 2 * ROWS, 2 * ROWS), 2 * ROWS)
                    pltpu.make_async_copy(source.at[at], out.at[dev, place_at], sem).start()

                @pl.when(slot >= count)
                def _():
                    flag[0] = 1

    for half in range(2):

        @pl.when(core == half)
        def _():
            place(half, own)

        @pl.when(core != half)
        def _():
            place(half, mate)

    if noted:
        row = lax.broadcasted_iota(jnp.int32, (NOTES, LANES), 0)

        @pl.loop(0, devices)
        def _(dev):
            tile = jnp.where(row == 4 * count, flag[0], 0)
            for slot in range(count):
                value = notes[dev, slot]
                tile = jnp.where(row == 4 * slot, (value >> LEN_BITS) + 1, tile)
                tile = jnp.where(row == 4 * slot + 1, (value & 0xFFFF) >> 8, tile)
                tile = jnp.where(row == 4 * slot + 2, value & 0xFF, tile)
            out[dev, count * 2 * ROWS :, :] = tile.astype(jnp.float32).astype(jnp.bfloat16)

    @pl.loop(0, started[0])
    def _(_):
        pltpu.make_async_copy(own.at[0], out.at[0, pl.ds(0, 2 * ROWS)], sem).wait()


def pack(low, count, noted, wide_count, packed, core, own, mate, after):
    height = count * 2 * ROWS + (NOTES if noted else 0)
    return pl.pallas_call(
        functools.partial(pack_kernel, low, count, noted),
        out_shape=(
            jax.ShapeDtypeStruct((wide_count, height, LANES), jnp.bfloat16),
            jax.ShapeDtypeStruct((1,), jnp.int32),
        ),
        in_specs=[SMEM, SMEM, ANY, ANY, ANY],
        out_specs=(VMEM, SMEM),
        scratch_shapes=[
            pltpu.SMEM((wide_count,), jnp.int32),
            pltpu.SMEM((wide_count, count), jnp.int32),
            pltpu.SMEM((1,), jnp.int32),
            pltpu.SemaphoreType.DMA,
        ],
        cost_estimate=pl.CostEstimate(flops=0, bytes_accessed=wide_count * count * NT * 8, transcendentals=0),
        name="pack",
    )(packed, core, own, mate, after)


def read_notes(rows, count):
    notes = rows[:, count * 2 * ROWS :, 0].astype(jnp.float32).astype(jnp.int32)
    fields = notes[:, : 4 * count].reshape(-1, count, 4)
    return fields[..., 0] - 1, fields[..., 1] * 256 + fields[..., 2], notes[:, 4 * count]


def whiten_kernel(
    part, source, length, picks, got, more, first, twist, second, *refs
):
    white, payload, held, spectra, sem, sems = refs[-6:]
    stations = held.shape[0]
    first_more = got.shape[0] * BASE
    batch = 4

    @pl.loop(0, stations)
    def _(station):
        code = source[station]
        over = code - first_more

        @pl.when(over < 0)
        def _():
            place_at = pl.ds(pl.multiple_of((code & 1) * 2 * ROWS, 2 * ROWS), 2 * ROWS)
            pltpu.make_async_copy(got.at[code >> 1, place_at], held.at[station], sems.at[station // batch]).start()

        @pl.when(over >= 0)
        def _():
            place_at = pl.ds(0, 2 * ROWS)
            pltpu.make_async_copy(more.at[over, place_at], held.at[station], sems.at[station // batch]).start()

    row = lax.broadcasted_iota(jnp.int32, (2 * ROWS, LANES), 0)
    lane = lax.broadcasted_iota(jnp.int32, (2 * ROWS, LANES), 1)
    left = lax.broadcasted_iota(jnp.int32, (ROWS // 2, LANES), 1) < ROWS
    place = (2 * part + (row & 1)) * NT + (row >> 1) * LANES + lane

    def two_stations(station):
        sides = []
        for at in range(2):
            values = held[station + at].astype(jnp.float32)
            sides.append(jnp.where(place < length[station + at], values, 0.0).astype(jnp.bfloat16))
        values = jnp.concatenate(sides, 1)
        values = jnp.concatenate([values, values], 0)
        mixed = jnp.dot(first[...], values, preferred_element_type=jnp.float32)
        parts = []
        for at in range(2):
            for seg in range(2):
                real = mixed[2 * seg * ROWS : (2 * seg + 1) * ROWS, at * LANES : (at + 1) * LANES]
                imag = mixed[(2 * seg + 1) * ROWS : (2 * seg + 2) * ROWS, at * LANES : (at + 1) * LANES]
                turned_re = real * twist[0] + imag * twist[1]
                turned_im = imag * twist[0] - real * twist[1]
                parts.append(jnp.concatenate([turned_re, turned_im], 1))
        turned = jnp.concatenate(parts, 0)
        high = turned.astype(jnp.bfloat16)
        low = (turned - high.astype(jnp.float32)).astype(jnp.bfloat16)
        upper = jnp.dot(high, second[...], preferred_element_type=jnp.float32)
        lower = jnp.dot(low, second[:, :LANES], preferred_element_type=jnp.float32)
        spectrum = upper[:, :LANES] + (upper[:, LANES:] + lower)
        for at in range(2):
            for seg in range(2):
                begin = (2 * at + seg) * ROWS
                side = spectrum[begin : begin + ROWS]
                power = jnp.sum(side * side, axis=0, keepdims=True)
                power = (power + pltpu.roll(power, LANES // 2, 1)) * (1.0 / ROWS)
                scale = 1.0 / jnp.sqrt(power + 1e-06)
                side = side * scale
                upper, lower = side[: ROWS // 2], side[ROWS // 2 :]
                real = jnp.where(left, upper, pltpu.roll(lower, ROWS, 1))
                imag = jnp.where(left, pltpu.roll(upper, ROWS, 1), lower)
                spectra[station + at, seg, : ROWS // 2] = real.astype(jnp.bfloat16)
                spectra[station + at, seg, ROWS // 2 :] = imag.astype(jnp.bfloat16)

    @pl.loop(0, stations // batch)
    def _(at):
        these = held.at[pl.ds(at * batch, batch)]
        pltpu.make_async_copy(these, these, sems.at[at]).wait()
        for two in range(0, batch, 2):
            two_stations(batch * at + two)

    stops, rows = picks.shape

    @pl.loop(0, stops)
    def _(stop):
        for at in range(rows):
            pltpu.make_async_copy(spectra.at[picks[stop, at]], payload.at[stop, at], sem).start()

    whole = pltpu.make_async_copy(spectra, white, sems.at[0])
    whole.start()
    pltpu.make_async_copy(payload, payload, sem).wait()
    whole.wait()


def whiten(part, source, length, picks, got, more, tables, after):
    stops, rows = picks.shape
    return pl.pallas_call(
        functools.partial(whiten_kernel, part),
        out_shape=(
            jax.ShapeDtypeStruct((ST_DEV, 2, ROWS, LANES), jnp.bfloat16),
            jax.ShapeDtypeStruct((stops, rows, 2, ROWS, LANES), jnp.bfloat16),
        ),
        in_specs=[SMEM, SMEM, SMEM, ANY, ANY, VMEM, VMEM, VMEM] + [ANY] * len(after),
        out_specs=(ANY, ANY),
        scratch_shapes=[
            pltpu.VMEM((ST_DEV, 2 * ROWS, LANES), jnp.bfloat16),
            pltpu.VMEM((ST_DEV, 2, ROWS, LANES), jnp.bfloat16),
            pltpu.SemaphoreType.DMA,
            pltpu.SemaphoreType.DMA((ST_DEV // 4,)),
        ],
        cost_estimate=pl.CostEstimate(
            flops=2 * ST_DEV * 2 * ROWS * 256 * 400, bytes_accessed=4 * 1024 * 1024, transcendentals=0
        ),
        name="whiten",
    )(source, length, picks, got, more, *tables, *after)


def cross_rows(near_pick, near, far, cross, fresh, ready):
    stops, rows = near_pick.shape
    side = rows // 2
    step = 16
    half = ROWS // 2

    @pl.loop(0, stops)
    def _(stop):
        ready(stop)
        for two in range(2):
            first = two * side
            own = [near_pick[stop, first + i] for i in range(side)]

            @pl.loop(0, half // step)
            def _(chunk):
                real = pl.ds(pl.multiple_of(chunk * step, step), step)
                imag = pl.ds(pl.multiple_of(half + chunk * step, step), step)

                def both(ref, row):
                    return [
                        (ref[row, s, real, :].astype(jnp.float32), ref[row, s, imag, :].astype(jnp.float32))
                        for s in range(2)
                    ]

                here = [both(near, own[i]) for i in range(side)]
                for j in range(side):
                    there = both(far.at[stop], first + j)
                    for i in range(side):
                        pair = ((stop * 2 + two) * side + i) * side + j
                        total_re = sum(n[0] * f[0] + n[1] * f[1] for n, f in zip(here[i], there))
                        total_im = sum(n[1] * f[0] - n[0] * f[1] for n, f in zip(here[i], there))
                        for total, add in ((total_re, 0), (total_im, half)):
                            at = pl.ds(pl.multiple_of(pair * ROWS + add + chunk * step, step), step)
                            if fresh:
                                cross[at, :] = total
                            else:
                                cross[at, :] += total


def cross_kernel(stops, near_pick, white, home, *refs):
    far_in = refs[: stops - 1]
    out, near, far, cross, sem, sems, out_sem = refs[stops - 1 :]
    load = pltpu.make_async_copy(white, near, sem)
    load.start()
    pltpu.make_async_copy(home.at[0], far.at[0], sems.at[0]).start()
    for stop in range(1, stops):
        pltpu.make_async_copy(far_in[stop - 1], far.at[stop], sems.at[stop]).start()
    load.wait()

    def ready(stop):
        pltpu.make_async_copy(far.at[stop], far.at[stop], sems.at[stop]).wait()

    cross_rows(near_pick, near, far, cross, True, ready)
    copy = pltpu.make_async_copy(cross, out, out_sem)
    copy.start()
    copy.wait()


def cross_first(near_pick, white, home, far):
    stops, rows = near_pick.shape
    pairs = stops * rows * rows // 2
    return pl.pallas_call(
        functools.partial(cross_kernel, stops),
        out_shape=jax.ShapeDtypeStruct((pairs * ROWS, LANES), jnp.float32),
        in_specs=[SMEM] + [ANY] * (stops + 1),
        out_specs=ANY,
        scratch_shapes=[
            pltpu.VMEM(white.shape, jnp.bfloat16),
            pltpu.VMEM(home.shape, jnp.bfloat16),
            pltpu.VMEM((pairs * ROWS, LANES), jnp.float32),
            pltpu.SemaphoreType.DMA,
            pltpu.SemaphoreType.DMA((stops,)),
            pltpu.SemaphoreType.DMA,
        ],
        compiler_params=pltpu.CompilerParams(vmem_limit_bytes=20 * 1024 * 1024),
        cost_estimate=pl.CostEstimate(
            flops=pairs * ROWS * LANES * 16, bytes_accessed=24 * 1024 * 1024, transcendentals=0
        ),
        name="cross_first",
    )(near_pick, white, home, *far)


def lag_kernel(
    near_pick, far_at, begun, white, far_in, table, last, mask, out, near, far, cross, tables, sem, sems, table_sem
):
    stops = near_pick.shape[0]
    pairs = out.shape[0]
    rows = pairs * ROWS // stops
    load = pltpu.make_async_copy(white, near, sem)
    load.start()
    for stop in range(stops):
        these = pl.ds(stop * rows, rows)
        pltpu.make_async_copy(far_in.at[far_at[stop]], far.at[stop], sems.at[0, stop]).start()
        pltpu.make_async_copy(begun.at[these], cross.at[these], sems.at[1, stop]).start()
    load_table = pltpu.make_async_copy(table, tables, table_sem)
    load_table.start()
    load.wait()

    def ready(stop):
        these = cross.at[pl.ds(pl.multiple_of(stop * rows, rows), rows)]
        pltpu.make_async_copy(far.at[stop], far.at[stop], sems.at[0, stop]).wait()
        pltpu.make_async_copy(these, these, sems.at[1, stop]).wait()

    cross_rows(near_pick, near, far, cross, False, ready)
    load_table.wait()
    group = 8
    depth = group * LANES
    half = LAGS // 2
    turns = ROWS // 2 // group

    def product(turn, edge):
        base = turn * group
        slabs = [
            cross[pl.ds(base + k, pairs, stride=ROWS), :].astype(jnp.bfloat16) for k in range(group)
        ]
        if edge is not None:
            for k in range(group):
                edge += slabs[k].astype(jnp.float32) * last[base + k]
        part = jnp.dot(
            jnp.concatenate(slabs, 1),
            tables[pl.ds(pl.multiple_of(base * LANES, depth), depth), :],
            preferred_element_type=jnp.float32,
        )
        return part, edge

    out[:, :half] = jnp.zeros((pairs, half), jnp.float32)
    out[:, half:] = jnp.zeros((pairs, half), jnp.float32)

    def even_step(turn, edge):
        part, edge = product(turn, edge)
        out[:, :half] += part
        return edge

    edge = lax.fori_loop(0, turns, even_step, jnp.zeros((pairs, LANES), jnp.float32))

    @pl.loop(turns, 2 * turns)
    def _(turn):
        out[:, half:] += product(turn, None)[0]

    edge = jnp.sum(edge, axis=1, keepdims=True)
    lane = lax.broadcasted_iota(jnp.int32, (pairs, LANES), 1)
    mirror = (LANES - lane) % LANES
    first = lane == 0
    listed = mask[...]
    count = half // LANES
    before, after = [], []
    for block in range(count):
        even = out[:, block * LANES : (block + 1) * LANES]
        odd = out[:, half + block * LANES : half + (block + 1) * LANES]
        if block == 0:
            edge = edge + odd
            odd = jnp.where(first, 0.0, odd)
        before.append(even - odd)
        after.append(even + odd)
    for block in range(count):
        turned = jnp.take_along_axis(before[count - 1 - block], mirror, axis=1)
        start = edge if block == 0 else before[count - block]
        out[:, block * LANES : (block + 1) * LANES] = jnp.where(first, start, turned) * listed
        out[:, half + block * LANES : half + (block + 1) * LANES] = after[block] * listed


def lagged(near_pick, far_at, begun, white, far, table, last, mask):
    pairs = mask.shape[0]
    stops = near_pick.shape[0]
    return pl.pallas_call(
        lag_kernel,
        out_shape=jax.ShapeDtypeStruct((pairs, LAGS), jnp.float32),
        in_specs=[SMEM, SMEM] + [ANY] * 4 + [VMEM, VMEM],
        out_specs=VMEM,
        scratch_shapes=[
            pltpu.VMEM(white.shape, jnp.bfloat16),
            pltpu.VMEM(far.shape, jnp.bfloat16),
            pltpu.VMEM((pairs * ROWS, LANES), jnp.float32),
            pltpu.VMEM(table.shape, jnp.bfloat16),
            pltpu.SemaphoreType.DMA,
            pltpu.SemaphoreType.DMA((2, stops)),
            pltpu.SemaphoreType.DMA,
        ],
        compiler_params=pltpu.CompilerParams(vmem_limit_bytes=40 * 1024 * 1024),
        cost_estimate=pl.CostEstimate(
            flops=2 * pairs * NF * LAGS, bytes_accessed=24 * 1024 * 1024, transcendentals=0
        ),
        name="lagged",
    )(near_pick, far_at, begun, white, far, table, last, mask)


def empty(shape):
    return pl.pallas_call(
        lambda out: None,
        out_shape=jax.ShapeDtypeStruct(shape, jnp.bfloat16),
        out_specs=ANY,
        name="empty",
    )()


def on_device(records, lengths, owners, own_pick, visit_pick, pair_mask):
    wide_count = lax.axis_size("wide")
    stops = lax.axis_size("blk")
    column = lax.axis_index("wide")
    group = lax.axis_index("blk")
    core = column % 2
    swap = [(i, i ^ 1) for i in range(wide_count)]
    slots = records.shape[1]
    steps = jnp.arange(stops, dtype=jnp.int32)

    packed = jnp.where(owners[0] >= 0, (owners[0] << LEN_BITS) + lengths[0], -1)
    mate_packed = lax.ppermute(packed, "wide", swap)
    chip_packed = jnp.where(core == 0, jnp.stack([packed, mate_packed]), jnp.stack([mate_packed, packed]))
    core_at = core.reshape(1)

    tiles = records[0].reshape(slots, SEG, ROWS, LANES)

    def halves(part):
        return tiles[:, 2 * part : 2 * part + 2].transpose(0, 2, 1, 3).reshape(slots, 2 * ROWS, LANES)

    def send(payload):
        return lax.all_to_all(payload, "wide", split_axis=0, concat_axis=0, tiled=True)

    own_a = halves(0)
    mate_a = lax.ppermute(own_a, "wide", swap)
    load_a, flag_a = pack(0, BASE, True, wide_count, chip_packed, core_at, own_a, mate_a, core_at)
    got_a = send(load_a)
    own_b = jnp.where(flag_a[0] >= 0, halves(1), 0.0)
    mate_b = lax.ppermute(own_b, "wide", swap)
    load_b, flag_b = pack(0, BASE, False, wide_count, chip_packed, core_at, own_b, mate_b, load_a)
    got_b = send(load_b)
    visits = jnp.where(flag_a[0] >= 0, visit_pick[0, 0].reshape(stops, -1), 0)
    by_stop = jnp.stack(
        [visits[0]]
        + [
            lax.ppermute(visits[stop], "blk", [(i, (i - stop) % stops) for i in range(stops)])
            for stop in range(1, stops)
        ]
    )
    by_dest = by_stop[(steps - group) % stops]

    station, length, spilled = read_notes(got_a, BASE)
    spilled = jnp.max(spilled) > 0

    def late():
        rows = [
            pack(BASE, EXTRA, True, wide_count, chip_packed, core_at, own, mate, core_at)[0]
            for own, mate in ((own_a, mate_a), (own_b, mate_b))
        ]
        return tuple(send(row) for row in rows)

    more = lax.cond(
        spilled,
        late,
        lambda: tuple(empty((wide_count, EXTRA * 2 * ROWS + NOTES, LANES)) for _ in range(2)),
    )
    more_station, more_length, _ = read_notes(more[0], EXTRA)
    station = jnp.concatenate([station.reshape(-1), jnp.where(spilled, more_station.reshape(-1), -1)])
    length = jnp.concatenate([length.reshape(-1), more_length.reshape(-1)])
    chosen = station[None, :] == jnp.arange(ST_DEV, dtype=jnp.int32)[:, None]
    codes = jnp.arange(station.shape[0], dtype=jnp.int32)
    source = jnp.sum(jnp.where(chosen, codes[None], 0), axis=1)
    length = jnp.sum(jnp.where(chosen, length[None], 0), axis=1)

    tables = [jnp.asarray(table) for table in transform_tables()]
    near_pick = own_pick[0, 0].reshape(stops, -1)
    white_a, payload_a = whiten(0, source, length, by_stop, got_a, more[0], tables, [])
    far_a = [
        lax.ppermute(payload_a[stop], "blk", [(i, (i + stop) % stops) for i in range(stops)])
        for stop in range(1, stops)
    ]
    white_b, payload_b = whiten(1, source, length, by_dest, got_b, more[1], tables, far_a)
    far_b = lax.all_to_all(payload_b, "blk", split_axis=0, concat_axis=0, tiled=True)

    begun = cross_first(near_pick, white_a, payload_a, far_a)
    far_at = (group - steps) % stops
    mask = pair_mask[0, 0].astype(jnp.float32).reshape(-1, 1)
    table, last = lag_tables()
    result = lagged(near_pick, far_at, begun, white_b, far_b, jnp.asarray(table), jnp.asarray(last), mask)
    return result.reshape((1, 1) + pair_mask.shape[2:] + (LAGS,))


def solution(mesh):
    return jax.shard_map(
        on_device,
        mesh=mesh,
        in_specs=(
            P("blk", "wide", None, None),
            P("blk", "wide"),
            P("blk", "wide"),
            P("blk", "wide", None, None, None),
            P("blk", "wide", None, None, None),
            P("blk", "wide", None, None, None, None),
        ),
        out_specs=P("blk", "wide", None, None, None, None, None),
        check_vma=False,
    )
```

```python
import functools
import math

import jax
import jax.numpy as jnp
import numpy as np
from jax import lax
from jax.experimental import pallas as pl
from jax.experimental.pallas import tpu as pltpu
from jax.sharding import PartitionSpec as P

ST_DEV = 24
SEG = 4
NT = 8192
NF = 4096
LAGS = 1024
ROWS = 64
LANES = 128
BASE = 2
EXTRA = 1
LEN_BITS = 16
NOTES = 16
ALL_VMEM = 60 * 1024 * 1024
SMEM = pl.BlockSpec(memory_space=pltpu.SMEM)
VMEM = pl.BlockSpec(memory_space=pltpu.VMEM)
ANY = pl.BlockSpec(memory_space=pl.ANY)


def split_bf16(values):
    high = values.astype(jnp.bfloat16)
    low = (values - high.astype(np.float64)).astype(jnp.bfloat16)
    return high, low


def transform_tables():
    first = np.arange(ROWS)
    second = np.arange(LANES)
    half = np.arange(LANES // 2)
    angle = 2.0 * math.pi / ROWS * (first[:, None] * first[None, :] % ROWS)
    wave = np.concatenate([np.cos(angle), -np.sin(angle)], 0)
    wave = np.einsum("ab,kn->aknb", np.eye(2), wave).reshape(4 * ROWS, 2 * ROWS)
    first_table = np.concatenate(split_bf16(wave), 1)
    twist = 2.0 * math.pi / NT * (first[:, None] * second[None, :] % NT)
    twist_table = np.stack([np.cos(twist), np.sin(twist)]).astype(np.float32)
    angle = 2.0 * math.pi / LANES * (second[:, None] * half[None, :] % LANES)
    cos, sin = np.cos(angle), np.sin(angle)
    wave = np.concatenate([np.concatenate([cos, -sin], 1), np.concatenate([sin, cos], 1)], 0)
    second_table = np.concatenate(split_bf16(wave), 1)
    return first_table, twist_table, second_table


def lag_tables():
    row = np.arange(ROWS // 2, dtype=np.int64)
    lane = np.arange(LANES, dtype=np.int64)
    bins = (row[:, None] + ROWS // 2 * (lane // ROWS)) + ROWS * (lane % ROWS)
    bins = bins.reshape(-1)
    weight = np.where(bins == 0, 0.5, 1.0).astype(np.float32) / np.float32(math.sqrt(NF * SEG))

    def at(delay):
        phase = bins[:, None] * delay[None, :] % NT
        return phase.astype(np.float32) * np.float32(2.0 * math.pi / NT)

    ahead = at(np.arange(LAGS // 2, dtype=np.int64))
    edge = at(np.array([NT - LAGS // 2], dtype=np.int64))
    cos = weight[:, None] * np.cos(ahead)
    sin = -weight[:, None] * np.sin(ahead)
    sin[:, :1] = -weight[:, None] * np.sin(edge)
    last = (weight[:, None] * np.cos(edge)).reshape(ROWS // 2, 1, LANES)
    return (
        np.concatenate([cos, sin], 0).astype(jnp.bfloat16),
        last.astype(jnp.bfloat16).astype(np.float32),
    )


def pack_kernel(low, count, noted, packed, core_ref, own, mate, after, out, flag, fill, notes, started, sem):
    core = core_ref[0]
    slots = packed.shape[1]
    devices = out.shape[0]
    started[0] = 0
    flag[0] = 0

    @pl.loop(0, devices)
    def _(dev):
        fill[dev] = 0
        for slot in range(count):
            notes[dev, slot] = -1

    def place(half, source):
        @pl.loop(0, slots)
        def _(at):
            value = packed[half, at]

            @pl.when(value >= 0)
            def _():
                dev = ((value >> LEN_BITS) * 2731) >> 16
                rank = fill[dev]
                fill[dev] = rank + 1
                slot = (rank >> 1) - low

                @pl.when(((rank & 1) == core) & (slot >= 0) & (slot < count))
                def _():
                    started[0] += 1
                    notes[dev, slot] = value - ((dev * ST_DEV) << LEN_BITS)
                    place_at = pl.ds(pl.multiple_of(slot * 2 * ROWS, 2 * ROWS), 2 * ROWS)
                    pltpu.make_async_copy(source.at[at], out.at[dev, place_at], sem).start()

                @pl.when(slot >= count)
                def _():
                    flag[0] = 1

    for half in range(2):

        @pl.when(core == half)
        def _():
            place(half, own)

        @pl.when(core != half)
        def _():
            place(half, mate)

    if noted:
        row = lax.broadcasted_iota(jnp.int32, (NOTES, LANES), 0)

        @pl.loop(0, devices)
        def _(dev):
            tile = jnp.where(row == 4 * count, flag[0], 0)
            for slot in range(count):
                value = notes[dev, slot]
                tile = jnp.where(row == 4 * slot, (value >> LEN_BITS) + 1, tile)
                tile = jnp.where(row == 4 * slot + 1, (value & 0xFFFF) >> 8, tile)
                tile = jnp.where(row == 4 * slot + 2, value & 0xFF, tile)
            out[dev, count * 2 * ROWS :, :] = tile.astype(jnp.float32).astype(jnp.bfloat16)

    @pl.loop(0, started[0])
    def _(_):
        pltpu.make_async_copy(own.at[0], out.at[0, pl.ds(0, 2 * ROWS)], sem).wait()


def pack(low, count, noted, wide_count, packed, core, own, mate, after):
    height = count * 2 * ROWS + (NOTES if noted else 0)
    return pl.pallas_call(
        functools.partial(pack_kernel, low, count, noted),
        out_shape=(
            jax.ShapeDtypeStruct((wide_count, height, LANES), jnp.bfloat16),
            jax.ShapeDtypeStruct((1,), jnp.int32),
        ),
        in_specs=[SMEM, SMEM, ANY, ANY, ANY],
        out_specs=(VMEM, SMEM),
        scratch_shapes=[
            pltpu.SMEM((wide_count,), jnp.int32),
            pltpu.SMEM((wide_count, count), jnp.int32),
            pltpu.SMEM((1,), jnp.int32),
            pltpu.SemaphoreType.DMA,
        ],
        cost_estimate=pl.CostEstimate(flops=0, bytes_accessed=wide_count * count * NT * 8, transcendentals=0),
        name="pack",
    )(packed, core, own, mate, after)


def read_notes(rows, count):
    notes = rows[:, count * 2 * ROWS :, 0].astype(jnp.float32).astype(jnp.int32)
    fields = notes[:, : 4 * count].reshape(-1, count, 4)
    return fields[..., 0] - 1, fields[..., 1] * 256 + fields[..., 2], notes[:, 4 * count]


def whiten_kernel(
    part, source, length, picks, got, more, first, twist, second, *refs
):
    white, payload, held, spectra, sem, sems = refs[-6:]
    stations = held.shape[0]
    first_more = got.shape[0] * BASE
    batch = 8

    @pl.loop(0, stations)
    def _(station):
        code = source[station]
        over = code - first_more

        @pl.when(over < 0)
        def _():
            place_at = pl.ds(pl.multiple_of((code & 1) * 2 * ROWS, 2 * ROWS), 2 * ROWS)
            pltpu.make_async_copy(got.at[code >> 1, place_at], held.at[station], sems.at[station // batch]).start()

        @pl.when(over >= 0)
        def _():
            place_at = pl.ds(0, 2 * ROWS)
            pltpu.make_async_copy(more.at[over, place_at], held.at[station], sems.at[station // batch]).start()

    row = lax.broadcasted_iota(jnp.int32, (2 * ROWS, LANES), 0)
    lane = lax.broadcasted_iota(jnp.int32, (2 * ROWS, LANES), 1)
    left = lax.broadcasted_iota(jnp.int32, (ROWS // 2, LANES), 1) < ROWS
    place = (2 * part + (row & 1)) * NT + (row >> 1) * LANES + lane

    def two_stations(station):
        sides = []
        for at in range(2):
            values = held[station + at].astype(jnp.float32)
            sides.append(jnp.where(place < length[station + at], values, 0.0).astype(jnp.bfloat16))
        values = jnp.concatenate(sides, 1)
        values = jnp.concatenate([values, values], 0)
        mixed = jnp.dot(first[...], values, preferred_element_type=jnp.float32)
        parts = []
        for at in range(2):
            for seg in range(2):
                real = mixed[2 * seg * ROWS : (2 * seg + 1) * ROWS, at * LANES : (at + 1) * LANES]
                imag = mixed[(2 * seg + 1) * ROWS : (2 * seg + 2) * ROWS, at * LANES : (at + 1) * LANES]
                turned_re = real * twist[0] + imag * twist[1]
                turned_im = imag * twist[0] - real * twist[1]
                parts.append(jnp.concatenate([turned_re, turned_im], 1))
        turned = jnp.concatenate(parts, 0)
        high = turned.astype(jnp.bfloat16)
        low = (turned - high.astype(jnp.float32)).astype(jnp.bfloat16)
        upper = jnp.dot(high, second[...], preferred_element_type=jnp.float32)
        lower = jnp.dot(low, second[:, :LANES], preferred_element_type=jnp.float32)
        spectrum = upper[:, :LANES] + (upper[:, LANES:] + lower)
        for at in range(2):
            for seg in range(2):
                begin = (2 * at + seg) * ROWS
                side = spectrum[begin : begin + ROWS]
                power = jnp.sum(side * side, axis=0, keepdims=True)
                power = (power + pltpu.roll(power, LANES // 2, 1)) * (1.0 / ROWS)
                scale = 1.0 / jnp.sqrt(power + 1e-06)
                side = side * scale
                upper, lower = side[: ROWS // 2], side[ROWS // 2 :]
                real = jnp.where(left, upper, pltpu.roll(lower, ROWS, 1))
                imag = jnp.where(left, pltpu.roll(upper, ROWS, 1), lower)
                spectra[station + at, seg, : ROWS // 2] = real.astype(jnp.bfloat16)
                spectra[station + at, seg, ROWS // 2 :] = imag.astype(jnp.bfloat16)

    @pl.loop(0, stations // batch)
    def _(at):
        these = held.at[pl.ds(at * batch, batch)]
        pltpu.make_async_copy(these, these, sems.at[at]).wait()
        for two in range(0, batch, 2):
            two_stations(batch * at + two)

    stops, rows = picks.shape

    @pl.loop(0, stops)
    def _(stop):
        for at in range(rows):
            pltpu.make_async_copy(spectra.at[picks[stop, at]], payload.at[stop, at], sem).start()

    whole = pltpu.make_async_copy(spectra, white, sems.at[0])
    whole.start()
    pltpu.make_async_copy(payload, payload, sem).wait()
    whole.wait()


def whiten(part, source, length, picks, got, more, tables, after):
    stops, rows = picks.shape
    return pl.pallas_call(
        functools.partial(whiten_kernel, part),
        out_shape=(
            jax.ShapeDtypeStruct((ST_DEV, 2, ROWS, LANES), jnp.bfloat16),
            jax.ShapeDtypeStruct((stops, rows, 2, ROWS, LANES), jnp.bfloat16),
        ),
        in_specs=[SMEM, SMEM, SMEM, ANY, ANY, VMEM, VMEM, VMEM] + [ANY] * len(after),
        out_specs=(ANY, ANY),
        scratch_shapes=[
            pltpu.VMEM((ST_DEV, 2 * ROWS, LANES), jnp.bfloat16),
            pltpu.VMEM((ST_DEV, 2, ROWS, LANES), jnp.bfloat16),
            pltpu.SemaphoreType.DMA,
            pltpu.SemaphoreType.DMA((ST_DEV // 8,)),
        ],
        cost_estimate=pl.CostEstimate(
            flops=2 * ST_DEV * 2 * ROWS * 256 * 400, bytes_accessed=4 * 1024 * 1024, transcendentals=0
        ),
        name="whiten",
    )(source, length, picks, got, more, *tables, *after)


def cross_rows(near_pick, near, far, cross, fresh, ready):
    stops, rows = near_pick.shape
    side = rows // 2
    step = 16
    half = ROWS // 2

    @pl.loop(0, stops)
    def _(stop):
        ready(stop)
        for two in range(2):
            first = two * side
            own = [near_pick[stop, first + i] for i in range(side)]

            @pl.loop(0, half // step)
            def _(chunk):
                real = pl.ds(pl.multiple_of(chunk * step, step), step)
                imag = pl.ds(pl.multiple_of(half + chunk * step, step), step)

                def both(ref, row):
                    return [
                        (ref[row, s, real, :].astype(jnp.float32), ref[row, s, imag, :].astype(jnp.float32))
                        for s in range(2)
                    ]

                here = [both(near, own[i]) for i in range(side)]
                for j in range(side):
                    there = both(far.at[stop], first + j)
                    for i in range(side):
                        pair = ((stop * 2 + two) * side + i) * side + j
                        total_re = sum(n[0] * f[0] + n[1] * f[1] for n, f in zip(here[i], there))
                        total_im = sum(n[1] * f[0] - n[0] * f[1] for n, f in zip(here[i], there))
                        for total, add in ((total_re, 0), (total_im, half)):
                            at = pl.ds(pl.multiple_of(pair * ROWS + add + chunk * step, step), step)
                            if fresh:
                                cross[at, :] = total
                            else:
                                cross[at, :] += total


def cross_kernel(stops, near_pick, white, home, *refs):
    far_in = refs[: stops - 1]
    out, near, far, cross, sem, sems, out_sem = refs[stops - 1 :]
    load = pltpu.make_async_copy(white, near, sem)
    load.start()
    pltpu.make_async_copy(home.at[0], far.at[0], sems.at[0]).start()
    for stop in range(1, stops):
        pltpu.make_async_copy(far_in[stop - 1], far.at[stop], sems.at[stop]).start()
    load.wait()

    def ready(stop):
        pltpu.make_async_copy(far.at[stop], far.at[stop], sems.at[stop]).wait()

    cross_rows(near_pick, near, far, cross, True, ready)
    copy = pltpu.make_async_copy(cross, out, out_sem)
    copy.start()
    copy.wait()


def cross_first(near_pick, white, home, far):
    stops, rows = near_pick.shape
    pairs = stops * rows * rows // 2
    return pl.pallas_call(
        functools.partial(cross_kernel, stops),
        out_shape=jax.ShapeDtypeStruct((pairs * ROWS, LANES), jnp.float32),
        in_specs=[SMEM] + [ANY] * (stops + 1),
        out_specs=ANY,
        scratch_shapes=[
            pltpu.VMEM(white.shape, jnp.bfloat16),
            pltpu.VMEM(home.shape, jnp.bfloat16),
            pltpu.VMEM((pairs * ROWS, LANES), jnp.float32),
            pltpu.SemaphoreType.DMA,
            pltpu.SemaphoreType.DMA((stops,)),
            pltpu.SemaphoreType.DMA,
        ],
        compiler_params=pltpu.CompilerParams(vmem_limit_bytes=ALL_VMEM),
        cost_estimate=pl.CostEstimate(
            flops=pairs * ROWS * LANES * 16, bytes_accessed=24 * 1024 * 1024, transcendentals=0
        ),
        name="cross_first",
    )(near_pick, white, home, *far)


def lag_kernel(
    near_pick, far_at, begun, white, far_in, table, last, mask, out, near, far, cross, tables, sem, sems, table_sem
):
    stops = near_pick.shape[0]
    pairs = out.shape[0]
    rows = pairs * ROWS // stops
    load = pltpu.make_async_copy(white, near, sem)
    load.start()
    for stop in range(stops):
        these = pl.ds(stop * rows, rows)
        pltpu.make_async_copy(far_in.at[far_at[stop]], far.at[stop], sems.at[0, stop]).start()
        pltpu.make_async_copy(begun.at[these], cross.at[these], sems.at[1, stop]).start()
    load_table = pltpu.make_async_copy(table, tables, table_sem)
    load_table.start()
    load.wait()

    def ready(stop):
        these = cross.at[pl.ds(pl.multiple_of(stop * rows, rows), rows)]
        pltpu.make_async_copy(far.at[stop], far.at[stop], sems.at[0, stop]).wait()
        pltpu.make_async_copy(these, these, sems.at[1, stop]).wait()

    cross_rows(near_pick, near, far, cross, False, ready)
    load_table.wait()
    group = 8
    depth = group * LANES
    half = LAGS // 2
    turns = ROWS // 2 // group

    def product(turn, edge):
        base = turn * group
        slabs = [
            cross[pl.ds(base + k, pairs, stride=ROWS), :].astype(jnp.bfloat16) for k in range(group)
        ]
        if edge is not None:
            for k in range(group):
                edge += slabs[k].astype(jnp.float32) * last[base + k]
        part = jnp.dot(
            jnp.concatenate(slabs, 1),
            tables[pl.ds(pl.multiple_of(base * LANES, depth), depth), :],
            preferred_element_type=jnp.float32,
        )
        return part, edge

    out[:, :half] = jnp.zeros((pairs, half), jnp.float32)
    out[:, half:] = jnp.zeros((pairs, half), jnp.float32)

    def even_step(turn, edge):
        part, edge = product(turn, edge)
        out[:, :half] += part
        return edge

    edge = lax.fori_loop(0, turns, even_step, jnp.zeros((pairs, LANES), jnp.float32))

    @pl.loop(turns, 2 * turns)
    def _(turn):
        out[:, half:] += product(turn, None)[0]

    edge = jnp.sum(edge, axis=1, keepdims=True)
    lane = lax.broadcasted_iota(jnp.int32, (pairs, LANES), 1)
    mirror = (LANES - lane) % LANES
    first = lane == 0
    listed = mask[...]
    count = half // LANES
    before, after = [], []
    for block in range(count):
        even = out[:, block * LANES : (block + 1) * LANES]
        odd = out[:, half + block * LANES : half + (block + 1) * LANES]
        if block == 0:
            edge = edge + odd
            odd = jnp.where(first, 0.0, odd)
        before.append(even - odd)
        after.append(even + odd)
    for block in range(count):
        turned = jnp.take_along_axis(before[count - 1 - block], mirror, axis=1)
        start = edge if block == 0 else before[count - block]
        out[:, block * LANES : (block + 1) * LANES] = jnp.where(first, start, turned) * listed
        out[:, half + block * LANES : half + (block + 1) * LANES] = after[block] * listed


def lagged(near_pick, far_at, begun, white, far, table, last, mask):
    pairs = mask.shape[0]
    stops = near_pick.shape[0]
    return pl.pallas_call(
        lag_kernel,
        out_shape=jax.ShapeDtypeStruct((pairs, LAGS), jnp.float32),
        in_specs=[SMEM, SMEM] + [ANY] * 4 + [VMEM, VMEM],
        out_specs=VMEM,
        scratch_shapes=[
            pltpu.VMEM(white.shape, jnp.bfloat16),
            pltpu.VMEM(far.shape, jnp.bfloat16),
            pltpu.VMEM((pairs * ROWS, LANES), jnp.float32),
            pltpu.VMEM(table.shape, jnp.bfloat16),
            pltpu.SemaphoreType.DMA,
            pltpu.SemaphoreType.DMA((2, stops)),
            pltpu.SemaphoreType.DMA,
        ],
        compiler_params=pltpu.CompilerParams(vmem_limit_bytes=ALL_VMEM),
        cost_estimate=pl.CostEstimate(
            flops=2 * pairs * NF * LAGS, bytes_accessed=24 * 1024 * 1024, transcendentals=0
        ),
        name="lagged",
    )(near_pick, far_at, begun, white, far, table, last, mask)


def empty(shape):
    return pl.pallas_call(
        lambda out: None,
        out_shape=jax.ShapeDtypeStruct(shape, jnp.bfloat16),
        out_specs=ANY,
        name="empty",
    )()


def on_device(records, lengths, owners, own_pick, visit_pick, pair_mask):
    wide_count = lax.axis_size("wide")
    stops = lax.axis_size("blk")
    column = lax.axis_index("wide")
    group = lax.axis_index("blk")
    core = column % 2
    swap = [(i, i ^ 1) for i in range(wide_count)]
    slots = records.shape[1]
    steps = jnp.arange(stops, dtype=jnp.int32)

    packed = jnp.where(owners[0] >= 0, (owners[0] << LEN_BITS) + lengths[0], -1)
    mate_packed = lax.ppermute(packed, "wide", swap)
    chip_packed = jnp.where(core == 0, jnp.stack([packed, mate_packed]), jnp.stack([mate_packed, packed]))
    core_at = core.reshape(1)

    tiles = records[0].reshape(slots, SEG, ROWS, LANES)

    def halves(part):
        return tiles[:, 2 * part : 2 * part + 2].transpose(0, 2, 1, 3).reshape(slots, 2 * ROWS, LANES)

    def send(payload):
        return lax.all_to_all(payload, "wide", split_axis=0, concat_axis=0, tiled=True)

    own_a = halves(0)
    mate_a = lax.ppermute(own_a, "wide", swap)
    load_a, flag_a = pack(0, BASE, True, wide_count, chip_packed, core_at, own_a, mate_a, core_at)
    got_a = send(load_a)
    own_b = jnp.where(flag_a[0] >= 0, halves(1), 0.0)
    mate_b = lax.ppermute(own_b, "wide", swap)
    visits = jnp.where(flag_a[0] >= 0, visit_pick[0, 0].reshape(stops, -1), 0)
    by_stop = jnp.stack(
        [visits[0]]
        + [
            lax.ppermute(visits[stop], "blk", [(i, (i - stop) % stops) for i in range(stops)])
            for stop in range(1, stops)
        ]
    )
    load_b, _ = pack(0, BASE, False, wide_count, chip_packed, core_at, own_b, mate_b, by_stop)
    got_b = send(load_b)
    by_dest = by_stop[(steps - group) % stops]

    station, length, spilled = read_notes(got_a, BASE)
    spilled = jnp.max(spilled) > 0

    def late():
        rows = [
            send(pack(BASE, EXTRA, True, wide_count, chip_packed, core_at, own, mate, core_at)[0])
            for own, mate in ((own_a, mate_a), (own_b, mate_b))
        ]
        more_station, more_length, _ = read_notes(rows[0], EXTRA)
        return rows[0], rows[1], more_station.reshape(-1), more_length.reshape(-1)

    def never():
        rows = [empty((wide_count, EXTRA * 2 * ROWS + NOTES, LANES)) for _ in range(2)]
        return rows[0], rows[1], jnp.full((wide_count * EXTRA,), -1), jnp.zeros((wide_count * EXTRA,), jnp.int32)

    more_a, more_b, more_station, more_length = lax.cond(spilled, late, never)
    station = jnp.concatenate([station.reshape(-1), more_station])
    length = jnp.concatenate([length.reshape(-1), more_length])
    chosen = station[None, :] == jnp.arange(ST_DEV, dtype=jnp.int32)[:, None]
    codes = jnp.arange(station.shape[0], dtype=jnp.int32)
    source = jnp.sum(jnp.where(chosen, codes[None], 0), axis=1)
    length = jnp.sum(jnp.where(chosen, length[None], 0), axis=1)

    tables = [jnp.asarray(table) for table in transform_tables()]
    near_pick = own_pick[0, 0].reshape(stops, -1)
    white_a, payload_a = whiten(0, source, length, by_stop, got_a, more_a, tables, [])
    far_a = [
        lax.ppermute(payload_a[stop], "blk", [(i, (i + stop) % stops) for i in range(stops)])
        for stop in range(1, stops)
    ]
    white_b, payload_b = whiten(1, source, length, by_dest, got_b, more_b, tables, far_a)
    far_b = lax.all_to_all(payload_b, "blk", split_axis=0, concat_axis=0, tiled=True)

    begun = cross_first(near_pick, white_a, payload_a, far_a)
    far_at = (group - steps) % stops
    mask = pair_mask[0, 0].astype(jnp.float32).reshape(-1, 1)
    table, last = lag_tables()
    result = lagged(near_pick, far_at, begun, white_b, far_b, jnp.asarray(table), jnp.asarray(last), mask)
    return result.reshape((1, 1) + pair_mask.shape[2:] + (LAGS,))


def solution(mesh):
    return jax.shard_map(
        on_device,
        mesh=mesh,
        in_specs=(
            P("blk", "wide", None, None),
            P("blk", "wide"),
            P("blk", "wide"),
            P("blk", "wide", None, None, None),
            P("blk", "wide", None, None, None),
            P("blk", "wide", None, None, None, None),
        ),
        out_specs=P("blk", "wide", None, None, None, None, None),
        check_vma=False,
    )
```

```python
import functools
import math

import jax
import jax.numpy as jnp
import numpy as np
from jax import lax
from jax.experimental import pallas as pl
from jax.experimental.pallas import tpu as pltpu
from jax.sharding import PartitionSpec as P

ST_DEV = 24
SEG = 4
NT = 8192
NF = 4096
LAGS = 1024
ROWS = 64
LANES = 128
BASE = 3
EXTRA = 3
SPILL = 12
LEN_BITS = 16
NOTES = 16
ALL_VMEM = 60 * 1024 * 1024
SMEM = pl.BlockSpec(memory_space=pltpu.SMEM)
VMEM = pl.BlockSpec(memory_space=pltpu.VMEM)
ANY = pl.BlockSpec(memory_space=pl.ANY)


def split_bf16(values):
    high = values.astype(jnp.bfloat16)
    low = (values - high.astype(np.float64)).astype(jnp.bfloat16)
    return high, low


def transform_tables():
    first = np.arange(ROWS)
    second = np.arange(LANES)
    half = np.arange(LANES // 2)
    angle = 2.0 * math.pi / ROWS * (first[:, None] * first[None, :] % ROWS)
    wave = np.concatenate([np.cos(angle), -np.sin(angle)], 0)
    wave = np.einsum("ab,kn->akbn", np.eye(2), wave).reshape(4 * ROWS, 2 * ROWS)
    first_table = np.concatenate(split_bf16(wave), 1)
    twist = 2.0 * math.pi / NT * (first[:, None] * second[None, :] % NT)
    twist_table = np.stack([np.cos(twist), np.sin(twist)]).astype(np.float32)
    angle = 2.0 * math.pi / LANES * (second[:, None] * half[None, :] % LANES)
    cos, sin = np.cos(angle), np.sin(angle)
    wave = np.concatenate([np.concatenate([cos, -sin], 1), np.concatenate([sin, cos], 1)], 0)
    second_table = np.concatenate(split_bf16(wave), 1)
    return first_table, twist_table, second_table


def lag_tables():
    row = np.arange(ROWS // 2, dtype=np.int64)
    lane = np.arange(LANES, dtype=np.int64)
    bins = (row[:, None] + ROWS // 2 * (lane // ROWS)) + ROWS * (lane % ROWS)
    bins = bins.reshape(-1)
    weight = np.where(bins == 0, 0.5, 1.0).astype(np.float32) / np.float32(math.sqrt(NF * SEG))

    def at(delay):
        phase = bins[:, None] * delay[None, :] % NT
        return phase.astype(np.float32) * np.float32(2.0 * math.pi / NT)

    ahead = at(np.arange(LAGS // 2, dtype=np.int64))
    edge = at(np.array([NT - LAGS // 2], dtype=np.int64))
    cos = weight[:, None] * np.cos(ahead)
    sin = -weight[:, None] * np.sin(ahead)
    sin[:, :1] = -weight[:, None] * np.sin(edge)
    last = (weight[:, None] * np.cos(edge)).reshape(ROWS // 2, 1, LANES)
    return (
        np.concatenate([cos, sin], 0).astype(jnp.bfloat16),
        last.astype(jnp.bfloat16).astype(np.float32),
    )


def owner_of(value):
    return ((value >> LEN_BITS) * 2731) >> 16


def unit(slot):
    return pl.ds(pl.multiple_of(slot * ROWS, ROWS), ROWS)


def spill_kernel(table, core_ref, keep, give, same, other, plan, fill, started, sem):
    core = core_ref[0]
    slots = table.shape[1]
    started[0] = 0

    @pl.loop(0, fill.shape[0])
    def _(dev):
        fill[dev] = 0

    for half in range(2):

        @pl.loop(0, slots)
        def _(at):
            value = table[half, at]
            plan[half, at] = -1

            @pl.when(value >= 0)
            def _():
                dev = owner_of(value)
                rank = fill[dev]
                fill[dev] = rank + 1

                @pl.when(rank < BASE)
                def _():
                    plan[half, at] = dev * 4 + rank

                @pl.when((rank >= BASE) & (core == half) & (started[0] < SPILL))
                def _():
                    index = started[0]
                    started[0] = index + 1
                    pltpu.make_async_copy(keep.at[at], same.at[index], sem).start()
                    pltpu.make_async_copy(give.at[at], other.at[index], sem).start()

    @pl.loop(0, 2 * started[0])
    def _(_):
        pltpu.make_async_copy(keep.at[0], same.at[0], sem).wait()


def spill(wide_count, table, core, keep, give):
    buffer = jax.ShapeDtypeStruct((SPILL, ROWS, LANES), jnp.bfloat16)
    return pl.pallas_call(
        spill_kernel,
        out_shape=(
            buffer,
            buffer,
            jax.ShapeDtypeStruct((2, table.shape[1]), jnp.int32),
            jax.ShapeDtypeStruct((wide_count,), jnp.int32),
        ),
        in_specs=[SMEM, SMEM, ANY, ANY],
        out_specs=(VMEM, VMEM, SMEM, SMEM),
        scratch_shapes=[pltpu.SMEM((1,), jnp.int32), pltpu.SemaphoreType.DMA],
        cost_estimate=pl.CostEstimate(flops=0, bytes_accessed=2**20, transcendentals=0),
        name="spill",
    )(table, core, keep, give)


def route_kernel(table, plan, held, guests, tiles, flag, fill, theirs, notes, taken):
    slots = plan.shape[1]
    devices = held.shape[0]
    flag[0] = 0

    @pl.loop(0, devices)
    def _(dev):
        fill[dev] = held[dev]
        theirs[dev] = 0
        for slot in range(BASE):
            notes[dev, slot] = -1

    for half in range(2):
        for at in range(SPILL):
            guests[half, at] = -1

        @pl.loop(0, slots)
        def _(at):
            code = plan[half, at]

            @pl.when(code >= 0)
            def _():
                dev = code >> 2
                notes[dev, code & 3] = table[half, at] - ((dev * ST_DEV) << LEN_BITS)

    for half in range(2):
        taken[0] = 0

        @pl.loop(0, slots)
        def _(at):
            value = table[2 + half, at]

            @pl.when(value >= 0)
            def _():
                dev = owner_of(value)
                rank = theirs[dev]
                theirs[dev] = rank + 1

                @pl.when(rank >= BASE)
                def _():
                    index = taken[0]
                    slot = fill[dev]
                    fits = (index < SPILL) & (slot < BASE)

                    @pl.when(fits)
                    def _():
                        fill[dev] = slot + 1
                        guests[half, index] = dev * 4 + slot
                        notes[dev, slot] = value - ((dev * ST_DEV) << LEN_BITS)

                    @pl.when(jnp.logical_not(fits))
                    def _():
                        flag[0] = 1

                    taken[0] = index + 1

    write_notes(tiles, 0, notes, flag[0])


def write_notes(out, begin, notes, flag):
    count = notes.shape[1]
    row = lax.broadcasted_iota(jnp.int32, (NOTES, LANES), 0)

    @pl.loop(0, notes.shape[0])
    def _(dev):
        tile = jnp.where(row == 4 * count, flag, 0)
        for slot in range(count):
            value = notes[dev, slot]
            tile = jnp.where(row == 4 * slot, (value >> LEN_BITS) + 1, tile)
            tile = jnp.where(row == 4 * slot + 1, (value & 0xFFFF) >> 8, tile)
            tile = jnp.where(row == 4 * slot + 2, value & 0xFF, tile)
        out[dev, begin : begin + NOTES, :] = tile.astype(jnp.float32).astype(jnp.bfloat16)


def route(table, plan, held):
    devices = held.shape[0]
    return pl.pallas_call(
        route_kernel,
        out_shape=(
            jax.ShapeDtypeStruct((2, SPILL), jnp.int32),
            jax.ShapeDtypeStruct((devices, NOTES, LANES), jnp.bfloat16),
            jax.ShapeDtypeStruct((1,), jnp.int32),
        ),
        in_specs=[SMEM] * 3,
        out_specs=(SMEM, VMEM, SMEM),
        scratch_shapes=[
            pltpu.SMEM((devices,), jnp.int32),
            pltpu.SMEM((devices,), jnp.int32),
            pltpu.SMEM((devices, BASE), jnp.int32),
            pltpu.SMEM((1,), jnp.int32),
        ],
        cost_estimate=pl.CostEstimate(flops=0, bytes_accessed=2**18, transcendentals=0),
        name="route",
    )(table, plan, held)


def pack_kernel(noted, plan, guests, core_ref, keep, mate, same, other, *refs):
    tiles = refs[0] if noted else None
    out, flag, started, sem = refs[-4:]
    core = core_ref[0]
    started[0] = 0
    flag[0] = 0

    def place(codes, half, count, source):
        @pl.loop(0, count)
        def _(at):
            code = codes[half, at]

            @pl.when(code >= 0)
            def _():
                started[0] += 1
                pltpu.make_async_copy(source.at[at], out.at[code >> 2, unit(code & 3)], sem).start()

    for half in range(2):

        @pl.when(core == half)
        def _():
            place(plan, half, plan.shape[1], keep)
            place(guests, half, SPILL, same)

        @pl.when(core != half)
        def _():
            place(plan, half, plan.shape[1], mate)
            place(guests, half, SPILL, other)

    if noted:

        @pl.loop(0, out.shape[0])
        def _(dev):
            out[dev, BASE * ROWS :, :] = tiles[dev]

    @pl.loop(0, started[0])
    def _(_):
        pltpu.make_async_copy(keep.at[0], out.at[0, unit(0)], sem).wait()


def pack(plan, guests, core, keep, mate, same, other, tiles, after):
    wide_count = tiles.shape[0]
    noted = after is None
    last = tiles if noted else after
    return pl.pallas_call(
        functools.partial(pack_kernel, noted),
        out_shape=(
            jax.ShapeDtypeStruct((wide_count, BASE * ROWS + (NOTES if noted else 0), LANES), jnp.bfloat16),
            jax.ShapeDtypeStruct((1,), jnp.int32),
        ),
        in_specs=[SMEM, SMEM, SMEM, ANY, ANY, ANY, ANY, VMEM if noted else ANY],
        out_specs=(VMEM, SMEM),
        scratch_shapes=[pltpu.SMEM((1,), jnp.int32), pltpu.SemaphoreType.DMA],
        cost_estimate=pl.CostEstimate(flops=0, bytes_accessed=wide_count * BASE * NT * 4, transcendentals=0),
        name="pack",
    )(plan, guests, core, keep, mate, same, other, last)


def late_kernel(table, core_ref, keep, mate, out, fill, notes, started, sem):
    core = core_ref[0]
    started[0] = 0

    @pl.loop(0, out.shape[0])
    def _(dev):
        fill[dev] = 0
        for slot in range(EXTRA):
            notes[dev, slot] = -1

    def place(half, source):
        @pl.loop(0, table.shape[1])
        def _(at):
            value = table[half, at]

            @pl.when(value >= 0)
            def _():
                dev = owner_of(value)
                rank = fill[dev]
                fill[dev] = rank + 1

                @pl.when((rank >= BASE) & (rank < BASE + EXTRA))
                def _():
                    started[0] += 1
                    notes[dev, rank - BASE] = value - ((dev * ST_DEV) << LEN_BITS)
                    pltpu.make_async_copy(source.at[at], out.at[dev, unit(rank - BASE)], sem).start()

    for half in range(2):

        @pl.when(core == half)
        def _():
            place(half, keep)

        @pl.when(core != half)
        def _():
            place(half, mate)

    write_notes(out, EXTRA * ROWS, notes, 0)

    @pl.loop(0, started[0])
    def _(_):
        pltpu.make_async_copy(keep.at[0], out.at[0, unit(0)], sem).wait()


def pack_late(wide_count, table, core, keep, mate):
    return pl.pallas_call(
        late_kernel,
        out_shape=jax.ShapeDtypeStruct((wide_count, EXTRA * ROWS + NOTES, LANES), jnp.bfloat16),
        in_specs=[SMEM, SMEM, ANY, ANY],
        out_specs=VMEM,
        scratch_shapes=[
            pltpu.SMEM((wide_count,), jnp.int32),
            pltpu.SMEM((wide_count, EXTRA), jnp.int32),
            pltpu.SMEM((1,), jnp.int32),
            pltpu.SemaphoreType.DMA,
        ],
        cost_estimate=pl.CostEstimate(flops=0, bytes_accessed=wide_count * EXTRA * NT * 4, transcendentals=0),
        name="pack_late",
    )(table, core, keep, mate)


def read_notes(rows, count):
    notes = rows[::2, count * ROWS :, 0].astype(jnp.float32).astype(jnp.int32)
    fields = notes[:, : 4 * count].reshape(-1, count, 4)
    station, length = fields[..., 0] - 1, fields[..., 1] * 256 + fields[..., 2]
    return station.reshape(-1), length.reshape(-1), notes[:, 4 * count]


def whiten_kernel(
    part, parts, source, length, picks, got, more, first, twist, second, *refs
):
    held, spectra, sem, sems = refs[-4:]
    stops, rows = picks.shape
    white = refs[-5 - parts]
    payload = refs[-4 - parts : -4]
    stations = held.shape[0]
    first_more = got.shape[0] // 2 * BASE
    batch = 8

    def fetch(rows, code, count, station):
        for seg in range(2):
            source_at = rows.at[2 * (code // count) + seg, unit(code % count)]
            pltpu.make_async_copy(source_at, held.at[station, unit(seg)], sems.at[station // batch]).start()

    @pl.loop(0, stations)
    def _(station):
        code = source[station]

        @pl.when(code < first_more)
        def _():
            fetch(got, code, BASE, station)

        @pl.when(code >= first_more)
        def _():
            fetch(more, code - first_more, EXTRA, station)

    row = lax.broadcasted_iota(jnp.int32, (2 * ROWS, LANES), 0)
    lane = lax.broadcasted_iota(jnp.int32, (2 * ROWS, LANES), 1)
    left = lax.broadcasted_iota(jnp.int32, (ROWS // 2, LANES), 1) < ROWS
    place = (2 * part + row // ROWS) * NT + (row % ROWS) * LANES + lane

    def two_stations(station):
        sides = []
        for at in range(2):
            values = held[station + at].astype(jnp.float32)
            sides.append(jnp.where(place < length[station + at], values, 0.0).astype(jnp.bfloat16))
        values = jnp.concatenate(sides, 1)
        values = jnp.concatenate([values, values], 0)
        mixed = jnp.dot(first[...], values, preferred_element_type=jnp.float32)
        parts = []
        for at in range(2):
            for seg in range(2):
                real = mixed[2 * seg * ROWS : (2 * seg + 1) * ROWS, at * LANES : (at + 1) * LANES]
                imag = mixed[(2 * seg + 1) * ROWS : (2 * seg + 2) * ROWS, at * LANES : (at + 1) * LANES]
                turned_re = real * twist[0] + imag * twist[1]
                turned_im = imag * twist[0] - real * twist[1]
                parts.append(jnp.concatenate([turned_re, turned_im], 1))
        turned = jnp.concatenate(parts, 0)
        high = turned.astype(jnp.bfloat16)
        low = (turned - high.astype(jnp.float32)).astype(jnp.bfloat16)
        upper = jnp.dot(high, second[...], preferred_element_type=jnp.float32)
        lower = jnp.dot(low, second[:, :LANES], preferred_element_type=jnp.float32)
        spectrum = upper[:, :LANES] + (upper[:, LANES:] + lower)
        for at in range(2):
            for seg in range(2):
                begin = (2 * at + seg) * ROWS
                side = spectrum[begin : begin + ROWS]
                power = jnp.sum(side * side, axis=0, keepdims=True)
                power = (power + pltpu.roll(power, LANES // 2, 1)) * (1.0 / ROWS)
                scale = 1.0 / jnp.sqrt(power + 1e-06)
                side = side * scale
                upper, lower = side[: ROWS // 2], side[ROWS // 2 :]
                real = jnp.where(left, upper, pltpu.roll(lower, ROWS, 1))
                imag = jnp.where(left, pltpu.roll(upper, ROWS, 1), lower)
                spectra[station + at, seg, : ROWS // 2] = real.astype(jnp.bfloat16)
                spectra[station + at, seg, ROWS // 2 :] = imag.astype(jnp.bfloat16)

    @pl.loop(0, stations // batch)
    def _(at):
        these = held.at[pl.ds(at * batch, batch)]
        pltpu.make_async_copy(these, these, sems.at[at]).wait()
        for two in range(0, batch, 2):
            two_stations(batch * at + two)

    each = stops // parts
    for piece in range(parts):

        @pl.loop(0, each)
        def _(stop):
            for at in range(rows):
                row = spectra.at[picks[piece * each + stop, at]]
                pltpu.make_async_copy(row, payload[piece].at[stop, at], sem).start()

    whole = pltpu.make_async_copy(spectra, white, sems.at[0])
    whole.start()
    for piece in range(parts):
        pltpu.make_async_copy(payload[piece], payload[piece], sem).wait()
    whole.wait()


def whiten(part, parts, source, length, picks, got, more, tables, after):
    stops, rows = picks.shape
    piece = jax.ShapeDtypeStruct((stops // parts, rows, 2, ROWS, LANES), jnp.bfloat16)
    return pl.pallas_call(
        functools.partial(whiten_kernel, part, parts),
        out_shape=(jax.ShapeDtypeStruct((ST_DEV, 2, ROWS, LANES), jnp.bfloat16),) + (piece,) * parts,
        in_specs=[SMEM, SMEM, SMEM, ANY, ANY, VMEM, VMEM, VMEM] + [ANY] * len(after),
        out_specs=(ANY,) * (1 + parts),
        scratch_shapes=[
            pltpu.VMEM((ST_DEV, 2 * ROWS, LANES), jnp.bfloat16),
            pltpu.VMEM((ST_DEV, 2, ROWS, LANES), jnp.bfloat16),
            pltpu.SemaphoreType.DMA,
            pltpu.SemaphoreType.DMA((ST_DEV // 8,)),
        ],
        cost_estimate=pl.CostEstimate(
            flops=2 * ST_DEV * 2 * ROWS * 256 * 400, bytes_accessed=4 * 1024 * 1024, transcendentals=0
        ),
        name="whiten",
    )(source, length, picks, got, more, *tables, *after)


def cross_rows(near_pick, near, far, cross, fresh, ready):
    stops, rows = near_pick.shape
    side = rows // 2
    step = 16
    half = ROWS // 2

    @pl.loop(0, stops)
    def _(stop):
        ready(stop)
        for two in range(2):
            first = two * side
            own = [near_pick[stop, first + i] for i in range(side)]

            @pl.loop(0, half // step)
            def _(chunk):
                real = pl.ds(pl.multiple_of(chunk * step, step), step)
                imag = pl.ds(pl.multiple_of(half + chunk * step, step), step)

                def both(ref, row):
                    return [
                        (ref[row, s, real, :].astype(jnp.float32), ref[row, s, imag, :].astype(jnp.float32))
                        for s in range(2)
                    ]

                here = [both(near, own[i]) for i in range(side)]
                for j in range(side):
                    there = both(far.at[stop], first + j)
                    for i in range(side):
                        pair = ((stop * 2 + two) * side + i) * side + j
                        total_re = sum(n[0] * f[0] + n[1] * f[1] for n, f in zip(here[i], there))
                        total_im = sum(n[1] * f[0] - n[0] * f[1] for n, f in zip(here[i], there))
                        for total, add in ((total_re, 0), (total_im, half)):
                            at = pl.ds(pl.multiple_of(pair * ROWS + add + chunk * step, step), step)
                            if fresh:
                                cross[at, :] = total
                            else:
                                cross[at, :] += total


def cross_kernel(stops, near_pick, white, home, *refs):
    far_in = refs[: stops - 1]
    out, near, far, cross, sem, sems, out_sem = refs[stops - 1 :]
    load = pltpu.make_async_copy(white, near, sem)
    load.start()
    pltpu.make_async_copy(home, far.at[0], sems.at[0]).start()
    for stop in range(1, stops):
        pltpu.make_async_copy(far_in[stop - 1], far.at[stop], sems.at[stop]).start()
    load.wait()

    def ready(stop):
        pltpu.make_async_copy(far.at[stop], far.at[stop], sems.at[stop]).wait()

    cross_rows(near_pick, near, far, cross, True, ready)
    copy = pltpu.make_async_copy(cross, out, out_sem)
    copy.start()
    copy.wait()


def cross_first(near_pick, white, home, far):
    stops, rows = near_pick.shape
    pairs = stops * rows * rows // 2
    return pl.pallas_call(
        functools.partial(cross_kernel, stops),
        out_shape=jax.ShapeDtypeStruct((pairs * ROWS, LANES), jnp.float32),
        in_specs=[SMEM] + [ANY] * (stops + 1),
        out_specs=ANY,
        scratch_shapes=[
            pltpu.VMEM(white.shape, jnp.bfloat16),
            pltpu.VMEM((stops,) + home.shape, jnp.bfloat16),
            pltpu.VMEM((pairs * ROWS, LANES), jnp.float32),
            pltpu.SemaphoreType.DMA,
            pltpu.SemaphoreType.DMA((stops,)),
            pltpu.SemaphoreType.DMA,
        ],
        compiler_params=pltpu.CompilerParams(vmem_limit_bytes=ALL_VMEM),
        cost_estimate=pl.CostEstimate(
            flops=pairs * ROWS * LANES * 16, bytes_accessed=24 * 1024 * 1024, transcendentals=0
        ),
        name="cross_first",
    )(near_pick, white, home, *far)


def lag_kernel(
    near_pick, far_at, begun, white, far_in, table, last, mask, out, near, far, cross, tables, sem, sems, table_sem
):
    stops = near_pick.shape[0]
    pairs = out.shape[0]
    rows = pairs * ROWS // stops
    load = pltpu.make_async_copy(white, near, sem)
    load.start()
    for stop in range(stops):
        these = pl.ds(stop * rows, rows)
        pltpu.make_async_copy(far_in.at[far_at[stop]], far.at[stop], sems.at[0, stop]).start()
        pltpu.make_async_copy(begun.at[these], cross.at[these], sems.at[1, stop]).start()
    load_table = pltpu.make_async_copy(table, tables, table_sem)
    load_table.start()
    load.wait()

    def ready(stop):
        these = cross.at[pl.ds(pl.multiple_of(stop * rows, rows), rows)]
        pltpu.make_async_copy(far.at[stop], far.at[stop], sems.at[0, stop]).wait()
        pltpu.make_async_copy(these, these, sems.at[1, stop]).wait()

    cross_rows(near_pick, near, far, cross, False, ready)
    load_table.wait()
    group = 8
    depth = group * LANES
    half = LAGS // 2
    turns = ROWS // 2 // group

    def product(turn, edge):
        base = turn * group
        slabs = [
            cross[pl.ds(base + k, pairs, stride=ROWS), :].astype(jnp.bfloat16) for k in range(group)
        ]
        if edge is not None:
            for k in range(group):
                edge += slabs[k].astype(jnp.float32) * last[base + k]
        part = jnp.dot(
            jnp.concatenate(slabs, 1),
            tables[pl.ds(pl.multiple_of(base * LANES, depth), depth), :],
            preferred_element_type=jnp.float32,
        )
        return part, edge

    out[:, :half] = jnp.zeros((pairs, half), jnp.float32)
    out[:, half:] = jnp.zeros((pairs, half), jnp.float32)

    def even_step(turn, edge):
        part, edge = product(turn, edge)
        out[:, :half] += part
        return edge

    edge = lax.fori_loop(0, turns, even_step, jnp.zeros((pairs, LANES), jnp.float32))

    @pl.loop(turns, 2 * turns)
    def _(turn):
        out[:, half:] += product(turn, None)[0]

    edge = jnp.sum(edge, axis=1, keepdims=True)
    lane = lax.broadcasted_iota(jnp.int32, (pairs, LANES), 1)
    mirror = (LANES - lane) % LANES
    first = lane == 0
    listed = mask[...]
    count = half // LANES
    before, after = [], []
    for block in range(count):
        even = out[:, block * LANES : (block + 1) * LANES]
        odd = out[:, half + block * LANES : half + (block + 1) * LANES]
        if block == 0:
            edge = edge + odd
            odd = jnp.where(first, 0.0, odd)
        before.append(even - odd)
        after.append(even + odd)
    for block in range(count):
        turned = jnp.take_along_axis(before[count - 1 - block], mirror, axis=1)
        start = edge if block == 0 else before[count - block]
        out[:, block * LANES : (block + 1) * LANES] = jnp.where(first, start, turned) * listed
        out[:, half + block * LANES : half + (block + 1) * LANES] = after[block] * listed


def lagged(near_pick, far_at, begun, white, far, table, last, mask):
    pairs = mask.shape[0]
    stops = near_pick.shape[0]
    return pl.pallas_call(
        lag_kernel,
        out_shape=jax.ShapeDtypeStruct((pairs, LAGS), jnp.float32),
        in_specs=[SMEM, SMEM] + [ANY] * 4 + [VMEM, VMEM],
        out_specs=VMEM,
        scratch_shapes=[
            pltpu.VMEM(white.shape, jnp.bfloat16),
            pltpu.VMEM(far.shape, jnp.bfloat16),
            pltpu.VMEM((pairs * ROWS, LANES), jnp.float32),
            pltpu.VMEM(table.shape, jnp.bfloat16),
            pltpu.SemaphoreType.DMA,
            pltpu.SemaphoreType.DMA((2, stops)),
            pltpu.SemaphoreType.DMA,
        ],
        compiler_params=pltpu.CompilerParams(vmem_limit_bytes=ALL_VMEM),
        cost_estimate=pl.CostEstimate(
            flops=2 * pairs * NF * LAGS, bytes_accessed=24 * 1024 * 1024, transcendentals=0
        ),
        name="lagged",
    )(near_pick, far_at, begun, white, far, table, last, mask)


def empty(shape):
    return pl.pallas_call(
        lambda out: None,
        out_shape=jax.ShapeDtypeStruct(shape, jnp.bfloat16),
        out_specs=ANY,
        name="empty",
    )()


def on_device(records, lengths, owners, own_pick, visit_pick, pair_mask):
    wide_count = lax.axis_size("wide")
    stops = lax.axis_size("blk")
    column = lax.axis_index("wide")
    group = lax.axis_index("blk")
    core = column % 2
    slots = records.shape[1]
    steps = jnp.arange(stops, dtype=jnp.int32)
    core_at = core.reshape(1)

    def across(shard, bits):
        return lax.ppermute(shard, "wide", [(i, i ^ bits) for i in range(wide_count)])

    over = wide_count // 2
    packed = jnp.where(owners[0] >= 0, (owners[0] << LEN_BITS) + lengths[0], -1)
    others = [across(packed, bits) for bits in (1, over, over + 1)]
    table = jnp.where(
        core == 0,
        jnp.stack([packed, others[0], others[1], others[2]]),
        jnp.stack([others[0], packed, others[2], others[1]]),
    )

    def segments(part):
        sides = [records[0][:, 2 * part + seg].reshape(slots, ROWS, LANES) for seg in range(2)]
        return jnp.where(core == 0, sides[0], sides[1]), jnp.where(core == 0, sides[1], sides[0])

    def send(payload):
        return lax.all_to_all(payload, "wide", split_axis=0, concat_axis=0, tiled=True)

    keep_a, give_a = segments(0)
    mate_a = across(give_a, 1)
    same_a, other_a, plan, held = spill(wide_count, table, core_at, keep_a, give_a)
    same_a, other_a = across(same_a, over), across(other_a, over + 1)
    guests, tiles, _ = route(table, plan, held)
    load_a, flag_a = pack(plan, guests, core_at, keep_a, mate_a, same_a, other_a, tiles, None)
    got_a = send(load_a)
    keep_b, give_b = (jnp.where(flag_a[0] >= 0, side, 0.0) for side in segments(1))
    mate_b = across(give_b, 1)
    same_b, other_b, _, _ = spill(wide_count, table, core_at, keep_b, give_b)
    same_b, other_b = across(same_b, over), across(other_b, over + 1)
    visits = jnp.where(flag_a[0] >= 0, visit_pick[0, 0].reshape(stops, -1), 0)
    by_stop = jnp.stack(
        [visits[0]]
        + [
            lax.ppermute(visits[stop], "blk", [(i, (i - stop) % stops) for i in range(stops)])
            for stop in range(1, stops)
        ]
    )
    load_b, _ = pack(plan, guests, core_at, keep_b, mate_b, same_b, other_b, tiles, by_stop)
    got_b = send(load_b)
    by_dest = by_stop[(steps - group) % stops]

    station, length, spilled = read_notes(got_a, BASE)
    spilled = jnp.max(spilled) > 0

    def late():
        rows = [
            send(pack_late(wide_count, table, core_at, keep, mate))
            for keep, mate in ((keep_a, mate_a), (keep_b, mate_b))
        ]
        return (rows[0], rows[1]) + read_notes(rows[0], EXTRA)[:2]

    def never():
        rows = [empty((wide_count, EXTRA * ROWS + NOTES, LANES)) for _ in range(2)]
        count = wide_count // 2 * EXTRA
        return rows[0], rows[1], jnp.full((count,), -1, jnp.int32), jnp.zeros((count,), jnp.int32)

    more_a, more_b, more_station, more_length = lax.cond(spilled, late, never)
    station = jnp.concatenate([station, more_station])
    length = jnp.concatenate([length, more_length])
    chosen = station[None, :] == jnp.arange(ST_DEV, dtype=jnp.int32)[:, None]
    codes = jnp.arange(station.shape[0], dtype=jnp.int32)
    source = jnp.max(jnp.where(chosen, codes[None], 0), axis=1)
    length = jnp.max(jnp.where(chosen, length[None], 0), axis=1)

    tables = [jnp.asarray(table) for table in transform_tables()]
    near_pick = own_pick[0, 0].reshape(stops, -1)
    white_a, home, *payload_a = whiten(0, stops, source, length, by_stop, got_a, more_a, tables, [])
    far_a = [
        lax.ppermute(payload_a[stop - 1][0], "blk", [(i, (i + stop) % stops) for i in range(stops)])
        for stop in range(1, stops)
    ]
    white_b, payload_b = whiten(1, 1, source, length, by_dest, got_b, more_b, tables, far_a)
    far_b = lax.all_to_all(payload_b, "blk", split_axis=0, concat_axis=0, tiled=True)

    begun = cross_first(near_pick, white_a, home[0], far_a)
    far_at = (group - steps) % stops
    mask = pair_mask[0, 0].astype(jnp.float32).reshape(-1, 1)
    lags, last = lag_tables()
    result = lagged(near_pick, far_at, begun, white_b, far_b, jnp.asarray(lags), jnp.asarray(last), mask)
    return result.reshape((1, 1) + pair_mask.shape[2:] + (LAGS,))


def solution(mesh):
    return jax.shard_map(
        on_device,
        mesh=mesh,
        in_specs=(
            P("blk", "wide", None, None),
            P("blk", "wide"),
            P("blk", "wide"),
            P("blk", "wide", None, None, None),
            P("blk", "wide", None, None, None),
            P("blk", "wide", None, None, None, None),
        ),
        out_specs=P("blk", "wide", None, None, None, None, None),
        check_vma=False,
    )
```

```python
import functools
import math

import jax
import jax.numpy as jnp
import numpy as np
from jax import lax
from jax.experimental import pallas as pl
from jax.experimental.pallas import tpu as pltpu
from jax.sharding import PartitionSpec as P

ST_DEV = 24
SEG = 4
NT = 8192
NF = 4096
LAGS = 1024
ROWS = 64
LANES = 128
BASE = 3
EXTRA = 3
SPILL = 12
LEN_BITS = 16
NOTES = 16
SMEM = pl.BlockSpec(memory_space=pltpu.SMEM)
VMEM = pl.BlockSpec(memory_space=pltpu.VMEM)
ANY = pl.BlockSpec(memory_space=pl.ANY)


def split_bf16(values):
    high = values.astype(jnp.bfloat16)
    low = (values - high.astype(np.float64)).astype(jnp.bfloat16)
    return high, low


def transform_tables():
    first = np.arange(ROWS)
    second = np.arange(LANES)
    half = np.arange(LANES // 2)
    angle = 2.0 * math.pi / ROWS * (first[:, None] * first[None, :] % ROWS)
    wave = np.concatenate([np.cos(angle), -np.sin(angle)], 0)
    wave = np.einsum("ab,kn->aknb", np.eye(2), wave).reshape(4 * ROWS, 2 * ROWS)
    first_table = np.concatenate(split_bf16(wave), 1)
    twist = 2.0 * math.pi / NT * (first[:, None] * second[None, :] % NT)
    twist_table = np.stack([np.cos(twist), np.sin(twist)]).astype(np.float32)
    angle = 2.0 * math.pi / LANES * (second[:, None] * half[None, :] % LANES)
    cos, sin = np.cos(angle), np.sin(angle)
    wave = np.concatenate([np.concatenate([cos, -sin], 1), np.concatenate([sin, cos], 1)], 0)
    second_table = np.concatenate(split_bf16(wave), 1)
    return first_table, twist_table, second_table


def lag_tables():
    row = np.arange(ROWS // 2, dtype=np.int64)
    lane = np.arange(LANES, dtype=np.int64)
    bins = (row[:, None] + ROWS // 2 * (lane // ROWS)) + ROWS * (lane % ROWS)
    bins = bins.reshape(-1)
    weight = np.where(bins == 0, 0.5, 1.0).astype(np.float32) / np.float32(math.sqrt(NF * SEG))

    def at(delay):
        phase = bins[:, None] * delay[None, :] % NT
        return phase.astype(np.float32) * np.float32(2.0 * math.pi / NT)

    ahead = at(np.arange(LAGS // 2, dtype=np.int64))
    edge = at(np.array([NT - LAGS // 2], dtype=np.int64))
    cos = weight[:, None] * np.cos(ahead)
    sin = -weight[:, None] * np.sin(ahead)
    sin[:, :1] = -weight[:, None] * np.sin(edge)
    last = (weight[:, None] * np.cos(edge)).reshape(ROWS // 2, 1, LANES)
    return (
        np.concatenate([cos, sin], 0).astype(jnp.bfloat16),
        last.astype(jnp.bfloat16).astype(np.float32),
    )


def owner_of(value):
    return ((value >> LEN_BITS) * 2731) >> 16


def unit(slot):
    return pl.ds(pl.multiple_of(slot * ROWS, ROWS), ROWS)


def spill_kernel(table, core_ref, own, same, other, plan, fill, notes, started, sem):
    core = core_ref[0]
    slots = table.shape[1]
    started[0] = 0

    @pl.loop(0, fill.shape[0])
    def _(dev):
        fill[dev] = 0
        for slot in range(BASE):
            notes[dev, slot] = -1

    for half in range(2):

        @pl.loop(0, slots)
        def _(at):
            value = table[half, at]
            plan[half, at] = -1

            @pl.when(value >= 0)
            def _():
                dev = owner_of(value)
                rank = fill[dev]
                fill[dev] = rank + 1

                @pl.when(rank < BASE)
                def _():
                    plan[half, at] = dev * 4 + rank
                    notes[dev, rank] = value - ((dev * ST_DEV) << LEN_BITS)

                @pl.when((rank >= BASE) & (core == half) & (started[0] < SPILL))
                def _():
                    index = started[0]
                    started[0] = index + 1
                    pltpu.make_async_copy(own.at[at, unit(core)], same.at[index], sem).start()
                    pltpu.make_async_copy(own.at[at, unit(1 - core)], other.at[index], sem).start()

    @pl.loop(0, 2 * started[0])
    def _(_):
        pltpu.make_async_copy(own.at[0, unit(0)], same.at[0], sem).wait()


def spill(wide_count, table, core, own):
    buffer = jax.ShapeDtypeStruct((SPILL, ROWS, LANES), jnp.bfloat16)
    return pl.pallas_call(
        spill_kernel,
        out_shape=(
            buffer,
            buffer,
            jax.ShapeDtypeStruct((2, table.shape[1]), jnp.int32),
            jax.ShapeDtypeStruct((wide_count,), jnp.int32),
            jax.ShapeDtypeStruct((wide_count, BASE), jnp.int32),
        ),
        in_specs=[SMEM, SMEM, ANY],
        out_specs=(VMEM, VMEM, SMEM, SMEM, SMEM),
        scratch_shapes=[pltpu.SMEM((1,), jnp.int32), pltpu.SemaphoreType.DMA],
        cost_estimate=pl.CostEstimate(flops=0, bytes_accessed=2**20, transcendentals=0),
        name="spill",
    )(table, core, own)


def route_kernel(table, plan, held, noted, guests, tiles, flag, fill, theirs, notes, taken):
    slots = plan.shape[1]
    devices = held.shape[0]
    flag[0] = 0

    @pl.loop(0, devices)
    def _(dev):
        fill[dev] = held[dev]
        theirs[dev] = 0
        for slot in range(BASE):
            notes[dev, slot] = noted[dev, slot]

    for half in range(2):
        for at in range(SPILL):
            guests[half, at] = -1

    for half in range(2):
        taken[0] = 0

        @pl.loop(0, slots)
        def _(at):
            value = table[2 + half, at]

            @pl.when(value >= 0)
            def _():
                dev = owner_of(value)
                rank = theirs[dev]
                theirs[dev] = rank + 1

                @pl.when(rank >= BASE)
                def _():
                    index = taken[0]
                    slot = fill[dev]
                    fits = (index < SPILL) & (slot < BASE)

                    @pl.when(fits)
                    def _():
                        fill[dev] = slot + 1
                        guests[half, index] = dev * 4 + slot
                        notes[dev, slot] = value - ((dev * ST_DEV) << LEN_BITS)

                    @pl.when(jnp.logical_not(fits))
                    def _():
                        flag[0] = 1

                    taken[0] = index + 1

    write_notes(tiles, 0, notes, flag[0])


def write_notes(out, begin, notes, flag):
    count = notes.shape[1]
    row = lax.broadcasted_iota(jnp.int32, (NOTES, LANES), 0)

    @pl.loop(0, notes.shape[0])
    def _(dev):
        tile = jnp.where(row == 4 * count, flag, 0)
        for slot in range(count):
            value = notes[dev, slot]
            tile = jnp.where(row == 4 * slot, (value >> LEN_BITS) + 1, tile)
            tile = jnp.where(row == 4 * slot + 1, (value & 0xFFFF) >> 8, tile)
            tile = jnp.where(row == 4 * slot + 2, value & 0xFF, tile)
        out[dev, begin : begin + NOTES, :] = tile.astype(jnp.float32).astype(jnp.bfloat16)


def route(table, plan, held, noted):
    devices = held.shape[0]
    return pl.pallas_call(
        route_kernel,
        out_shape=(
            jax.ShapeDtypeStruct((2, SPILL), jnp.int32),
            jax.ShapeDtypeStruct((devices, NOTES, LANES), jnp.bfloat16),
            jax.ShapeDtypeStruct((1,), jnp.int32),
        ),
        in_specs=[SMEM] * 4,
        out_specs=(SMEM, VMEM, SMEM),
        scratch_shapes=[
            pltpu.SMEM((devices,), jnp.int32),
            pltpu.SMEM((devices,), jnp.int32),
            pltpu.SMEM((devices, BASE), jnp.int32),
            pltpu.SMEM((1,), jnp.int32),
        ],
        cost_estimate=pl.CostEstimate(flops=0, bytes_accessed=2**18, transcendentals=0),
        name="route",
    )(table, plan, held, noted)


def pack_kernel(noted, plan, guests, core_ref, own, mate, same, other, *refs):
    tiles = refs[0] if noted else None
    out, flag, started, sem = refs[-4:]
    core = core_ref[0]
    started[0] = 0
    flag[0] = 0

    def place(codes, half, count, source, guest):
        @pl.loop(0, count)
        def _(at):
            code = codes[half, at]

            @pl.when(code >= 0)
            def _():
                started[0] += 1
                rows = source.at[at] if guest else source.at[at, unit(core)]
                pltpu.make_async_copy(rows, out.at[code >> 2, unit(code & 3)], sem).start()

    for half in range(2):

        @pl.when(core == half)
        def _():
            place(plan, half, plan.shape[1], own, False)
            place(guests, half, SPILL, same, True)

        @pl.when(core != half)
        def _():
            place(plan, half, plan.shape[1], mate, False)
            place(guests, half, SPILL, other, True)

    if noted:

        @pl.loop(0, out.shape[0])
        def _(dev):
            out[dev, BASE * ROWS :, :] = tiles[dev]

    @pl.loop(0, started[0])
    def _(_):
        pltpu.make_async_copy(own.at[0, unit(0)], out.at[0, unit(0)], sem).wait()


def pack(plan, guests, core, own, mate, same, other, tiles, after):
    wide_count = tiles.shape[0]
    noted = after is None
    last = tiles if noted else after
    return pl.pallas_call(
        functools.partial(pack_kernel, noted),
        out_shape=(
            jax.ShapeDtypeStruct((wide_count, BASE * ROWS + (NOTES if noted else 0), LANES), jnp.bfloat16),
            jax.ShapeDtypeStruct((1,), jnp.int32),
        ),
        in_specs=[SMEM, SMEM, SMEM, ANY, ANY, ANY, ANY, VMEM if noted else ANY],
        out_specs=(VMEM, SMEM),
        scratch_shapes=[pltpu.SMEM((1,), jnp.int32), pltpu.SemaphoreType.DMA],
        cost_estimate=pl.CostEstimate(flops=0, bytes_accessed=wide_count * BASE * NT * 4, transcendentals=0),
        name="pack",
    )(plan, guests, core, own, mate, same, other, last)


def late_kernel(table, core_ref, own, mate, out, fill, notes, started, sem):
    core = core_ref[0]
    started[0] = 0

    @pl.loop(0, out.shape[0])
    def _(dev):
        fill[dev] = 0
        for slot in range(EXTRA):
            notes[dev, slot] = -1

    def place(half, source):
        @pl.loop(0, table.shape[1])
        def _(at):
            value = table[half, at]

            @pl.when(value >= 0)
            def _():
                dev = owner_of(value)
                rank = fill[dev]
                fill[dev] = rank + 1

                @pl.when((rank >= BASE) & (rank < BASE + EXTRA))
                def _():
                    started[0] += 1
                    notes[dev, rank - BASE] = value - ((dev * ST_DEV) << LEN_BITS)
                    rows = source.at[at, unit(core)]
                    pltpu.make_async_copy(rows, out.at[dev, unit(rank - BASE)], sem).start()

    for half in range(2):

        @pl.when(core == half)
        def _():
            place(half, own)

        @pl.when(core != half)
        def _():
            place(half, mate)

    write_notes(out, EXTRA * ROWS, notes, 0)

    @pl.loop(0, started[0])
    def _(_):
        pltpu.make_async_copy(own.at[0, unit(0)], out.at[0, unit(0)], sem).wait()


def pack_late(wide_count, table, core, own, mate):
    return pl.pallas_call(
        late_kernel,
        out_shape=jax.ShapeDtypeStruct((wide_count, EXTRA * ROWS + NOTES, LANES), jnp.bfloat16),
        in_specs=[SMEM, SMEM, ANY, ANY],
        out_specs=VMEM,
        scratch_shapes=[
            pltpu.SMEM((wide_count,), jnp.int32),
            pltpu.SMEM((wide_count, EXTRA), jnp.int32),
            pltpu.SMEM((1,), jnp.int32),
            pltpu.SemaphoreType.DMA,
        ],
        cost_estimate=pl.CostEstimate(flops=0, bytes_accessed=wide_count * EXTRA * NT * 4, transcendentals=0),
        name="pack_late",
    )(table, core, own, mate)


def read_notes(rows, count):
    notes = rows[::2, count * ROWS :, 0].astype(jnp.float32).astype(jnp.int32)
    fields = notes[:, : 4 * count].reshape(-1, count, 4)
    station, length = fields[..., 0] - 1, fields[..., 1] * 256 + fields[..., 2]
    return station.reshape(-1), length.reshape(-1), notes[:, 4 * count]


def whiten_kernel(
    part, parts, source, length, picks, got, more, first, twist, second, *refs
):
    held, spectra, sem, sems = refs[-4:]
    stops, rows = picks.shape
    white = refs[-5 - parts]
    payload = refs[-4 - parts : -4]
    stations = held.shape[0]
    first_more = got.shape[0] // 2 * BASE
    batch = 8

    def fetch(rows, code, count, station):
        for seg in range(2):
            source_at = rows.at[2 * (code // count) + seg, unit(code % count)]
            pltpu.make_async_copy(source_at, held.at[station, unit(seg)], sems.at[station // batch]).start()

    @pl.loop(0, stations)
    def _(station):
        code = source[station]

        @pl.when(code < first_more)
        def _():
            fetch(got, code, BASE, station)

        @pl.when(code >= first_more)
        def _():
            fetch(more, code - first_more, EXTRA, station)

    row = lax.broadcasted_iota(jnp.int32, (2 * ROWS, LANES), 0)
    lane = lax.broadcasted_iota(jnp.int32, (2 * ROWS, LANES), 1)
    left = lax.broadcasted_iota(jnp.int32, (ROWS // 2, LANES), 1) < ROWS
    place = (2 * part + (row & 1)) * NT + (row >> 1) * LANES + lane

    def two_stations(station):
        sides = []
        for at in range(2):
            values = held[station + at].astype(jnp.float32)
            sides.append(jnp.where(place < length[station + at], values, 0.0).astype(jnp.bfloat16))
        values = jnp.concatenate(sides, 1)
        values = jnp.concatenate([values, values], 0)
        mixed = jnp.dot(first[...], values, preferred_element_type=jnp.float32)
        parts = []
        for at in range(2):
            for seg in range(2):
                real = mixed[2 * seg * ROWS : (2 * seg + 1) * ROWS, at * LANES : (at + 1) * LANES]
                imag = mixed[(2 * seg + 1) * ROWS : (2 * seg + 2) * ROWS, at * LANES : (at + 1) * LANES]
                turned_re = real * twist[0] + imag * twist[1]
                turned_im = imag * twist[0] - real * twist[1]
                parts.append(jnp.concatenate([turned_re, turned_im], 1))
        turned = jnp.concatenate(parts, 0)
        high = turned.astype(jnp.bfloat16)
        low = (turned - high.astype(jnp.float32)).astype(jnp.bfloat16)
        upper = jnp.dot(high, second[...], preferred_element_type=jnp.float32)
        lower = jnp.dot(low, second[:, :LANES], preferred_element_type=jnp.float32)
        spectrum = upper[:, :LANES] + (upper[:, LANES:] + lower)
        for at in range(2):
            for seg in range(2):
                begin = (2 * at + seg) * ROWS
                side = spectrum[begin : begin + ROWS]
                power = jnp.sum(side * side, axis=0, keepdims=True)
                power = (power + pltpu.roll(power, LANES // 2, 1)) * (1.0 / ROWS)
                scale = 1.0 / jnp.sqrt(power + 1e-06)
                side = side * scale
                upper, lower = side[: ROWS // 2], side[ROWS // 2 :]
                real = jnp.where(left, upper, pltpu.roll(lower, ROWS, 1))
                imag = jnp.where(left, pltpu.roll(upper, ROWS, 1), lower)
                spectra[station + at, seg, : ROWS // 2] = real.astype(jnp.bfloat16)
                spectra[station + at, seg, ROWS // 2 :] = imag.astype(jnp.bfloat16)

    @pl.loop(0, stations // batch)
    def _(at):
        these = held.at[pl.ds(at * batch, batch)]
        pltpu.make_async_copy(these, these, sems.at[at]).wait()
        for two in range(0, batch, 2):
            two_stations(batch * at + two)

    each = stops // parts
    for piece in range(parts):

        @pl.loop(0, each)
        def _(stop):
            for at in range(rows):
                row = spectra.at[picks[piece * each + stop, at]]
                pltpu.make_async_copy(row, payload[piece].at[stop, at], sem).start()

    whole = pltpu.make_async_copy(spectra, white, sems.at[0])
    whole.start()
    for piece in range(parts):
        pltpu.make_async_copy(payload[piece], payload[piece], sem).wait()
    whole.wait()


def whiten(part, parts, source, length, picks, got, more, tables, after):
    stops, rows = picks.shape
    piece = jax.ShapeDtypeStruct((stops // parts, rows, 2, ROWS, LANES), jnp.bfloat16)
    return pl.pallas_call(
        functools.partial(whiten_kernel, part, parts),
        out_shape=(jax.ShapeDtypeStruct((ST_DEV, 2, ROWS, LANES), jnp.bfloat16),) + (piece,) * parts,
        in_specs=[SMEM, SMEM, SMEM, ANY, ANY, VMEM, VMEM, VMEM] + [ANY] * len(after),
        out_specs=(ANY,) * (1 + parts),
        scratch_shapes=[
            pltpu.VMEM((ST_DEV, 2 * ROWS, LANES), jnp.bfloat16),
            pltpu.VMEM((ST_DEV, 2, ROWS, LANES), jnp.bfloat16),
            pltpu.SemaphoreType.DMA,
            pltpu.SemaphoreType.DMA((ST_DEV // 8,)),
        ],
        cost_estimate=pl.CostEstimate(
            flops=2 * ST_DEV * 2 * ROWS * 256 * 400, bytes_accessed=4 * 1024 * 1024, transcendentals=0
        ),
        name="whiten",
    )(source, length, picks, got, more, *tables, *after)


def cross_rows(near_pick, near, far, cross, fresh, ready):
    stops, rows = near_pick.shape
    side = rows // 2
    step = 16
    half = ROWS // 2

    @pl.loop(0, stops)
    def _(stop):
        ready(stop)
        for two in range(2):
            first = two * side
            own = [near_pick[stop, first + i] for i in range(side)]

            @pl.loop(0, half // step)
            def _(chunk):
                real = pl.ds(pl.multiple_of(chunk * step, step), step)
                imag = pl.ds(pl.multiple_of(half + chunk * step, step), step)

                def both(ref, row):
                    return [
                        (ref[row, s, real, :].astype(jnp.float32), ref[row, s, imag, :].astype(jnp.float32))
                        for s in range(2)
                    ]

                here = [both(near, own[i]) for i in range(side)]
                for j in range(side):
                    there = both(far.at[stop], first + j)
                    for i in range(side):
                        pair = ((stop * 2 + two) * side + i) * side + j
                        total_re = sum(n[0] * f[0] + n[1] * f[1] for n, f in zip(here[i], there))
                        total_im = sum(n[1] * f[0] - n[0] * f[1] for n, f in zip(here[i], there))
                        for total, add in ((total_re, 0), (total_im, half)):
                            at = pl.ds(pl.multiple_of(pair * ROWS + add + chunk * step, step), step)
                            if fresh:
                                cross[at, :] = total
                            else:
                                cross[at, :] += total


def lag_kernel(stops, near_pick, far_at, white_a, home, *refs):
    far_a = refs[: stops - 1]
    white_b, far_b, table, last, mask, result, near, far, cross, out, tables, sem, sems, table_sem = refs[stops - 1 :]
    pairs = out.shape[0]
    copies = [pltpu.make_async_copy(white, near.at[part], sem.at[part]) for part, white in enumerate((white_a, white_b))]
    copies[0].start()
    pltpu.make_async_copy(home, far.at[0, 0], sems.at[0, 0]).start()
    for stop in range(1, stops):
        pltpu.make_async_copy(far_a[stop - 1], far.at[0, stop], sems.at[0, stop]).start()
    copies[1].start()
    for stop in range(stops):
        pltpu.make_async_copy(far_b.at[far_at[stop]], far.at[1, stop], sems.at[1, stop]).start()
    load_table = pltpu.make_async_copy(table, tables, table_sem)
    load_table.start()
    for part in range(2):

        def ready(stop):
            pltpu.make_async_copy(far.at[part, stop], far.at[part, stop], sems.at[part, stop]).wait()

        copies[part].wait()
        cross_rows(near_pick, near.at[part], far.at[part], cross, part == 0, ready)
    load_table.wait()
    group = 8
    depth = group * LANES
    half = LAGS // 2
    turns = ROWS // 2 // group

    def product(turn, edge):
        base = turn * group
        slabs = [
            cross[pl.ds(base + k, pairs, stride=ROWS), :].astype(jnp.bfloat16) for k in range(group)
        ]
        if edge is not None:
            for k in range(group):
                edge += slabs[k].astype(jnp.float32) * last[base + k]
        part = jnp.dot(
            jnp.concatenate(slabs, 1),
            tables[pl.ds(pl.multiple_of(base * LANES, depth), depth), :],
            preferred_element_type=jnp.float32,
        )
        return part, edge

    out[:, :half] = jnp.zeros((pairs, half), jnp.float32)
    out[:, half:] = jnp.zeros((pairs, half), jnp.float32)

    def even_step(turn, edge):
        part, edge = product(turn, edge)
        out[:, :half] += part
        return edge

    edge = lax.fori_loop(0, turns, even_step, jnp.zeros((pairs, LANES), jnp.float32))

    @pl.loop(turns, 2 * turns)
    def _(turn):
        out[:, half:] += product(turn, None)[0]

    edge = jnp.sum(edge, axis=1, keepdims=True)
    lane = lax.broadcasted_iota(jnp.int32, (pairs, LANES), 1)
    mirror = (LANES - lane) % LANES
    first = lane == 0
    listed = mask[...]
    count = half // LANES
    before, after = [], []
    for block in range(count):
        even = out[:, block * LANES : (block + 1) * LANES]
        odd = out[:, half + block * LANES : half + (block + 1) * LANES]
        if block == 0:
            edge = edge + odd
            odd = jnp.where(first, 0.0, odd)
        before.append(even - odd)
        after.append(even + odd)
    for block in range(count):
        turned = jnp.take_along_axis(before[count - 1 - block], mirror, axis=1)
        start = edge if block == 0 else before[count - block]
        lags = pl.ds(block * LANES, LANES)
        result[:, :, lags] = (jnp.where(first, start, turned) * listed).reshape(result.shape[:2] + (LANES,))
        lags = pl.ds(half + block * LANES, LANES)
        result[:, :, lags] = (after[block] * listed).reshape(result.shape[:2] + (LANES,))


def lagged(near_pick, far_at, white_a, home, far_a, white_b, far_b, table, last, mask):
    pairs = mask.shape[0]
    stops, rows = near_pick.shape
    side = rows // 2
    return pl.pallas_call(
        functools.partial(lag_kernel, stops),
        out_shape=jax.ShapeDtypeStruct((pairs // side, side, LAGS), jnp.float32),
        in_specs=[SMEM, SMEM] + [ANY] * (stops + 4) + [VMEM, VMEM],
        out_specs=VMEM,
        scratch_shapes=[
            pltpu.VMEM((2,) + white_a.shape, jnp.bfloat16),
            pltpu.VMEM((2,) + far_b.shape, jnp.bfloat16),
            pltpu.VMEM((pairs * ROWS, LANES), jnp.float32),
            pltpu.VMEM((pairs, LAGS), jnp.float32),
            pltpu.VMEM(table.shape, jnp.bfloat16),
            pltpu.SemaphoreType.DMA((2,)),
            pltpu.SemaphoreType.DMA((2, stops)),
            pltpu.SemaphoreType.DMA,
        ],
        compiler_params=pltpu.CompilerParams(vmem_limit_bytes=60 * 1024 * 1024),
        cost_estimate=pl.CostEstimate(
            flops=2 * pairs * NF * LAGS, bytes_accessed=16 * 1024 * 1024, transcendentals=0
        ),
        name="lagged",
    )(near_pick, far_at, white_a, home, *far_a, white_b, far_b, table, last, mask)


def empty(shape):
    return pl.pallas_call(
        lambda out: None,
        out_shape=jax.ShapeDtypeStruct(shape, jnp.bfloat16),
        out_specs=ANY,
        name="empty",
    )()


def on_device(records, lengths, owners, own_pick, visit_pick, pair_mask):
    wide_count = lax.axis_size("wide")
    stops = lax.axis_size("blk")
    column = lax.axis_index("wide")
    group = lax.axis_index("blk")
    core = column % 2
    slots = records.shape[1]
    steps = jnp.arange(stops, dtype=jnp.int32)
    core_at = core.reshape(1)

    def across(shard, bits):
        return lax.ppermute(shard, "wide", [(i, i ^ bits) for i in range(wide_count)])

    over = wide_count // 2
    packed = jnp.where(owners[0] >= 0, (owners[0] << LEN_BITS) + lengths[0], -1)
    others = [across(packed, bits) for bits in (1, over, over + 1)]
    table = jnp.where(
        core == 0,
        jnp.stack([packed, others[0], others[1], others[2]]),
        jnp.stack([others[0], packed, others[2], others[1]]),
    )

    blocks = records[0].reshape(slots, SEG, ROWS, LANES)

    def halves(part):
        return blocks[:, 2 * part : 2 * part + 2].transpose(0, 2, 1, 3).reshape(slots, 2 * ROWS, LANES)

    def send(payload):
        return lax.all_to_all(payload, "wide", split_axis=0, concat_axis=0, tiled=True)

    own_a = halves(0)
    mate_a = across(own_a, 1)
    same_a, other_a, plan, held, noted = spill(wide_count, table, core_at, own_a)
    same_a, other_a = across(same_a, over), across(other_a, over + 1)
    guests, tiles, _ = route(table, plan, held, noted)
    load_a, flag_a = pack(plan, guests, core_at, own_a, mate_a, same_a, other_a, tiles, None)
    got_a = send(load_a)
    own_b = jnp.where(flag_a[0] >= 0, halves(1), 0.0)
    mate_b = across(own_b, 1)
    same_b, other_b, *_ = spill(wide_count, table, core_at, own_b)
    same_b, other_b = across(same_b, over), across(other_b, over + 1)
    visits = jnp.where(flag_a[0] >= 0, visit_pick[0, 0].reshape(stops, -1), 0)
    by_stop = jnp.stack(
        [visits[0]]
        + [
            lax.ppermute(visits[stop], "blk", [(i, (i - stop) % stops) for i in range(stops)])
            for stop in range(1, stops)
        ]
    )
    load_b, _ = pack(plan, guests, core_at, own_b, mate_b, same_b, other_b, tiles, by_stop)
    got_b = send(load_b)
    by_dest = by_stop[(steps - group) % stops]

    station, length, spilled = read_notes(got_a, BASE)
    spilled = jnp.max(spilled) > 0

    def late():
        rows = [
            send(pack_late(wide_count, table, core_at, own, mate))
            for own, mate in ((own_a, mate_a), (own_b, mate_b))
        ]
        return (rows[0], rows[1]) + read_notes(rows[0], EXTRA)[:2]

    def never():
        rows = [empty((wide_count, EXTRA * ROWS + NOTES, LANES)) for _ in range(2)]
        count = wide_count // 2 * EXTRA
        return rows[0], rows[1], jnp.full((count,), -1, jnp.int32), jnp.zeros((count,), jnp.int32)

    more_a, more_b, more_station, more_length = lax.cond(spilled, late, never)
    station = jnp.concatenate([station, more_station])
    length = jnp.concatenate([length, more_length])
    chosen = station[None, :] == jnp.arange(ST_DEV, dtype=jnp.int32)[:, None]
    codes = jnp.arange(station.shape[0], dtype=jnp.int32)
    source = jnp.max(jnp.where(chosen, codes[None], 0), axis=1)
    length = jnp.max(jnp.where(chosen, length[None], 0), axis=1)

    tables = [jnp.asarray(table) for table in transform_tables()]
    near_pick = own_pick[0, 0].reshape(stops, -1)
    white_a, home, *payload_a = whiten(0, stops, source, length, by_stop, got_a, more_a, tables, [])
    far_a = [
        lax.ppermute(payload_a[stop - 1][0], "blk", [(i, (i + stop) % stops) for i in range(stops)])
        for stop in range(1, stops)
    ]
    white_b, payload_b = whiten(1, 1, source, length, by_dest, got_b, more_b, tables, far_a)
    far_b = lax.all_to_all(payload_b, "blk", split_axis=0, concat_axis=0, tiled=True)

    far_at = (group - steps) % stops
    mask = pair_mask[0, 0].astype(jnp.float32).reshape(-1, 1)
    lags, last = lag_tables()
    result = lagged(near_pick, far_at, white_a, home[0], far_a, white_b, far_b, jnp.asarray(lags), jnp.asarray(last), mask)
    return result.reshape((1, 1) + pair_mask.shape[2:] + (LAGS,))


def solution(mesh):
    return jax.shard_map(
        on_device,
        mesh=mesh,
        in_specs=(
            P("blk", "wide", None, None),
            P("blk", "wide"),
            P("blk", "wide"),
            P("blk", "wide", None, None, None),
            P("blk", "wide", None, None, None),
            P("blk", "wide", None, None, None, None),
        ),
        out_specs=P("blk", "wide", None, None, None, None, None),
        check_vma=False,
    )
```

```python
import functools
import math

import jax
import jax.numpy as jnp
import numpy as np
from jax import lax
from jax.experimental import pallas as pl
from jax.experimental.pallas import tpu as pltpu
from jax.sharding import PartitionSpec as P

ST_DEV = 24
SEG = 4
NT = 8192
NF = 4096
LAGS = 1024
ROWS = 64
LANES = 128
MOST = 6
SLOTS = (4, 3)
SPILL = 12
LEN_BITS = 16
NOTES = 16
SMEM = pl.BlockSpec(memory_space=pltpu.SMEM)
VMEM = pl.BlockSpec(memory_space=pltpu.VMEM)
ANY = pl.BlockSpec(memory_space=pl.ANY)


def split_bf16(values):
    high = values.astype(jnp.bfloat16)
    low = (values - high.astype(np.float64)).astype(jnp.bfloat16)
    return high, low


def transform_tables():
    first = np.arange(ROWS)
    second = np.arange(LANES)
    half = np.arange(LANES // 2)
    angle = 2.0 * math.pi / ROWS * (first[:, None] * first[None, :] % ROWS)
    wave = np.concatenate([np.cos(angle), -np.sin(angle)], 0)
    wave = np.einsum("ab,kn->aknb", np.eye(2), wave).reshape(4 * ROWS, 2 * ROWS)
    first_table = np.concatenate(split_bf16(wave), 1)
    twist = 2.0 * math.pi / NT * (first[:, None] * second[None, :] % NT)
    twist_table = np.stack([np.cos(twist), np.sin(twist)]).astype(np.float32)
    angle = 2.0 * math.pi / LANES * (second[:, None] * half[None, :] % LANES)
    cos, sin = np.cos(angle), np.sin(angle)
    wave = np.concatenate([np.concatenate([cos, -sin], 1), np.concatenate([sin, cos], 1)], 0)
    second_table = np.concatenate(split_bf16(wave), 1)
    return first_table, twist_table, second_table


def lag_tables():
    row = np.arange(ROWS // 2, dtype=np.int64)
    lane = np.arange(LANES, dtype=np.int64)
    bins = (row[:, None] + ROWS // 2 * (lane // ROWS)) + ROWS * (lane % ROWS)
    bins = bins.reshape(-1)
    weight = np.where(bins == 0, 0.5, 1.0).astype(np.float32) / np.float32(math.sqrt(NF * SEG))

    def at(delay):
        phase = bins[:, None] * delay[None, :] % NT
        return phase.astype(np.float32) * np.float32(2.0 * math.pi / NT)

    ahead = at(np.arange(LAGS // 2, dtype=np.int64))
    edge = at(np.array([NT - LAGS // 2], dtype=np.int64))
    cos = weight[:, None] * np.cos(ahead)
    sin = -weight[:, None] * np.sin(ahead)
    sin[:, :1] = -weight[:, None] * np.sin(edge)
    last = (weight[:, None] * np.cos(edge)).reshape(ROWS // 2, 1, LANES)
    return (
        np.concatenate([cos, sin], 0).astype(jnp.bfloat16),
        last.astype(jnp.bfloat16).astype(np.float32),
    )


def owner_of(value):
    return ((value >> LEN_BITS) * 2731) >> 16


def unit(slot):
    return pl.ds(pl.multiple_of(slot * ROWS, ROWS), ROWS)


def rows_kernel(low, count, noted, table, core_ref, own, mate, *refs):
    base = refs[0] if noted else None
    out, flag, fill, notes, started, sem = refs[-6:]
    core = core_ref[0]
    started[0] = 0
    flag[0] = 0

    @pl.loop(0, out.shape[0])
    def _(dev):
        fill[dev] = 0
        for slot in range(count):
            notes[dev, slot] = -1

    def place(half, source):
        @pl.loop(0, table.shape[1])
        def _(at):
            value = table[half, at]

            @pl.when(value >= 0)
            def _():
                dev = owner_of(value)
                rank = fill[dev]
                fill[dev] = rank + 1

                @pl.when((rank >= low) & (rank < low + count))
                def _():
                    started[0] += 1
                    notes[dev, rank - low] = value - ((dev * ST_DEV) << LEN_BITS)
                    rows = source.at[at, unit(core)]
                    pltpu.make_async_copy(rows, out.at[dev, unit(rank - low)], sem).start()

                @pl.when(rank >= low + count)
                def _():
                    flag[0] = 1

    for half in range(2):

        @pl.when(core == half)
        def _():
            place(half, own)

        @pl.when(core != half)
        def _():
            place(half, mate)

    if noted:
        row = lax.broadcasted_iota(jnp.int32, (NOTES, LANES), 0)
        table_rows = base[...]

        @pl.loop(0, out.shape[0])
        def _(dev):
            tile = jnp.where(row == 3 * count, flag[0], table_rows)
            for slot in range(count):
                value = notes[dev, slot]
                tile = jnp.where(row == 3 * slot, (value >> LEN_BITS) + 1, tile)
                tile = jnp.where(row == 3 * slot + 1, (value & 0xFFFF) >> 8, tile)
                tile = jnp.where(row == 3 * slot + 2, value & 0xFF, tile)
            out[dev, count * ROWS :, :] = tile.astype(jnp.float32).astype(jnp.bfloat16)

    @pl.loop(0, started[0])
    def _(_):
        pltpu.make_async_copy(own.at[0, unit(0)], out.at[0, unit(0)], sem).wait()


def pack_rows(low, count, wide_count, table, core, own, mate, base):
    noted = base is not None
    return pl.pallas_call(
        functools.partial(rows_kernel, low, count, noted),
        out_shape=(
            jax.ShapeDtypeStruct((wide_count, count * ROWS + (NOTES if noted else 0), LANES), jnp.bfloat16),
            jax.ShapeDtypeStruct((1,), jnp.int32),
        ),
        in_specs=[SMEM, SMEM, ANY, ANY] + [VMEM] * noted,
        out_specs=(VMEM, SMEM),
        scratch_shapes=[
            pltpu.SMEM((wide_count,), jnp.int32),
            pltpu.SMEM((wide_count, count), jnp.int32),
            pltpu.SMEM((1,), jnp.int32),
            pltpu.SemaphoreType.DMA,
        ],
        cost_estimate=pl.CostEstimate(flops=0, bytes_accessed=wide_count * count * NT * 4, transcendentals=0),
        name="pack_rows",
    )(table, core, own, mate, *([base] * noted))


def spill_kernel(base, table, core_ref, own, same, other, plan, fill, started, sem):
    core = core_ref[0]
    slots = table.shape[1]
    started[0] = 0

    @pl.loop(0, fill.shape[0])
    def _(dev):
        fill[dev] = 0

    for half in range(2):

        @pl.loop(0, slots)
        def _(at):
            value = table[half, at]
            plan[half, at] = -1

            @pl.when(value >= 0)
            def _():
                dev = owner_of(value)
                rank = fill[dev]
                fill[dev] = rank + 1

                @pl.when(rank < base)
                def _():
                    plan[half, at] = dev * 4 + rank

                @pl.when((rank >= base) & (core == half) & (started[0] < SPILL))
                def _():
                    index = started[0]
                    started[0] = index + 1
                    pltpu.make_async_copy(own.at[at, unit(core)], same.at[index], sem).start()
                    pltpu.make_async_copy(own.at[at, unit(1 - core)], other.at[index], sem).start()

    @pl.loop(0, 2 * started[0])
    def _(_):
        pltpu.make_async_copy(own.at[0, unit(0)], same.at[0], sem).wait()


def spill(base, wide_count, table, core, own):
    buffer = jax.ShapeDtypeStruct((SPILL, ROWS, LANES), jnp.bfloat16)
    return pl.pallas_call(
        functools.partial(spill_kernel, base),
        out_shape=(
            buffer,
            buffer,
            jax.ShapeDtypeStruct((2, table.shape[1]), jnp.int32),
            jax.ShapeDtypeStruct((wide_count,), jnp.int32),
        ),
        in_specs=[SMEM, SMEM, ANY],
        out_specs=(VMEM, VMEM, SMEM, SMEM),
        scratch_shapes=[pltpu.SMEM((1,), jnp.int32), pltpu.SemaphoreType.DMA],
        cost_estimate=pl.CostEstimate(flops=0, bytes_accessed=2**20, transcendentals=0),
        name="spill",
    )(table, core, own)


def pack_kernel(base, table, plan, held, core_ref, own, mate, same, other, after, out, fill, theirs, started, taken, sem):
    core = core_ref[0]
    started[0] = 0

    @pl.loop(0, out.shape[0])
    def _(dev):
        fill[dev] = held[dev]
        theirs[dev] = 0

    def place(half, source, guests):
        @pl.loop(0, plan.shape[1])
        def _(at):
            code = plan[half, at]

            @pl.when(code >= 0)
            def _():
                started[0] += 1
                rows = source.at[at, unit(core)]
                pltpu.make_async_copy(rows, out.at[code >> 2, unit(code & 3)], sem).start()

        taken[0] = 0

        @pl.loop(0, plan.shape[1])
        def _(at):
            value = table[2 + half, at]

            @pl.when(value >= 0)
            def _():
                dev = owner_of(value)
                rank = theirs[dev]
                theirs[dev] = rank + 1

                @pl.when(rank >= base)
                def _():
                    index = taken[0]
                    slot = fill[dev]
                    taken[0] = index + 1

                    @pl.when((index < SPILL) & (slot < base))
                    def _():
                        fill[dev] = slot + 1
                        started[0] += 1
                        pltpu.make_async_copy(guests.at[index], out.at[dev, unit(slot)], sem).start()

    for half in range(2):

        @pl.when(core == half)
        def _():
            place(half, own, same)

        @pl.when(core != half)
        def _():
            place(half, mate, other)

    @pl.loop(0, started[0])
    def _(_):
        pltpu.make_async_copy(own.at[0, unit(0)], out.at[0, unit(0)], sem).wait()


def pack_planned(base, table, plan, held, core, own, mate, same, other, after):
    wide_count = held.shape[0]
    return pl.pallas_call(
        functools.partial(pack_kernel, base),
        out_shape=jax.ShapeDtypeStruct((wide_count, base * ROWS, LANES), jnp.bfloat16),
        in_specs=[SMEM] * 4 + [ANY] * 5,
        out_specs=VMEM,
        scratch_shapes=[
            pltpu.SMEM((wide_count,), jnp.int32),
            pltpu.SMEM((wide_count,), jnp.int32),
            pltpu.SMEM((1,), jnp.int32),
            pltpu.SMEM((1,), jnp.int32),
            pltpu.SemaphoreType.DMA,
        ],
        cost_estimate=pl.CostEstimate(flops=0, bytes_accessed=wide_count * base * NT * 4, transcendentals=0),
        name="pack_planned",
    )(table, plan, held, core, own, mate, same, other, after)


def table_notes(packed):
    owner = (packed >> LEN_BITS) + 1
    length = jnp.where(packed >= 0, packed & 0xFFFF, 0)
    parts = jnp.concatenate([owner >> 8, owner & 0xFF, length >> 8, length & 0xFF])
    rows = 3 * LANES - parts.shape[0]
    parts = jnp.pad(parts, (0, rows)).reshape(3, LANES)
    return jnp.pad(parts, ((NOTES - 3, 0), (0, 0)))


def read_slots(rows, count):
    notes = rows[::2, count * ROWS : count * ROWS + 3 * count + 1, 0].astype(jnp.float32).astype(jnp.int32)
    fields = notes[:, : 3 * count].reshape(-1, count, 3)
    station, length = fields[..., 0] - 1, fields[..., 1] * 256 + fields[..., 2]
    return station.reshape(-1), length.reshape(-1), notes[:, 3 * count]


def read_table(rows, slots, chips):
    parts = rows[:, -3:, :].astype(jnp.float32).astype(jnp.int32)
    parts = parts.reshape(rows.shape[0], -1)[:, : 4 * slots].reshape(chips, 2, 4, slots)
    return (parts[:, :, 0] * 256 + parts[:, :, 1] - 1).reshape(chips, 2 * slots)


def second_places(owner, column, base):
    chips, entries = owner.shape
    extra = MOST - base
    slots = entries // 2
    listed = owner >= 0
    dev = jnp.where(listed, owner // ST_DEV, -1)
    order = jnp.arange(entries, dtype=jnp.int32)
    earlier = order[None, :] < order[:, None]
    alike = (dev[:, :, None] == dev[:, None, :]) & earlier
    rank = jnp.sum(alike.astype(jnp.int32), axis=2)
    over = listed & (rank >= base)
    near = earlier & (order[None, :] // slots == order[:, None] // slots)
    index = jnp.sum((over[:, None, :] & near).astype(jnp.int32), axis=2)
    sent = over & (index < SPILL)
    guest = jnp.sum((alike & sent[:, None, :]).astype(jnp.int32), axis=2)
    host_dev = jnp.concatenate([dev[chips // 2 :], dev[: chips // 2]])
    host_held = jnp.sum((dev[:, :, None] == host_dev[:, None, :]).astype(jnp.int32), axis=2)
    slot = host_held + guest
    fits = sent & (slot < base)
    chip = jnp.arange(chips, dtype=jnp.int32)[:, None]
    host = (chip + chips // 2) % chips
    code = jnp.where(rank < base, chip * base + rank, chips * base + chip * extra + rank - base)
    code = jnp.where(fits, host * base + slot, code)
    local = column * ST_DEV + jnp.arange(ST_DEV, dtype=jnp.int32)
    chosen = owner[None] == local[:, None, None]
    return jnp.sum(jnp.where(chosen, code[None], 0), axis=(1, 2)), jnp.any(over & jnp.logical_not(fits))


def whiten_kernel(
    part, parts, source, length, picks, got, more, first, twist, second, *refs
):
    held, spectra, sem, sems = refs[-4:]
    stops, rows = picks.shape
    white = refs[-5 - parts]
    payload = refs[-4 - parts : -4]
    stations = held.shape[0]
    base = SLOTS[part]
    first_more = got.shape[0] // 2 * base
    batch = 8

    def fetch(rows, code, count, station):
        for seg in range(2):
            source_at = rows.at[2 * (code // count) + seg, unit(code % count)]
            pltpu.make_async_copy(source_at, held.at[station, unit(seg)], sems.at[station // batch]).start()

    @pl.loop(0, stations)
    def _(station):
        code = source[station]

        @pl.when(code < first_more)
        def _():
            fetch(got, code, base, station)

        @pl.when(code >= first_more)
        def _():
            fetch(more, code - first_more, MOST - base, station)

    row = lax.broadcasted_iota(jnp.int32, (2 * ROWS, LANES), 0)
    lane = lax.broadcasted_iota(jnp.int32, (2 * ROWS, LANES), 1)
    left = lax.broadcasted_iota(jnp.int32, (ROWS // 2, LANES), 1) < ROWS
    place = (2 * part + (row & 1)) * NT + (row >> 1) * LANES + lane

    def two_stations(station):
        sides = []
        for at in range(2):
            values = held[station + at].astype(jnp.float32)
            sides.append(jnp.where(place < length[station + at], values, 0.0).astype(jnp.bfloat16))
        values = jnp.concatenate(sides, 1)
        values = jnp.concatenate([values, values], 0)
        mixed = jnp.dot(first[...], values, preferred_element_type=jnp.float32)
        parts = []
        for at in range(2):
            for seg in range(2):
                real = mixed[2 * seg * ROWS : (2 * seg + 1) * ROWS, at * LANES : (at + 1) * LANES]
                imag = mixed[(2 * seg + 1) * ROWS : (2 * seg + 2) * ROWS, at * LANES : (at + 1) * LANES]
                turned_re = real * twist[0] + imag * twist[1]
                turned_im = imag * twist[0] - real * twist[1]
                parts.append(jnp.concatenate([turned_re, turned_im], 1))
        turned = jnp.concatenate(parts, 0)
        high = turned.astype(jnp.bfloat16)
        low = (turned - high.astype(jnp.float32)).astype(jnp.bfloat16)
        upper = jnp.dot(high, second[...], preferred_element_type=jnp.float32)
        lower = jnp.dot(low, second[:, :LANES], preferred_element_type=jnp.float32)
        spectrum = upper[:, :LANES] + (upper[:, LANES:] + lower)
        for at in range(2):
            for seg in range(2):
                begin = (2 * at + seg) * ROWS
                side = spectrum[begin : begin + ROWS]
                power = jnp.sum(side * side, axis=0, keepdims=True)
                power = (power + pltpu.roll(power, LANES // 2, 1)) * (1.0 / ROWS)
                scale = 1.0 / jnp.sqrt(power + 1e-06)
                side = side * scale
                upper, lower = side[: ROWS // 2], side[ROWS // 2 :]
                real = jnp.where(left, upper, pltpu.roll(lower, ROWS, 1))
                imag = jnp.where(left, pltpu.roll(upper, ROWS, 1), lower)
                spectra[station + at, seg, : ROWS // 2] = real.astype(jnp.bfloat16)
                spectra[station + at, seg, ROWS // 2 :] = imag.astype(jnp.bfloat16)

    @pl.loop(0, stations // batch)
    def _(at):
        these = held.at[pl.ds(at * batch, batch)]
        pltpu.make_async_copy(these, these, sems.at[at]).wait()
        for two in range(0, batch, 2):
            two_stations(batch * at + two)

    each = stops // parts
    for piece in range(parts):

        @pl.loop(0, each)
        def _(stop):
            for at in range(rows):
                row = spectra.at[picks[piece * each + stop, at]]
                pltpu.make_async_copy(row, payload[piece].at[stop, at], sem).start()

    whole = pltpu.make_async_copy(spectra, white, sems.at[0])
    whole.start()
    for piece in range(parts):
        pltpu.make_async_copy(payload[piece], payload[piece], sem).wait()
    whole.wait()


def whiten(part, parts, source, length, picks, got, more, tables, after):
    stops, rows = picks.shape
    piece = jax.ShapeDtypeStruct((stops // parts, rows, 2, ROWS, LANES), jnp.bfloat16)
    return pl.pallas_call(
        functools.partial(whiten_kernel, part, parts),
        out_shape=(jax.ShapeDtypeStruct((ST_DEV, 2, ROWS, LANES), jnp.bfloat16),) + (piece,) * parts,
        in_specs=[SMEM, SMEM, SMEM, ANY, ANY, VMEM, VMEM, VMEM] + [ANY] * len(after),
        out_specs=(ANY,) * (1 + parts),
        scratch_shapes=[
            pltpu.VMEM((ST_DEV, 2 * ROWS, LANES), jnp.bfloat16),
            pltpu.VMEM((ST_DEV, 2, ROWS, LANES), jnp.bfloat16),
            pltpu.SemaphoreType.DMA,
            pltpu.SemaphoreType.DMA((ST_DEV // 8,)),
        ],
        cost_estimate=pl.CostEstimate(
            flops=2 * ST_DEV * 2 * ROWS * 256 * 400, bytes_accessed=4 * 1024 * 1024, transcendentals=0
        ),
        name="whiten",
    )(source, length, picks, got, more, *tables, *after)


def cross_rows(near_pick, near, far, cross, fresh, ready):
    stops, rows = near_pick.shape
    side = rows // 2
    step = 16
    half = ROWS // 2

    @pl.loop(0, stops)
    def _(stop):
        ready(stop)
        for two in range(2):
            first = two * side
            own = [near_pick[stop, first + i] for i in range(side)]

            @pl.loop(0, half // step)
            def _(chunk):
                real = pl.ds(pl.multiple_of(chunk * step, step), step)
                imag = pl.ds(pl.multiple_of(half + chunk * step, step), step)

                def both(ref, row):
                    return [
                        (ref[row, s, real, :].astype(jnp.float32), ref[row, s, imag, :].astype(jnp.float32))
                        for s in range(2)
                    ]

                here = [both(near, own[i]) for i in range(side)]
                for j in range(side):
                    there = both(far.at[stop], first + j)
                    for i in range(side):
                        pair = ((stop * 2 + two) * side + i) * side + j
                        total_re = sum(n[0] * f[0] + n[1] * f[1] for n, f in zip(here[i], there))
                        total_im = sum(n[1] * f[0] - n[0] * f[1] for n, f in zip(here[i], there))
                        for total, add in ((total_re, 0), (total_im, half)):
                            at = pl.ds(pl.multiple_of(pair * ROWS + add + chunk * step, step), step)
                            if fresh:
                                cross[at, :] = total
                            else:
                                cross[at, :] += total


def lag_kernel(stops, near_pick, far_at, white_a, home, *refs):
    far_a = refs[: stops - 1]
    white_b, far_b, table, last, mask, result, near, far, cross, out, tables, sem, sems, table_sem = refs[stops - 1 :]
    pairs = out.shape[0]
    copies = [pltpu.make_async_copy(white, near.at[part], sem.at[part]) for part, white in enumerate((white_a, white_b))]
    copies[0].start()
    pltpu.make_async_copy(home, far.at[0, 0], sems.at[0, 0]).start()
    for stop in range(1, stops):
        pltpu.make_async_copy(far_a[stop - 1], far.at[0, stop], sems.at[0, stop]).start()
    copies[1].start()
    for stop in range(stops):
        pltpu.make_async_copy(far_b.at[far_at[stop]], far.at[1, stop], sems.at[1, stop]).start()
    load_table = pltpu.make_async_copy(table, tables, table_sem)
    load_table.start()
    for part in range(2):

        def ready(stop):
            pltpu.make_async_copy(far.at[part, stop], far.at[part, stop], sems.at[part, stop]).wait()

        copies[part].wait()
        cross_rows(near_pick, near.at[part], far.at[part], cross, part == 0, ready)
    load_table.wait()
    group = 8
    depth = group * LANES
    half = LAGS // 2
    turns = ROWS // 2 // group

    def product(turn, edge):
        base = turn * group
        slabs = [
            cross[pl.ds(base + k, pairs, stride=ROWS), :].astype(jnp.bfloat16) for k in range(group)
        ]
        if edge is not None:
            for k in range(group):
                edge += slabs[k].astype(jnp.float32) * last[base + k]
        part = jnp.dot(
            jnp.concatenate(slabs, 1),
            tables[pl.ds(pl.multiple_of(base * LANES, depth), depth), :],
            preferred_element_type=jnp.float32,
        )
        return part, edge

    out[:, :half] = jnp.zeros((pairs, half), jnp.float32)
    out[:, half:] = jnp.zeros((pairs, half), jnp.float32)

    def even_step(turn, edge):
        part, edge = product(turn, edge)
        out[:, :half] += part
        return edge

    edge = lax.fori_loop(0, turns, even_step, jnp.zeros((pairs, LANES), jnp.float32))

    @pl.loop(turns, 2 * turns)
    def _(turn):
        out[:, half:] += product(turn, None)[0]

    edge = jnp.sum(edge, axis=1, keepdims=True)
    lane = lax.broadcasted_iota(jnp.int32, (pairs, LANES), 1)
    mirror = (LANES - lane) % LANES
    first = lane == 0
    listed = mask[...]
    count = half // LANES
    before, after = [], []
    for block in range(count):
        even = out[:, block * LANES : (block + 1) * LANES]
        odd = out[:, half + block * LANES : half + (block + 1) * LANES]
        if block == 0:
            edge = edge + odd
            odd = jnp.where(first, 0.0, odd)
        before.append(even - odd)
        after.append(even + odd)
    for block in range(count):
        turned = jnp.take_along_axis(before[count - 1 - block], mirror, axis=1)
        start = edge if block == 0 else before[count - block]
        lags = pl.ds(block * LANES, LANES)
        result[:, :, lags] = (jnp.where(first, start, turned) * listed).reshape(result.shape[:2] + (LANES,))
        lags = pl.ds(half + block * LANES, LANES)
        result[:, :, lags] = (after[block] * listed).reshape(result.shape[:2] + (LANES,))


def lagged(near_pick, far_at, white_a, home, far_a, white_b, far_b, table, last, mask):
    pairs = mask.shape[0]
    stops, rows = near_pick.shape
    side = rows // 2
    return pl.pallas_call(
        functools.partial(lag_kernel, stops),
        out_shape=jax.ShapeDtypeStruct((pairs // side, side, LAGS), jnp.float32),
        in_specs=[SMEM, SMEM] + [ANY] * (stops + 4) + [VMEM, VMEM],
        out_specs=VMEM,
        scratch_shapes=[
            pltpu.VMEM((2,) + white_a.shape, jnp.bfloat16),
            pltpu.VMEM((2,) + far_b.shape, jnp.bfloat16),
            pltpu.VMEM((pairs * ROWS, LANES), jnp.float32),
            pltpu.VMEM((pairs, LAGS), jnp.float32),
            pltpu.VMEM(table.shape, jnp.bfloat16),
            pltpu.SemaphoreType.DMA((2,)),
            pltpu.SemaphoreType.DMA((2, stops)),
            pltpu.SemaphoreType.DMA,
        ],
        compiler_params=pltpu.CompilerParams(vmem_limit_bytes=60 * 1024 * 1024),
        cost_estimate=pl.CostEstimate(
            flops=2 * pairs * NF * LAGS, bytes_accessed=16 * 1024 * 1024, transcendentals=0
        ),
        name="lagged",
    )(near_pick, far_at, white_a, home, *far_a, white_b, far_b, table, last, mask)


def empty(shape):
    return pl.pallas_call(
        lambda out: None,
        out_shape=jax.ShapeDtypeStruct(shape, jnp.bfloat16),
        out_specs=ANY,
        name="empty",
    )()


def on_device(records, lengths, owners, own_pick, visit_pick, pair_mask):
    wide_count = lax.axis_size("wide")
    stops = lax.axis_size("blk")
    column = lax.axis_index("wide")
    group = lax.axis_index("blk")
    core = column % 2
    slots = records.shape[1]
    steps = jnp.arange(stops, dtype=jnp.int32)
    core_at = core.reshape(1)

    def across(shard, bits):
        return lax.ppermute(shard, "wide", [(i, i ^ bits) for i in range(wide_count)])

    over = wide_count // 2
    packed = jnp.where(owners[0] >= 0, (owners[0] << LEN_BITS) + lengths[0], -1)
    others = [across(packed, bits) for bits in (1, over, over + 1)]
    table = jnp.where(
        core == 0,
        jnp.stack([packed, others[0], others[1], others[2]]),
        jnp.stack([others[0], packed, others[2], others[1]]),
    )

    blocks = records[0].reshape(slots, SEG, ROWS, LANES)

    def halves(part):
        return blocks[:, 2 * part : 2 * part + 2].transpose(0, 2, 1, 3).reshape(slots, 2 * ROWS, LANES)

    def send(payload):
        return lax.all_to_all(payload, "wide", split_axis=0, concat_axis=0, tiled=True)

    own_a = halves(0)
    mate_a = across(own_a, 1)
    base_a, base_b = SLOTS
    load_a, flag_a = pack_rows(0, base_a, wide_count, table, core_at, own_a, mate_a, table_notes(packed))
    got_a = send(load_a)
    own_b = jnp.where(flag_a[0] >= 0, halves(1), 0.0)
    mate_b = across(own_b, 1)
    same_b, other_b, plan, held = spill(base_b, wide_count, table, core_at, own_b)
    same_b, other_b = across(same_b, over), across(other_b, over + 1)
    visits = jnp.where(flag_a[0] >= 0, visit_pick[0, 0].reshape(1, stops, -1), 0)
    bit = 1
    while bit < stops:
        theirs = lax.ppermute(visits, "blk", [(i, i ^ bit) for i in range(stops)])
        upper = (group // bit) % 2 == 1
        visits = jnp.concatenate([jnp.where(upper, theirs, visits), jnp.where(upper, visits, theirs)])
        bit *= 2
    by_dest = visits[steps, (steps - group) % stops]
    by_stop = by_dest[(steps + group) % stops]
    load_b = pack_planned(base_b, table, plan, held, core_at, own_b, mate_b, same_b, other_b, by_stop)
    got_b = send(load_b)

    def late_rows(low, own, mate):
        return send(pack_rows(low, MOST - low, wide_count, table, core_at, own, mate, jnp.zeros_like(table_notes(packed)))[0])

    def late_a():
        rows = late_rows(base_a, own_a, mate_a)
        return (rows,) + read_slots(rows, MOST - base_a)[:2]

    def never_a():
        count = wide_count // 2 * (MOST - base_a)
        rows = empty((wide_count, (MOST - base_a) * ROWS + NOTES, LANES))
        return rows, jnp.full((count,), -1, jnp.int32), jnp.zeros((count,), jnp.int32)

    station, length, spilled = read_slots(got_a, base_a)
    more_a, more_station, more_length = lax.cond(jnp.max(spilled) > 0, late_a, never_a)
    station = jnp.concatenate([station, more_station])
    length = jnp.concatenate([length, more_length])
    chosen = station[None, :] == jnp.arange(ST_DEV, dtype=jnp.int32)[:, None]
    codes = jnp.arange(station.shape[0], dtype=jnp.int32)
    source_a = jnp.sum(jnp.where(chosen, codes[None], 0), axis=1)
    length = jnp.sum(jnp.where(chosen, length[None], 0), axis=1)

    owner = read_table(got_a, slots, wide_count // 2)
    source_b, unplaced = second_places(owner, column, base_b)
    more_b = lax.cond(
        unplaced,
        lambda: late_rows(base_b, own_b, mate_b),
        lambda: empty((wide_count, (MOST - base_b) * ROWS + NOTES, LANES)),
    )

    tables = [jnp.asarray(table) for table in transform_tables()]
    near_pick = own_pick[0, 0].reshape(stops, -1)
    white_a, home, *payload_a = whiten(0, stops, source_a, length, by_stop, got_a, more_a, tables, [])
    far_a = [
        lax.ppermute(payload_a[stop - 1][0], "blk", [(i, (i + stop) % stops) for i in range(stops)])
        for stop in range(1, stops)
    ]
    white_b, payload_b = whiten(1, 1, source_b, length, by_dest, got_b, more_b, tables, far_a)
    far_b = lax.all_to_all(payload_b, "blk", split_axis=0, concat_axis=0, tiled=True)

    far_at = (group - steps) % stops
    mask = pair_mask[0, 0].astype(jnp.float32).reshape(-1, 1)
    lags, last = lag_tables()
    result = lagged(near_pick, far_at, white_a, home[0], far_a, white_b, far_b, jnp.asarray(lags), jnp.asarray(last), mask)
    return result.reshape((1, 1) + pair_mask.shape[2:] + (LAGS,))


def solution(mesh):
    return jax.shard_map(
        on_device,
        mesh=mesh,
        in_specs=(
            P("blk", "wide", None, None),
            P("blk", "wide"),
            P("blk", "wide"),
            P("blk", "wide", None, None, None),
            P("blk", "wide", None, None, None),
            P("blk", "wide", None, None, None, None),
        ),
        out_specs=P("blk", "wide", None, None, None, None, None),
        check_vma=False,
    )
```

```python
import functools
import math

import jax
import jax.numpy as jnp
import numpy as np
from jax import lax
from jax.experimental import pallas as pl
from jax.experimental.pallas import tpu as pltpu
from jax.sharding import PartitionSpec as P

ST_DEV = 24
SEG = 4
NT = 8192
NF = 4096
LAGS = 1024
ROWS = 64
LANES = 128
MOST = 6
SLOTS = (4, 3)
SPILL = 12
LAG_VMEM = 60 * 1024 * 1024
LEN_BITS = 16
NOTES = 16
SMEM = pl.BlockSpec(memory_space=pltpu.SMEM)
VMEM = pl.BlockSpec(memory_space=pltpu.VMEM)
ANY = pl.BlockSpec(memory_space=pl.ANY)


def split_bf16(values):
    high = values.astype(jnp.bfloat16)
    low = (values - high.astype(np.float64)).astype(jnp.bfloat16)
    return high, low


def transform_tables():
    first = np.arange(ROWS)
    second = np.arange(LANES)
    half = np.arange(LANES // 2)
    angle = 2.0 * math.pi / ROWS * (first[:, None] * first[None, :] % ROWS)
    wave = np.concatenate([np.cos(angle), -np.sin(angle)], 0)
    wave = np.einsum("ab,kn->aknb", np.eye(2), wave).reshape(4 * ROWS, 2 * ROWS)
    first_table = np.concatenate(split_bf16(wave), 1)
    twist = 2.0 * math.pi / NT * (first[:, None] * second[None, :] % NT)
    twist_table = np.stack([np.cos(twist), np.sin(twist)]).astype(np.float32)
    angle = 2.0 * math.pi / LANES * (second[:, None] * half[None, :] % LANES)
    cos, sin = np.cos(angle), np.sin(angle)
    wave = np.concatenate([np.concatenate([cos, -sin], 1), np.concatenate([sin, cos], 1)], 0)
    second_table = np.concatenate(split_bf16(wave), 1)
    return first_table, twist_table, second_table


def lag_tables():
    row = np.arange(ROWS // 2, dtype=np.int64)
    lane = np.arange(LANES, dtype=np.int64)
    bins = (row[:, None] + ROWS // 2 * (lane // ROWS)) + ROWS * (lane % ROWS)
    bins = bins.reshape(-1)
    weight = np.where(bins == 0, 0.5, 1.0).astype(np.float32) / np.float32(math.sqrt(NF * SEG))

    def at(delay):
        phase = bins[:, None] * delay[None, :] % NT
        return phase.astype(np.float32) * np.float32(2.0 * math.pi / NT)

    ahead = at(np.arange(LAGS // 2, dtype=np.int64))
    edge = at(np.array([NT - LAGS // 2], dtype=np.int64))
    cos = weight[:, None] * np.cos(ahead)
    sin = -weight[:, None] * np.sin(ahead)
    sin[:, :1] = -weight[:, None] * np.sin(edge)
    last = (weight[:, None] * np.cos(edge)).reshape(ROWS // 2, 1, LANES)
    return (
        np.concatenate([cos, sin], 0).astype(jnp.bfloat16),
        last.astype(jnp.bfloat16).astype(np.float32),
    )


def owner_of(value):
    return ((value >> LEN_BITS) * 2731) >> 16


def unit(slot):
    return pl.ds(pl.multiple_of(slot * ROWS, ROWS), ROWS)


def write_notes(out, begin, notes, flag, base):
    count = notes.shape[1]
    row = lax.broadcasted_iota(jnp.int32, (NOTES, LANES), 0)

    @pl.loop(0, notes.shape[0])
    def _(dev):
        tile = jnp.where(row == 3 * count, flag, base)
        for slot in range(count):
            value = notes[dev, slot]
            tile = jnp.where(row == 3 * slot, (value >> LEN_BITS) + 1, tile)
            tile = jnp.where(row == 3 * slot + 1, (value & 0xFFFF) >> 8, tile)
            tile = jnp.where(row == 3 * slot + 2, value & 0xFF, tile)
        out[dev, begin : begin + NOTES, :] = tile.astype(jnp.float32).astype(jnp.bfloat16)


def rows_kernel(low, count, table, core_ref, own, mate, out, flag, fill, notes, started, sem):
    core = core_ref[0]
    started[0] = 0
    flag[0] = 0

    @pl.loop(0, out.shape[0])
    def _(dev):
        fill[dev] = 0
        for slot in range(count):
            notes[dev, slot] = -1

    def place(half, source):
        @pl.loop(0, table.shape[1])
        def _(at):
            value = table[half, at]

            @pl.when(value >= 0)
            def _():
                dev = owner_of(value)
                rank = fill[dev]
                fill[dev] = rank + 1

                @pl.when((rank >= low) & (rank < low + count))
                def _():
                    started[0] += 1
                    notes[dev, rank - low] = value - ((dev * ST_DEV) << LEN_BITS)
                    rows = source.at[at, unit(core)]
                    pltpu.make_async_copy(rows, out.at[dev, unit(rank - low)], sem).start()

                @pl.when(rank >= low + count)
                def _():
                    flag[0] = 1

    for half in range(2):

        @pl.when(core == half)
        def _():
            place(half, own)

        @pl.when(core != half)
        def _():
            place(half, mate)

    write_notes(out, count * ROWS, notes, flag[0], jnp.zeros((NOTES, LANES), jnp.int32))

    @pl.loop(0, started[0])
    def _(_):
        pltpu.make_async_copy(own.at[0, unit(0)], out.at[0, unit(0)], sem).wait()


def pack_rows(low, count, wide_count, table, core, own, mate):
    return pl.pallas_call(
        functools.partial(rows_kernel, low, count),
        out_shape=(
            jax.ShapeDtypeStruct((wide_count, count * ROWS + NOTES, LANES), jnp.bfloat16),
            jax.ShapeDtypeStruct((1,), jnp.int32),
        ),
        in_specs=[SMEM, SMEM, ANY, ANY],
        out_specs=(VMEM, SMEM),
        scratch_shapes=[
            pltpu.SMEM((wide_count,), jnp.int32),
            pltpu.SMEM((wide_count, count), jnp.int32),
            pltpu.SMEM((1,), jnp.int32),
            pltpu.SemaphoreType.DMA,
        ],
        cost_estimate=pl.CostEstimate(flops=0, bytes_accessed=wide_count * count * NT * 4, transcendentals=0),
        name="pack_rows",
    )(table, core, own, mate)


def plan_kernel(count, table, base, plan, tiles, fill, notes, flag):
    flag[0] = 0

    @pl.loop(0, fill.shape[0])
    def _(dev):
        fill[dev] = 0
        for slot in range(count):
            notes[dev, slot] = -1

    for half in range(2):

        @pl.loop(0, table.shape[1])
        def _(at):
            value = table[half, at]
            plan[half, at] = -1

            @pl.when(value >= 0)
            def _():
                dev = owner_of(value)
                rank = fill[dev]
                fill[dev] = rank + 1

                @pl.when(rank < count)
                def _():
                    plan[half, at] = dev * 4 + rank
                    notes[dev, rank] = value - ((dev * ST_DEV) << LEN_BITS)

                @pl.when(rank >= count)
                def _():
                    flag[0] = 1

    write_notes(tiles, 0, notes, flag[0], base[...])


def plan_rows(count, wide_count, table, base):
    return pl.pallas_call(
        functools.partial(plan_kernel, count),
        out_shape=(
            jax.ShapeDtypeStruct((2, table.shape[1]), jnp.int32),
            jax.ShapeDtypeStruct((wide_count, NOTES, LANES), jnp.bfloat16),
            jax.ShapeDtypeStruct((wide_count,), jnp.int32),
        ),
        in_specs=[SMEM, VMEM],
        out_specs=(SMEM, VMEM, SMEM),
        scratch_shapes=[pltpu.SMEM((wide_count, count), jnp.int32), pltpu.SMEM((1,), jnp.int32)],
        cost_estimate=pl.CostEstimate(flops=2**16, bytes_accessed=2**18, transcendentals=0),
        name="plan_rows",
    )(table, base)


def first_kernel(count, base_next, table, plan, held, core_ref, own, mate, tiles, out, token, theirs, flag, taken, started, sem):
    core = core_ref[0]
    started[0] = 0
    token[0] = 0
    flag[0] = 0

    def place(half, source):
        @pl.loop(0, plan.shape[1])
        def _(at):
            code = plan[half, at]

            @pl.when(code >= 0)
            def _():
                started[0] += 1
                rows = source.at[at, unit(core)]
                pltpu.make_async_copy(rows, out.at[code >> 2, unit(code & 3)], sem).start()

    for half in range(2):

        @pl.when(core == half)
        def _():
            place(half, own)

        @pl.when(core != half)
        def _():
            place(half, mate)

    @pl.loop(0, out.shape[0])
    def _(dev):
        theirs[dev] = 0

    for half in range(2):
        taken[0] = 0

        @pl.loop(0, plan.shape[1])
        def _(at):
            value = table[2 + half, at]

            @pl.when(value >= 0)
            def _():
                dev = owner_of(value)
                rank = theirs[dev]
                theirs[dev] = rank + 1

                @pl.when(rank >= base_next)
                def _():
                    index = taken[0]
                    taken[0] = index + 1

                    @pl.when((index >= SPILL) | (held[dev] + rank >= 2 * base_next))
                    def _():
                        flag[0] = 1

    row = lax.broadcasted_iota(jnp.int32, (NOTES, LANES), 0)
    raised = jnp.where(row == 3 * count, flag[0], 0).astype(jnp.float32)

    @pl.loop(0, out.shape[0], unroll=4)
    def _(dev):
        out[dev, count * ROWS :, :] = jnp.maximum(tiles[dev].astype(jnp.float32), raised).astype(jnp.bfloat16)

    @pl.loop(0, started[0])
    def _(_):
        pltpu.make_async_copy(own.at[0, unit(0)], out.at[0, unit(0)], sem).wait()


def pack_first(count, base_next, table, plan, held, core, own, mate, tiles):
    wide_count = held.shape[0]
    return pl.pallas_call(
        functools.partial(first_kernel, count, base_next),
        out_shape=(
            jax.ShapeDtypeStruct((wide_count, count * ROWS + NOTES, LANES), jnp.bfloat16),
            jax.ShapeDtypeStruct((1,), jnp.int32),
        ),
        in_specs=[SMEM] * 4 + [ANY, ANY, VMEM],
        out_specs=(VMEM, SMEM),
        scratch_shapes=[pltpu.SMEM((wide_count,), jnp.int32)]
        + [pltpu.SMEM((1,), jnp.int32)] * 3
        + [pltpu.SemaphoreType.DMA],
        cost_estimate=pl.CostEstimate(flops=0, bytes_accessed=wide_count * count * NT * 4, transcendentals=0),
        name="pack_first",
    )(table, plan, held, core, own, mate, tiles)


def spill_kernel(base, table, core_ref, own, same, other, plan, fill, started, sem):
    core = core_ref[0]
    slots = table.shape[1]
    started[0] = 0

    @pl.loop(0, fill.shape[0])
    def _(dev):
        fill[dev] = 0

    for half in range(2):

        @pl.loop(0, slots)
        def _(at):
            value = table[half, at]
            plan[half, at] = -1

            @pl.when(value >= 0)
            def _():
                dev = owner_of(value)
                rank = fill[dev]
                fill[dev] = rank + 1

                @pl.when(rank < base)
                def _():
                    plan[half, at] = dev * 4 + rank

                @pl.when((rank >= base) & (core == half) & (started[0] < SPILL))
                def _():
                    index = started[0]
                    started[0] = index + 1
                    pltpu.make_async_copy(own.at[at, unit(core)], same.at[index], sem).start()
                    pltpu.make_async_copy(own.at[at, unit(1 - core)], other.at[index], sem).start()

    @pl.loop(0, 2 * started[0])
    def _(_):
        pltpu.make_async_copy(own.at[0, unit(0)], same.at[0], sem).wait()


def spill(base, wide_count, table, core, own):
    buffer = jax.ShapeDtypeStruct((SPILL, ROWS, LANES), jnp.bfloat16)
    return pl.pallas_call(
        functools.partial(spill_kernel, base),
        out_shape=(
            buffer,
            buffer,
            jax.ShapeDtypeStruct((2, table.shape[1]), jnp.int32),
            jax.ShapeDtypeStruct((wide_count,), jnp.int32),
        ),
        in_specs=[SMEM, SMEM, ANY],
        out_specs=(VMEM, VMEM, SMEM, SMEM),
        scratch_shapes=[pltpu.SMEM((1,), jnp.int32), pltpu.SemaphoreType.DMA],
        cost_estimate=pl.CostEstimate(flops=0, bytes_accessed=2**20, transcendentals=0),
        name="spill",
    )(table, core, own)


def pack_kernel(base, table, plan, held, core_ref, own, mate, same, other, after, out, fill, theirs, started, taken, sem):
    core = core_ref[0]
    started[0] = 0

    @pl.loop(0, out.shape[0])
    def _(dev):
        fill[dev] = held[dev]
        theirs[dev] = 0

    def place(half, source, guests):
        @pl.loop(0, plan.shape[1])
        def _(at):
            code = plan[half, at]

            @pl.when(code >= 0)
            def _():
                started[0] += 1
                rows = source.at[at, unit(core)]
                pltpu.make_async_copy(rows, out.at[code >> 2, unit(code & 3)], sem).start()

        taken[0] = 0

        @pl.loop(0, plan.shape[1])
        def _(at):
            value = table[2 + half, at]

            @pl.when(value >= 0)
            def _():
                dev = owner_of(value)
                rank = theirs[dev]
                theirs[dev] = rank + 1

                @pl.when(rank >= base)
                def _():
                    index = taken[0]
                    slot = fill[dev]
                    taken[0] = index + 1

                    @pl.when((index < SPILL) & (slot < base))
                    def _():
                        fill[dev] = slot + 1
                        started[0] += 1
                        pltpu.make_async_copy(guests.at[index], out.at[dev, unit(slot)], sem).start()

    for half in range(2):

        @pl.when(core == half)
        def _():
            place(half, own, same)

        @pl.when(core != half)
        def _():
            place(half, mate, other)

    @pl.loop(0, started[0])
    def _(_):
        pltpu.make_async_copy(own.at[0, unit(0)], out.at[0, unit(0)], sem).wait()


def pack_planned(base, table, plan, held, core, own, mate, same, other, after):
    wide_count = held.shape[0]
    return pl.pallas_call(
        functools.partial(pack_kernel, base),
        out_shape=jax.ShapeDtypeStruct((wide_count, base * ROWS, LANES), jnp.bfloat16),
        in_specs=[SMEM] * 4 + [ANY] * 5,
        out_specs=VMEM,
        scratch_shapes=[
            pltpu.SMEM((wide_count,), jnp.int32),
            pltpu.SMEM((wide_count,), jnp.int32),
            pltpu.SMEM((1,), jnp.int32),
            pltpu.SMEM((1,), jnp.int32),
            pltpu.SemaphoreType.DMA,
        ],
        cost_estimate=pl.CostEstimate(flops=0, bytes_accessed=wide_count * base * NT * 4, transcendentals=0),
        name="pack_planned",
    )(table, plan, held, core, own, mate, same, other, after)


def table_notes(packed):
    owner = (packed >> LEN_BITS) + 1
    length = jnp.where(packed >= 0, packed & 0xFFFF, 0)
    parts = jnp.concatenate([owner >> 8, owner & 0xFF, length >> 8, length & 0xFF])
    rows = 3 * LANES - parts.shape[0]
    parts = jnp.pad(parts, (0, rows)).reshape(3, LANES)
    return jnp.pad(parts, ((NOTES - 3, 0), (0, 0)))


def read_slots(rows, count):
    notes = rows[::2, count * ROWS : count * ROWS + 3 * count + 1, 0].astype(jnp.float32).astype(jnp.int32)
    fields = notes[:, : 3 * count].reshape(-1, count, 3)
    station, length = fields[..., 0] - 1, fields[..., 1] * 256 + fields[..., 2]
    return station.reshape(-1), length.reshape(-1), notes[:, 3 * count]


def read_table(rows, slots, chips):
    parts = rows[:, -3:, :].astype(jnp.float32).astype(jnp.int32)
    parts = parts.reshape(rows.shape[0], -1)[:, : 4 * slots].reshape(chips, 2, 4, slots)
    return (parts[:, :, 0] * 256 + parts[:, :, 1] - 1).reshape(chips, 2 * slots)


def second_places(owner, column, base):
    chips, entries = owner.shape
    extra = MOST - base
    slots = entries // 2
    listed = owner >= 0
    dev = jnp.where(listed, owner // ST_DEV, -1)
    order = jnp.arange(entries, dtype=jnp.int32)
    earlier = order[None, :] < order[:, None]
    alike = (dev[:, :, None] == dev[:, None, :]) & earlier
    rank = jnp.sum(alike.astype(jnp.int32), axis=2)
    over = listed & (rank >= base)
    near = earlier & (order[None, :] // slots == order[:, None] // slots)
    index = jnp.sum((over[:, None, :] & near).astype(jnp.int32), axis=2)
    sent = over & (index < SPILL)
    guest = jnp.sum((alike & sent[:, None, :]).astype(jnp.int32), axis=2)
    host_dev = jnp.concatenate([dev[chips // 2 :], dev[: chips // 2]])
    host_held = jnp.sum((dev[:, :, None] == host_dev[:, None, :]).astype(jnp.int32), axis=2)
    slot = host_held + guest
    fits = sent & (slot < base)
    chip = jnp.arange(chips, dtype=jnp.int32)[:, None]
    host = (chip + chips // 2) % chips
    code = jnp.where(rank < base, chip * base + rank, chips * base + chip * extra + rank - base)
    code = jnp.where(fits, host * base + slot, code)
    local = column * ST_DEV + jnp.arange(ST_DEV, dtype=jnp.int32)
    chosen = owner[None] == local[:, None, None]
    return jnp.sum(jnp.where(chosen, code[None], 0), axis=(1, 2))


def whiten_kernel(
    part, parts, source, length, picks, got, more, first, twist, second, *refs
):
    token, held, spectra, sem, sems = refs[-5:]
    stops, rows = picks.shape
    white = refs[-6 - parts]
    payload = refs[-5 - parts : -5]
    token[0] = 0
    stations = held.shape[0]
    base = SLOTS[part]
    first_more = got.shape[0] // 2 * base
    batch = 8

    def fetch(rows, code, count, station):
        for seg in range(2):
            source_at = rows.at[2 * (code // count) + seg, unit(code % count)]
            pltpu.make_async_copy(source_at, held.at[station, unit(seg)], sems.at[station // batch]).start()

    @pl.loop(0, stations)
    def _(station):
        code = source[station]

        @pl.when(code < first_more)
        def _():
            fetch(got, code, base, station)

        @pl.when(code >= first_more)
        def _():
            fetch(more, code - first_more, MOST - base, station)

    row = lax.broadcasted_iota(jnp.int32, (2 * ROWS, LANES), 0)
    lane = lax.broadcasted_iota(jnp.int32, (2 * ROWS, LANES), 1)
    left = lax.broadcasted_iota(jnp.int32, (ROWS // 2, LANES), 1) < ROWS
    place = (2 * part + (row & 1)) * NT + (row >> 1) * LANES + lane

    def two_stations(station):
        sides = []
        for at in range(2):
            values = held[station + at].astype(jnp.float32)
            sides.append(jnp.where(place < length[station + at], values, 0.0).astype(jnp.bfloat16))
        values = jnp.concatenate(sides, 1)
        values = jnp.concatenate([values, values], 0)
        mixed = jnp.dot(first[...], values, preferred_element_type=jnp.float32)
        parts = []
        for at in range(2):
            for seg in range(2):
                real = mixed[2 * seg * ROWS : (2 * seg + 1) * ROWS, at * LANES : (at + 1) * LANES]
                imag = mixed[(2 * seg + 1) * ROWS : (2 * seg + 2) * ROWS, at * LANES : (at + 1) * LANES]
                turned_re = real * twist[0] + imag * twist[1]
                turned_im = imag * twist[0] - real * twist[1]
                parts.append(jnp.concatenate([turned_re, turned_im], 1))
        turned = jnp.concatenate(parts, 0)
        high = turned.astype(jnp.bfloat16)
        low = (turned - high.astype(jnp.float32)).astype(jnp.bfloat16)
        upper = jnp.dot(high, second[...], preferred_element_type=jnp.float32)
        lower = jnp.dot(low, second[:, :LANES], preferred_element_type=jnp.float32)
        spectrum = upper[:, :LANES] + (upper[:, LANES:] + lower)
        for at in range(2):
            for seg in range(2):
                begin = (2 * at + seg) * ROWS
                side = spectrum[begin : begin + ROWS]
                power = jnp.sum(side * side, axis=0, keepdims=True)
                power = (power + pltpu.roll(power, LANES // 2, 1)) * (1.0 / ROWS)
                scale = 1.0 / jnp.sqrt(power + 1e-06)
                side = side * scale
                upper, lower = side[: ROWS // 2], side[ROWS // 2 :]
                real = jnp.where(left, upper, pltpu.roll(lower, ROWS, 1))
                imag = jnp.where(left, pltpu.roll(upper, ROWS, 1), lower)
                spectra[station + at, seg, : ROWS // 2] = real.astype(jnp.bfloat16)
                spectra[station + at, seg, ROWS // 2 :] = imag.astype(jnp.bfloat16)

    @pl.loop(0, stations // batch)
    def _(at):
        these = held.at[pl.ds(at * batch, batch)]
        pltpu.make_async_copy(these, these, sems.at[at]).wait()
        for two in range(0, batch, 2):
            two_stations(batch * at + two)

    each = stops // parts
    for piece in range(parts):

        @pl.loop(0, each)
        def _(stop):
            for at in range(rows):
                row = spectra.at[picks[piece * each + stop, at]]
                pltpu.make_async_copy(row, payload[piece].at[stop, at], sem).start()

    whole = pltpu.make_async_copy(spectra, white, sems.at[0])
    whole.start()
    for piece in range(parts):
        pltpu.make_async_copy(payload[piece], payload[piece], sem).wait()
    whole.wait()


def whiten(part, parts, source, length, picks, got, more, tables, after):
    stops, rows = picks.shape
    piece = jax.ShapeDtypeStruct((stops // parts, rows, 2, ROWS, LANES), jnp.bfloat16)
    return pl.pallas_call(
        functools.partial(whiten_kernel, part, parts),
        out_shape=(jax.ShapeDtypeStruct((ST_DEV, 2, ROWS, LANES), jnp.bfloat16),)
        + (piece,) * parts
        + (jax.ShapeDtypeStruct((1,), jnp.int32),),
        in_specs=[SMEM, SMEM, SMEM, ANY, ANY, VMEM, VMEM, VMEM] + [ANY] * len(after),
        out_specs=(ANY,) * (1 + parts) + (SMEM,),
        scratch_shapes=[
            pltpu.VMEM((ST_DEV, 2 * ROWS, LANES), jnp.bfloat16),
            pltpu.VMEM((ST_DEV, 2, ROWS, LANES), jnp.bfloat16),
            pltpu.SemaphoreType.DMA,
            pltpu.SemaphoreType.DMA((ST_DEV // 8,)),
        ],
        cost_estimate=pl.CostEstimate(flops=2**20, bytes_accessed=2**18, transcendentals=0),
        name="whiten",
    )(source, length, picks, got, more, *tables, *after)


def cross_rows(near_pick, near, far, cross, fresh, ready):
    stops, rows = near_pick.shape
    side = rows // 2
    step = 16
    half = ROWS // 2

    @pl.loop(0, stops)
    def _(stop):
        ready(stop)
        for two in range(2):
            first = two * side
            own = [near_pick[stop, first + i] for i in range(side)]

            @pl.loop(0, half // step)
            def _(chunk):
                real = pl.ds(pl.multiple_of(chunk * step, step), step)
                imag = pl.ds(pl.multiple_of(half + chunk * step, step), step)

                def both(ref, row):
                    return [
                        (ref[row, s, real, :].astype(jnp.float32), ref[row, s, imag, :].astype(jnp.float32))
                        for s in range(2)
                    ]

                here = [both(near, own[i]) for i in range(side)]
                for j in range(side):
                    there = both(far.at[stop], first + j)
                    for i in range(side):
                        pair = ((stop * 2 + two) * side + i) * side + j
                        total_re = sum(n[0] * f[0] + n[1] * f[1] for n, f in zip(here[i], there))
                        total_im = sum(n[1] * f[0] - n[0] * f[1] for n, f in zip(here[i], there))
                        for total, add in ((total_re, 0), (total_im, half)):
                            at = pl.ds(pl.multiple_of(pair * ROWS + add + chunk * step, step), step)
                            if fresh:
                                cross[at, :] = total
                            else:
                                cross[at, :] += total


def lag_product(cross, tables, last, out, edge, exact):
    pairs = out.shape[0]
    group = 8
    depth = group * LANES
    half = LAGS // 2
    turns = ROWS // 2 // group

    def product(turn, even):
        base = turn * group
        slabs = [cross[pl.ds(base + k, pairs, stride=ROWS), :] for k in range(group)]
        high = [slab.astype(jnp.bfloat16) for slab in slabs]
        if even:
            total = edge[...]
            for k in range(group):
                total += (slabs[k] if exact else high[k].astype(jnp.float32)) * last[base + k]
            edge[...] = total
        rows = jnp.concatenate(high, 1)
        if exact:
            low = [(slab - part.astype(jnp.float32)).astype(jnp.bfloat16) for slab, part in zip(slabs, high)]
            rows = jnp.concatenate([rows, jnp.concatenate(low, 1)], 0)
        part = jnp.dot(
            rows,
            tables[pl.ds(pl.multiple_of(base * LANES, depth), depth), :],
            preferred_element_type=jnp.float32,
        )
        return part[:pairs] + part[pairs:] if exact else part

    @pl.loop(0, turns)
    def _(turn):
        out[:, :half] += product(turn, True)

    @pl.loop(turns, 2 * turns)
    def _(turn):
        out[:, half:] += product(turn, False)


def first_lag_kernel(stops, near_pick, white, home, *refs):
    far_in = refs[: stops - 1]
    table, last, out, edge, near, far, cross, tables, sem, sems, table_sem = refs[stops - 1 :]
    load = pltpu.make_async_copy(white, near, sem)
    load.start()
    pltpu.make_async_copy(home, far.at[0], sems.at[0]).start()
    for stop in range(1, stops):
        pltpu.make_async_copy(far_in[stop - 1], far.at[stop], sems.at[stop]).start()
    load_table = pltpu.make_async_copy(table, tables, table_sem)
    load_table.start()
    out[...] = jnp.zeros_like(out)
    edge[...] = jnp.zeros_like(edge)
    load.wait()

    def ready(stop):
        pltpu.make_async_copy(far.at[stop], far.at[stop], sems.at[stop]).wait()

    cross_rows(near_pick, near, far, cross, True, ready)
    load_table.wait()
    lag_product(cross, tables, last, out, edge, True)


def last_lag_kernel(
    near_pick, far_at, begun, begun_edge, white, far_in, table, last, mask,
    result, near, far, cross, out, edge, tables, sem, sems, table_sem,
):
    stops = near_pick.shape[0]
    pairs = out.shape[0]
    half = LAGS // 2
    load = pltpu.make_async_copy(white, near, sem.at[0])
    load.start()
    for stop in range(stops):
        pltpu.make_async_copy(far_in.at[far_at[stop]], far.at[stop], sems.at[stop]).start()
    load_table = pltpu.make_async_copy(table, tables, table_sem)
    load_table.start()
    before = [pltpu.make_async_copy(begun, out, sem.at[1]), pltpu.make_async_copy(begun_edge, edge, sem.at[2])]
    for copy in before:
        copy.start()
    load.wait()

    def ready(stop):
        pltpu.make_async_copy(far.at[stop], far.at[stop], sems.at[stop]).wait()

    cross_rows(near_pick, near, far, cross, True, ready)
    load_table.wait()
    for copy in before:
        copy.wait()
    lag_product(cross, tables, last, out, edge, False)
    first_lag = jnp.sum(edge[...], axis=1, keepdims=True)
    lane = lax.broadcasted_iota(jnp.int32, (pairs, LANES), 1)
    mirror = (LANES - lane) % LANES
    first = lane == 0
    listed = mask[...]
    count = half // LANES
    back, ahead = [], []
    for block in range(count):
        even = out[:, block * LANES : (block + 1) * LANES]
        odd = out[:, half + block * LANES : half + (block + 1) * LANES]
        if block == 0:
            first_lag = first_lag + odd
            odd = jnp.where(first, 0.0, odd)
        back.append(even - odd)
        ahead.append(even + odd)
    for block in range(count):
        turned = jnp.take_along_axis(back[count - 1 - block], mirror, axis=1)
        start = first_lag if block == 0 else back[count - block]
        lags = pl.ds(block * LANES, LANES)
        result[:, :, lags] = (jnp.where(first, start, turned) * listed).reshape(result.shape[:2] + (LANES,))
        lags = pl.ds(half + block * LANES, LANES)
        result[:, :, lags] = (ahead[block] * listed).reshape(result.shape[:2] + (LANES,))


def lag_scratch(white, stops, pairs, table):
    return [
        pltpu.VMEM(white.shape, jnp.bfloat16),
        pltpu.VMEM((stops, 8, 2, ROWS, LANES), jnp.bfloat16),
        pltpu.VMEM((pairs * ROWS, LANES), jnp.float32),
    ], [pltpu.VMEM(table.shape, jnp.bfloat16)]


def lagged_first(near_pick, white, home, far, table, last):
    stops, rows = near_pick.shape
    pairs = stops * rows * rows // 2
    scratch, table_scratch = lag_scratch(white, stops, pairs, table)
    return pl.pallas_call(
        functools.partial(first_lag_kernel, stops),
        out_shape=(
            jax.ShapeDtypeStruct((pairs, LAGS), jnp.float32),
            jax.ShapeDtypeStruct((pairs, LANES), jnp.float32),
        ),
        in_specs=[SMEM] + [ANY] * (stops + 2) + [VMEM],
        out_specs=(VMEM, VMEM),
        scratch_shapes=scratch
        + table_scratch
        + [pltpu.SemaphoreType.DMA, pltpu.SemaphoreType.DMA((stops,)), pltpu.SemaphoreType.DMA],
        compiler_params=pltpu.CompilerParams(vmem_limit_bytes=LAG_VMEM),
        cost_estimate=pl.CostEstimate(
            flops=4 * pairs * NF * LAGS, bytes_accessed=16 * 1024 * 1024, transcendentals=0
        ),
        name="lagged_first",
    )(near_pick, white, home, *far, table, last)


def lagged_last(near_pick, far_at, begun, edge, white, far, table, last, mask):
    stops, rows = near_pick.shape
    side = rows // 2
    pairs = mask.shape[0]
    scratch, table_scratch = lag_scratch(white, stops, pairs, table)
    return pl.pallas_call(
        last_lag_kernel,
        out_shape=jax.ShapeDtypeStruct((pairs // side, side, LAGS), jnp.float32),
        in_specs=[SMEM, SMEM] + [ANY] * 5 + [VMEM, VMEM],
        out_specs=VMEM,
        scratch_shapes=scratch
        + [pltpu.VMEM((pairs, LAGS), jnp.float32), pltpu.VMEM((pairs, LANES), jnp.float32)]
        + table_scratch
        + [pltpu.SemaphoreType.DMA((3,)), pltpu.SemaphoreType.DMA((stops,)), pltpu.SemaphoreType.DMA],
        compiler_params=pltpu.CompilerParams(vmem_limit_bytes=LAG_VMEM),
        cost_estimate=pl.CostEstimate(
            flops=2 * pairs * NF * LAGS, bytes_accessed=16 * 1024 * 1024, transcendentals=0
        ),
        name="lagged_last",
    )(near_pick, far_at, begun, edge, white, far, table, last, mask)


def empty(shape):
    return pl.pallas_call(
        lambda out: None,
        out_shape=jax.ShapeDtypeStruct(shape, jnp.bfloat16),
        out_specs=ANY,
        name="empty",
    )()


def on_device(records, lengths, owners, own_pick, visit_pick, pair_mask):
    wide_count = lax.axis_size("wide")
    stops = lax.axis_size("blk")
    column = lax.axis_index("wide")
    group = lax.axis_index("blk")
    core = column % 2
    slots = records.shape[1]
    steps = jnp.arange(stops, dtype=jnp.int32)
    core_at = core.reshape(1)

    def flip(bits):
        return [(i, i ^ bits) for i in range(wide_count)]

    def across(shard, bits):
        return lax.ppermute(shard, "wide", flip(bits))

    over = wide_count // 2
    packed = jnp.where(owners[0] >= 0, (owners[0] << LEN_BITS) + lengths[0], -1)
    others = [across(packed, bits) for bits in (1, over, over + 1)]
    table = jnp.where(
        core == 0,
        jnp.stack([packed, others[0], others[1], others[2]]),
        jnp.stack([others[0], packed, others[2], others[1]]),
    )

    blocks = records[0].reshape(slots, SEG, ROWS, LANES)

    def halves(part):
        return blocks[:, 2 * part : 2 * part + 2].transpose(0, 2, 1, 3).reshape(slots, 2 * ROWS, LANES)

    def send(payload):
        return lax.all_to_all(payload, "wide", split_axis=0, concat_axis=0, tiled=True)

    own_a = halves(0)
    mate_a = across(own_a, 1)
    base_a, base_b = SLOTS
    plan_a, tiles, held_a = plan_rows(base_a, wide_count, table, table_notes(packed))
    load_a, token = pack_first(base_a, base_b, table, plan_a, held_a, core_at, own_a, mate_a, tiles)
    got_a = send(load_a)
    own_b = jnp.where(token[0] >= 0, halves(1), 0.0)
    mate_b = across(own_b, 1)
    same_b, other_b, plan, held = spill(base_b, wide_count, table, core_at, own_b)
    same_b, other_b = across(same_b, over), across(other_b, over + 1)
    visits = jnp.where(token[0] >= 0, visit_pick[0, 0].reshape(1, stops, -1), 0)
    bit = 1
    while bit < stops:
        theirs = lax.ppermute(visits, "blk", [(i, i ^ bit) for i in range(stops)])
        upper = (group // bit) % 2 == 1
        visits = jnp.concatenate([jnp.where(upper, theirs, visits), jnp.where(upper, visits, theirs)])
        bit *= 2
    by_dest = visits[steps, (steps - group) % stops]
    by_stop = by_dest[(steps + group) % stops]
    load_b = pack_planned(base_b, table, plan, held, core_at, own_b, mate_b, same_b, other_b, by_stop)
    got_b = send(load_b)

    def late_rows(low, own, mate):
        payload = pack_rows(low, MOST - low, wide_count, table, core_at, own, mate)[0]
        arrived = [lax.ppermute(payload[column ^ bits], "wide", flip(bits)) for bits in range(1, wide_count)]
        arrived = jnp.stack([payload[column]] + arrived)
        return arrived[column ^ jnp.arange(wide_count, dtype=jnp.int32)]

    def late():
        first = late_rows(base_a, own_a, mate_a)
        second = late_rows(base_b, own_b, mate_b)
        return (first, second) + read_slots(first, MOST - base_a)[:2]

    def never():
        count = wide_count // 2 * (MOST - base_a)
        rows = [empty((wide_count, (MOST - base) * ROWS + NOTES, LANES)) for base in SLOTS]
        return rows[0], rows[1], jnp.full((count,), -1, jnp.int32), jnp.zeros((count,), jnp.int32)

    station, length, spilled = read_slots(got_a, base_a)
    more_a, more_b, more_station, more_length = lax.cond(jnp.max(spilled) > 0, late, never)
    station = jnp.concatenate([station, more_station])
    length = jnp.concatenate([length, more_length])
    chosen = station[None, :] == jnp.arange(ST_DEV, dtype=jnp.int32)[:, None]
    codes = jnp.arange(station.shape[0], dtype=jnp.int32)
    source_a = jnp.sum(jnp.where(chosen, codes[None], 0), axis=1)
    length = jnp.sum(jnp.where(chosen, length[None], 0), axis=1)

    tables = [jnp.asarray(table) for table in transform_tables()]
    near_pick = own_pick[0, 0].reshape(stops, -1)
    white_a, home, *payload_a, _ = whiten(0, stops, source_a, length, by_stop, got_a, more_a, tables, [])
    far_a = [
        lax.ppermute(payload_a[stop - 1][0], "blk", [(i, (i + stop) % stops) for i in range(stops)])
        for stop in range(1, stops)
    ]
    source_b = second_places(read_table(got_a, slots, wide_count // 2), column, base_b)
    white_b, payload_b, _ = whiten(1, 1, source_b, length, by_dest, got_b, more_b, tables, far_a)
    far_b = lax.all_to_all(payload_b, "blk", split_axis=0, concat_axis=0, tiled=True)

    far_at = (group - steps) % stops
    mask = pair_mask[0, 0].astype(jnp.float32).reshape(-1, 1)
    lags, last = (jnp.asarray(table) for table in lag_tables())
    begun, edge = lagged_first(near_pick, white_a, home[0], far_a, lags, last)
    result = lagged_last(near_pick, far_at, begun, edge, white_b, far_b, lags, last, mask)
    return result.reshape((1, 1) + pair_mask.shape[2:] + (LAGS,))


def solution(mesh):
    return jax.shard_map(
        on_device,
        mesh=mesh,
        in_specs=(
            P("blk", "wide", None, None),
            P("blk", "wide"),
            P("blk", "wide"),
            P("blk", "wide", None, None, None),
            P("blk", "wide", None, None, None),
            P("blk", "wide", None, None, None, None),
        ),
        out_specs=P("blk", "wide", None, None, None, None, None),
        check_vma=False,
    )
```

```python
import functools
import math

import jax
import jax.numpy as jnp
import numpy as np
from jax import lax
from jax.experimental import pallas as pl
from jax.experimental.pallas import tpu as pltpu
from jax.sharding import PartitionSpec as P

ST_DEV = 24
SEG = 4
NT = 8192
NF = 4096
LAGS = 1024
ROWS = 64
LANES = 128
MOST = 6
SLOTS = (4, 3)
SPILL = 12
LAG_VMEM = 60 * 1024 * 1024
LEN_BITS = 16
NOTES = 16
SMEM = pl.BlockSpec(memory_space=pltpu.SMEM)
VMEM = pl.BlockSpec(memory_space=pltpu.VMEM)
ANY = pl.BlockSpec(memory_space=pl.ANY)


def split_bf16(values):
    high = values.astype(jnp.bfloat16)
    low = (values - high.astype(np.float64)).astype(jnp.bfloat16)
    return high, low


def transform_tables():
    first = np.arange(ROWS)
    second = np.arange(LANES)
    half = np.arange(LANES // 2)
    angle = 2.0 * math.pi / ROWS * (first[:, None] * first[None, :] % ROWS)
    wave = np.concatenate([np.cos(angle), -np.sin(angle)], 0)
    wave = np.einsum("ab,kn->aknb", np.eye(2), wave).reshape(4 * ROWS, 2 * ROWS)
    first_table = np.concatenate(split_bf16(wave), 1)
    twist = 2.0 * math.pi / NT * (first[:, None] * second[None, :] % NT)
    twist_table = np.stack([np.cos(twist), np.sin(twist)]).astype(np.float32)
    angle = 2.0 * math.pi / LANES * (second[:, None] * half[None, :] % LANES)
    cos, sin = np.cos(angle), np.sin(angle)
    wave = np.concatenate([np.concatenate([cos, -sin], 1), np.concatenate([sin, cos], 1)], 0)
    second_table = np.concatenate(split_bf16(wave), 1)
    return first_table, twist_table, second_table


def lag_tables():
    row = np.arange(ROWS // 2, dtype=np.int64)
    lane = np.arange(LANES, dtype=np.int64)
    bins = (row[:, None] + ROWS // 2 * (lane // ROWS)) + ROWS * (lane % ROWS)
    bins = bins.reshape(-1)
    weight = np.where(bins == 0, 0.5, 1.0).astype(np.float32) / np.float32(math.sqrt(NF * SEG))

    def at(delay):
        phase = bins[:, None] * delay[None, :] % NT
        return phase.astype(np.float32) * np.float32(2.0 * math.pi / NT)

    ahead = at(np.arange(LAGS // 2, dtype=np.int64))
    edge = at(np.array([NT - LAGS // 2], dtype=np.int64))
    cos = weight[:, None] * np.cos(ahead)
    sin = -weight[:, None] * np.sin(ahead)
    sin[:, :1] = -weight[:, None] * np.sin(edge)
    last = (weight[:, None] * np.cos(edge)).reshape(ROWS // 2, 1, LANES)
    return (
        np.concatenate([cos, sin], 0).astype(jnp.bfloat16),
        last.astype(jnp.bfloat16).astype(np.float32),
    )


def owner_of(value):
    return ((value >> LEN_BITS) * 2731) >> 16


def unit(slot):
    return pl.ds(pl.multiple_of(slot * ROWS, ROWS), ROWS)


def write_notes(out, begin, notes, flag, base):
    count = notes.shape[1]
    row = lax.broadcasted_iota(jnp.int32, (NOTES, LANES), 0)

    @pl.loop(0, notes.shape[0])
    def _(dev):
        tile = jnp.where(row == 3 * count, flag, base)
        for slot in range(count):
            value = notes[dev, slot]
            tile = jnp.where(row == 3 * slot, (value >> LEN_BITS) + 1, tile)
            tile = jnp.where(row == 3 * slot + 1, (value & 0xFFFF) >> 8, tile)
            tile = jnp.where(row == 3 * slot + 2, value & 0xFF, tile)
        out[dev, begin : begin + NOTES, :] = tile.astype(jnp.float32).astype(jnp.bfloat16)


def valid_slots(table, row):
    return table[row, table.shape[1] - 1]


def rows_kernel(low, count, table, core_ref, own, mate, out, fill, notes, started, sem):
    core = core_ref[0]
    started[0] = 0

    @pl.loop(0, out.shape[0])
    def _(dev):
        fill[dev] = 0
        for slot in range(count):
            notes[dev, slot] = -1

    def place(half, source):
        @pl.loop(0, valid_slots(table, half))
        def _(at):
            value = table[half, at]
            dev = owner_of(value)
            rank = fill[dev]
            fill[dev] = rank + 1

            @pl.when((rank >= low) & (rank < low + count))
            def _():
                started[0] += 1
                notes[dev, rank - low] = value - ((dev * ST_DEV) << LEN_BITS)
                rows = source.at[at, unit(core)]
                pltpu.make_async_copy(rows, out.at[dev, unit(rank - low)], sem).start()

    for half in range(2):

        @pl.when(core == half)
        def _():
            place(half, own)

        @pl.when(core != half)
        def _():
            place(half, mate)

    write_notes(out, count * ROWS, notes, 0, jnp.zeros((NOTES, LANES), jnp.int32))

    @pl.loop(0, started[0])
    def _(_):
        pltpu.make_async_copy(own.at[0, unit(0)], out.at[0, unit(0)], sem).wait()


def pack_rows(low, count, wide_count, table, core, own, mate):
    return pl.pallas_call(
        functools.partial(rows_kernel, low, count),
        out_shape=jax.ShapeDtypeStruct((wide_count, count * ROWS + NOTES, LANES), jnp.bfloat16),
        in_specs=[SMEM, SMEM, ANY, ANY],
        out_specs=VMEM,
        scratch_shapes=[
            pltpu.SMEM((wide_count,), jnp.int32),
            pltpu.SMEM((wide_count, count), jnp.int32),
            pltpu.SMEM((1,), jnp.int32),
            pltpu.SemaphoreType.DMA,
        ],
        cost_estimate=pl.CostEstimate(flops=0, bytes_accessed=wide_count * count * NT * 4, transcendentals=0),
        name="pack_rows",
    )(table, core, own, mate)


def plan_kernel(count, base_next, table, base, plan, tiles, fill, notes, theirs, flag):
    flag[0] = 0

    @pl.loop(0, fill.shape[0])
    def _(dev):
        fill[dev] = 0
        theirs[dev] = 0
        for slot in range(count):
            notes[dev, slot] = -1

    for half in range(2):

        @pl.loop(0, valid_slots(table, half))
        def _(at):
            value = table[half, at]
            dev = owner_of(value)
            rank = fill[dev]
            fill[dev] = rank + 1
            fits = rank < count
            plan[half, at] = jnp.where(fits, dev * 4 + rank, -1)

            @pl.when(fits)
            def _():
                notes[dev, rank] = value - ((dev * ST_DEV) << LEN_BITS)

            @pl.when(jnp.logical_not(fits))
            def _():
                flag[0] = 1

    for half in range(2):

        def check(at, index):
            dev = owner_of(table[2 + half, at])
            rank = theirs[dev]
            theirs[dev] = rank + 1
            spilled = rank >= base_next

            @pl.when(spilled & ((index >= SPILL) | (fill[dev] + rank >= 2 * base_next)))
            def _():
                flag[0] = 1

            return index + spilled.astype(jnp.int32)

        lax.fori_loop(0, valid_slots(table, 2 + half), check, 0)

    write_notes(tiles, 0, notes, flag[0], base[...])


def plan_rows(count, base_next, wide_count, table, base):
    return pl.pallas_call(
        functools.partial(plan_kernel, count, base_next),
        out_shape=(
            jax.ShapeDtypeStruct((2, table.shape[1] - 1), jnp.int32),
            jax.ShapeDtypeStruct((wide_count, NOTES, LANES), jnp.bfloat16),
            jax.ShapeDtypeStruct((wide_count,), jnp.int32),
        ),
        in_specs=[SMEM, VMEM],
        out_specs=(SMEM, VMEM, SMEM),
        scratch_shapes=[
            pltpu.SMEM((wide_count, count), jnp.int32),
            pltpu.SMEM((wide_count,), jnp.int32),
            pltpu.SMEM((1,), jnp.int32),
        ],
        cost_estimate=pl.CostEstimate(flops=2**16, bytes_accessed=2**18, transcendentals=0),
        name="plan_rows",
    )(table, base)


def first_kernel(count, table, plan, core_ref, own, mate, tiles, out, token, started, sem):
    core = core_ref[0]
    started[0] = 0
    token[0] = 0

    def place(half, source):
        @pl.loop(0, valid_slots(table, half))
        def _(at):
            code = plan[half, at]

            @pl.when(code >= 0)
            def _():
                started[0] += 1
                rows = source.at[at, unit(core)]
                pltpu.make_async_copy(rows, out.at[code >> 2, unit(code & 3)], sem).start()

    for half in range(2):

        @pl.when(core == half)
        def _():
            place(half, own)

        @pl.when(core != half)
        def _():
            place(half, mate)

    @pl.loop(0, out.shape[0], unroll=4)
    def _(dev):
        out[dev, count * ROWS :, :] = tiles[dev]

    @pl.loop(0, started[0])
    def _(_):
        pltpu.make_async_copy(own.at[0, unit(0)], out.at[0, unit(0)], sem).wait()


def pack_first(count, table, plan, core, own, mate, tiles):
    wide_count = tiles.shape[0]
    return pl.pallas_call(
        functools.partial(first_kernel, count),
        out_shape=(
            jax.ShapeDtypeStruct((wide_count, count * ROWS + NOTES, LANES), jnp.bfloat16),
            jax.ShapeDtypeStruct((1,), jnp.int32),
        ),
        in_specs=[SMEM] * 3 + [ANY, ANY, VMEM],
        out_specs=(VMEM, SMEM),
        scratch_shapes=[pltpu.SMEM((1,), jnp.int32), pltpu.SemaphoreType.DMA],
        cost_estimate=pl.CostEstimate(flops=0, bytes_accessed=wide_count * count * NT * 4, transcendentals=0),
        name="pack_first",
    )(table, plan, core, own, mate, tiles)


def spill_kernel(base, table, core_ref, own, same, other, plan, fill, started, sem):
    core = core_ref[0]
    started[0] = 0

    @pl.loop(0, fill.shape[0])
    def _(dev):
        fill[dev] = 0

    for half in range(2):

        @pl.loop(0, valid_slots(table, half))
        def _(at):
            dev = owner_of(table[half, at])
            rank = fill[dev]
            fill[dev] = rank + 1
            plan[half, at] = jnp.where(rank < base, dev * 4 + rank, -1)

            @pl.when((rank >= base) & (core == half) & (started[0] < SPILL))
            def _():
                index = started[0]
                started[0] = index + 1
                pltpu.make_async_copy(own.at[at, unit(core)], same.at[index], sem).start()
                pltpu.make_async_copy(own.at[at, unit(1 - core)], other.at[index], sem).start()

    @pl.loop(0, 2 * started[0])
    def _(_):
        pltpu.make_async_copy(own.at[0, unit(0)], same.at[0], sem).wait()


def spill(base, wide_count, table, core, own):
    buffer = jax.ShapeDtypeStruct((SPILL, ROWS, LANES), jnp.bfloat16)
    return pl.pallas_call(
        functools.partial(spill_kernel, base),
        out_shape=(
            buffer,
            buffer,
            jax.ShapeDtypeStruct((2, table.shape[1] - 1), jnp.int32),
            jax.ShapeDtypeStruct((wide_count,), jnp.int32),
        ),
        in_specs=[SMEM, SMEM, ANY],
        out_specs=(VMEM, VMEM, SMEM, SMEM),
        scratch_shapes=[pltpu.SMEM((1,), jnp.int32), pltpu.SemaphoreType.DMA],
        cost_estimate=pl.CostEstimate(flops=0, bytes_accessed=2**20, transcendentals=0),
        name="spill",
    )(table, core, own)


def pack_kernel(base, table, plan, held, core_ref, own, mate, same, other, after, out, fill, theirs, started, taken, sem):
    core = core_ref[0]
    started[0] = 0

    @pl.loop(0, out.shape[0])
    def _(dev):
        fill[dev] = held[dev]
        theirs[dev] = 0

    def place(half, source, guests):
        @pl.loop(0, valid_slots(table, half))
        def _(at):
            code = plan[half, at]

            @pl.when(code >= 0)
            def _():
                started[0] += 1
                rows = source.at[at, unit(core)]
                pltpu.make_async_copy(rows, out.at[code >> 2, unit(code & 3)], sem).start()

        taken[0] = 0

        @pl.loop(0, valid_slots(table, 2 + half))
        def _(at):
            dev = owner_of(table[2 + half, at])
            rank = theirs[dev]
            theirs[dev] = rank + 1

            @pl.when(rank >= base)
            def _():
                index = taken[0]
                slot = fill[dev]
                taken[0] = index + 1

                @pl.when((index < SPILL) & (slot < base))
                def _():
                    fill[dev] = slot + 1
                    started[0] += 1
                    pltpu.make_async_copy(guests.at[index], out.at[dev, unit(slot)], sem).start()

    for half in range(2):

        @pl.when(core == half)
        def _():
            place(half, own, same)

        @pl.when(core != half)
        def _():
            place(half, mate, other)

    @pl.loop(0, started[0])
    def _(_):
        pltpu.make_async_copy(own.at[0, unit(0)], out.at[0, unit(0)], sem).wait()


def pack_planned(base, table, plan, held, core, own, mate, same, other, after):
    wide_count = held.shape[0]
    return pl.pallas_call(
        functools.partial(pack_kernel, base),
        out_shape=jax.ShapeDtypeStruct((wide_count, base * ROWS, LANES), jnp.bfloat16),
        in_specs=[SMEM] * 4 + [ANY] * 5,
        out_specs=VMEM,
        scratch_shapes=[
            pltpu.SMEM((wide_count,), jnp.int32),
            pltpu.SMEM((wide_count,), jnp.int32),
            pltpu.SMEM((1,), jnp.int32),
            pltpu.SMEM((1,), jnp.int32),
            pltpu.SemaphoreType.DMA,
        ],
        cost_estimate=pl.CostEstimate(flops=0, bytes_accessed=wide_count * base * NT * 4, transcendentals=0),
        name="pack_planned",
    )(table, plan, held, core, own, mate, same, other, after)


def table_notes(packed):
    owner = (packed >> LEN_BITS) + 1
    length = jnp.where(packed >= 0, packed & 0xFFFF, 0)
    parts = jnp.concatenate([owner >> 8, owner & 0xFF, length >> 8, length & 0xFF])
    rows = 3 * LANES - parts.shape[0]
    parts = jnp.pad(parts, (0, rows)).reshape(3, LANES)
    return jnp.pad(parts, ((NOTES - 3, 0), (0, 0)))


def read_slots(rows, count):
    notes = rows[::2, count * ROWS : count * ROWS + 3 * count + 1, 0].astype(jnp.float32).astype(jnp.int32)
    fields = notes[:, : 3 * count].reshape(-1, count, 3)
    station, length = fields[..., 0] - 1, fields[..., 1] * 256 + fields[..., 2]
    return station.reshape(-1), length.reshape(-1), notes[:, 3 * count]


def read_table(rows, slots, chips):
    parts = rows[:, -3:, :].astype(jnp.float32).astype(jnp.int32)
    parts = parts.reshape(rows.shape[0], -1)[:, : 4 * slots].reshape(chips, 2, 4, slots)
    return (parts[:, :, 0] * 256 + parts[:, :, 1] - 1).reshape(chips, 2 * slots)


def second_places(owner, column, base):
    chips, entries = owner.shape
    extra = MOST - base
    slots = entries // 2
    listed = owner >= 0
    dev = jnp.where(listed, owner // ST_DEV, -1)
    order = jnp.arange(entries, dtype=jnp.int32)
    earlier = order[None, :] < order[:, None]
    alike = (dev[:, :, None] == dev[:, None, :]) & earlier
    rank = jnp.sum(alike.astype(jnp.int32), axis=2)
    over = listed & (rank >= base)
    near = earlier & (order[None, :] // slots == order[:, None] // slots)
    index = jnp.sum((over[:, None, :] & near).astype(jnp.int32), axis=2)
    sent = over & (index < SPILL)
    guest = jnp.sum((alike & sent[:, None, :]).astype(jnp.int32), axis=2)
    host_dev = jnp.concatenate([dev[chips // 2 :], dev[: chips // 2]])
    host_held = jnp.sum((dev[:, :, None] == host_dev[:, None, :]).astype(jnp.int32), axis=2)
    slot = host_held + guest
    fits = sent & (slot < base)
    chip = jnp.arange(chips, dtype=jnp.int32)[:, None]
    host = (chip + chips // 2) % chips
    code = jnp.where(rank < base, chip * base + rank, chips * base + chip * extra + rank - base)
    code = jnp.where(fits, host * base + slot, code)
    local = column * ST_DEV + jnp.arange(ST_DEV, dtype=jnp.int32)
    chosen = owner[None] == local[:, None, None]
    return jnp.sum(jnp.where(chosen, code[None], 0), axis=(1, 2))


def whiten_kernel(
    part, parts, source, length, picks, got, more, first, twist, second, *refs
):
    token, held, spectra, sem, sems = refs[-5:]
    stops, rows = picks.shape
    white = refs[-6 - parts]
    payload = refs[-5 - parts : -5]
    token[0] = 0
    stations = held.shape[0]
    base = SLOTS[part]
    first_more = got.shape[0] // 2 * base
    batch = 8

    def fetch(rows, code, count, station):
        for seg in range(2):
            source_at = rows.at[2 * (code // count) + seg, unit(code % count)]
            pltpu.make_async_copy(source_at, held.at[station, unit(seg)], sems.at[station // batch]).start()

    @pl.loop(0, stations)
    def _(station):
        code = source[station]

        @pl.when(code < first_more)
        def _():
            fetch(got, code, base, station)

        @pl.when(code >= first_more)
        def _():
            fetch(more, code - first_more, MOST - base, station)

    row = lax.broadcasted_iota(jnp.int32, (2 * ROWS, LANES), 0)
    lane = lax.broadcasted_iota(jnp.int32, (2 * ROWS, LANES), 1)
    left = lax.broadcasted_iota(jnp.int32, (ROWS // 2, LANES), 1) < ROWS
    place = (2 * part + (row & 1)) * NT + (row >> 1) * LANES + lane

    def two_stations(station):
        sides = []
        for at in range(2):
            values = held[station + at].astype(jnp.float32)
            sides.append(jnp.where(place < length[station + at], values, 0.0).astype(jnp.bfloat16))
        values = jnp.concatenate(sides, 1)
        values = jnp.concatenate([values, values], 0)
        mixed = jnp.dot(first[...], values, preferred_element_type=jnp.float32)
        parts = []
        for at in range(2):
            for seg in range(2):
                real = mixed[2 * seg * ROWS : (2 * seg + 1) * ROWS, at * LANES : (at + 1) * LANES]
                imag = mixed[(2 * seg + 1) * ROWS : (2 * seg + 2) * ROWS, at * LANES : (at + 1) * LANES]
                turned_re = real * twist[0] + imag * twist[1]
                turned_im = imag * twist[0] - real * twist[1]
                parts.append(jnp.concatenate([turned_re, turned_im], 1))
        turned = jnp.concatenate(parts, 0)
        high = turned.astype(jnp.bfloat16)
        low = (turned - high.astype(jnp.float32)).astype(jnp.bfloat16)
        upper = jnp.dot(high, second[...], preferred_element_type=jnp.float32)
        lower = jnp.dot(low, second[:, :LANES], preferred_element_type=jnp.float32)
        spectrum = upper[:, :LANES] + (upper[:, LANES:] + lower)
        for at in range(2):
            for seg in range(2):
                begin = (2 * at + seg) * ROWS
                side = spectrum[begin : begin + ROWS]
                power = jnp.sum(side * side, axis=0, keepdims=True)
                power = (power + pltpu.roll(power, LANES // 2, 1)) * (1.0 / ROWS)
                scale = 1.0 / jnp.sqrt(power + 1e-06)
                side = side * scale
                upper, lower = side[: ROWS // 2], side[ROWS // 2 :]
                real = jnp.where(left, upper, pltpu.roll(lower, ROWS, 1))
                imag = jnp.where(left, pltpu.roll(upper, ROWS, 1), lower)
                spectra[station + at, seg, : ROWS // 2] = real.astype(jnp.bfloat16)
                spectra[station + at, seg, ROWS // 2 :] = imag.astype(jnp.bfloat16)

    @pl.loop(0, stations // batch)
    def _(at):
        these = held.at[pl.ds(at * batch, batch)]
        pltpu.make_async_copy(these, these, sems.at[at]).wait()
        for two in range(0, batch, 2):
            two_stations(batch * at + two)

    each = stops // parts
    for piece in range(parts):

        @pl.loop(0, each)
        def _(stop):
            for at in range(rows):
                row = spectra.at[picks[piece * each + stop, at]]
                pltpu.make_async_copy(row, payload[piece].at[stop, at], sem).start()

    whole = pltpu.make_async_copy(spectra, white, sems.at[0])
    whole.start()
    for piece in range(parts):
        pltpu.make_async_copy(payload[piece], payload[piece], sem).wait()
    whole.wait()


def whiten(part, parts, source, length, picks, got, more, tables, after):
    stops, rows = picks.shape
    piece = jax.ShapeDtypeStruct((stops // parts, rows, 2, ROWS, LANES), jnp.bfloat16)
    return pl.pallas_call(
        functools.partial(whiten_kernel, part, parts),
        out_shape=(jax.ShapeDtypeStruct((ST_DEV, 2, ROWS, LANES), jnp.bfloat16),)
        + (piece,) * parts
        + (jax.ShapeDtypeStruct((1,), jnp.int32),),
        in_specs=[SMEM, SMEM, SMEM, ANY, ANY, VMEM, VMEM, VMEM] + [ANY] * len(after),
        out_specs=(ANY,) * (1 + parts) + (SMEM,),
        scratch_shapes=[
            pltpu.VMEM((ST_DEV, 2 * ROWS, LANES), jnp.bfloat16),
            pltpu.VMEM((ST_DEV, 2, ROWS, LANES), jnp.bfloat16),
            pltpu.SemaphoreType.DMA,
            pltpu.SemaphoreType.DMA((ST_DEV // 8,)),
        ],
        cost_estimate=pl.CostEstimate(flops=2**20, bytes_accessed=2**18, transcendentals=0),
        name="whiten",
    )(source, length, picks, got, more, *tables, *after)


def cross_rows(near_pick, near, far, cross, fresh, ready):
    stops, rows = near_pick.shape
    side = rows // 2
    step = 16
    half = ROWS // 2

    @pl.loop(0, stops)
    def _(stop):
        ready(stop)
        for two in range(2):
            first = two * side
            own = [near_pick[stop, first + i] for i in range(side)]

            @pl.loop(0, half // step)
            def _(chunk):
                real = pl.ds(pl.multiple_of(chunk * step, step), step)
                imag = pl.ds(pl.multiple_of(half + chunk * step, step), step)

                def both(ref, row):
                    return [
                        (ref[row, s, real, :].astype(jnp.float32), ref[row, s, imag, :].astype(jnp.float32))
                        for s in range(2)
                    ]

                here = [both(near, own[i]) for i in range(side)]
                for j in range(side):
                    there = both(far.at[stop], first + j)
                    for i in range(side):
                        pair = ((stop * 2 + two) * side + i) * side + j
                        total_re = sum(n[0] * f[0] + n[1] * f[1] for n, f in zip(here[i], there))
                        total_im = sum(n[1] * f[0] - n[0] * f[1] for n, f in zip(here[i], there))
                        for total, add in ((total_re, 0), (total_im, half)):
                            at = pl.ds(pl.multiple_of(pair * ROWS + add + chunk * step, step), step)
                            if fresh:
                                cross[at, :] = total
                            else:
                                cross[at, :] += total


def lag_product(cross, tables, last, out, edge, exact):
    pairs = out.shape[0]
    group = 8
    depth = group * LANES
    half = LAGS // 2
    turns = ROWS // 2 // group

    def product(turn, even):
        base = turn * group
        slabs = [cross[pl.ds(base + k, pairs, stride=ROWS), :] for k in range(group)]
        high = [slab.astype(jnp.bfloat16) for slab in slabs]
        if even:
            total = edge[...]
            for k in range(group):
                total += (slabs[k] if exact else high[k].astype(jnp.float32)) * last[base + k]
            edge[...] = total
        rows = jnp.concatenate(high, 1)
        if exact:
            low = [(slab - part.astype(jnp.float32)).astype(jnp.bfloat16) for slab, part in zip(slabs, high)]
            rows = jnp.concatenate([rows, jnp.concatenate(low, 1)], 0)
        part = jnp.dot(
            rows,
            tables[pl.ds(pl.multiple_of(base * LANES, depth), depth), :],
            preferred_element_type=jnp.float32,
        )
        return part[:pairs] + part[pairs:] if exact else part

    @pl.loop(0, turns)
    def _(turn):
        out[:, :half] += product(turn, True)

    @pl.loop(turns, 2 * turns)
    def _(turn):
        out[:, half:] += product(turn, False)


def first_lag_kernel(stops, near_pick, white, home, *refs):
    far_in = refs[: stops - 1]
    table, last, out, edge, near, far, cross, tables, sem, sems, table_sem = refs[stops - 1 :]
    load = pltpu.make_async_copy(white, near, sem)
    load.start()
    pltpu.make_async_copy(home, far.at[0], sems.at[0]).start()
    for stop in range(1, stops):
        pltpu.make_async_copy(far_in[stop - 1], far.at[stop], sems.at[stop]).start()
    load_table = pltpu.make_async_copy(table, tables, table_sem)
    load_table.start()
    out[...] = jnp.zeros_like(out)
    edge[...] = jnp.zeros_like(edge)
    load.wait()

    def ready(stop):
        pltpu.make_async_copy(far.at[stop], far.at[stop], sems.at[stop]).wait()

    cross_rows(near_pick, near, far, cross, True, ready)
    load_table.wait()
    lag_product(cross, tables, last, out, edge, True)


def last_lag_kernel(
    near_pick, far_at, begun, begun_edge, white, far_in, table, last, mask,
    result, near, far, cross, out, edge, tables, sem, sems, table_sem,
):
    stops = near_pick.shape[0]
    pairs = out.shape[0]
    half = LAGS // 2
    load = pltpu.make_async_copy(white, near, sem.at[0])
    load.start()
    for stop in range(stops):
        pltpu.make_async_copy(far_in.at[far_at[stop]], far.at[stop], sems.at[stop]).start()
    load_table = pltpu.make_async_copy(table, tables, table_sem)
    load_table.start()
    before = [pltpu.make_async_copy(begun, out, sem.at[1]), pltpu.make_async_copy(begun_edge, edge, sem.at[2])]
    for copy in before:
        copy.start()
    load.wait()

    def ready(stop):
        pltpu.make_async_copy(far.at[stop], far.at[stop], sems.at[stop]).wait()

    cross_rows(near_pick, near, far, cross, True, ready)
    load_table.wait()
    for copy in before:
        copy.wait()
    lag_product(cross, tables, last, out, edge, False)
    first_lag = jnp.sum(edge[...], axis=1, keepdims=True)
    lane = lax.broadcasted_iota(jnp.int32, (pairs, LANES), 1)
    mirror = (LANES - lane) % LANES
    first = lane == 0
    listed = mask[...]
    count = half // LANES
    back, ahead = [], []
    for block in range(count):
        even = out[:, block * LANES : (block + 1) * LANES]
        odd = out[:, half + block * LANES : half + (block + 1) * LANES]
        if block == 0:
            first_lag = first_lag + odd
            odd = jnp.where(first, 0.0, odd)
        back.append(even - odd)
        ahead.append(even + odd)
    for block in range(count):
        turned = jnp.take_along_axis(back[count - 1 - block], mirror, axis=1)
        start = first_lag if block == 0 else back[count - block]
        lags = pl.ds(block * LANES, LANES)
        result[:, :, lags] = (jnp.where(first, start, turned) * listed).reshape(result.shape[:2] + (LANES,))
        lags = pl.ds(half + block * LANES, LANES)
        result[:, :, lags] = (ahead[block] * listed).reshape(result.shape[:2] + (LANES,))


def lag_scratch(white, stops, pairs, table):
    return [
        pltpu.VMEM(white.shape, jnp.bfloat16),
        pltpu.VMEM((stops, 8, 2, ROWS, LANES), jnp.bfloat16),
        pltpu.VMEM((pairs * ROWS, LANES), jnp.float32),
    ], [pltpu.VMEM(table.shape, jnp.bfloat16)]


def lagged_first(near_pick, white, home, far, table, last):
    stops, rows = near_pick.shape
    pairs = stops * rows * rows // 2
    scratch, table_scratch = lag_scratch(white, stops, pairs, table)
    return pl.pallas_call(
        functools.partial(first_lag_kernel, stops),
        out_shape=(
            jax.ShapeDtypeStruct((pairs, LAGS), jnp.float32),
            jax.ShapeDtypeStruct((pairs, LANES), jnp.float32),
        ),
        in_specs=[SMEM] + [ANY] * (stops + 2) + [VMEM],
        out_specs=(VMEM, VMEM),
        scratch_shapes=scratch
        + table_scratch
        + [pltpu.SemaphoreType.DMA, pltpu.SemaphoreType.DMA((stops,)), pltpu.SemaphoreType.DMA],
        compiler_params=pltpu.CompilerParams(vmem_limit_bytes=LAG_VMEM),
        cost_estimate=pl.CostEstimate(
            flops=4 * pairs * NF * LAGS, bytes_accessed=16 * 1024 * 1024, transcendentals=0
        ),
        name="lagged_first",
    )(near_pick, white, home, *far, table, last)


def lagged_last(near_pick, far_at, begun, edge, white, far, table, last, mask):
    stops, rows = near_pick.shape
    side = rows // 2
    pairs = mask.shape[0]
    scratch, table_scratch = lag_scratch(white, stops, pairs, table)
    return pl.pallas_call(
        last_lag_kernel,
        out_shape=jax.ShapeDtypeStruct((pairs // side, side, LAGS), jnp.float32),
        in_specs=[SMEM, SMEM] + [ANY] * 5 + [VMEM, VMEM],
        out_specs=VMEM,
        scratch_shapes=scratch
        + [pltpu.VMEM((pairs, LAGS), jnp.float32), pltpu.VMEM((pairs, LANES), jnp.float32)]
        + table_scratch
        + [pltpu.SemaphoreType.DMA((3,)), pltpu.SemaphoreType.DMA((stops,)), pltpu.SemaphoreType.DMA],
        compiler_params=pltpu.CompilerParams(vmem_limit_bytes=LAG_VMEM),
        cost_estimate=pl.CostEstimate(
            flops=2 * pairs * NF * LAGS, bytes_accessed=16 * 1024 * 1024, transcendentals=0
        ),
        name="lagged_last",
    )(near_pick, far_at, begun, edge, white, far, table, last, mask)


def empty(shape):
    return pl.pallas_call(
        lambda out: None,
        out_shape=jax.ShapeDtypeStruct(shape, jnp.bfloat16),
        out_specs=ANY,
        name="empty",
    )()


def on_device(records, lengths, owners, own_pick, visit_pick, pair_mask):
    wide_count = lax.axis_size("wide")
    stops = lax.axis_size("blk")
    column = lax.axis_index("wide")
    group = lax.axis_index("blk")
    core = column % 2
    slots = records.shape[1]
    steps = jnp.arange(stops, dtype=jnp.int32)
    core_at = core.reshape(1)

    def flip(bits):
        return [(i, i ^ bits) for i in range(wide_count)]

    def across(shard, bits):
        return lax.ppermute(shard, "wide", flip(bits))

    over = wide_count // 2
    packed = jnp.where(owners[0] >= 0, (owners[0] << LEN_BITS) + lengths[0], -1)
    counted = jnp.concatenate([packed, jnp.sum((packed >= 0).astype(jnp.int32), keepdims=True)])
    others = [across(counted, bits) for bits in (1, over, over + 1)]
    table = jnp.where(
        core == 0,
        jnp.stack([counted, others[0], others[1], others[2]]),
        jnp.stack([others[0], counted, others[2], others[1]]),
    )

    blocks = records[0].reshape(slots, SEG, ROWS, LANES)

    def halves(part):
        return blocks[:, 2 * part : 2 * part + 2].transpose(0, 2, 1, 3).reshape(slots, 2 * ROWS, LANES)

    def send(payload):
        return lax.all_to_all(payload, "wide", split_axis=0, concat_axis=0, tiled=True)

    own_a = halves(0)
    mate_a = across(own_a, 1)
    base_a, base_b = SLOTS
    plan_a, tiles, _ = plan_rows(base_a, base_b, wide_count, table, table_notes(packed))
    load_a, token = pack_first(base_a, table, plan_a, core_at, own_a, mate_a, tiles)
    got_a = send(load_a)
    own_b = jnp.where(token[0] >= 0, halves(1), 0.0)
    mate_b = across(own_b, 1)
    same_b, other_b, plan, held = spill(base_b, wide_count, table, core_at, own_b)
    same_b, other_b = across(same_b, over), across(other_b, over + 1)
    visits = jnp.where(token[0] >= 0, visit_pick[0, 0].reshape(1, stops, -1), 0)
    bit = 1
    while bit < stops:
        theirs = lax.ppermute(visits, "blk", [(i, i ^ bit) for i in range(stops)])
        upper = (group // bit) % 2 == 1
        visits = jnp.concatenate([jnp.where(upper, theirs, visits), jnp.where(upper, visits, theirs)])
        bit *= 2
    by_dest = visits[steps, (steps - group) % stops]
    by_stop = by_dest[(steps + group) % stops]
    load_b = pack_planned(base_b, table, plan, held, core_at, own_b, mate_b, same_b, other_b, by_stop)
    got_b = send(load_b)

    def late_rows(low, own, mate):
        return send(pack_rows(low, MOST - low, wide_count, table, core_at, own, mate))

    def late():
        first = late_rows(base_a, own_a, mate_a)
        second = late_rows(base_b, own_b, mate_b)
        return (first, second) + read_slots(first, MOST - base_a)[:2]

    def never():
        count = wide_count // 2 * (MOST - base_a)
        rows = [empty((wide_count, (MOST - base) * ROWS + NOTES, LANES)) for base in SLOTS]
        return rows[0], rows[1], jnp.full((count,), -1, jnp.int32), jnp.zeros((count,), jnp.int32)

    station, length, spilled = read_slots(got_a, base_a)
    more_a, more_b, more_station, more_length = lax.cond(jnp.max(spilled) > 0, late, never)
    station = jnp.concatenate([station, more_station])
    length = jnp.concatenate([length, more_length])
    chosen = station[None, :] == jnp.arange(ST_DEV, dtype=jnp.int32)[:, None]
    codes = jnp.arange(station.shape[0], dtype=jnp.int32)
    source_a = jnp.sum(jnp.where(chosen, codes[None], 0), axis=1)
    length = jnp.sum(jnp.where(chosen, length[None], 0), axis=1)

    tables = [jnp.asarray(table) for table in transform_tables()]
    near_pick = own_pick[0, 0].reshape(stops, -1)
    white_a, home, *payload_a, _ = whiten(0, stops, source_a, length, by_stop, got_a, more_a, tables, [])
    far_a = [
        lax.ppermute(payload_a[stop - 1][0], "blk", [(i, (i + stop) % stops) for i in range(stops)])
        for stop in range(1, stops)
    ]
    source_b = second_places(read_table(got_a, slots, wide_count // 2), column, base_b)
    white_b, payload_b, _ = whiten(1, 1, source_b, length, by_dest, got_b, more_b, tables, far_a)
    far_b = lax.all_to_all(payload_b, "blk", split_axis=0, concat_axis=0, tiled=True)

    far_at = (group - steps) % stops
    mask = pair_mask[0, 0].astype(jnp.float32).reshape(-1, 1)
    lags, last = (jnp.asarray(table) for table in lag_tables())
    begun, edge = lagged_first(near_pick, white_a, home[0], far_a, lags, last)
    result = lagged_last(near_pick, far_at, begun, edge, white_b, far_b, lags, last, mask)
    return result.reshape((1, 1) + pair_mask.shape[2:] + (LAGS,))


def solution(mesh):
    return jax.shard_map(
        on_device,
        mesh=mesh,
        in_specs=(
            P("blk", "wide", None, None),
            P("blk", "wide"),
            P("blk", "wide"),
            P("blk", "wide", None, None, None),
            P("blk", "wide", None, None, None),
            P("blk", "wide", None, None, None, None),
        ),
        out_specs=P("blk", "wide", None, None, None, None, None),
        check_vma=False,
    )
```

```python
import functools
import math

import jax
import jax.numpy as jnp
import numpy as np
from jax import lax
from jax.experimental import pallas as pl
from jax.experimental.pallas import tpu as pltpu
from jax.sharding import PartitionSpec as P

ST_DEV = 24
SEG = 4
NT = 8192
NF = 4096
LAGS = 1024
ROWS = 64
LANES = 128
MOST = 6
SLOTS = (4, 3)
SPILL = 12
LAG_VMEM = 60 * 1024 * 1024
LAST_VMEM = 60 * 1024 * 1024
LEN_BITS = 16
NOTES = 16
SMEM = pl.BlockSpec(memory_space=pltpu.SMEM)
VMEM = pl.BlockSpec(memory_space=pltpu.VMEM)
ANY = pl.BlockSpec(memory_space=pl.ANY)


def split_bf16(values):
    high = values.astype(jnp.bfloat16)
    low = (values - high.astype(np.float64)).astype(jnp.bfloat16)
    return high, low


def transform_tables():
    first = np.arange(ROWS)
    second = np.arange(LANES)
    half = np.arange(LANES // 2)
    angle = 2.0 * math.pi / ROWS * (first[:, None] * first[None, :] % ROWS)
    wave = np.concatenate([np.cos(angle), -np.sin(angle)], 0)
    wave = np.einsum("ab,kn->aknb", np.eye(2), wave).reshape(4 * ROWS, 2 * ROWS)
    first_table = np.concatenate(split_bf16(wave), 1)
    twist = 2.0 * math.pi / NT * (first[:, None] * second[None, :] % NT)
    twist_table = np.stack([np.cos(twist), np.sin(twist)]).astype(np.float32)
    angle = 2.0 * math.pi / LANES * (second[:, None] * half[None, :] % LANES)
    cos, sin = np.cos(angle), np.sin(angle)
    wave = np.concatenate([np.concatenate([cos, -sin], 1), np.concatenate([sin, cos], 1)], 0)
    second_table = np.concatenate(split_bf16(wave), 1)
    return first_table, twist_table, second_table


def lag_tables():
    row = np.arange(ROWS // 2, dtype=np.int64)
    lane = np.arange(LANES, dtype=np.int64)
    bins = (row[:, None] + ROWS // 2 * (lane // ROWS)) + ROWS * (lane % ROWS)
    bins = bins.reshape(-1)
    weight = np.where(bins == 0, 0.5, 1.0).astype(np.float32) / np.float32(math.sqrt(NF * SEG))

    def at(delay):
        phase = bins[:, None] * delay[None, :] % NT
        return phase.astype(np.float32) * np.float32(2.0 * math.pi / NT)

    ahead = at(np.arange(LAGS // 2, dtype=np.int64))
    edge = at(np.array([NT - LAGS // 2], dtype=np.int64))
    cos = weight[:, None] * np.cos(ahead)
    sin = -weight[:, None] * np.sin(ahead)
    sin[:, :1] = -weight[:, None] * np.sin(edge)
    last = (weight[:, None] * np.cos(edge)).reshape(ROWS // 2, 1, LANES)
    return (
        np.concatenate([cos, sin], 0).astype(jnp.bfloat16),
        last.astype(jnp.bfloat16).astype(np.float32),
    )


def owner_of(value):
    return ((value >> LEN_BITS) * 2731) >> 16


def unit(slot):
    return pl.ds(pl.multiple_of(slot * ROWS, ROWS), ROWS)


def write_notes(out, begin, notes, flag, base):
    count = notes.shape[1]
    row = lax.broadcasted_iota(jnp.int32, (NOTES, LANES), 0)

    @pl.loop(0, notes.shape[0])
    def _(dev):
        tile = jnp.where(row == 3 * count, flag, base)
        for slot in range(count):
            value = notes[dev, slot]
            tile = jnp.where(row == 3 * slot, (value >> LEN_BITS) + 1, tile)
            tile = jnp.where(row == 3 * slot + 1, (value & 0xFFFF) >> 8, tile)
            tile = jnp.where(row == 3 * slot + 2, value & 0xFF, tile)
        out[dev, begin : begin + NOTES, :] = tile.astype(jnp.float32).astype(jnp.bfloat16)


def valid_slots(table, row):
    return table[row, table.shape[1] - 1]


def rows_kernel(low, count, table, core_ref, own, mate, out, fill, notes, started, sem):
    core = core_ref[0]
    started[0] = 0

    @pl.loop(0, out.shape[0])
    def _(dev):
        fill[dev] = 0
        for slot in range(count):
            notes[dev, slot] = -1

    def place(half, source):
        @pl.loop(0, valid_slots(table, half))
        def _(at):
            value = table[half, at]
            dev = owner_of(value)
            rank = fill[dev]
            fill[dev] = rank + 1

            @pl.when((rank >= low) & (rank < low + count))
            def _():
                started[0] += 1
                notes[dev, rank - low] = value - ((dev * ST_DEV) << LEN_BITS)
                rows = source.at[at, unit(core)]
                pltpu.make_async_copy(rows, out.at[dev, unit(rank - low)], sem).start()

    for half in range(2):

        @pl.when(core == half)
        def _():
            place(half, own)

        @pl.when(core != half)
        def _():
            place(half, mate)

    write_notes(out, count * ROWS, notes, 0, jnp.zeros((NOTES, LANES), jnp.int32))

    @pl.loop(0, started[0])
    def _(_):
        pltpu.make_async_copy(own.at[0, unit(0)], out.at[0, unit(0)], sem).wait()


def pack_rows(low, count, wide_count, table, core, own, mate):
    return pl.pallas_call(
        functools.partial(rows_kernel, low, count),
        out_shape=jax.ShapeDtypeStruct((wide_count, count * ROWS + NOTES, LANES), jnp.bfloat16),
        in_specs=[SMEM, SMEM, ANY, ANY],
        out_specs=VMEM,
        scratch_shapes=[
            pltpu.SMEM((wide_count,), jnp.int32),
            pltpu.SMEM((wide_count, count), jnp.int32),
            pltpu.SMEM((1,), jnp.int32),
            pltpu.SemaphoreType.DMA,
        ],
        cost_estimate=pl.CostEstimate(flops=0, bytes_accessed=wide_count * count * NT * 4, transcendentals=0),
        name="pack_rows",
    )(table, core, own, mate)


def plan_kernel(count, base_next, table, base, plan, tiles, fill, notes, theirs, flag):
    flag[0] = 0

    @pl.loop(0, fill.shape[0])
    def _(dev):
        fill[dev] = 0
        theirs[dev] = 0
        for slot in range(count):
            notes[dev, slot] = -1

    for half in range(2):

        @pl.loop(0, valid_slots(table, half))
        def _(at):
            value = table[half, at]
            dev = owner_of(value)
            rank = fill[dev]
            fill[dev] = rank + 1
            fits = rank < count
            plan[half, at] = jnp.where(fits, dev * 4 + rank, -1)

            @pl.when(fits)
            def _():
                notes[dev, rank] = value - ((dev * ST_DEV) << LEN_BITS)

            @pl.when(jnp.logical_not(fits))
            def _():
                flag[0] = 1

    for half in range(2):

        def check(at, index):
            dev = owner_of(table[2 + half, at])
            rank = theirs[dev]
            theirs[dev] = rank + 1
            spilled = rank >= base_next

            @pl.when(spilled & ((index >= SPILL) | (fill[dev] + rank >= 2 * base_next)))
            def _():
                flag[0] = 1

            return index + spilled.astype(jnp.int32)

        lax.fori_loop(0, valid_slots(table, 2 + half), check, 0)

    write_notes(tiles, 0, notes, flag[0], base[...])


def plan_rows(count, base_next, wide_count, table, base):
    return pl.pallas_call(
        functools.partial(plan_kernel, count, base_next),
        out_shape=(
            jax.ShapeDtypeStruct((2, table.shape[1] - 1), jnp.int32),
            jax.ShapeDtypeStruct((wide_count, NOTES, LANES), jnp.bfloat16),
            jax.ShapeDtypeStruct((wide_count,), jnp.int32),
        ),
        in_specs=[SMEM, VMEM],
        out_specs=(SMEM, VMEM, SMEM),
        scratch_shapes=[
            pltpu.SMEM((wide_count, count), jnp.int32),
            pltpu.SMEM((wide_count,), jnp.int32),
            pltpu.SMEM((1,), jnp.int32),
        ],
        cost_estimate=pl.CostEstimate(flops=2**16, bytes_accessed=2**18, transcendentals=0),
        name="plan_rows",
    )(table, base)


def first_kernel(count, table, plan, core_ref, own, mate, tiles, out, token, started, sem):
    core = core_ref[0]
    started[0] = 0
    token[0] = 0

    def place(half, source):
        @pl.loop(0, valid_slots(table, half))
        def _(at):
            code = plan[half, at]

            @pl.when(code >= 0)
            def _():
                started[0] += 1
                rows = source.at[at, unit(core)]
                pltpu.make_async_copy(rows, out.at[code >> 2, unit(code & 3)], sem).start()

    for half in range(2):

        @pl.when(core == half)
        def _():
            place(half, own)

        @pl.when(core != half)
        def _():
            place(half, mate)

    @pl.loop(0, out.shape[0], unroll=4)
    def _(dev):
        out[dev, count * ROWS :, :] = tiles[dev]

    @pl.loop(0, started[0])
    def _(_):
        pltpu.make_async_copy(own.at[0, unit(0)], out.at[0, unit(0)], sem).wait()


def pack_first(count, table, plan, core, own, mate, tiles):
    wide_count = tiles.shape[0]
    return pl.pallas_call(
        functools.partial(first_kernel, count),
        out_shape=(
            jax.ShapeDtypeStruct((wide_count, count * ROWS + NOTES, LANES), jnp.bfloat16),
            jax.ShapeDtypeStruct((1,), jnp.int32),
        ),
        in_specs=[SMEM] * 3 + [ANY, ANY, VMEM],
        out_specs=(VMEM, SMEM),
        scratch_shapes=[pltpu.SMEM((1,), jnp.int32), pltpu.SemaphoreType.DMA],
        cost_estimate=pl.CostEstimate(flops=0, bytes_accessed=wide_count * count * NT * 4, transcendentals=0),
        name="pack_first",
    )(table, plan, core, own, mate, tiles)


def spill_kernel(base, table, core_ref, own, same, other, plan, fill, started, sem):
    core = core_ref[0]
    started[0] = 0

    @pl.loop(0, fill.shape[0])
    def _(dev):
        fill[dev] = 0

    for half in range(2):

        @pl.loop(0, valid_slots(table, half))
        def _(at):
            dev = owner_of(table[half, at])
            rank = fill[dev]
            fill[dev] = rank + 1
            plan[half, at] = jnp.where(rank < base, dev * 4 + rank, -1)

            @pl.when((rank >= base) & (core == half) & (started[0] < SPILL))
            def _():
                index = started[0]
                started[0] = index + 1
                pltpu.make_async_copy(own.at[at, unit(core)], same.at[index], sem).start()
                pltpu.make_async_copy(own.at[at, unit(1 - core)], other.at[index], sem).start()

    @pl.loop(0, 2 * started[0])
    def _(_):
        pltpu.make_async_copy(own.at[0, unit(0)], same.at[0], sem).wait()


def spill(base, wide_count, table, core, own):
    buffer = jax.ShapeDtypeStruct((SPILL, ROWS, LANES), jnp.bfloat16)
    return pl.pallas_call(
        functools.partial(spill_kernel, base),
        out_shape=(
            buffer,
            buffer,
            jax.ShapeDtypeStruct((2, table.shape[1] - 1), jnp.int32),
            jax.ShapeDtypeStruct((wide_count,), jnp.int32),
        ),
        in_specs=[SMEM, SMEM, ANY],
        out_specs=(VMEM, VMEM, SMEM, SMEM),
        scratch_shapes=[pltpu.SMEM((1,), jnp.int32), pltpu.SemaphoreType.DMA],
        cost_estimate=pl.CostEstimate(flops=0, bytes_accessed=2**20, transcendentals=0),
        name="spill",
    )(table, core, own)


def pack_kernel(base, table, plan, held, core_ref, own, mate, same, other, after, out, fill, theirs, started, taken, sem):
    core = core_ref[0]
    started[0] = 0

    @pl.loop(0, out.shape[0])
    def _(dev):
        fill[dev] = held[dev]
        theirs[dev] = 0

    def place(half, source, guests):
        @pl.loop(0, valid_slots(table, half))
        def _(at):
            code = plan[half, at]

            @pl.when(code >= 0)
            def _():
                started[0] += 1
                rows = source.at[at, unit(core)]
                pltpu.make_async_copy(rows, out.at[code >> 2, unit(code & 3)], sem).start()

        taken[0] = 0

        @pl.loop(0, valid_slots(table, 2 + half))
        def _(at):
            dev = owner_of(table[2 + half, at])
            rank = theirs[dev]
            theirs[dev] = rank + 1

            @pl.when(rank >= base)
            def _():
                index = taken[0]
                slot = fill[dev]
                taken[0] = index + 1

                @pl.when((index < SPILL) & (slot < base))
                def _():
                    fill[dev] = slot + 1
                    started[0] += 1
                    pltpu.make_async_copy(guests.at[index], out.at[dev, unit(slot)], sem).start()

    for half in range(2):

        @pl.when(core == half)
        def _():
            place(half, own, same)

        @pl.when(core != half)
        def _():
            place(half, mate, other)

    @pl.loop(0, started[0])
    def _(_):
        pltpu.make_async_copy(own.at[0, unit(0)], out.at[0, unit(0)], sem).wait()


def pack_planned(base, table, plan, held, core, own, mate, same, other, after):
    wide_count = held.shape[0]
    return pl.pallas_call(
        functools.partial(pack_kernel, base),
        out_shape=jax.ShapeDtypeStruct((wide_count, base * ROWS, LANES), jnp.bfloat16),
        in_specs=[SMEM] * 4 + [ANY] * 5,
        out_specs=VMEM,
        scratch_shapes=[
            pltpu.SMEM((wide_count,), jnp.int32),
            pltpu.SMEM((wide_count,), jnp.int32),
            pltpu.SMEM((1,), jnp.int32),
            pltpu.SMEM((1,), jnp.int32),
            pltpu.SemaphoreType.DMA,
        ],
        cost_estimate=pl.CostEstimate(flops=0, bytes_accessed=wide_count * base * NT * 4, transcendentals=0),
        name="pack_planned",
    )(table, plan, held, core, own, mate, same, other, after)


def table_notes(packed):
    owner = (packed >> LEN_BITS) + 1
    length = jnp.where(packed >= 0, packed & 0xFFFF, 0)
    parts = jnp.concatenate([owner >> 8, owner & 0xFF, length >> 8, length & 0xFF])
    rows = 3 * LANES - parts.shape[0]
    parts = jnp.pad(parts, (0, rows)).reshape(3, LANES)
    return jnp.pad(parts, ((NOTES - 3, 0), (0, 0)))


def read_slots(rows, count):
    notes = rows[::2, count * ROWS : count * ROWS + 3 * count + 1, 0].astype(jnp.float32).astype(jnp.int32)
    fields = notes[:, : 3 * count].reshape(-1, count, 3)
    station, length = fields[..., 0] - 1, fields[..., 1] * 256 + fields[..., 2]
    return station.reshape(-1), length.reshape(-1), notes[:, 3 * count]


def read_table(rows, slots, chips):
    parts = rows[:, -3:, :].astype(jnp.float32).astype(jnp.int32)
    parts = parts.reshape(rows.shape[0], -1)[:, : 4 * slots].reshape(chips, 2, 4, slots)
    return (parts[:, :, 0] * 256 + parts[:, :, 1] - 1).reshape(chips, 2 * slots)


def second_places(owner, column, base):
    chips, entries = owner.shape
    extra = MOST - base
    slots = entries // 2
    listed = owner >= 0
    dev = jnp.where(listed, owner // ST_DEV, -1)
    order = jnp.arange(entries, dtype=jnp.int32)
    earlier = order[None, :] < order[:, None]
    alike = (dev[:, :, None] == dev[:, None, :]) & earlier
    rank = jnp.sum(alike.astype(jnp.int32), axis=2)
    over = listed & (rank >= base)
    near = earlier & (order[None, :] // slots == order[:, None] // slots)
    index = jnp.sum((over[:, None, :] & near).astype(jnp.int32), axis=2)
    sent = over & (index < SPILL)
    guest = jnp.sum((alike & sent[:, None, :]).astype(jnp.int32), axis=2)
    host_dev = jnp.concatenate([dev[chips // 2 :], dev[: chips // 2]])
    host_held = jnp.sum((dev[:, :, None] == host_dev[:, None, :]).astype(jnp.int32), axis=2)
    slot = host_held + guest
    fits = sent & (slot < base)
    chip = jnp.arange(chips, dtype=jnp.int32)[:, None]
    host = (chip + chips // 2) % chips
    code = jnp.where(rank < base, chip * base + rank, chips * base + chip * extra + rank - base)
    code = jnp.where(fits, host * base + slot, code)
    local = column * ST_DEV + jnp.arange(ST_DEV, dtype=jnp.int32)
    chosen = owner[None] == local[:, None, None]
    return jnp.sum(jnp.where(chosen, code[None], 0), axis=(1, 2))


def whiten_kernel(
    part, parts, source, length, picks, got, more, first, twist, second, *refs
):
    token, held, spectra, sem, sems = refs[-5:]
    stops, rows = picks.shape
    white = refs[-6 - parts]
    payload = refs[-5 - parts : -5]
    token[0] = 0
    stations = held.shape[0]
    base = SLOTS[part]
    first_more = got.shape[0] // 2 * base
    batch = 8

    def fetch(rows, code, count, station):
        for seg in range(2):
            source_at = rows.at[2 * (code // count) + seg, unit(code % count)]
            pltpu.make_async_copy(source_at, held.at[station, unit(seg)], sems.at[station // batch]).start()

    @pl.loop(0, stations)
    def _(station):
        code = source[station]

        @pl.when(code < first_more)
        def _():
            fetch(got, code, base, station)

        @pl.when(code >= first_more)
        def _():
            fetch(more, code - first_more, MOST - base, station)

    row = lax.broadcasted_iota(jnp.int32, (2 * ROWS, LANES), 0)
    lane = lax.broadcasted_iota(jnp.int32, (2 * ROWS, LANES), 1)
    left = lax.broadcasted_iota(jnp.int32, (ROWS // 2, LANES), 1) < ROWS
    place = (2 * part + (row & 1)) * NT + (row >> 1) * LANES + lane

    def two_stations(station):
        sides = []
        for at in range(2):
            values = held[station + at].astype(jnp.float32)
            sides.append(jnp.where(place < length[station + at], values, 0.0).astype(jnp.bfloat16))
        values = jnp.concatenate(sides, 1)
        values = jnp.concatenate([values, values], 0)
        mixed = jnp.dot(first[...], values, preferred_element_type=jnp.float32)
        parts = []
        for at in range(2):
            for seg in range(2):
                real = mixed[2 * seg * ROWS : (2 * seg + 1) * ROWS, at * LANES : (at + 1) * LANES]
                imag = mixed[(2 * seg + 1) * ROWS : (2 * seg + 2) * ROWS, at * LANES : (at + 1) * LANES]
                turned_re = real * twist[0] + imag * twist[1]
                turned_im = imag * twist[0] - real * twist[1]
                parts.append(jnp.concatenate([turned_re, turned_im], 1))
        turned = jnp.concatenate(parts, 0)
        high = turned.astype(jnp.bfloat16)
        low = (turned - high.astype(jnp.float32)).astype(jnp.bfloat16)
        upper = jnp.dot(high, second[...], preferred_element_type=jnp.float32)
        lower = jnp.dot(low, second[:, :LANES], preferred_element_type=jnp.float32)
        spectrum = upper[:, :LANES] + (upper[:, LANES:] + lower)
        for at in range(2):
            for seg in range(2):
                begin = (2 * at + seg) * ROWS
                side = spectrum[begin : begin + ROWS]
                power = jnp.sum(side * side, axis=0, keepdims=True)
                power = (power + pltpu.roll(power, LANES // 2, 1)) * (1.0 / ROWS)
                scale = 1.0 / jnp.sqrt(power + 1e-06)
                side = side * scale
                upper, lower = side[: ROWS // 2], side[ROWS // 2 :]
                real = jnp.where(left, upper, pltpu.roll(lower, ROWS, 1))
                imag = jnp.where(left, pltpu.roll(upper, ROWS, 1), lower)
                spectra[station + at, seg, : ROWS // 2] = real.astype(jnp.bfloat16)
                spectra[station + at, seg, ROWS // 2 :] = imag.astype(jnp.bfloat16)

    @pl.loop(0, stations // batch)
    def _(at):
        these = held.at[pl.ds(at * batch, batch)]
        pltpu.make_async_copy(these, these, sems.at[at]).wait()
        for two in range(0, batch, 2):
            two_stations(batch * at + two)

    each = stops // parts
    for piece in range(parts):

        @pl.loop(0, each)
        def _(stop):
            for at in range(rows):
                row = spectra.at[picks[piece * each + stop, at]]
                pltpu.make_async_copy(row, payload[piece].at[stop, at], sem).start()

    whole = pltpu.make_async_copy(spectra, white, sems.at[0])
    whole.start()
    for piece in range(parts):
        pltpu.make_async_copy(payload[piece], payload[piece], sem).wait()
    whole.wait()


def whiten(part, parts, source, length, picks, got, more, tables, after):
    stops, rows = picks.shape
    piece = jax.ShapeDtypeStruct((stops // parts, rows, 2, ROWS, LANES), jnp.bfloat16)
    return pl.pallas_call(
        functools.partial(whiten_kernel, part, parts),
        out_shape=(jax.ShapeDtypeStruct((ST_DEV, 2, ROWS, LANES), jnp.bfloat16),)
        + (piece,) * parts
        + (jax.ShapeDtypeStruct((1,), jnp.int32),),
        in_specs=[SMEM, SMEM, SMEM, ANY, ANY, VMEM, VMEM, VMEM] + [ANY] * len(after),
        out_specs=(ANY,) * (1 + parts) + (SMEM,),
        scratch_shapes=[
            pltpu.VMEM((ST_DEV, 2 * ROWS, LANES), jnp.bfloat16),
            pltpu.VMEM((ST_DEV, 2, ROWS, LANES), jnp.bfloat16),
            pltpu.SemaphoreType.DMA,
            pltpu.SemaphoreType.DMA((ST_DEV // 8,)),
        ],
        cost_estimate=pl.CostEstimate(flops=2**20, bytes_accessed=2**18, transcendentals=0),
        name="whiten",
    )(source, length, picks, got, more, *tables, *after)


def cross_rows(near_pick, near, far, cross, fresh, ready):
    stops, rows = near_pick.shape
    side = rows // 2
    step = 16
    half = ROWS // 2

    @pl.loop(0, stops)
    def _(stop):
        ready(stop)
        for two in range(2):
            first = two * side
            own = [near_pick[stop, first + i] for i in range(side)]

            @pl.loop(0, half // step)
            def _(chunk):
                real = pl.ds(pl.multiple_of(chunk * step, step), step)
                imag = pl.ds(pl.multiple_of(half + chunk * step, step), step)

                def both(ref, row):
                    return [
                        (ref[row, s, real, :].astype(jnp.float32), ref[row, s, imag, :].astype(jnp.float32))
                        for s in range(2)
                    ]

                here = [both(near, own[i]) for i in range(side)]
                for j in range(side):
                    there = both(far.at[stop], first + j)
                    for i in range(side):
                        pair = ((stop * 2 + two) * side + i) * side + j
                        total_re = sum(n[0] * f[0] + n[1] * f[1] for n, f in zip(here[i], there))
                        total_im = sum(n[1] * f[0] - n[0] * f[1] for n, f in zip(here[i], there))
                        for total, add in ((total_re, 0), (total_im, half)):
                            at = pl.ds(pl.multiple_of(pair * ROWS + add + chunk * step, step), step)
                            if fresh:
                                cross[at, :] = total
                            else:
                                cross[at, :] += total


def lag_product(cross, tables, last, out, edge, exact):
    pairs = out.shape[0]
    group = 32
    depth = group * LANES
    half = LAGS // 2
    turns = ROWS // 2 // group

    def product(turn, even):
        base = turn * group
        slabs = [cross[pl.ds(base + k, pairs, stride=ROWS), :] for k in range(group)]
        high = [slab.astype(jnp.bfloat16) for slab in slabs]
        if even:
            total = edge[...]
            for k in range(group):
                total += (slabs[k] if exact else high[k].astype(jnp.float32)) * last[base + k]
            edge[...] = total
        rows = jnp.concatenate(high, 1)
        if exact:
            low = [(slab - part.astype(jnp.float32)).astype(jnp.bfloat16) for slab, part in zip(slabs, high)]
            rows = jnp.concatenate([rows, jnp.concatenate(low, 1)], 0)
        part = jnp.dot(
            rows,
            tables[pl.ds(pl.multiple_of(base * LANES, depth), depth), :],
            preferred_element_type=jnp.float32,
        )
        return part[:pairs] + part[pairs:] if exact else part

    @pl.loop(0, turns)
    def _(turn):
        out[:, :half] += product(turn, True)

    @pl.loop(turns, 2 * turns)
    def _(turn):
        out[:, half:] += product(turn, False)


def first_lag_kernel(stops, near_pick, white, home, *refs):
    far_in = refs[: stops - 1]
    table, last, out, edge, near, far, cross, tables, sem, sems, table_sem = refs[stops - 1 :]
    load = pltpu.make_async_copy(white, near, sem)
    load.start()
    pltpu.make_async_copy(home, far.at[0], sems.at[0]).start()
    for stop in range(1, stops):
        pltpu.make_async_copy(far_in[stop - 1], far.at[stop], sems.at[stop]).start()
    load_table = pltpu.make_async_copy(table, tables, table_sem)
    load_table.start()
    out[...] = jnp.zeros_like(out)
    edge[...] = jnp.zeros_like(edge)
    load.wait()

    def ready(stop):
        pltpu.make_async_copy(far.at[stop], far.at[stop], sems.at[stop]).wait()

    cross_rows(near_pick, near, far, cross, True, ready)
    load_table.wait()
    lag_product(cross, tables, last, out, edge, True)


def last_lag_kernel(
    near_pick, far_at, begun, begun_edge, white, far_in, table, last, mask,
    result, near, far, cross, out, edge, tables, sem, sems, table_sem,
):
    stops = near_pick.shape[0]
    pairs = out.shape[0]
    half = LAGS // 2
    load = pltpu.make_async_copy(white, near, sem.at[0])
    load.start()
    for stop in range(stops):
        pltpu.make_async_copy(far_in.at[far_at[stop]], far.at[stop], sems.at[stop]).start()
    load_table = pltpu.make_async_copy(table, tables, table_sem)
    load_table.start()
    before = [pltpu.make_async_copy(begun, out, sem.at[1]), pltpu.make_async_copy(begun_edge, edge, sem.at[2])]
    for copy in before:
        copy.start()
    load.wait()

    def ready(stop):
        pltpu.make_async_copy(far.at[stop], far.at[stop], sems.at[stop]).wait()

    cross_rows(near_pick, near, far, cross, True, ready)
    load_table.wait()
    for copy in before:
        copy.wait()
    lag_product(cross, tables, last, out, edge, False)
    first_lag = jnp.sum(edge[...], axis=1, keepdims=True)
    lane = lax.broadcasted_iota(jnp.int32, (pairs, LANES), 1)
    mirror = (LANES - lane) % LANES
    first = lane == 0
    listed = mask[...]
    count = half // LANES
    back, ahead = [], []
    for block in range(count):
        even = out[:, block * LANES : (block + 1) * LANES]
        odd = out[:, half + block * LANES : half + (block + 1) * LANES]
        if block == 0:
            first_lag = first_lag + odd
            odd = jnp.where(first, 0.0, odd)
        back.append(even - odd)
        ahead.append(even + odd)
    for block in range(count):
        turned = jnp.take_along_axis(back[count - 1 - block], mirror, axis=1)
        start = first_lag if block == 0 else back[count - block]
        lags = pl.ds(block * LANES, LANES)
        result[:, :, lags] = (jnp.where(first, start, turned) * listed).reshape(result.shape[:2] + (LANES,))
        lags = pl.ds(half + block * LANES, LANES)
        result[:, :, lags] = (ahead[block] * listed).reshape(result.shape[:2] + (LANES,))


def lag_scratch(white, stops, pairs, table):
    return [
        pltpu.VMEM(white.shape, jnp.bfloat16),
        pltpu.VMEM((stops, 8, 2, ROWS, LANES), jnp.bfloat16),
        pltpu.VMEM((pairs * ROWS, LANES), jnp.float32),
    ], [pltpu.VMEM(table.shape, jnp.bfloat16)]


def lagged_first(near_pick, white, home, far, table, last):
    stops, rows = near_pick.shape
    pairs = stops * rows * rows // 2
    scratch, table_scratch = lag_scratch(white, stops, pairs, table)
    return pl.pallas_call(
        functools.partial(first_lag_kernel, stops),
        out_shape=(
            jax.ShapeDtypeStruct((pairs, LAGS), jnp.float32),
            jax.ShapeDtypeStruct((pairs, LANES), jnp.float32),
        ),
        in_specs=[SMEM] + [ANY] * (stops + 2) + [VMEM],
        out_specs=(VMEM, VMEM),
        scratch_shapes=scratch
        + table_scratch
        + [pltpu.SemaphoreType.DMA, pltpu.SemaphoreType.DMA((stops,)), pltpu.SemaphoreType.DMA],
        compiler_params=pltpu.CompilerParams(vmem_limit_bytes=LAG_VMEM),
        cost_estimate=pl.CostEstimate(
            flops=4 * pairs * NF * LAGS, bytes_accessed=16 * 1024 * 1024, transcendentals=0
        ),
        name="lagged_first",
    )(near_pick, white, home, *far, table, last)


def lagged_last(near_pick, far_at, begun, edge, white, far, table, last, mask):
    stops, rows = near_pick.shape
    side = rows // 2
    pairs = mask.shape[0]
    scratch, table_scratch = lag_scratch(white, stops, pairs, table)
    return pl.pallas_call(
        last_lag_kernel,
        out_shape=jax.ShapeDtypeStruct((pairs // side, side, LAGS), jnp.float32),
        in_specs=[SMEM, SMEM] + [ANY] * 5 + [VMEM, VMEM],
        out_specs=VMEM,
        scratch_shapes=scratch
        + [pltpu.VMEM((pairs, LAGS), jnp.float32), pltpu.VMEM((pairs, LANES), jnp.float32)]
        + table_scratch
        + [pltpu.SemaphoreType.DMA((3,)), pltpu.SemaphoreType.DMA((stops,)), pltpu.SemaphoreType.DMA],
        compiler_params=pltpu.CompilerParams(vmem_limit_bytes=LAST_VMEM),
        cost_estimate=pl.CostEstimate(
            flops=2 * pairs * NF * LAGS, bytes_accessed=16 * 1024 * 1024, transcendentals=0
        ),
        name="lagged_last",
    )(near_pick, far_at, begun, edge, white, far, table, last, mask)


def empty(shape):
    return pl.pallas_call(
        lambda out: None,
        out_shape=jax.ShapeDtypeStruct(shape, jnp.bfloat16),
        out_specs=ANY,
        name="empty",
    )()


def on_device(records, lengths, owners, own_pick, visit_pick, pair_mask):
    wide_count = lax.axis_size("wide")
    stops = lax.axis_size("blk")
    column = lax.axis_index("wide")
    group = lax.axis_index("blk")
    core = column % 2
    slots = records.shape[1]
    steps = jnp.arange(stops, dtype=jnp.int32)
    core_at = core.reshape(1)

    def flip(bits):
        return [(i, i ^ bits) for i in range(wide_count)]

    def across(shard, bits):
        return lax.ppermute(shard, "wide", flip(bits))

    over = wide_count // 2
    packed = jnp.where(owners[0] >= 0, (owners[0] << LEN_BITS) + lengths[0], -1)
    counted = jnp.concatenate([packed, jnp.sum((packed >= 0).astype(jnp.int32), keepdims=True)])
    others = [across(counted, bits) for bits in (1, over, over + 1)]
    table = jnp.where(
        core == 0,
        jnp.stack([counted, others[0], others[1], others[2]]),
        jnp.stack([others[0], counted, others[2], others[1]]),
    )

    blocks = records[0].reshape(slots, SEG, ROWS, LANES)

    def halves(part, never_below):
        start = 2 * part + jnp.minimum(never_below, 0)
        half = lax.dynamic_slice_in_dim(blocks, start, 2, 1)
        return half.transpose(0, 2, 1, 3).reshape(slots, 2 * ROWS, LANES)

    def send(payload):
        return lax.all_to_all(payload, "wide", split_axis=0, concat_axis=0, tiled=True)

    own_a = halves(0, counted[-1])
    mate_a = across(own_a, 1)
    base_a, base_b = SLOTS
    plan_a, tiles, _ = plan_rows(base_a, base_b, wide_count, table, table_notes(packed))
    load_a, token = pack_first(base_a, table, plan_a, core_at, own_a, mate_a, tiles)
    got_a = send(load_a)
    own_b = halves(1, token[0])
    mate_b = across(own_b, 1)
    same_b, other_b, plan, held = spill(base_b, wide_count, table, core_at, own_b)
    same_b, other_b = across(same_b, over), across(other_b, over + 1)
    visits = jnp.where(token[0] >= 0, visit_pick[0, 0].reshape(1, stops, -1), 0)
    bit = 1
    while bit < stops:
        theirs = lax.ppermute(visits, "blk", [(i, i ^ bit) for i in range(stops)])
        upper = (group // bit) % 2 == 1
        visits = jnp.concatenate([jnp.where(upper, theirs, visits), jnp.where(upper, visits, theirs)])
        bit *= 2
    by_dest = visits[steps, (steps - group) % stops]
    by_stop = by_dest[(steps + group) % stops]
    load_b = pack_planned(base_b, table, plan, held, core_at, own_b, mate_b, same_b, other_b, by_stop)
    got_b = send(load_b)

    def late_rows(low, own, mate):
        return send(pack_rows(low, MOST - low, wide_count, table, core_at, own, mate))

    def late():
        first = late_rows(base_a, own_a, mate_a)
        second = late_rows(base_b, own_b, mate_b)
        return (first, second) + read_slots(first, MOST - base_a)[:2]

    def never():
        count = wide_count // 2 * (MOST - base_a)
        rows = [empty((wide_count, (MOST - base) * ROWS + NOTES, LANES)) for base in SLOTS]
        return rows[0], rows[1], jnp.full((count,), -1, jnp.int32), jnp.zeros((count,), jnp.int32)

    station, length, spilled = read_slots(got_a, base_a)
    more_a, more_b, more_station, more_length = lax.cond(jnp.max(spilled) > 0, late, never)
    station = jnp.concatenate([station, more_station])
    length = jnp.concatenate([length, more_length])
    chosen = station[None, :] == jnp.arange(ST_DEV, dtype=jnp.int32)[:, None]
    codes = jnp.arange(station.shape[0], dtype=jnp.int32)
    source_a = jnp.sum(jnp.where(chosen, codes[None], 0), axis=1)
    length = jnp.sum(jnp.where(chosen, length[None], 0), axis=1)

    tables = [jnp.asarray(table) for table in transform_tables()]
    near_pick = own_pick[0, 0].reshape(stops, -1)
    white_a, home, *payload_a, _ = whiten(0, stops, source_a, length, by_stop, got_a, more_a, tables, [])
    far_a = [
        lax.ppermute(payload_a[stop - 1][0], "blk", [(i, (i + stop) % stops) for i in range(stops)])
        for stop in range(1, stops)
    ]
    source_b = second_places(read_table(got_a, slots, wide_count // 2), column, base_b)
    white_b, payload_b, _ = whiten(1, 1, source_b, length, by_dest, got_b, more_b, tables, far_a)
    far_b = lax.all_to_all(payload_b, "blk", split_axis=0, concat_axis=0, tiled=True)

    far_at = (group - steps) % stops
    mask = pair_mask[0, 0].astype(jnp.float32).reshape(-1, 1)
    lags, last = (jnp.asarray(table) for table in lag_tables())
    begun, edge = lagged_first(near_pick, white_a, home[0], far_a, lags, last)
    result = lagged_last(near_pick, far_at, begun, edge, white_b, far_b, lags, last, mask)
    return result.reshape((1, 1) + pair_mask.shape[2:] + (LAGS,))


def solution(mesh):
    return jax.shard_map(
        on_device,
        mesh=mesh,
        in_specs=(
            P("blk", "wide", None, None),
            P("blk", "wide"),
            P("blk", "wide"),
            P("blk", "wide", None, None, None),
            P("blk", "wide", None, None, None),
            P("blk", "wide", None, None, None, None),
        ),
        out_specs=P("blk", "wide", None, None, None, None, None),
        check_vma=False,
    )
```

```python
import functools
import math

import jax
import jax.numpy as jnp
import numpy as np
from jax import lax
from jax.experimental import pallas as pl
from jax.experimental.pallas import tpu as pltpu
from jax.sharding import PartitionSpec as P

ST_DEV = 24
SEG = 4
NT = 8192
NF = 4096
LAGS = 1024
ROWS = 64
LANES = 128
MOST = 6
SLOTS = (4, 3)
SPILL = 12
LAG_VMEM = 60 * 1024 * 1024
LAST_VMEM = 60 * 1024 * 1024
LEN_BITS = 16
NOTES = 16
SMEM = pl.BlockSpec(memory_space=pltpu.SMEM)
VMEM = pl.BlockSpec(memory_space=pltpu.VMEM)
ANY = pl.BlockSpec(memory_space=pl.ANY)


def split_bf16(values):
    high = values.astype(jnp.bfloat16)
    low = (values - high.astype(np.float64)).astype(jnp.bfloat16)
    return high, low


def transform_tables():
    first = np.arange(ROWS)
    second = np.arange(LANES)
    half = np.arange(LANES // 2)
    angle = 2.0 * math.pi / ROWS * (first[:, None] * first[None, :] % ROWS)
    wave = np.concatenate([np.cos(angle), -np.sin(angle)], 0)
    wave = np.einsum("ab,kn->aknb", np.eye(2), wave).reshape(4 * ROWS, 2 * ROWS)
    first_table = np.concatenate(split_bf16(wave), 1)
    twist = 2.0 * math.pi / NT * (first[:, None] * second[None, :] % NT)
    twist_table = np.stack([np.cos(twist), np.sin(twist)]).astype(np.float32)
    angle = 2.0 * math.pi / LANES * (second[:, None] * half[None, :] % LANES)
    cos, sin = np.cos(angle), np.sin(angle)
    wave = np.concatenate([np.concatenate([cos, -sin], 1), np.concatenate([sin, cos], 1)], 0)
    second_table = np.concatenate(split_bf16(wave), 1)
    return first_table, twist_table, second_table


def lag_tables():
    row = np.arange(ROWS // 2, dtype=np.int64)
    lane = np.arange(LANES, dtype=np.int64)
    bins = (row[:, None] + ROWS // 2 * (lane // ROWS)) + ROWS * (lane % ROWS)
    bins = bins.reshape(-1)
    weight = np.where(bins == 0, 0.5, 1.0).astype(np.float32) / np.float32(math.sqrt(NF * SEG))

    def at(delay):
        phase = bins[:, None] * delay[None, :] % NT
        return phase.astype(np.float32) * np.float32(2.0 * math.pi / NT)

    ahead = at(np.arange(LAGS // 2, dtype=np.int64))
    edge = at(np.array([NT - LAGS // 2], dtype=np.int64))
    cos = weight[:, None] * np.cos(ahead)
    sin = -weight[:, None] * np.sin(ahead)
    sin[:, :1] = -weight[:, None] * np.sin(edge)
    last = (weight[:, None] * np.cos(edge)).reshape(ROWS // 2, 1, LANES)
    return (
        np.concatenate([cos, sin], 0).astype(jnp.bfloat16),
        last.astype(jnp.bfloat16).astype(np.float32),
    )


def owner_of(value):
    return ((value >> LEN_BITS) * 2731) >> 16


def unit(slot):
    return pl.ds(pl.multiple_of(slot * ROWS, ROWS), ROWS)


def write_notes(out, begin, notes, flag, base):
    count = notes.shape[1]
    row = lax.broadcasted_iota(jnp.int32, (NOTES, LANES), 0)

    @pl.loop(0, notes.shape[0])
    def _(dev):
        tile = jnp.where(row == 3 * count, flag, base)
        for slot in range(count):
            value = notes[dev, slot]
            tile = jnp.where(row == 3 * slot, (value >> LEN_BITS) + 1, tile)
            tile = jnp.where(row == 3 * slot + 1, (value & 0xFFFF) >> 8, tile)
            tile = jnp.where(row == 3 * slot + 2, value & 0xFF, tile)
        out[dev, begin : begin + NOTES, :] = tile.astype(jnp.float32).astype(jnp.bfloat16)


def valid_slots(table, row):
    return table[row, table.shape[1] - 1]


def rows_kernel(low, count, table, core_ref, own, mate, out, fill, notes, started, sem):
    core = core_ref[0]
    started[0] = 0

    @pl.loop(0, out.shape[0])
    def _(dev):
        fill[dev] = 0
        for slot in range(count):
            notes[dev, slot] = -1

    def place(half, source):
        @pl.loop(0, valid_slots(table, half))
        def _(at):
            value = table[half, at]
            dev = owner_of(value)
            rank = fill[dev]
            fill[dev] = rank + 1

            @pl.when((rank >= low) & (rank < low + count))
            def _():
                started[0] += 1
                notes[dev, rank - low] = value - ((dev * ST_DEV) << LEN_BITS)
                rows = source.at[at, unit(core)]
                pltpu.make_async_copy(rows, out.at[dev, unit(rank - low)], sem).start()

    for half in range(2):

        @pl.when(core == half)
        def _():
            place(half, own)

        @pl.when(core != half)
        def _():
            place(half, mate)

    write_notes(out, count * ROWS, notes, 0, jnp.zeros((NOTES, LANES), jnp.int32))

    @pl.loop(0, started[0])
    def _(_):
        pltpu.make_async_copy(own.at[0, unit(0)], out.at[0, unit(0)], sem).wait()


def pack_rows(low, count, wide_count, table, core, own, mate):
    return pl.pallas_call(
        functools.partial(rows_kernel, low, count),
        out_shape=jax.ShapeDtypeStruct((wide_count, count * ROWS + NOTES, LANES), jnp.bfloat16),
        in_specs=[SMEM, SMEM, ANY, ANY],
        out_specs=VMEM,
        scratch_shapes=[
            pltpu.SMEM((wide_count,), jnp.int32),
            pltpu.SMEM((wide_count, count), jnp.int32),
            pltpu.SMEM((1,), jnp.int32),
            pltpu.SemaphoreType.DMA,
        ],
        cost_estimate=pl.CostEstimate(flops=0, bytes_accessed=wide_count * count * NT * 4, transcendentals=0),
        name="pack_rows",
    )(table, core, own, mate)


def plan_kernel(count, base_next, table, base, plan, tiles, fill, notes, theirs, flag):
    flag[0] = 0

    @pl.loop(0, fill.shape[0])
    def _(dev):
        fill[dev] = 0
        theirs[dev] = 0
        for slot in range(count):
            notes[dev, slot] = -1

    for half in range(2):

        @pl.loop(0, valid_slots(table, half))
        def _(at):
            value = table[half, at]
            dev = owner_of(value)
            rank = fill[dev]
            fill[dev] = rank + 1
            fits = rank < count
            plan[half, at] = jnp.where(fits, dev * 4 + rank, -1)

            @pl.when(fits)
            def _():
                notes[dev, rank] = value - ((dev * ST_DEV) << LEN_BITS)

            @pl.when(jnp.logical_not(fits))
            def _():
                flag[0] = 1

    for half in range(2):

        def check(at, index):
            dev = owner_of(table[2 + half, at])
            rank = theirs[dev]
            theirs[dev] = rank + 1
            spilled = rank >= base_next

            @pl.when(spilled & ((index >= SPILL) | (fill[dev] + rank >= 2 * base_next)))
            def _():
                flag[0] = 1

            return index + spilled.astype(jnp.int32)

        lax.fori_loop(0, valid_slots(table, 2 + half), check, 0)

    write_notes(tiles, 0, notes, flag[0], base[...])


def plan_rows(count, base_next, wide_count, table, base):
    return pl.pallas_call(
        functools.partial(plan_kernel, count, base_next),
        out_shape=(
            jax.ShapeDtypeStruct((2, table.shape[1] - 1), jnp.int32),
            jax.ShapeDtypeStruct((wide_count, NOTES, LANES), jnp.bfloat16),
            jax.ShapeDtypeStruct((wide_count,), jnp.int32),
        ),
        in_specs=[SMEM, VMEM],
        out_specs=(SMEM, VMEM, SMEM),
        scratch_shapes=[
            pltpu.SMEM((wide_count, count), jnp.int32),
            pltpu.SMEM((wide_count,), jnp.int32),
            pltpu.SMEM((1,), jnp.int32),
        ],
        cost_estimate=pl.CostEstimate(flops=2**16, bytes_accessed=2**18, transcendentals=0),
        name="plan_rows",
    )(table, base)


def first_kernel(count, table, plan, core_ref, own, mate, tiles, out, token, started, sem):
    core = core_ref[0]
    started[0] = 0
    token[0] = 0

    def place(half, source):
        @pl.loop(0, valid_slots(table, half))
        def _(at):
            code = plan[half, at]

            @pl.when(code >= 0)
            def _():
                started[0] += 1
                rows = source.at[at, unit(core)]
                pltpu.make_async_copy(rows, out.at[code >> 2, unit(code & 3)], sem).start()

    for half in range(2):

        @pl.when(core == half)
        def _():
            place(half, own)

        @pl.when(core != half)
        def _():
            place(half, mate)

    @pl.loop(0, out.shape[0], unroll=4)
    def _(dev):
        out[dev, count * ROWS :, :] = tiles[dev]

    @pl.loop(0, started[0])
    def _(_):
        pltpu.make_async_copy(own.at[0, unit(0)], out.at[0, unit(0)], sem).wait()


def pack_first(count, table, plan, core, own, mate, tiles):
    wide_count = tiles.shape[0]
    return pl.pallas_call(
        functools.partial(first_kernel, count),
        out_shape=(
            jax.ShapeDtypeStruct((wide_count, count * ROWS + NOTES, LANES), jnp.bfloat16),
            jax.ShapeDtypeStruct((1,), jnp.int32),
        ),
        in_specs=[SMEM] * 3 + [ANY, ANY, VMEM],
        out_specs=(VMEM, SMEM),
        scratch_shapes=[pltpu.SMEM((1,), jnp.int32), pltpu.SemaphoreType.DMA],
        cost_estimate=pl.CostEstimate(flops=0, bytes_accessed=wide_count * count * NT * 4, transcendentals=0),
        name="pack_first",
    )(table, plan, core, own, mate, tiles)


def spill_kernel(base, table, core_ref, own, same, other, plan, fill, started, sem):
    core = core_ref[0]
    started[0] = 0

    @pl.loop(0, fill.shape[0])
    def _(dev):
        fill[dev] = 0

    for half in range(2):

        @pl.loop(0, valid_slots(table, half))
        def _(at):
            dev = owner_of(table[half, at])
            rank = fill[dev]
            fill[dev] = rank + 1
            plan[half, at] = jnp.where(rank < base, dev * 4 + rank, -1)

            @pl.when((rank >= base) & (core == half) & (started[0] < SPILL))
            def _():
                index = started[0]
                started[0] = index + 1
                pltpu.make_async_copy(own.at[at, unit(core)], same.at[index], sem).start()
                pltpu.make_async_copy(own.at[at, unit(1 - core)], other.at[index], sem).start()

    @pl.loop(0, 2 * started[0])
    def _(_):
        pltpu.make_async_copy(own.at[0, unit(0)], same.at[0], sem).wait()


def spill(base, wide_count, table, core, own):
    buffer = jax.ShapeDtypeStruct((SPILL, ROWS, LANES), jnp.bfloat16)
    return pl.pallas_call(
        functools.partial(spill_kernel, base),
        out_shape=(
            buffer,
            buffer,
            jax.ShapeDtypeStruct((2, table.shape[1] - 1), jnp.int32),
            jax.ShapeDtypeStruct((wide_count,), jnp.int32),
        ),
        in_specs=[SMEM, SMEM, ANY],
        out_specs=(VMEM, VMEM, SMEM, SMEM),
        scratch_shapes=[pltpu.SMEM((1,), jnp.int32), pltpu.SemaphoreType.DMA],
        cost_estimate=pl.CostEstimate(flops=0, bytes_accessed=2**20, transcendentals=0),
        name="spill",
    )(table, core, own)


def pack_kernel(base, table, plan, held, core_ref, own, mate, same, other, after, out, fill, theirs, started, taken, sem):
    core = core_ref[0]
    started[0] = 0

    @pl.loop(0, out.shape[0])
    def _(dev):
        fill[dev] = held[dev]
        theirs[dev] = 0

    def place(half, source, guests):
        @pl.loop(0, valid_slots(table, half))
        def _(at):
            code = plan[half, at]

            @pl.when(code >= 0)
            def _():
                started[0] += 1
                rows = source.at[at, unit(core)]
                pltpu.make_async_copy(rows, out.at[code >> 2, unit(code & 3)], sem).start()

        taken[0] = 0

        @pl.loop(0, valid_slots(table, 2 + half))
        def _(at):
            dev = owner_of(table[2 + half, at])
            rank = theirs[dev]
            theirs[dev] = rank + 1

            @pl.when(rank >= base)
            def _():
                index = taken[0]
                slot = fill[dev]
                taken[0] = index + 1

                @pl.when((index < SPILL) & (slot < base))
                def _():
                    fill[dev] = slot + 1
                    started[0] += 1
                    pltpu.make_async_copy(guests.at[index], out.at[dev, unit(slot)], sem).start()

    for half in range(2):

        @pl.when(core == half)
        def _():
            place(half, own, same)

        @pl.when(core != half)
        def _():
            place(half, mate, other)

    @pl.loop(0, started[0])
    def _(_):
        pltpu.make_async_copy(own.at[0, unit(0)], out.at[0, unit(0)], sem).wait()


def pack_planned(base, table, plan, held, core, own, mate, same, other, after):
    wide_count = held.shape[0]
    return pl.pallas_call(
        functools.partial(pack_kernel, base),
        out_shape=jax.ShapeDtypeStruct((wide_count, base * ROWS, LANES), jnp.bfloat16),
        in_specs=[SMEM] * 4 + [ANY] * 5,
        out_specs=VMEM,
        scratch_shapes=[
            pltpu.SMEM((wide_count,), jnp.int32),
            pltpu.SMEM((wide_count,), jnp.int32),
            pltpu.SMEM((1,), jnp.int32),
            pltpu.SMEM((1,), jnp.int32),
            pltpu.SemaphoreType.DMA,
        ],
        cost_estimate=pl.CostEstimate(flops=0, bytes_accessed=wide_count * base * NT * 4, transcendentals=0),
        name="pack_planned",
    )(table, plan, held, core, own, mate, same, other, after)


def table_notes(packed):
    owner = (packed >> LEN_BITS) + 1
    length = jnp.where(packed >= 0, packed & 0xFFFF, 0)
    parts = jnp.concatenate([owner >> 8, owner & 0xFF, length >> 8, length & 0xFF])
    rows = 3 * LANES - parts.shape[0]
    parts = jnp.pad(parts, (0, rows)).reshape(3, LANES)
    return jnp.pad(parts, ((NOTES - 3, 0), (0, 0)))


def read_slots(rows, count):
    notes = rows[::2, count * ROWS : count * ROWS + 3 * count + 1, 0].astype(jnp.float32).astype(jnp.int32)
    fields = notes[:, : 3 * count].reshape(-1, count, 3)
    station, length = fields[..., 0] - 1, fields[..., 1] * 256 + fields[..., 2]
    return station.reshape(-1), length.reshape(-1), notes[:, 3 * count]


def read_table(rows, slots, chips):
    parts = rows[:, -3:, :].astype(jnp.float32).astype(jnp.int32)
    parts = parts.reshape(rows.shape[0], -1)[:, : 4 * slots].reshape(chips, 2, 4, slots)
    return (parts[:, :, 0] * 256 + parts[:, :, 1] - 1).reshape(chips, 2 * slots)


def second_places(owner, column, base):
    chips, entries = owner.shape
    extra = MOST - base
    slots = entries // 2
    listed = owner >= 0
    dev = jnp.where(listed, owner // ST_DEV, -1)
    order = jnp.arange(entries, dtype=jnp.int32)
    earlier = order[None, :] < order[:, None]
    alike = (dev[:, :, None] == dev[:, None, :]) & earlier
    rank = jnp.sum(alike.astype(jnp.int32), axis=2)
    over = listed & (rank >= base)
    near = earlier & (order[None, :] // slots == order[:, None] // slots)
    index = jnp.sum((over[:, None, :] & near).astype(jnp.int32), axis=2)
    sent = over & (index < SPILL)
    guest = jnp.sum((alike & sent[:, None, :]).astype(jnp.int32), axis=2)
    host_dev = jnp.concatenate([dev[chips // 2 :], dev[: chips // 2]])
    host_held = jnp.sum((dev[:, :, None] == host_dev[:, None, :]).astype(jnp.int32), axis=2)
    slot = host_held + guest
    fits = sent & (slot < base)
    chip = jnp.arange(chips, dtype=jnp.int32)[:, None]
    host = (chip + chips // 2) % chips
    code = jnp.where(rank < base, chip * base + rank, chips * base + chip * extra + rank - base)
    code = jnp.where(fits, host * base + slot, code)
    local = column * ST_DEV + jnp.arange(ST_DEV, dtype=jnp.int32)
    chosen = owner[None] == local[:, None, None]
    return jnp.sum(jnp.where(chosen, code[None], 0), axis=(1, 2))


def whiten_kernel(
    part, parts, source, length, picks, got, more, first, twist, second, *refs
):
    token, held, spectra, sem, sems = refs[-5:]
    stops, rows = picks.shape
    white = refs[-6 - parts]
    payload = refs[-5 - parts : -5]
    token[0] = 0
    stations = held.shape[0]
    base = SLOTS[part]
    first_more = got.shape[0] // 2 * base
    batch = 8

    def fetch(rows, code, count, station):
        for seg in range(2):
            source_at = rows.at[2 * (code // count) + seg, unit(code % count)]
            pltpu.make_async_copy(source_at, held.at[station, unit(seg)], sems.at[station // batch]).start()

    @pl.loop(0, stations)
    def _(station):
        code = source[station]

        @pl.when(code < first_more)
        def _():
            fetch(got, code, base, station)

        @pl.when(code >= first_more)
        def _():
            fetch(more, code - first_more, MOST - base, station)

    row = lax.broadcasted_iota(jnp.int32, (2 * ROWS, LANES), 0)
    lane = lax.broadcasted_iota(jnp.int32, (2 * ROWS, LANES), 1)
    left = lax.broadcasted_iota(jnp.int32, (ROWS // 2, LANES), 1) < ROWS
    place = (2 * part + (row & 1)) * NT + (row >> 1) * LANES + lane

    def two_stations(station):
        sides = []
        for at in range(2):
            values = held[station + at].astype(jnp.float32)
            sides.append(jnp.where(place < length[station + at], values, 0.0).astype(jnp.bfloat16))
        values = jnp.concatenate(sides, 1)
        values = jnp.concatenate([values, values], 0)
        mixed = jnp.dot(first[...], values, preferred_element_type=jnp.float32)
        parts = []
        for at in range(2):
            for seg in range(2):
                real = mixed[2 * seg * ROWS : (2 * seg + 1) * ROWS, at * LANES : (at + 1) * LANES]
                imag = mixed[(2 * seg + 1) * ROWS : (2 * seg + 2) * ROWS, at * LANES : (at + 1) * LANES]
                turned_re = real * twist[0] + imag * twist[1]
                turned_im = imag * twist[0] - real * twist[1]
                parts.append(jnp.concatenate([turned_re, turned_im], 1))
        turned = jnp.concatenate(parts, 0)
        high = turned.astype(jnp.bfloat16)
        low = (turned - high.astype(jnp.float32)).astype(jnp.bfloat16)
        upper = jnp.dot(high, second[...], preferred_element_type=jnp.float32)
        lower = jnp.dot(low, second[:, :LANES], preferred_element_type=jnp.float32)
        spectrum = upper[:, :LANES] + (upper[:, LANES:] + lower)
        for at in range(2):
            for seg in range(2):
                begin = (2 * at + seg) * ROWS
                side = spectrum[begin : begin + ROWS]
                power = jnp.sum(side * side, axis=0, keepdims=True)
                power = (power + pltpu.roll(power, LANES // 2, 1)) * (1.0 / ROWS)
                scale = 1.0 / jnp.sqrt(power + 1e-06)
                side = side * scale
                upper, lower = side[: ROWS // 2], side[ROWS // 2 :]
                real = jnp.where(left, upper, pltpu.roll(lower, ROWS, 1))
                imag = jnp.where(left, pltpu.roll(upper, ROWS, 1), lower)
                spectra[station + at, seg, : ROWS // 2] = real.astype(jnp.bfloat16)
                spectra[station + at, seg, ROWS // 2 :] = imag.astype(jnp.bfloat16)

    @pl.loop(0, stations // batch)
    def _(at):
        these = held.at[pl.ds(at * batch, batch)]
        pltpu.make_async_copy(these, these, sems.at[at]).wait()
        for two in range(0, batch, 2):
            two_stations(batch * at + two)

    each = stops // parts
    for piece in range(parts):

        @pl.loop(0, each)
        def _(stop):
            for at in range(rows):
                row = spectra.at[picks[piece * each + stop, at]]
                pltpu.make_async_copy(row, payload[piece].at[stop, at], sem).start()

    whole = pltpu.make_async_copy(spectra, white, sems.at[0])
    whole.start()
    for piece in range(parts):
        pltpu.make_async_copy(payload[piece], payload[piece], sem).wait()
    whole.wait()


def whiten(part, parts, source, length, picks, got, more, tables, after):
    stops, rows = picks.shape
    piece = jax.ShapeDtypeStruct((stops // parts, rows, 2, ROWS, LANES), jnp.bfloat16)
    return pl.pallas_call(
        functools.partial(whiten_kernel, part, parts),
        out_shape=(jax.ShapeDtypeStruct((ST_DEV, 2, ROWS, LANES), jnp.bfloat16),)
        + (piece,) * parts
        + (jax.ShapeDtypeStruct((1,), jnp.int32),),
        in_specs=[SMEM, SMEM, SMEM, ANY, ANY, VMEM, VMEM, VMEM] + [ANY] * len(after),
        out_specs=(ANY,) * (1 + parts) + (SMEM,),
        scratch_shapes=[
            pltpu.VMEM((ST_DEV, 2 * ROWS, LANES), jnp.bfloat16),
            pltpu.VMEM((ST_DEV, 2, ROWS, LANES), jnp.bfloat16),
            pltpu.SemaphoreType.DMA,
            pltpu.SemaphoreType.DMA((ST_DEV // 8,)),
        ],
        cost_estimate=pl.CostEstimate(flops=2**20, bytes_accessed=2**18, transcendentals=0),
        name="whiten",
    )(source, length, picks, got, more, *tables, *after)


def cross_rows(near_pick, near, far, cross, fresh, ready):
    stops, rows = near_pick.shape
    side = rows // 2
    step = 16
    half = ROWS // 2

    @pl.loop(0, stops)
    def _(stop):
        ready(stop)
        for two in range(2):
            first = two * side
            own = [near_pick[stop, first + i] for i in range(side)]

            @pl.loop(0, half // step)
            def _(chunk):
                real = pl.ds(pl.multiple_of(chunk * step, step), step)
                imag = pl.ds(pl.multiple_of(half + chunk * step, step), step)

                def both(ref, row):
                    return [
                        (ref[row, s, real, :].astype(jnp.float32), ref[row, s, imag, :].astype(jnp.float32))
                        for s in range(2)
                    ]

                here = [both(near, own[i]) for i in range(side)]
                for j in range(side):
                    there = both(far.at[stop], first + j)
                    for i in range(side):
                        pair = ((stop * 2 + two) * side + i) * side + j
                        total_re = sum(n[0] * f[0] + n[1] * f[1] for n, f in zip(here[i], there))
                        total_im = sum(n[1] * f[0] - n[0] * f[1] for n, f in zip(here[i], there))
                        for total, add in ((total_re, 0), (total_im, half)):
                            at = pl.ds(pl.multiple_of(pair * ROWS + add + chunk * step, step), step)
                            if fresh:
                                cross[at, :] = total
                            else:
                                cross[at, :] += total


def lag_product(cross, tables, last, out, edge, exact):
    pairs = out.shape[0]
    group = 32
    depth = group * LANES
    half = LAGS // 2
    turns = ROWS // 2 // group

    def product(turn, even):
        base = turn * group
        slabs = [cross[pl.ds(base + k, pairs, stride=ROWS), :] for k in range(group)]
        high = [slab.astype(jnp.bfloat16) for slab in slabs]
        if even:
            total = edge[...]
            for k in range(group):
                total += (slabs[k] if exact else high[k].astype(jnp.float32)) * last[base + k]
            edge[...] = total
        rows = jnp.concatenate(high, 1)
        if exact:
            low = [(slab - part.astype(jnp.float32)).astype(jnp.bfloat16) for slab, part in zip(slabs, high)]
            rows = jnp.concatenate([rows, jnp.concatenate(low, 1)], 0)
        part = jnp.dot(
            rows,
            tables[pl.ds(pl.multiple_of(base * LANES, depth), depth), :],
            preferred_element_type=jnp.float32,
        )
        return part[:pairs] + part[pairs:] if exact else part

    @pl.loop(0, turns)
    def _(turn):
        out[:, :half] += product(turn, True)

    @pl.loop(turns, 2 * turns)
    def _(turn):
        out[:, half:] += product(turn, False)


def first_lag_kernel(stops, near_pick, white, home, *refs):
    far_in = refs[: stops - 1]
    table, last, out, edge, near, far, cross, tables, sem, sems, table_sem = refs[stops - 1 :]
    load = pltpu.make_async_copy(white, near, sem)
    load.start()
    pltpu.make_async_copy(home, far.at[0], sems.at[0]).start()
    for stop in range(1, stops):
        pltpu.make_async_copy(far_in[stop - 1], far.at[stop], sems.at[stop]).start()
    load_table = pltpu.make_async_copy(table, tables, table_sem)
    load_table.start()
    out[...] = jnp.zeros_like(out)
    edge[...] = jnp.zeros_like(edge)
    load.wait()

    def ready(stop):
        pltpu.make_async_copy(far.at[stop], far.at[stop], sems.at[stop]).wait()

    cross_rows(near_pick, near, far, cross, True, ready)
    load_table.wait()
    lag_product(cross, tables, last, out, edge, True)


def last_lag_kernel(
    near_pick, far_at, begun, begun_edge, white, far_in, table, last, mask,
    result, near, far, cross, out, edge, tables, sem, sems, table_sem,
):
    stops = near_pick.shape[0]
    pairs = out.shape[0]
    half = LAGS // 2
    load = pltpu.make_async_copy(white, near, sem.at[0])
    load.start()
    for stop in range(stops):
        pltpu.make_async_copy(far_in.at[far_at[stop]], far.at[stop], sems.at[stop]).start()
    load_table = pltpu.make_async_copy(table, tables, table_sem)
    load_table.start()
    before = [pltpu.make_async_copy(begun, out, sem.at[1]), pltpu.make_async_copy(begun_edge, edge, sem.at[2])]
    for copy in before:
        copy.start()
    load.wait()

    def ready(stop):
        pltpu.make_async_copy(far.at[stop], far.at[stop], sems.at[stop]).wait()

    cross_rows(near_pick, near, far, cross, True, ready)
    load_table.wait()
    for copy in before:
        copy.wait()
    lag_product(cross, tables, last, out, edge, False)
    first_lag = jnp.sum(edge[...], axis=1, keepdims=True)
    lane = lax.broadcasted_iota(jnp.int32, (pairs, LANES), 1)
    mirror = (LANES - lane) % LANES
    first = lane == 0
    listed = mask[...]
    count = half // LANES
    back, ahead = [], []
    for block in range(count):
        even = out[:, block * LANES : (block + 1) * LANES]
        odd = out[:, half + block * LANES : half + (block + 1) * LANES]
        if block == 0:
            first_lag = first_lag + odd
            odd = jnp.where(first, 0.0, odd)
        back.append(even - odd)
        ahead.append(even + odd)
    for block in range(count):
        turned = jnp.take_along_axis(back[count - 1 - block], mirror, axis=1)
        start = first_lag if block == 0 else back[count - block]
        lags = pl.ds(block * LANES, LANES)
        result[:, :, lags] = (jnp.where(first, start, turned) * listed).reshape(result.shape[:2] + (LANES,))
        lags = pl.ds(half + block * LANES, LANES)
        result[:, :, lags] = (ahead[block] * listed).reshape(result.shape[:2] + (LANES,))


def lag_scratch(white, stops, pairs, table):
    return [
        pltpu.VMEM(white.shape, jnp.bfloat16),
        pltpu.VMEM((stops, 8, 2, ROWS, LANES), jnp.bfloat16),
        pltpu.VMEM((pairs * ROWS, LANES), jnp.float32),
    ], [pltpu.VMEM(table.shape, jnp.bfloat16)]


def lagged_first(near_pick, white, home, far, table, last):
    stops, rows = near_pick.shape
    pairs = stops * rows * rows // 2
    scratch, table_scratch = lag_scratch(white, stops, pairs, table)
    return pl.pallas_call(
        functools.partial(first_lag_kernel, stops),
        out_shape=(
            jax.ShapeDtypeStruct((pairs, LAGS), jnp.float32),
            jax.ShapeDtypeStruct((pairs, LANES), jnp.float32),
        ),
        in_specs=[SMEM] + [ANY] * (stops + 2) + [VMEM],
        out_specs=(VMEM, VMEM),
        scratch_shapes=scratch
        + table_scratch
        + [pltpu.SemaphoreType.DMA, pltpu.SemaphoreType.DMA((stops,)), pltpu.SemaphoreType.DMA],
        compiler_params=pltpu.CompilerParams(vmem_limit_bytes=LAG_VMEM),
        cost_estimate=pl.CostEstimate(
            flops=4 * pairs * NF * LAGS, bytes_accessed=16 * 1024 * 1024, transcendentals=0
        ),
        name="lagged_first",
    )(near_pick, white, home, *far, table, last)


def lagged_last(near_pick, far_at, begun, edge, white, far, table, last, mask):
    stops, rows = near_pick.shape
    side = rows // 2
    pairs = mask.shape[0]
    scratch, table_scratch = lag_scratch(white, stops, pairs, table)
    return pl.pallas_call(
        last_lag_kernel,
        out_shape=jax.ShapeDtypeStruct((pairs // side, side, LAGS), jnp.float32),
        in_specs=[SMEM, SMEM] + [ANY] * 5 + [VMEM, VMEM],
        out_specs=VMEM,
        scratch_shapes=scratch
        + [pltpu.VMEM((pairs, LAGS), jnp.float32), pltpu.VMEM((pairs, LANES), jnp.float32)]
        + table_scratch
        + [pltpu.SemaphoreType.DMA((3,)), pltpu.SemaphoreType.DMA((stops,)), pltpu.SemaphoreType.DMA],
        compiler_params=pltpu.CompilerParams(vmem_limit_bytes=LAST_VMEM),
        cost_estimate=pl.CostEstimate(
            flops=2 * pairs * NF * LAGS, bytes_accessed=16 * 1024 * 1024, transcendentals=0
        ),
        name="lagged_last",
    )(near_pick, far_at, begun, edge, white, far, table, last, mask)


def empty(shape):
    return pl.pallas_call(
        lambda out: None,
        out_shape=jax.ShapeDtypeStruct(shape, jnp.bfloat16),
        out_specs=ANY,
        name="empty",
    )()


def on_device(records, lengths, owners, own_pick, visit_pick, pair_mask):
    wide_count = lax.axis_size("wide")
    stops = lax.axis_size("blk")
    column = lax.axis_index("wide")
    group = lax.axis_index("blk")
    core = column % 2
    slots = records.shape[1]
    steps = jnp.arange(stops, dtype=jnp.int32)
    core_at = core.reshape(1)

    def flip(bits):
        return [(i, i ^ bits) for i in range(wide_count)]

    def across(shard, bits):
        return lax.ppermute(shard, "wide", flip(bits))

    over = wide_count // 2
    packed = jnp.where(owners[0] >= 0, (owners[0] << LEN_BITS) + lengths[0], -1)
    counted = jnp.concatenate([packed, jnp.sum((packed >= 0).astype(jnp.int32), keepdims=True)])
    others = [across(counted, bits) for bits in (1, over, over + 1)]
    table = jnp.where(
        core == 0,
        jnp.stack([counted, others[0], others[1], others[2]]),
        jnp.stack([others[0], counted, others[2], others[1]]),
    )

    blocks = records[0].reshape(slots, SEG, ROWS, LANES)

    def halves(part, never_below):
        start = 2 * part + jnp.minimum(never_below, 0)
        half = lax.dynamic_slice_in_dim(blocks, start, 2, 1)
        return half.transpose(0, 2, 1, 3).reshape(slots, 2 * ROWS, LANES)

    def send(payload):
        return lax.all_to_all(payload, "wide", split_axis=0, concat_axis=0, tiled=True)

    own_a = halves(0, counted[-1])
    mate_a = across(own_a, 1)
    base_a, base_b = SLOTS
    plan_a, tiles, _ = plan_rows(base_a, base_b, wide_count, table, table_notes(packed))
    load_a, token = pack_first(base_a, table, plan_a, core_at, own_a, mate_a, tiles)
    got_a = send(load_a)
    own_b = halves(1, token[0])
    mate_b = across(own_b, 1)
    same_b, other_b, plan, held = spill(base_b, wide_count, table, core_at, own_b)
    same_b, other_b = across(same_b, over), across(other_b, over + 1)
    visits = jnp.where(token[0] >= 0, visit_pick[0, 0].reshape(1, stops, -1), 0)
    bit = 1
    while bit < stops:
        theirs = lax.ppermute(visits, "blk", [(i, i ^ bit) for i in range(stops)])
        upper = (group // bit) % 2 == 1
        visits = jnp.concatenate([jnp.where(upper, theirs, visits), jnp.where(upper, visits, theirs)])
        bit *= 2
    by_dest = visits[steps, (steps - group) % stops]
    by_stop = by_dest[(steps + group) % stops]
    load_b = pack_planned(base_b, table, plan, held, core_at, own_b, mate_b, same_b, other_b, by_stop)
    got_b = send(load_b)

    def late_rows(low, own, mate):
        return send(pack_rows(low, MOST - low, wide_count, table, core_at, own, mate))

    def late():
        first = late_rows(base_a, own_a, mate_a)
        second = late_rows(base_b, own_b, mate_b)
        return (first, second) + read_slots(first, MOST - base_a)[:2]

    def never():
        count = wide_count // 2 * (MOST - base_a)
        rows = [empty((wide_count, (MOST - base) * ROWS + NOTES, LANES)) for base in SLOTS]
        return rows[0], rows[1], jnp.full((count,), -1, jnp.int32), jnp.zeros((count,), jnp.int32)

    station, length, spilled = read_slots(got_a, base_a)
    more_a, more_b, more_station, more_length = lax.cond(jnp.max(spilled) > 0, late, never)
    station = jnp.concatenate([station, more_station])
    length = jnp.concatenate([length, more_length])
    chosen = station[None, :] == jnp.arange(ST_DEV, dtype=jnp.int32)[:, None]
    codes = jnp.arange(station.shape[0], dtype=jnp.int32)
    source_a = jnp.sum(jnp.where(chosen, codes[None], 0), axis=1)
    length = jnp.sum(jnp.where(chosen, length[None], 0), axis=1)

    tables = [jnp.asarray(table) for table in transform_tables()]
    near_pick = own_pick[0, 0].reshape(stops, -1)
    white_a, home, *payload_a, _ = whiten(0, stops, source_a, length, by_stop, got_a, more_a, tables, [])
    far_a = [
        lax.ppermute(payload_a[stop - 1][0], "blk", [(i, (i + stop) % stops) for i in range(stops)])
        for stop in range(1, stops)
    ]
    source_b = second_places(read_table(got_a, slots, wide_count // 2), column, base_b)
    white_b, payload_b, _ = whiten(1, 1, source_b, length, by_dest, got_b, more_b, tables, far_a[:5])
    far_b = lax.all_to_all(payload_b, "blk", split_axis=0, concat_axis=0, tiled=True)

    far_at = (group - steps) % stops
    mask = pair_mask[0, 0].astype(jnp.float32).reshape(-1, 1)
    lags, last = (jnp.asarray(table) for table in lag_tables())
    begun, edge = lagged_first(near_pick, white_a, home[0], far_a, lags, last)
    result = lagged_last(near_pick, far_at, begun, edge, white_b, far_b, lags, last, mask)
    return result.reshape((1, 1) + pair_mask.shape[2:] + (LAGS,))


def solution(mesh):
    return jax.shard_map(
        on_device,
        mesh=mesh,
        in_specs=(
            P("blk", "wide", None, None),
            P("blk", "wide"),
            P("blk", "wide"),
            P("blk", "wide", None, None, None),
            P("blk", "wide", None, None, None),
            P("blk", "wide", None, None, None, None),
        ),
        out_specs=P("blk", "wide", None, None, None, None, None),
        check_vma=False,
    )
```

```python
import functools
import math

import jax
import jax.numpy as jnp
import numpy as np
from jax import lax
from jax.experimental import pallas as pl
from jax.experimental.pallas import tpu as pltpu
from jax.sharding import PartitionSpec as P

ST_DEV = 24
SEG = 4
NT = 8192
NF = 4096
LAGS = 1024
ROWS = 64
LANES = 128
MOST = 6
SLOTS = (4, 3)
SPILL = 12
LAG_VMEM = 60 * 1024 * 1024
LAST_VMEM = 60 * 1024 * 1024
LEN_BITS = 16
NOTES = 16
SMEM = pl.BlockSpec(memory_space=pltpu.SMEM)
VMEM = pl.BlockSpec(memory_space=pltpu.VMEM)
ANY = pl.BlockSpec(memory_space=pl.ANY)


def split_bf16(values):
    high = values.astype(jnp.bfloat16)
    low = (values - high.astype(np.float64)).astype(jnp.bfloat16)
    return high, low


def transform_tables():
    first = np.arange(ROWS)
    second = np.arange(LANES)
    half = np.arange(LANES // 2)
    angle = 2.0 * math.pi / ROWS * (first[:, None] * first[None, :] % ROWS)
    wave = np.concatenate([np.cos(angle), -np.sin(angle)], 0)
    wave = np.einsum("ab,kn->aknb", np.eye(2), wave).reshape(4 * ROWS, 2 * ROWS)
    first_table = np.concatenate(split_bf16(wave), 1)
    twist = 2.0 * math.pi / NT * (first[:, None] * second[None, :] % NT)
    twist_table = np.stack([np.cos(twist), np.sin(twist)]).astype(np.float32)
    angle = 2.0 * math.pi / LANES * (second[:, None] * half[None, :] % LANES)
    cos, sin = np.cos(angle), np.sin(angle)
    wave = np.concatenate([np.concatenate([cos, -sin], 1), np.concatenate([sin, cos], 1)], 0)
    second_table = np.concatenate(split_bf16(wave), 1)
    return first_table, twist_table, second_table


def lag_tables():
    row = np.arange(ROWS // 2, dtype=np.int64)
    lane = np.arange(LANES, dtype=np.int64)
    bins = (row[:, None] + ROWS // 2 * (lane // ROWS)) + ROWS * (lane % ROWS)
    bins = bins.reshape(-1)
    weight = np.where(bins == 0, 0.5, 1.0).astype(np.float32) / np.float32(math.sqrt(NF * SEG))

    def at(delay):
        phase = bins[:, None] * delay[None, :] % NT
        return phase.astype(np.float32) * np.float32(2.0 * math.pi / NT)

    ahead = at(np.arange(LAGS // 2, dtype=np.int64))
    edge = at(np.array([NT - LAGS // 2], dtype=np.int64))
    cos = weight[:, None] * np.cos(ahead)
    sin = -weight[:, None] * np.sin(ahead)
    sin[:, :1] = -weight[:, None] * np.sin(edge)
    last = (weight[:, None] * np.cos(edge)).reshape(ROWS // 2, 1, LANES)
    return (
        np.concatenate([cos, sin], 0).astype(jnp.bfloat16),
        last.astype(jnp.bfloat16).astype(np.float32),
    )


def owner_of(value):
    return ((value >> LEN_BITS) * 2731) >> 16


def unit(slot):
    return pl.ds(pl.multiple_of(slot * ROWS, ROWS), ROWS)


def write_notes(out, begin, notes, flag, base):
    count = notes.shape[1]
    row = lax.broadcasted_iota(jnp.int32, (NOTES, LANES), 0)

    @pl.loop(0, notes.shape[0])
    def _(dev):
        tile = jnp.where(row == 3 * count, flag, base)
        for slot in range(count):
            value = notes[dev, slot]
            tile = jnp.where(row == 3 * slot, (value >> LEN_BITS) + 1, tile)
            tile = jnp.where(row == 3 * slot + 1, (value & 0xFFFF) >> 8, tile)
            tile = jnp.where(row == 3 * slot + 2, value & 0xFF, tile)
        out[dev, begin : begin + NOTES, :] = tile.astype(jnp.float32).astype(jnp.bfloat16)


def valid_slots(table, row):
    return table[row, table.shape[1] - 1]


def rows_kernel(low, count, table, core_ref, own, mate, out, fill, notes, started, sem):
    core = core_ref[0]
    started[0] = 0

    @pl.loop(0, out.shape[0])
    def _(dev):
        fill[dev] = 0
        for slot in range(count):
            notes[dev, slot] = -1

    def place(half, source):
        @pl.loop(0, valid_slots(table, half))
        def _(at):
            value = table[half, at]
            dev = owner_of(value)
            rank = fill[dev]
            fill[dev] = rank + 1

            @pl.when((rank >= low) & (rank < low + count))
            def _():
                started[0] += 1
                notes[dev, rank - low] = value - ((dev * ST_DEV) << LEN_BITS)
                rows = source.at[at, unit(core)]
                pltpu.make_async_copy(rows, out.at[dev, unit(rank - low)], sem).start()

    for half in range(2):

        @pl.when(core == half)
        def _():
            place(half, own)

        @pl.when(core != half)
        def _():
            place(half, mate)

    write_notes(out, count * ROWS, notes, 0, jnp.zeros((NOTES, LANES), jnp.int32))

    @pl.loop(0, started[0])
    def _(_):
        pltpu.make_async_copy(own.at[0, unit(0)], out.at[0, unit(0)], sem).wait()


def pack_rows(low, count, wide_count, table, core, own, mate):
    return pl.pallas_call(
        functools.partial(rows_kernel, low, count),
        out_shape=jax.ShapeDtypeStruct((wide_count, count * ROWS + NOTES, LANES), jnp.bfloat16),
        in_specs=[SMEM, SMEM, ANY, ANY],
        out_specs=VMEM,
        scratch_shapes=[
            pltpu.SMEM((wide_count,), jnp.int32),
            pltpu.SMEM((wide_count, count), jnp.int32),
            pltpu.SMEM((1,), jnp.int32),
            pltpu.SemaphoreType.DMA,
        ],
        cost_estimate=pl.CostEstimate(flops=0, bytes_accessed=wide_count * count * NT * 4, transcendentals=0),
        name="pack_rows",
    )(table, core, own, mate)


def plan_kernel(count, base_next, table, base, plan, tiles, fill, notes, theirs, flag):
    flag[0] = 0

    @pl.loop(0, fill.shape[0])
    def _(dev):
        fill[dev] = 0
        theirs[dev] = 0
        for slot in range(count):
            notes[dev, slot] = -1

    for half in range(2):

        @pl.loop(0, valid_slots(table, half))
        def _(at):
            value = table[half, at]
            dev = owner_of(value)
            rank = fill[dev]
            fill[dev] = rank + 1
            fits = rank < count
            plan[half, at] = jnp.where(fits, dev * 4 + rank, -1)

            @pl.when(fits)
            def _():
                notes[dev, rank] = value - ((dev * ST_DEV) << LEN_BITS)

            @pl.when(jnp.logical_not(fits))
            def _():
                flag[0] = 1

    for half in range(2):

        def check(at, index):
            dev = owner_of(table[2 + half, at])
            rank = theirs[dev]
            theirs[dev] = rank + 1
            spilled = rank >= base_next

            @pl.when(spilled & ((index >= SPILL) | (fill[dev] + rank >= 2 * base_next)))
            def _():
                flag[0] = 1

            return index + spilled.astype(jnp.int32)

        lax.fori_loop(0, valid_slots(table, 2 + half), check, 0)

    write_notes(tiles, 0, notes, flag[0], base[...])


def plan_rows(count, base_next, wide_count, table, base):
    return pl.pallas_call(
        functools.partial(plan_kernel, count, base_next),
        out_shape=(
            jax.ShapeDtypeStruct((2, table.shape[1] - 1), jnp.int32),
            jax.ShapeDtypeStruct((wide_count, NOTES, LANES), jnp.bfloat16),
            jax.ShapeDtypeStruct((wide_count,), jnp.int32),
        ),
        in_specs=[SMEM, VMEM],
        out_specs=(SMEM, VMEM, SMEM),
        scratch_shapes=[
            pltpu.SMEM((wide_count, count), jnp.int32),
            pltpu.SMEM((wide_count,), jnp.int32),
            pltpu.SMEM((1,), jnp.int32),
        ],
        cost_estimate=pl.CostEstimate(flops=2**16, bytes_accessed=2**18, transcendentals=0),
        name="plan_rows",
    )(table, base)


def first_kernel(count, table, plan, core_ref, own, mate, tiles, out, token, started, sem):
    core = core_ref[0]
    started[0] = 0
    token[0] = 0

    def place(half, source):
        @pl.loop(0, valid_slots(table, half))
        def _(at):
            code = plan[half, at]

            @pl.when(code >= 0)
            def _():
                started[0] += 1
                rows = source.at[at, unit(core)]
                pltpu.make_async_copy(rows, out.at[code >> 2, unit(code & 3)], sem).start()

    for half in range(2):

        @pl.when(core == half)
        def _():
            place(half, own)

        @pl.when(core != half)
        def _():
            place(half, mate)

    @pl.loop(0, out.shape[0], unroll=4)
    def _(dev):
        out[dev, count * ROWS :, :] = tiles[dev]

    @pl.loop(0, started[0])
    def _(_):
        pltpu.make_async_copy(own.at[0, unit(0)], out.at[0, unit(0)], sem).wait()


def pack_first(count, table, plan, core, own, mate, tiles):
    wide_count = tiles.shape[0]
    return pl.pallas_call(
        functools.partial(first_kernel, count),
        out_shape=(
            jax.ShapeDtypeStruct((wide_count, count * ROWS + NOTES, LANES), jnp.bfloat16),
            jax.ShapeDtypeStruct((1,), jnp.int32),
        ),
        in_specs=[SMEM] * 3 + [ANY, ANY, VMEM],
        out_specs=(VMEM, SMEM),
        scratch_shapes=[pltpu.SMEM((1,), jnp.int32), pltpu.SemaphoreType.DMA],
        cost_estimate=pl.CostEstimate(flops=0, bytes_accessed=wide_count * count * NT * 4, transcendentals=0),
        name="pack_first",
    )(table, plan, core, own, mate, tiles)


def spill_kernel(base, table, core_ref, own, same, other, plan, fill, started, sem):
    core = core_ref[0]
    started[0] = 0

    @pl.loop(0, fill.shape[0])
    def _(dev):
        fill[dev] = 0

    for half in range(2):

        @pl.loop(0, valid_slots(table, half))
        def _(at):
            dev = owner_of(table[half, at])
            rank = fill[dev]
            fill[dev] = rank + 1
            plan[half, at] = jnp.where(rank < base, dev * 4 + rank, -1)

            @pl.when((rank >= base) & (core == half) & (started[0] < SPILL))
            def _():
                index = started[0]
                started[0] = index + 1
                pltpu.make_async_copy(own.at[at, unit(core)], same.at[index], sem).start()
                pltpu.make_async_copy(own.at[at, unit(1 - core)], other.at[index], sem).start()

    @pl.loop(0, 2 * started[0])
    def _(_):
        pltpu.make_async_copy(own.at[0, unit(0)], same.at[0], sem).wait()


def spill(base, wide_count, table, core, own):
    buffer = jax.ShapeDtypeStruct((SPILL, ROWS, LANES), jnp.bfloat16)
    return pl.pallas_call(
        functools.partial(spill_kernel, base),
        out_shape=(
            buffer,
            buffer,
            jax.ShapeDtypeStruct((2, table.shape[1] - 1), jnp.int32),
            jax.ShapeDtypeStruct((wide_count,), jnp.int32),
        ),
        in_specs=[SMEM, SMEM, ANY],
        out_specs=(VMEM, VMEM, SMEM, SMEM),
        scratch_shapes=[pltpu.SMEM((1,), jnp.int32), pltpu.SemaphoreType.DMA],
        cost_estimate=pl.CostEstimate(flops=0, bytes_accessed=2**20, transcendentals=0),
        name="spill",
    )(table, core, own)


def pack_kernel(base, table, plan, held, core_ref, own, mate, same, other, after, out, fill, theirs, started, taken, sem):
    core = core_ref[0]
    started[0] = 0

    @pl.loop(0, out.shape[0])
    def _(dev):
        fill[dev] = held[dev]
        theirs[dev] = 0

    def place(half, source, guests):
        @pl.loop(0, valid_slots(table, half))
        def _(at):
            code = plan[half, at]

            @pl.when(code >= 0)
            def _():
                started[0] += 1
                rows = source.at[at, unit(core)]
                pltpu.make_async_copy(rows, out.at[code >> 2, unit(code & 3)], sem).start()

        taken[0] = 0

        @pl.loop(0, valid_slots(table, 2 + half))
        def _(at):
            dev = owner_of(table[2 + half, at])
            rank = theirs[dev]
            theirs[dev] = rank + 1

            @pl.when(rank >= base)
            def _():
                index = taken[0]
                slot = fill[dev]
                taken[0] = index + 1

                @pl.when((index < SPILL) & (slot < base))
                def _():
                    fill[dev] = slot + 1
                    started[0] += 1
                    pltpu.make_async_copy(guests.at[index], out.at[dev, unit(slot)], sem).start()

    for half in range(2):

        @pl.when(core == half)
        def _():
            place(half, own, same)

        @pl.when(core != half)
        def _():
            place(half, mate, other)

    @pl.loop(0, started[0])
    def _(_):
        pltpu.make_async_copy(own.at[0, unit(0)], out.at[0, unit(0)], sem).wait()


def pack_planned(base, table, plan, held, core, own, mate, same, other, after):
    wide_count = held.shape[0]
    return pl.pallas_call(
        functools.partial(pack_kernel, base),
        out_shape=jax.ShapeDtypeStruct((wide_count, base * ROWS, LANES), jnp.bfloat16),
        in_specs=[SMEM] * 4 + [ANY] * 5,
        out_specs=VMEM,
        scratch_shapes=[
            pltpu.SMEM((wide_count,), jnp.int32),
            pltpu.SMEM((wide_count,), jnp.int32),
            pltpu.SMEM((1,), jnp.int32),
            pltpu.SMEM((1,), jnp.int32),
            pltpu.SemaphoreType.DMA,
        ],
        cost_estimate=pl.CostEstimate(flops=0, bytes_accessed=wide_count * base * NT * 4, transcendentals=0),
        name="pack_planned",
    )(table, plan, held, core, own, mate, same, other, after)


def table_notes(packed):
    owner = (packed >> LEN_BITS) + 1
    length = jnp.where(packed >= 0, packed & 0xFFFF, 0)
    parts = jnp.concatenate([owner >> 8, owner & 0xFF, length >> 8, length & 0xFF])
    rows = 3 * LANES - parts.shape[0]
    parts = jnp.pad(parts, (0, rows)).reshape(3, LANES)
    return jnp.pad(parts, ((NOTES - 3, 0), (0, 0)))


def read_slots(rows, count):
    notes = rows[::2, count * ROWS : count * ROWS + 3 * count + 1, 0].astype(jnp.float32).astype(jnp.int32)
    fields = notes[:, : 3 * count].reshape(-1, count, 3)
    station, length = fields[..., 0] - 1, fields[..., 1] * 256 + fields[..., 2]
    return station.reshape(-1), length.reshape(-1), notes[:, 3 * count]


def read_table(rows, slots, chips):
    parts = rows[:, -3:, :].astype(jnp.float32).astype(jnp.int32)
    parts = parts.reshape(rows.shape[0], -1)[:, : 4 * slots].reshape(chips, 2, 4, slots)
    return (parts[:, :, 0] * 256 + parts[:, :, 1] - 1).reshape(chips, 2 * slots)


def second_places(owner, column, base):
    chips, entries = owner.shape
    extra = MOST - base
    slots = entries // 2
    listed = owner >= 0
    dev = jnp.where(listed, owner // ST_DEV, -1)
    order = jnp.arange(entries, dtype=jnp.int32)
    earlier = order[None, :] < order[:, None]
    alike = (dev[:, :, None] == dev[:, None, :]) & earlier
    rank = jnp.sum(alike.astype(jnp.int32), axis=2)
    over = listed & (rank >= base)
    near = earlier & (order[None, :] // slots == order[:, None] // slots)
    index = jnp.sum((over[:, None, :] & near).astype(jnp.int32), axis=2)
    sent = over & (index < SPILL)
    guest = jnp.sum((alike & sent[:, None, :]).astype(jnp.int32), axis=2)
    host_dev = jnp.concatenate([dev[chips // 2 :], dev[: chips // 2]])
    host_held = jnp.sum((dev[:, :, None] == host_dev[:, None, :]).astype(jnp.int32), axis=2)
    slot = host_held + guest
    fits = sent & (slot < base)
    chip = jnp.arange(chips, dtype=jnp.int32)[:, None]
    host = (chip + chips // 2) % chips
    code = jnp.where(rank < base, chip * base + rank, chips * base + chip * extra + rank - base)
    code = jnp.where(fits, host * base + slot, code)
    local = column * ST_DEV + jnp.arange(ST_DEV, dtype=jnp.int32)
    chosen = owner[None] == local[:, None, None]
    return jnp.sum(jnp.where(chosen, code[None], 0), axis=(1, 2))


def whiten_kernel(
    part, parts, source, length, picks, got, more, first, twist, second, *refs
):
    token, held, spectra, sem, sems = refs[-5:]
    stops, rows = picks.shape
    white = refs[-6 - parts]
    payload = refs[-5 - parts : -5]
    token[0] = 0
    stations = held.shape[0]
    base = SLOTS[part]
    first_more = got.shape[0] // 2 * base
    batch = 8

    def fetch(rows, code, count, station):
        for seg in range(2):
            source_at = rows.at[2 * (code // count) + seg, unit(code % count)]
            pltpu.make_async_copy(source_at, held.at[station, unit(seg)], sems.at[station // batch]).start()

    @pl.loop(0, stations)
    def _(station):
        code = source[station]

        @pl.when(code < first_more)
        def _():
            fetch(got, code, base, station)

        @pl.when(code >= first_more)
        def _():
            fetch(more, code - first_more, MOST - base, station)

    row = lax.broadcasted_iota(jnp.int32, (2 * ROWS, LANES), 0)
    lane = lax.broadcasted_iota(jnp.int32, (2 * ROWS, LANES), 1)
    left = lax.broadcasted_iota(jnp.int32, (ROWS // 2, LANES), 1) < ROWS
    place = (2 * part + (row & 1)) * NT + (row >> 1) * LANES + lane

    def two_stations(station):
        sides = []
        for at in range(2):
            values = held[station + at].astype(jnp.float32)
            sides.append(jnp.where(place < length[station + at], values, 0.0).astype(jnp.bfloat16))
        values = jnp.concatenate(sides, 1)
        values = jnp.concatenate([values, values], 0)
        mixed = jnp.dot(first[...], values, preferred_element_type=jnp.float32)
        parts = []
        for at in range(2):
            for seg in range(2):
                real = mixed[2 * seg * ROWS : (2 * seg + 1) * ROWS, at * LANES : (at + 1) * LANES]
                imag = mixed[(2 * seg + 1) * ROWS : (2 * seg + 2) * ROWS, at * LANES : (at + 1) * LANES]
                turned_re = real * twist[0] + imag * twist[1]
                turned_im = imag * twist[0] - real * twist[1]
                parts.append(jnp.concatenate([turned_re, turned_im], 1))
        turned = jnp.concatenate(parts, 0)
        high = turned.astype(jnp.bfloat16)
        low = (turned - high.astype(jnp.float32)).astype(jnp.bfloat16)
        upper = jnp.dot(high, second[...], preferred_element_type=jnp.float32)
        lower = jnp.dot(low, second[:, :LANES], preferred_element_type=jnp.float32)
        spectrum = upper[:, :LANES] + (upper[:, LANES:] + lower)
        for at in range(2):
            for seg in range(2):
                begin = (2 * at + seg) * ROWS
                side = spectrum[begin : begin + ROWS]
                power = jnp.sum(side * side, axis=0, keepdims=True)
                power = (power + pltpu.roll(power, LANES // 2, 1)) * (1.0 / ROWS)
                scale = 1.0 / jnp.sqrt(power + 1e-06)
                side = side * scale
                upper, lower = side[: ROWS // 2], side[ROWS // 2 :]
                real = jnp.where(left, upper, pltpu.roll(lower, ROWS, 1))
                imag = jnp.where(left, pltpu.roll(upper, ROWS, 1), lower)
                spectra[station + at, seg, : ROWS // 2] = real.astype(jnp.bfloat16)
                spectra[station + at, seg, ROWS // 2 :] = imag.astype(jnp.bfloat16)

    @pl.loop(0, stations // batch)
    def _(at):
        these = held.at[pl.ds(at * batch, batch)]
        pltpu.make_async_copy(these, these, sems.at[at]).wait()
        for two in range(0, batch, 2):
            two_stations(batch * at + two)

    each = stops // parts
    for piece in range(parts):

        @pl.loop(0, each)
        def _(stop):
            for at in range(rows):
                row = spectra.at[picks[piece * each + stop, at]]
                pltpu.make_async_copy(row, payload[piece].at[stop, at], sem).start()

    whole = pltpu.make_async_copy(spectra, white, sems.at[0])
    whole.start()
    for piece in range(parts):
        pltpu.make_async_copy(payload[piece], payload[piece], sem).wait()
    whole.wait()


def whiten(part, parts, source, length, picks, got, more, tables, after):
    stops, rows = picks.shape
    piece = jax.ShapeDtypeStruct((stops // parts, rows, 2, ROWS, LANES), jnp.bfloat16)
    return pl.pallas_call(
        functools.partial(whiten_kernel, part, parts),
        out_shape=(jax.ShapeDtypeStruct((ST_DEV, 2, ROWS, LANES), jnp.bfloat16),)
        + (piece,) * parts
        + (jax.ShapeDtypeStruct((1,), jnp.int32),),
        in_specs=[SMEM, SMEM, SMEM, ANY, ANY, VMEM, VMEM, VMEM] + [ANY] * len(after),
        out_specs=(ANY,) * (1 + parts) + (SMEM,),
        scratch_shapes=[
            pltpu.VMEM((ST_DEV, 2 * ROWS, LANES), jnp.bfloat16),
            pltpu.VMEM((ST_DEV, 2, ROWS, LANES), jnp.bfloat16),
            pltpu.SemaphoreType.DMA,
            pltpu.SemaphoreType.DMA((ST_DEV // 8,)),
        ],
        cost_estimate=pl.CostEstimate(flops=2**20, bytes_accessed=2**18, transcendentals=0),
        name="whiten",
    )(source, length, picks, got, more, *tables, *after)


def cross_rows(near_pick, near, far, cross, fresh, ready):
    stops, rows = near_pick.shape
    side = rows // 2
    step = 16
    half = ROWS // 2

    @pl.loop(0, stops)
    def _(stop):
        ready(stop)
        for two in range(2):
            first = two * side
            own = [near_pick[stop, first + i] for i in range(side)]

            @pl.loop(0, half // step)
            def _(chunk):
                real = pl.ds(pl.multiple_of(chunk * step, step), step)
                imag = pl.ds(pl.multiple_of(half + chunk * step, step), step)

                def both(ref, row):
                    return [
                        (ref[row, s, real, :].astype(jnp.float32), ref[row, s, imag, :].astype(jnp.float32))
                        for s in range(2)
                    ]

                here = [both(near, own[i]) for i in range(side)]
                for j in range(side):
                    there = both(far.at[stop], first + j)
                    for i in range(side):
                        pair = ((stop * 2 + two) * side + i) * side + j
                        total_re = sum(n[0] * f[0] + n[1] * f[1] for n, f in zip(here[i], there))
                        total_im = sum(n[1] * f[0] - n[0] * f[1] for n, f in zip(here[i], there))
                        for total, add in ((total_re, 0), (total_im, half)):
                            at = pl.ds(pl.multiple_of(pair * ROWS + add + chunk * step, step), step)
                            if fresh:
                                cross[at, :] = total
                            else:
                                cross[at, :] += total


def lag_product(cross, tables, last, out, edge, exact):
    pairs = out.shape[0]
    group = 32
    depth = group * LANES
    half = LAGS // 2
    turns = ROWS // 2 // group

    def product(turn, even):
        base = turn * group
        slabs = [cross[pl.ds(base + k, pairs, stride=ROWS), :] for k in range(group)]
        high = [slab.astype(jnp.bfloat16) for slab in slabs]
        if even:
            total = edge[...]
            for k in range(group):
                total += (slabs[k] if exact else high[k].astype(jnp.float32)) * last[base + k]
            edge[...] = total
        rows = jnp.concatenate(high, 1)
        if exact:
            low = [(slab - part.astype(jnp.float32)).astype(jnp.bfloat16) for slab, part in zip(slabs, high)]
            rows = jnp.concatenate([rows, jnp.concatenate(low, 1)], 0)
        part = jnp.dot(
            rows,
            tables[pl.ds(pl.multiple_of(base * LANES, depth), depth), :],
            preferred_element_type=jnp.float32,
        )
        return part[:pairs] + part[pairs:] if exact else part

    @pl.loop(0, turns)
    def _(turn):
        out[:, :half] += product(turn, True)

    @pl.loop(turns, 2 * turns)
    def _(turn):
        out[:, half:] += product(turn, False)


def first_lag_kernel(stops, near_pick, white, home, *refs):
    far_in = refs[: stops - 1]
    table, last, out, edge, near, far, cross, tables, sem, sems, table_sem = refs[stops - 1 :]
    load = pltpu.make_async_copy(white, near, sem)
    load.start()
    pltpu.make_async_copy(home, far.at[0], sems.at[0]).start()
    for stop in range(1, stops):
        pltpu.make_async_copy(far_in[stop - 1], far.at[stop], sems.at[stop]).start()
    load_table = pltpu.make_async_copy(table, tables, table_sem)
    load_table.start()
    out[...] = jnp.zeros_like(out)
    edge[...] = jnp.zeros_like(edge)
    load.wait()

    def ready(stop):
        pltpu.make_async_copy(far.at[stop], far.at[stop], sems.at[stop]).wait()

    cross_rows(near_pick, near, far, cross, True, ready)
    load_table.wait()
    lag_product(cross, tables, last, out, edge, True)


def last_lag_kernel(
    near_pick, far_at, begun, begun_edge, white, far_in, table, last, mask,
    result, near, far, cross, out, edge, tables, sem, sems, table_sem,
):
    stops = near_pick.shape[0]
    pairs = out.shape[0]
    half = LAGS // 2
    load = pltpu.make_async_copy(white, near, sem.at[0])
    load.start()
    for stop in range(stops):
        pltpu.make_async_copy(far_in.at[far_at[stop]], far.at[stop], sems.at[stop]).start()
    load_table = pltpu.make_async_copy(table, tables, table_sem)
    load_table.start()
    before = [pltpu.make_async_copy(begun, out, sem.at[1]), pltpu.make_async_copy(begun_edge, edge, sem.at[2])]
    for copy in before:
        copy.start()
    load.wait()

    def ready(stop):
        pltpu.make_async_copy(far.at[stop], far.at[stop], sems.at[stop]).wait()

    cross_rows(near_pick, near, far, cross, True, ready)
    load_table.wait()
    for copy in before:
        copy.wait()
    lag_product(cross, tables, last, out, edge, False)
    first_lag = jnp.sum(edge[...], axis=1, keepdims=True)
    lane = lax.broadcasted_iota(jnp.int32, (pairs, LANES), 1)
    mirror = (LANES - lane) % LANES
    first = lane == 0
    listed = mask[...]
    count = half // LANES
    back, ahead = [], []
    for block in range(count):
        even = out[:, block * LANES : (block + 1) * LANES]
        odd = out[:, half + block * LANES : half + (block + 1) * LANES]
        if block == 0:
            first_lag = first_lag + odd
            odd = jnp.where(first, 0.0, odd)
        back.append(even - odd)
        ahead.append(even + odd)
    for block in range(count):
        turned = jnp.take_along_axis(back[count - 1 - block], mirror, axis=1)
        start = first_lag if block == 0 else back[count - block]
        lags = pl.ds(block * LANES, LANES)
        result[:, :, lags] = (jnp.where(first, start, turned) * listed).reshape(result.shape[:2] + (LANES,))
        lags = pl.ds(half + block * LANES, LANES)
        result[:, :, lags] = (ahead[block] * listed).reshape(result.shape[:2] + (LANES,))


def lag_scratch(white, stops, pairs, table):
    return [
        pltpu.VMEM(white.shape, jnp.bfloat16),
        pltpu.VMEM((stops, 8, 2, ROWS, LANES), jnp.bfloat16),
        pltpu.VMEM((pairs * ROWS, LANES), jnp.float32),
    ], [pltpu.VMEM(table.shape, jnp.bfloat16)]


def lagged_first(near_pick, white, home, far, table, last):
    stops, rows = near_pick.shape
    pairs = stops * rows * rows // 2
    scratch, table_scratch = lag_scratch(white, stops, pairs, table)
    return pl.pallas_call(
        functools.partial(first_lag_kernel, stops),
        out_shape=(
            jax.ShapeDtypeStruct((pairs, LAGS), jnp.float32),
            jax.ShapeDtypeStruct((pairs, LANES), jnp.float32),
        ),
        in_specs=[SMEM] + [ANY] * (stops + 2) + [VMEM],
        out_specs=(VMEM, VMEM),
        scratch_shapes=scratch
        + table_scratch
        + [pltpu.SemaphoreType.DMA, pltpu.SemaphoreType.DMA((stops,)), pltpu.SemaphoreType.DMA],
        compiler_params=pltpu.CompilerParams(vmem_limit_bytes=LAG_VMEM),
        cost_estimate=pl.CostEstimate(
            flops=4 * pairs * NF * LAGS, bytes_accessed=16 * 1024 * 1024, transcendentals=0
        ),
        name="lagged_first",
    )(near_pick, white, home, *far, table, last)


def lagged_last(near_pick, far_at, begun, edge, white, far, table, last, mask):
    stops, rows = near_pick.shape
    side = rows // 2
    pairs = mask.shape[0]
    scratch, table_scratch = lag_scratch(white, stops, pairs, table)
    return pl.pallas_call(
        last_lag_kernel,
        out_shape=jax.ShapeDtypeStruct((pairs // side, side, LAGS), jnp.float32),
        in_specs=[SMEM, SMEM] + [ANY] * 5 + [VMEM, VMEM],
        out_specs=VMEM,
        scratch_shapes=scratch
        + [pltpu.VMEM((pairs, LAGS), jnp.float32), pltpu.VMEM((pairs, LANES), jnp.float32)]
        + table_scratch
        + [pltpu.SemaphoreType.DMA((3,)), pltpu.SemaphoreType.DMA((stops,)), pltpu.SemaphoreType.DMA],
        compiler_params=pltpu.CompilerParams(vmem_limit_bytes=LAST_VMEM),
        cost_estimate=pl.CostEstimate(
            flops=2 * pairs * NF * LAGS, bytes_accessed=16 * 1024 * 1024, transcendentals=0
        ),
        name="lagged_last",
    )(near_pick, far_at, begun, edge, white, far, table, last, mask)


def empty(shape):
    return pl.pallas_call(
        lambda out: None,
        out_shape=jax.ShapeDtypeStruct(shape, jnp.bfloat16),
        out_specs=ANY,
        name="empty",
    )()


def on_device(records, lengths, owners, own_pick, visit_pick, pair_mask):
    wide_count = lax.axis_size("wide")
    stops = lax.axis_size("blk")
    column = lax.axis_index("wide")
    group = lax.axis_index("blk")
    core = column % 2
    slots = records.shape[1]
    steps = jnp.arange(stops, dtype=jnp.int32)
    core_at = core.reshape(1)

    def flip(bits):
        return [(i, i ^ bits) for i in range(wide_count)]

    def across(shard, bits):
        return lax.ppermute(shard, "wide", flip(bits))

    over = wide_count // 2
    packed = jnp.where(owners[0] >= 0, (owners[0] << LEN_BITS) + lengths[0], -1)
    counted = jnp.concatenate([packed, jnp.sum((packed >= 0).astype(jnp.int32), keepdims=True)])
    others = [across(counted, bits) for bits in (1, over, over + 1)]
    table = jnp.where(
        core == 0,
        jnp.stack([counted, others[0], others[1], others[2]]),
        jnp.stack([others[0], counted, others[2], others[1]]),
    )

    blocks = records[0].reshape(slots, SEG, ROWS, LANES)

    def halves(part, never_below):
        start = 2 * part if never_below is None else 2 * part + jnp.minimum(never_below, 0)
        half = lax.dynamic_slice_in_dim(blocks, start, 2, 1)
        return half.transpose(0, 2, 1, 3).reshape(slots, 2 * ROWS, LANES)

    def send(payload):
        return lax.all_to_all(payload, "wide", split_axis=0, concat_axis=0, tiled=True)

    own_a = halves(0, None)
    mate_a = across(own_a, 1)
    base_a, base_b = SLOTS
    plan_a, tiles, _ = plan_rows(base_a, base_b, wide_count, table, table_notes(packed))
    load_a, token = pack_first(base_a, table, plan_a, core_at, own_a, mate_a, tiles)
    got_a = send(load_a)
    own_b = halves(1, token[0])
    mate_b = across(own_b, 1)
    same_b, other_b, plan, held = spill(base_b, wide_count, table, core_at, own_b)
    same_b, other_b = across(same_b, over), across(other_b, over + 1)
    visits = jnp.where(token[0] >= 0, visit_pick[0, 0].reshape(1, stops, -1), 0)
    bit = 1
    while bit < stops:
        theirs = lax.ppermute(visits, "blk", [(i, i ^ bit) for i in range(stops)])
        upper = (group // bit) % 2 == 1
        visits = jnp.concatenate([jnp.where(upper, theirs, visits), jnp.where(upper, visits, theirs)])
        bit *= 2
    by_dest = visits[steps, (steps - group) % stops]
    by_stop = by_dest[(steps + group) % stops]
    load_b = pack_planned(base_b, table, plan, held, core_at, own_b, mate_b, same_b, other_b, by_stop)
    got_b = send(load_b)

    def late_rows(low, own, mate):
        return send(pack_rows(low, MOST - low, wide_count, table, core_at, own, mate))

    def late():
        first = late_rows(base_a, own_a, mate_a)
        second = late_rows(base_b, own_b, mate_b)
        return (first, second) + read_slots(first, MOST - base_a)[:2]

    def never():
        count = wide_count // 2 * (MOST - base_a)
        rows = [empty((wide_count, (MOST - base) * ROWS + NOTES, LANES)) for base in SLOTS]
        return rows[0], rows[1], jnp.full((count,), -1, jnp.int32), jnp.zeros((count,), jnp.int32)

    station, length, spilled = read_slots(got_a, base_a)
    more_a, more_b, more_station, more_length = lax.cond(jnp.max(spilled) > 0, late, never)
    station = jnp.concatenate([station, more_station])
    length = jnp.concatenate([length, more_length])
    chosen = station[None, :] == jnp.arange(ST_DEV, dtype=jnp.int32)[:, None]
    codes = jnp.arange(station.shape[0], dtype=jnp.int32)
    source_a = jnp.sum(jnp.where(chosen, codes[None], 0), axis=1)
    length = jnp.sum(jnp.where(chosen, length[None], 0), axis=1)

    tables = [jnp.asarray(table) for table in transform_tables()]
    near_pick = own_pick[0, 0].reshape(stops, -1)
    white_a, home, *payload_a, _ = whiten(0, stops, source_a, length, by_stop, got_a, more_a, tables, [])
    far_a = [
        lax.ppermute(payload_a[stop - 1][0], "blk", [(i, (i + stop) % stops) for i in range(stops)])
        for stop in range(1, stops)
    ]
    source_b = second_places(read_table(got_a, slots, wide_count // 2), column, base_b)
    white_b, payload_b, _ = whiten(1, 1, source_b, length, by_dest, got_b, more_b, tables, far_a)
    far_b = lax.all_to_all(payload_b, "blk", split_axis=0, concat_axis=0, tiled=True)

    far_at = (group - steps) % stops
    mask = pair_mask[0, 0].astype(jnp.float32).reshape(-1, 1)
    lags, last = (jnp.asarray(table) for table in lag_tables())
    begun, edge = lagged_first(near_pick, white_a, home[0], far_a, lags, last)
    result = lagged_last(near_pick, far_at, begun, edge, white_b, far_b, lags, last, mask)
    return result.reshape((1, 1) + pair_mask.shape[2:] + (LAGS,))


def solution(mesh):
    return jax.shard_map(
        on_device,
        mesh=mesh,
        in_specs=(
            P("blk", "wide", None, None),
            P("blk", "wide"),
            P("blk", "wide"),
            P("blk", "wide", None, None, None),
            P("blk", "wide", None, None, None),
            P("blk", "wide", None, None, None, None),
        ),
        out_specs=P("blk", "wide", None, None, None, None, None),
        check_vma=False,
    )
```

```python
import functools
import math

import jax
import jax.numpy as jnp
import numpy as np
from jax import lax
from jax.experimental import pallas as pl
from jax.experimental.pallas import tpu as pltpu
from jax.sharding import PartitionSpec as P

ST_DEV = 24
SEG = 4
NT = 8192
NF = 4096
LAGS = 1024
ROWS = 64
LANES = 128
MOST = 6
SLOTS = (4, 3)
SPILL = 12
LAG_VMEM = 60 * 1024 * 1024
LEN_BITS = 16
NOTES = 16
SMEM = pl.BlockSpec(memory_space=pltpu.SMEM)
VMEM = pl.BlockSpec(memory_space=pltpu.VMEM)
ANY = pl.BlockSpec(memory_space=pl.ANY)


def split_bf16(values):
    high = values.astype(jnp.bfloat16)
    low = (values - high.astype(np.float64)).astype(jnp.bfloat16)
    return high, low


def transform_tables():
    first = np.arange(ROWS)
    second = np.arange(LANES)
    half = np.arange(LANES // 2)
    angle = 2.0 * math.pi / ROWS * (first[:, None] * first[None, :] % ROWS)
    wave = np.concatenate([np.cos(angle), -np.sin(angle)], 0)
    wave = np.einsum("ab,kn->aknb", np.eye(2), wave).reshape(4 * ROWS, 2 * ROWS)
    first_table = np.concatenate(split_bf16(wave), 1)
    twist = 2.0 * math.pi / NT * (first[:, None] * second[None, :] % NT)
    twist_table = np.stack([np.cos(twist), np.sin(twist)]).astype(np.float32)
    angle = 2.0 * math.pi / LANES * (second[:, None] * half[None, :] % LANES)
    cos, sin = np.cos(angle), np.sin(angle)
    wave = np.concatenate([np.concatenate([cos, -sin], 1), np.concatenate([sin, cos], 1)], 0)
    second_table = np.concatenate(split_bf16(wave), 1)
    return first_table, twist_table, second_table


def lag_tables():
    row = np.arange(ROWS // 2, dtype=np.int64)
    lane = np.arange(LANES, dtype=np.int64)
    bins = (row[:, None] + ROWS // 2 * (lane // ROWS)) + ROWS * (lane % ROWS)
    bins = bins.reshape(-1)
    weight = np.where(bins == 0, 0.5, 1.0).astype(np.float32) / np.float32(math.sqrt(NF * SEG))

    def at(delay):
        phase = bins[:, None] * delay[None, :] % NT
        return phase.astype(np.float32) * np.float32(2.0 * math.pi / NT)

    ahead = at(np.arange(LAGS // 2, dtype=np.int64))
    edge = at(np.array([NT - LAGS // 2], dtype=np.int64))
    cos = weight[:, None] * np.cos(ahead)
    sin = -weight[:, None] * np.sin(ahead)
    sin[:, :1] = -weight[:, None] * np.sin(edge)
    last = (weight[:, None] * np.cos(edge)).reshape(ROWS // 2, 1, LANES)
    return (
        np.concatenate([cos, sin], 0).astype(jnp.bfloat16),
        last.astype(jnp.bfloat16).astype(np.float32),
    )


def owner_of(value):
    return ((value >> LEN_BITS) * 2731) >> 16


def unit(slot):
    return pl.ds(pl.multiple_of(slot * ROWS, ROWS), ROWS)


def write_notes(out, begin, notes, flag, base):
    count = notes.shape[1]
    row = lax.broadcasted_iota(jnp.int32, (NOTES, LANES), 0)

    @pl.loop(0, notes.shape[0])
    def _(dev):
        tile = jnp.where(row == 3 * count, flag, base)
        for slot in range(count):
            value = notes[dev, slot]
            tile = jnp.where(row == 3 * slot, (value >> LEN_BITS) + 1, tile)
            tile = jnp.where(row == 3 * slot + 1, (value & 0xFFFF) >> 8, tile)
            tile = jnp.where(row == 3 * slot + 2, value & 0xFF, tile)
        out[dev, begin : begin + NOTES, :] = tile.astype(jnp.float32).astype(jnp.bfloat16)


def valid_slots(table, row):
    return table[row, table.shape[1] - 1]


def rows_kernel(low, count, table, core_ref, own, mate, out, fill, notes, started, sem):
    core = core_ref[0]
    started[0] = 0

    @pl.loop(0, out.shape[0])
    def _(dev):
        fill[dev] = 0
        for slot in range(count):
            notes[dev, slot] = -1

    def place(half, source):
        @pl.loop(0, valid_slots(table, half))
        def _(at):
            value = table[half, at]
            dev = owner_of(value)
            rank = fill[dev]
            fill[dev] = rank + 1

            @pl.when((rank >= low) & (rank < low + count))
            def _():
                started[0] += 1
                notes[dev, rank - low] = value - ((dev * ST_DEV) << LEN_BITS)
                rows = source.at[at, unit(core)]
                pltpu.make_async_copy(rows, out.at[dev, unit(rank - low)], sem).start()

    for half in range(2):

        @pl.when(core == half)
        def _():
            place(half, own)

        @pl.when(core != half)
        def _():
            place(half, mate)

    write_notes(out, count * ROWS, notes, 0, jnp.zeros((NOTES, LANES), jnp.int32))

    @pl.loop(0, started[0])
    def _(_):
        pltpu.make_async_copy(own.at[0, unit(0)], out.at[0, unit(0)], sem).wait()


def pack_rows(low, count, wide_count, table, core, own, mate):
    return pl.pallas_call(
        functools.partial(rows_kernel, low, count),
        out_shape=jax.ShapeDtypeStruct((wide_count, count * ROWS + NOTES, LANES), jnp.bfloat16),
        in_specs=[SMEM, SMEM, ANY, ANY],
        out_specs=VMEM,
        scratch_shapes=[
            pltpu.SMEM((wide_count,), jnp.int32),
            pltpu.SMEM((wide_count, count), jnp.int32),
            pltpu.SMEM((1,), jnp.int32),
            pltpu.SemaphoreType.DMA,
        ],
        cost_estimate=pl.CostEstimate(flops=0, bytes_accessed=wide_count * count * NT * 4, transcendentals=0),
        name="pack_rows",
    )(table, core, own, mate)


def plan_kernel(count, base_next, table, base, plan, tiles, fill, notes, theirs, flag):
    flag[0] = 0

    @pl.loop(0, fill.shape[0])
    def _(dev):
        fill[dev] = 0
        theirs[dev] = 0
        for slot in range(count):
            notes[dev, slot] = -1

    for half in range(2):

        @pl.loop(0, valid_slots(table, half))
        def _(at):
            value = table[half, at]
            dev = owner_of(value)
            rank = fill[dev]
            fill[dev] = rank + 1
            fits = rank < count
            plan[half, at] = jnp.where(fits, dev * 4 + rank, -1)

            @pl.when(fits)
            def _():
                notes[dev, rank] = value - ((dev * ST_DEV) << LEN_BITS)

            @pl.when(jnp.logical_not(fits))
            def _():
                flag[0] = 1

    for half in range(2):

        def check(at, index):
            dev = owner_of(table[2 + half, at])
            rank = theirs[dev]
            theirs[dev] = rank + 1
            spilled = rank >= base_next

            @pl.when(spilled & ((index >= SPILL) | (fill[dev] + rank >= 2 * base_next)))
            def _():
                flag[0] = 1

            return index + spilled.astype(jnp.int32)

        lax.fori_loop(0, valid_slots(table, 2 + half), check, 0)

    write_notes(tiles, 0, notes, flag[0], base[...])


def plan_rows(count, base_next, wide_count, table, base):
    return pl.pallas_call(
        functools.partial(plan_kernel, count, base_next),
        out_shape=(
            jax.ShapeDtypeStruct((2, table.shape[1] - 1), jnp.int32),
            jax.ShapeDtypeStruct((wide_count, NOTES, LANES), jnp.bfloat16),
            jax.ShapeDtypeStruct((wide_count,), jnp.int32),
        ),
        in_specs=[SMEM, VMEM],
        out_specs=(SMEM, VMEM, SMEM),
        scratch_shapes=[
            pltpu.SMEM((wide_count, count), jnp.int32),
            pltpu.SMEM((wide_count,), jnp.int32),
            pltpu.SMEM((1,), jnp.int32),
        ],
        cost_estimate=pl.CostEstimate(flops=2**16, bytes_accessed=2**18, transcendentals=0),
        name="plan_rows",
    )(table, base)


def first_kernel(count, table, plan, core_ref, own, mate, tiles, out, token, started, sem):
    core = core_ref[0]
    started[0] = 0
    token[0] = 0

    def place(half, source):
        @pl.loop(0, valid_slots(table, half))
        def _(at):
            code = plan[half, at]

            @pl.when(code >= 0)
            def _():
                started[0] += 1
                rows = source.at[at, unit(core)]
                pltpu.make_async_copy(rows, out.at[code >> 2, unit(code & 3)], sem).start()

    for half in range(2):

        @pl.when(core == half)
        def _():
            place(half, own)

        @pl.when(core != half)
        def _():
            place(half, mate)

    @pl.loop(0, out.shape[0], unroll=4)
    def _(dev):
        out[dev, count * ROWS :, :] = tiles[dev]

    @pl.loop(0, started[0])
    def _(_):
        pltpu.make_async_copy(own.at[0, unit(0)], out.at[0, unit(0)], sem).wait()


def pack_first(count, table, plan, core, own, mate, tiles):
    wide_count = tiles.shape[0]
    return pl.pallas_call(
        functools.partial(first_kernel, count),
        out_shape=(
            jax.ShapeDtypeStruct((wide_count, count * ROWS + NOTES, LANES), jnp.bfloat16),
            jax.ShapeDtypeStruct((1,), jnp.int32),
        ),
        in_specs=[SMEM] * 3 + [ANY, ANY, VMEM],
        out_specs=(VMEM, SMEM),
        scratch_shapes=[pltpu.SMEM((1,), jnp.int32), pltpu.SemaphoreType.DMA],
        cost_estimate=pl.CostEstimate(flops=0, bytes_accessed=wide_count * count * NT * 4, transcendentals=0),
        name="pack_first",
    )(table, plan, core, own, mate, tiles)


def spill_kernel(base, table, core_ref, own, same, other, plan, fill, started, sem):
    core = core_ref[0]
    started[0] = 0

    @pl.loop(0, fill.shape[0])
    def _(dev):
        fill[dev] = 0

    for half in range(2):

        @pl.loop(0, valid_slots(table, half))
        def _(at):
            dev = owner_of(table[half, at])
            rank = fill[dev]
            fill[dev] = rank + 1
            plan[half, at] = jnp.where(rank < base, dev * 4 + rank, -1)

            @pl.when((rank >= base) & (core == half) & (started[0] < SPILL))
            def _():
                index = started[0]
                started[0] = index + 1
                pltpu.make_async_copy(own.at[at, unit(core)], same.at[index], sem).start()
                pltpu.make_async_copy(own.at[at, unit(1 - core)], other.at[index], sem).start()

    @pl.loop(0, 2 * started[0])
    def _(_):
        pltpu.make_async_copy(own.at[0, unit(0)], same.at[0], sem).wait()


def spill(base, wide_count, table, core, own):
    buffer = jax.ShapeDtypeStruct((SPILL, ROWS, LANES), jnp.bfloat16)
    return pl.pallas_call(
        functools.partial(spill_kernel, base),
        out_shape=(
            buffer,
            buffer,
            jax.ShapeDtypeStruct((2, table.shape[1] - 1), jnp.int32),
            jax.ShapeDtypeStruct((wide_count,), jnp.int32),
        ),
        in_specs=[SMEM, SMEM, ANY],
        out_specs=(VMEM, VMEM, SMEM, SMEM),
        scratch_shapes=[pltpu.SMEM((1,), jnp.int32), pltpu.SemaphoreType.DMA],
        cost_estimate=pl.CostEstimate(flops=0, bytes_accessed=2**20, transcendentals=0),
        name="spill",
    )(table, core, own)


def pack_kernel(base, table, plan, held, core_ref, own, mate, same, other, after, out, fill, theirs, started, taken, sem):
    core = core_ref[0]
    started[0] = 0

    @pl.loop(0, out.shape[0])
    def _(dev):
        fill[dev] = held[dev]
        theirs[dev] = 0

    def place(half, source, guests):
        @pl.loop(0, valid_slots(table, half))
        def _(at):
            code = plan[half, at]

            @pl.when(code >= 0)
            def _():
                started[0] += 1
                rows = source.at[at, unit(core)]
                pltpu.make_async_copy(rows, out.at[code >> 2, unit(code & 3)], sem).start()

        taken[0] = 0

        @pl.loop(0, valid_slots(table, 2 + half))
        def _(at):
            dev = owner_of(table[2 + half, at])
            rank = theirs[dev]
            theirs[dev] = rank + 1

            @pl.when(rank >= base)
            def _():
                index = taken[0]
                slot = fill[dev]
                taken[0] = index + 1

                @pl.when((index < SPILL) & (slot < base))
                def _():
                    fill[dev] = slot + 1
                    started[0] += 1
                    pltpu.make_async_copy(guests.at[index], out.at[dev, unit(slot)], sem).start()

    for half in range(2):

        @pl.when(core == half)
        def _():
            place(half, own, same)

        @pl.when(core != half)
        def _():
            place(half, mate, other)

    @pl.loop(0, started[0])
    def _(_):
        pltpu.make_async_copy(own.at[0, unit(0)], out.at[0, unit(0)], sem).wait()


def pack_planned(base, table, plan, held, core, own, mate, same, other, after):
    wide_count = held.shape[0]
    return pl.pallas_call(
        functools.partial(pack_kernel, base),
        out_shape=jax.ShapeDtypeStruct((wide_count, base * ROWS, LANES), jnp.bfloat16),
        in_specs=[SMEM] * 4 + [ANY] * 5,
        out_specs=VMEM,
        scratch_shapes=[
            pltpu.SMEM((wide_count,), jnp.int32),
            pltpu.SMEM((wide_count,), jnp.int32),
            pltpu.SMEM((1,), jnp.int32),
            pltpu.SMEM((1,), jnp.int32),
            pltpu.SemaphoreType.DMA,
        ],
        cost_estimate=pl.CostEstimate(flops=0, bytes_accessed=wide_count * base * NT * 4, transcendentals=0),
        name="pack_planned",
    )(table, plan, held, core, own, mate, same, other, after)


def table_notes(packed):
    owner = (packed >> LEN_BITS) + 1
    length = jnp.where(packed >= 0, packed & 0xFFFF, 0)
    parts = jnp.concatenate([owner >> 8, owner & 0xFF, length >> 8, length & 0xFF])
    rows = 3 * LANES - parts.shape[0]
    parts = jnp.pad(parts, (0, rows)).reshape(3, LANES)
    return jnp.pad(parts, ((NOTES - 3, 0), (0, 0)))


def read_slots(rows, count):
    notes = rows[::2, count * ROWS : count * ROWS + 3 * count + 1, 0].astype(jnp.float32).astype(jnp.int32)
    fields = notes[:, : 3 * count].reshape(-1, count, 3)
    station, length = fields[..., 0] - 1, fields[..., 1] * 256 + fields[..., 2]
    return station.reshape(-1), length.reshape(-1), notes[:, 3 * count]


def read_table(rows, slots, chips):
    parts = rows[:, -3:, :].astype(jnp.float32).astype(jnp.int32)
    parts = parts.reshape(rows.shape[0], -1)[:, : 4 * slots].reshape(chips, 2, 4, slots)
    return (parts[:, :, 0] * 256 + parts[:, :, 1] - 1).reshape(chips, 2 * slots)


def second_places(owner, column, base):
    chips, entries = owner.shape
    extra = MOST - base
    slots = entries // 2
    listed = owner >= 0
    dev = jnp.where(listed, owner // ST_DEV, -1)
    order = jnp.arange(entries, dtype=jnp.int32)
    earlier = order[None, :] < order[:, None]
    alike = (dev[:, :, None] == dev[:, None, :]) & earlier
    rank = jnp.sum(alike.astype(jnp.int32), axis=2)
    over = listed & (rank >= base)
    near = earlier & (order[None, :] // slots == order[:, None] // slots)
    index = jnp.sum((over[:, None, :] & near).astype(jnp.int32), axis=2)
    sent = over & (index < SPILL)
    guest = jnp.sum((alike & sent[:, None, :]).astype(jnp.int32), axis=2)
    host_dev = jnp.concatenate([dev[chips // 2 :], dev[: chips // 2]])
    host_held = jnp.sum((dev[:, :, None] == host_dev[:, None, :]).astype(jnp.int32), axis=2)
    slot = host_held + guest
    fits = sent & (slot < base)
    chip = jnp.arange(chips, dtype=jnp.int32)[:, None]
    host = (chip + chips // 2) % chips
    code = jnp.where(rank < base, chip * base + rank, chips * base + chip * extra + rank - base)
    code = jnp.where(fits, host * base + slot, code)
    local = column * ST_DEV + jnp.arange(ST_DEV, dtype=jnp.int32)
    chosen = owner[None] == local[:, None, None]
    return jnp.sum(jnp.where(chosen, code[None], 0), axis=(1, 2))


def whiten_kernel(
    part, parts, source, length, picks, got, more, first, twist, second, *refs
):
    token, held, spectra, sem, sems = refs[-5:]
    stops, rows = picks.shape
    white = refs[-6 - parts]
    payload = refs[-5 - parts : -5]
    token[0] = 0
    stations = held.shape[0]
    base = SLOTS[part]
    first_more = got.shape[0] // 2 * base
    batch = 8

    def fetch(rows, code, count, station):
        for seg in range(2):
            source_at = rows.at[2 * (code // count) + seg, unit(code % count)]
            pltpu.make_async_copy(source_at, held.at[station, unit(seg)], sems.at[station // batch]).start()

    @pl.loop(0, stations)
    def _(station):
        code = source[station]

        @pl.when(code < first_more)
        def _():
            fetch(got, code, base, station)

        @pl.when(code >= first_more)
        def _():
            fetch(more, code - first_more, MOST - base, station)

    row = lax.broadcasted_iota(jnp.int32, (2 * ROWS, LANES), 0)
    lane = lax.broadcasted_iota(jnp.int32, (2 * ROWS, LANES), 1)
    left = lax.broadcasted_iota(jnp.int32, (ROWS // 2, LANES), 1) < ROWS
    place = (2 * part + (row & 1)) * NT + (row >> 1) * LANES + lane

    def two_stations(station):
        sides = []
        for at in range(2):
            values = held[station + at].astype(jnp.float32)
            sides.append(jnp.where(place < length[station + at], values, 0.0).astype(jnp.bfloat16))
        values = jnp.concatenate(sides, 1)
        values = jnp.concatenate([values, values], 0)
        mixed = jnp.dot(first[...], values, preferred_element_type=jnp.float32)
        parts = []
        for at in range(2):
            for seg in range(2):
                real = mixed[2 * seg * ROWS : (2 * seg + 1) * ROWS, at * LANES : (at + 1) * LANES]
                imag = mixed[(2 * seg + 1) * ROWS : (2 * seg + 2) * ROWS, at * LANES : (at + 1) * LANES]
                turned_re = real * twist[0] + imag * twist[1]
                turned_im = imag * twist[0] - real * twist[1]
                parts.append(jnp.concatenate([turned_re, turned_im], 1))
        turned = jnp.concatenate(parts, 0)
        high = turned.astype(jnp.bfloat16)
        low = (turned - high.astype(jnp.float32)).astype(jnp.bfloat16)
        upper = jnp.dot(high, second[...], preferred_element_type=jnp.float32)
        lower = jnp.dot(low, second[:, :LANES], preferred_element_type=jnp.float32)
        spectrum = upper[:, :LANES] + (upper[:, LANES:] + lower)
        for at in range(2):
            for seg in range(2):
                begin = (2 * at + seg) * ROWS
                side = spectrum[begin : begin + ROWS]
                power = jnp.sum(side * side, axis=0, keepdims=True)
                power = (power + pltpu.roll(power, LANES // 2, 1)) * (1.0 / ROWS)
                scale = 1.0 / jnp.sqrt(power + 1e-06)
                side = side * scale
                upper, lower = side[: ROWS // 2], side[ROWS // 2 :]
                real = jnp.where(left, upper, pltpu.roll(lower, ROWS, 1))
                imag = jnp.where(left, pltpu.roll(upper, ROWS, 1), lower)
                spectra[station + at, seg, : ROWS // 2] = real.astype(jnp.bfloat16)
                spectra[station + at, seg, ROWS // 2 :] = imag.astype(jnp.bfloat16)

    @pl.loop(0, stations // batch)
    def _(at):
        these = held.at[pl.ds(at * batch, batch)]
        pltpu.make_async_copy(these, these, sems.at[at]).wait()
        for two in range(0, batch, 2):
            two_stations(batch * at + two)

    each = stops // parts
    for piece in range(parts):

        @pl.loop(0, each)
        def _(stop):
            for at in range(rows):
                row = spectra.at[picks[piece * each + stop, at]]
                pltpu.make_async_copy(row, payload[piece].at[stop, at], sem).start()

    whole = pltpu.make_async_copy(spectra, white, sems.at[0])
    whole.start()
    for piece in range(parts):
        pltpu.make_async_copy(payload[piece], payload[piece], sem).wait()
    whole.wait()


def whiten(part, parts, source, length, picks, got, more, tables, after):
    stops, rows = picks.shape
    piece = jax.ShapeDtypeStruct((stops // parts, rows, 2, ROWS, LANES), jnp.bfloat16)
    return pl.pallas_call(
        functools.partial(whiten_kernel, part, parts),
        out_shape=(jax.ShapeDtypeStruct((ST_DEV, 2, ROWS, LANES), jnp.bfloat16),)
        + (piece,) * parts
        + (jax.ShapeDtypeStruct((1,), jnp.int32),),
        in_specs=[SMEM, SMEM, SMEM, ANY, ANY, VMEM, VMEM, VMEM] + [ANY] * len(after),
        out_specs=(ANY,) * (1 + parts) + (SMEM,),
        scratch_shapes=[
            pltpu.VMEM((ST_DEV, 2 * ROWS, LANES), jnp.bfloat16),
            pltpu.VMEM((ST_DEV, 2, ROWS, LANES), jnp.bfloat16),
            pltpu.SemaphoreType.DMA,
            pltpu.SemaphoreType.DMA((ST_DEV // 8,)),
        ],
        cost_estimate=pl.CostEstimate(flops=2**20, bytes_accessed=2**18, transcendentals=0),
        name="whiten",
    )(source, length, picks, got, more, *tables, *after)


def cross_rows(near_pick, near, far, cross, fresh, ready):
    stops, rows = near_pick.shape
    side = rows // 2
    step = 16
    half = ROWS // 2

    @pl.loop(0, stops)
    def _(stop):
        ready(stop)
        for two in range(2):
            first = two * side
            own = [near_pick[stop, first + i] for i in range(side)]

            @pl.loop(0, half // step)
            def _(chunk):
                real = pl.ds(pl.multiple_of(chunk * step, step), step)
                imag = pl.ds(pl.multiple_of(half + chunk * step, step), step)

                def both(ref, row):
                    return [
                        (ref[row, s, real, :].astype(jnp.float32), ref[row, s, imag, :].astype(jnp.float32))
                        for s in range(2)
                    ]

                here = [both(near, own[i]) for i in range(side)]
                for j in range(side):
                    there = both(far.at[stop], first + j)
                    for i in range(side):
                        pair = ((stop * 2 + two) * side + i) * side + j
                        total_re = sum(n[0] * f[0] + n[1] * f[1] for n, f in zip(here[i], there))
                        total_im = sum(n[1] * f[0] - n[0] * f[1] for n, f in zip(here[i], there))
                        for total, add in ((total_re, 0), (total_im, half)):
                            at = pl.ds(pl.multiple_of(pair * ROWS + add + chunk * step, step), step)
                            if fresh:
                                cross[at, :] = total
                            else:
                                cross[at, :] += total


def lag_product(cross, tables, last, out, edge, exact):
    pairs = out.shape[0]
    group = 8 if exact else 16
    depth = group * LANES
    half = LAGS // 2
    turns = ROWS // 2 // group

    def product(turn, even):
        base = turn * group
        slabs = [cross[pl.ds(base + k, pairs, stride=ROWS), :] for k in range(group)]
        high = [slab.astype(jnp.bfloat16) for slab in slabs]
        if even:
            total = edge[...]
            for k in range(group):
                total += (slabs[k] if exact else high[k].astype(jnp.float32)) * last[base + k]
            edge[...] = total
        rows = jnp.concatenate(high, 1)
        if exact:
            low = [(slab - part.astype(jnp.float32)).astype(jnp.bfloat16) for slab, part in zip(slabs, high)]
            rows = jnp.concatenate([rows, jnp.concatenate(low, 1)], 0)
        part = jnp.dot(
            rows,
            tables[pl.ds(pl.multiple_of(base * LANES, depth), depth), :],
            preferred_element_type=jnp.float32,
        )
        return part[:pairs] + part[pairs:] if exact else part

    @pl.loop(0, turns)
    def _(turn):
        out[:, :half] += product(turn, True)

    @pl.loop(turns, 2 * turns)
    def _(turn):
        out[:, half:] += product(turn, False)


def first_lag_kernel(stops, near_pick, white, home, *refs):
    far_in = refs[: stops - 1]
    table, last, out, edge, near, far, cross, tables, sem, sems, table_sem = refs[stops - 1 :]
    load = pltpu.make_async_copy(white, near, sem)
    load.start()
    pltpu.make_async_copy(home, far.at[0], sems.at[0]).start()
    for stop in range(1, stops):
        pltpu.make_async_copy(far_in[stop - 1], far.at[stop], sems.at[stop]).start()
    load_table = pltpu.make_async_copy(table, tables, table_sem)
    load_table.start()
    out[...] = jnp.zeros_like(out)
    edge[...] = jnp.zeros_like(edge)
    load.wait()

    def ready(stop):
        pltpu.make_async_copy(far.at[stop], far.at[stop], sems.at[stop]).wait()

    cross_rows(near_pick, near, far, cross, True, ready)
    load_table.wait()
    lag_product(cross, tables, last, out, edge, True)


def last_lag_kernel(
    near_pick, far_at, begun, begun_edge, white, far_in, table, last, mask,
    result, near, far, cross, out, edge, tables, sem, sems, table_sem,
):
    stops = near_pick.shape[0]
    pairs = out.shape[0]
    half = LAGS // 2
    load = pltpu.make_async_copy(white, near, sem.at[0])
    load.start()
    for stop in range(stops):
        pltpu.make_async_copy(far_in.at[far_at[stop]], far.at[stop], sems.at[stop]).start()
    load_table = pltpu.make_async_copy(table, tables, table_sem)
    load_table.start()
    before = [pltpu.make_async_copy(begun, out, sem.at[1]), pltpu.make_async_copy(begun_edge, edge, sem.at[2])]
    for copy in before:
        copy.start()
    load.wait()

    def ready(stop):
        pltpu.make_async_copy(far.at[stop], far.at[stop], sems.at[stop]).wait()

    cross_rows(near_pick, near, far, cross, True, ready)
    load_table.wait()
    for copy in before:
        copy.wait()
    lag_product(cross, tables, last, out, edge, False)
    first_lag = jnp.sum(edge[...], axis=1, keepdims=True)
    lane = lax.broadcasted_iota(jnp.int32, (pairs, LANES), 1)
    mirror = (LANES - lane) % LANES
    first = lane == 0
    listed = mask[...]
    count = half // LANES
    back, ahead = [], []
    for block in range(count):
        even = out[:, block * LANES : (block + 1) * LANES]
        odd = out[:, half + block * LANES : half + (block + 1) * LANES]
        if block == 0:
            first_lag = first_lag + odd
            odd = jnp.where(first, 0.0, odd)
        back.append(even - odd)
        ahead.append(even + odd)
    for block in range(count):
        turned = jnp.take_along_axis(back[count - 1 - block], mirror, axis=1)
        start = first_lag if block == 0 else back[count - block]
        lags = pl.ds(block * LANES, LANES)
        result[:, :, lags] = (jnp.where(first, start, turned) * listed).reshape(result.shape[:2] + (LANES,))
        lags = pl.ds(half + block * LANES, LANES)
        result[:, :, lags] = (ahead[block] * listed).reshape(result.shape[:2] + (LANES,))


def lag_scratch(white, stops, pairs, table):
    return [
        pltpu.VMEM(white.shape, jnp.bfloat16),
        pltpu.VMEM((stops, 8, 2, ROWS, LANES), jnp.bfloat16),
        pltpu.VMEM((pairs * ROWS, LANES), jnp.float32),
    ], [pltpu.VMEM(table.shape, jnp.bfloat16)]


def lagged_first(near_pick, white, home, far, table, last):
    stops, rows = near_pick.shape
    pairs = stops * rows * rows // 2
    scratch, table_scratch = lag_scratch(white, stops, pairs, table)
    return pl.pallas_call(
        functools.partial(first_lag_kernel, stops),
        out_shape=(
            jax.ShapeDtypeStruct((pairs, LAGS), jnp.float32),
            jax.ShapeDtypeStruct((pairs, LANES), jnp.float32),
        ),
        in_specs=[SMEM] + [ANY] * (stops + 2) + [VMEM],
        out_specs=(VMEM, VMEM),
        scratch_shapes=scratch
        + table_scratch
        + [pltpu.SemaphoreType.DMA, pltpu.SemaphoreType.DMA((stops,)), pltpu.SemaphoreType.DMA],
        compiler_params=pltpu.CompilerParams(vmem_limit_bytes=LAG_VMEM),
        cost_estimate=pl.CostEstimate(
            flops=4 * pairs * NF * LAGS, bytes_accessed=16 * 1024 * 1024, transcendentals=0
        ),
        name="lagged_first",
    )(near_pick, white, home, *far, table, last)


def lagged_last(near_pick, far_at, begun, edge, white, far, table, last, mask):
    stops, rows = near_pick.shape
    side = rows // 2
    pairs = mask.shape[0]
    scratch, table_scratch = lag_scratch(white, stops, pairs, table)
    return pl.pallas_call(
        last_lag_kernel,
        out_shape=jax.ShapeDtypeStruct((pairs // side, side, LAGS), jnp.float32),
        in_specs=[SMEM, SMEM] + [ANY] * 5 + [VMEM, VMEM],
        out_specs=VMEM,
        scratch_shapes=scratch
        + [pltpu.VMEM((pairs, LAGS), jnp.float32), pltpu.VMEM((pairs, LANES), jnp.float32)]
        + table_scratch
        + [pltpu.SemaphoreType.DMA((3,)), pltpu.SemaphoreType.DMA((stops,)), pltpu.SemaphoreType.DMA],
        compiler_params=pltpu.CompilerParams(vmem_limit_bytes=LAG_VMEM),
        cost_estimate=pl.CostEstimate(
            flops=2 * pairs * NF * LAGS, bytes_accessed=16 * 1024 * 1024, transcendentals=0
        ),
        name="lagged_last",
    )(near_pick, far_at, begun, edge, white, far, table, last, mask)


def empty(shape):
    return pl.pallas_call(
        lambda out: None,
        out_shape=jax.ShapeDtypeStruct(shape, jnp.bfloat16),
        out_specs=ANY,
        name="empty",
    )()


def on_device(records, lengths, owners, own_pick, visit_pick, pair_mask):
    wide_count = lax.axis_size("wide")
    stops = lax.axis_size("blk")
    column = lax.axis_index("wide")
    group = lax.axis_index("blk")
    core = column % 2
    slots = records.shape[1]
    steps = jnp.arange(stops, dtype=jnp.int32)
    core_at = core.reshape(1)

    def flip(bits):
        return [(i, i ^ bits) for i in range(wide_count)]

    def across(shard, bits):
        return lax.ppermute(shard, "wide", flip(bits))

    over = wide_count // 2
    packed = jnp.where(owners[0] >= 0, (owners[0] << LEN_BITS) + lengths[0], -1)
    counted = jnp.concatenate([packed, jnp.sum((packed >= 0).astype(jnp.int32), keepdims=True)])
    others = [across(counted, bits) for bits in (1, over, over + 1)]
    table = jnp.where(
        core == 0,
        jnp.stack([counted, others[0], others[1], others[2]]),
        jnp.stack([others[0], counted, others[2], others[1]]),
    )

    blocks = records[0].reshape(slots, SEG, ROWS, LANES)

    def halves(part):
        return blocks[:, 2 * part : 2 * part + 2].transpose(0, 2, 1, 3).reshape(slots, 2 * ROWS, LANES)

    def send(payload):
        return lax.all_to_all(payload, "wide", split_axis=0, concat_axis=0, tiled=True)

    own_a = halves(0)
    mate_a = across(own_a, 1)
    base_a, base_b = SLOTS
    plan_a, tiles, _ = plan_rows(base_a, base_b, wide_count, table, table_notes(packed))
    load_a, token = pack_first(base_a, table, plan_a, core_at, own_a, mate_a, tiles)
    got_a = send(load_a)
    own_b = jnp.where(token[0] >= 0, halves(1), 0.0)
    mate_b = across(own_b, 1)
    same_b, other_b, plan, held = spill(base_b, wide_count, table, core_at, own_b)
    same_b, other_b = across(same_b, over), across(other_b, over + 1)
    visits = jnp.where(token[0] >= 0, visit_pick[0, 0].reshape(1, stops, -1), 0)
    bit = 1
    while bit < stops:
        theirs = lax.ppermute(visits, "blk", [(i, i ^ bit) for i in range(stops)])
        upper = (group // bit) % 2 == 1
        visits = jnp.concatenate([jnp.where(upper, theirs, visits), jnp.where(upper, visits, theirs)])
        bit *= 2
    by_dest = visits[steps, (steps - group) % stops]
    by_stop = by_dest[(steps + group) % stops]
    load_b = pack_planned(base_b, table, plan, held, core_at, own_b, mate_b, same_b, other_b, by_stop)
    got_b = send(load_b)

    def late_rows(low, own, mate):
        return send(pack_rows(low, MOST - low, wide_count, table, core_at, own, mate))

    def late():
        first = late_rows(base_a, own_a, mate_a)
        second = late_rows(base_b, own_b, mate_b)
        return (first, second) + read_slots(first, MOST - base_a)[:2]

    def never():
        count = wide_count // 2 * (MOST - base_a)
        rows = [empty((wide_count, (MOST - base) * ROWS + NOTES, LANES)) for base in SLOTS]
        return rows[0], rows[1], jnp.full((count,), -1, jnp.int32), jnp.zeros((count,), jnp.int32)

    station, length, spilled = read_slots(got_a, base_a)
    more_a, more_b, more_station, more_length = lax.cond(jnp.max(spilled) > 0, late, never)
    station = jnp.concatenate([station, more_station])
    length = jnp.concatenate([length, more_length])
    chosen = station[None, :] == jnp.arange(ST_DEV, dtype=jnp.int32)[:, None]
    codes = jnp.arange(station.shape[0], dtype=jnp.int32)
    source_a = jnp.sum(jnp.where(chosen, codes[None], 0), axis=1)
    length = jnp.sum(jnp.where(chosen, length[None], 0), axis=1)

    tables = [jnp.asarray(table) for table in transform_tables()]
    near_pick = own_pick[0, 0].reshape(stops, -1)
    white_a, home, *payload_a, _ = whiten(0, stops, source_a, length, by_stop, got_a, more_a, tables, [])
    far_a = [
        lax.ppermute(payload_a[stop - 1][0], "blk", [(i, (i + stop) % stops) for i in range(stops)])
        for stop in range(1, stops)
    ]
    source_b = second_places(read_table(got_a, slots, wide_count // 2), column, base_b)
    white_b, payload_b, _ = whiten(1, 1, source_b, length, by_dest, got_b, more_b, tables, far_a)
    far_b = lax.all_to_all(payload_b, "blk", split_axis=0, concat_axis=0, tiled=True)

    far_at = (group - steps) % stops
    mask = pair_mask[0, 0].astype(jnp.float32).reshape(-1, 1)
    lags, last = (jnp.asarray(table) for table in lag_tables())
    begun, edge = lagged_first(near_pick, white_a, home[0], far_a, lags, last)
    result = lagged_last(near_pick, far_at, begun, edge, white_b, far_b, lags, last, mask)
    return result.reshape((1, 1) + pair_mask.shape[2:] + (LAGS,))


def solution(mesh):
    return jax.shard_map(
        on_device,
        mesh=mesh,
        in_specs=(
            P("blk", "wide", None, None),
            P("blk", "wide"),
            P("blk", "wide"),
            P("blk", "wide", None, None, None),
            P("blk", "wide", None, None, None),
            P("blk", "wide", None, None, None, None),
        ),
        out_specs=P("blk", "wide", None, None, None, None, None),
        check_vma=False,
    )
```
